32 devices in a mesh: seq: 8 (over z, x), kv: 4 (over y, core).
Axes of the slice: x: 2, y: 2, z: 4, core: 2. Of those that a mesh axis runs over, the one named last changes fastest.
Arguments:
- queries: bfloat16 [4096, 1024], P('seq'), may hold values from -88 to 88
- keys: bfloat16 [64, 64, 1024], P('seq', 'kv'), may hold values from -4 to 4
- values: bfloat16 [64, 64, 1024], P('seq', 'kv'), may hold values from -6 to 6
- layout: int32 [64, 15], replicated, may hold values from -1 to 63, as said below
- grad_out: bfloat16 [4096, 1024], P('seq'), may hold values from -6 to 6
Outputs:
- attended: bfloat16 [4096, 1024], P('seq')
- grad_q: bfloat16 [4096, 1024], P('seq')
- grad_k: bfloat16 [64, 64, 1024], P('seq', 'kv')
- grad_v: bfloat16 [64, 64, 1024], P('seq', 'kv')
The draws below stay inside these ranges and needn't reach their ends.
Inputs may be any that keep to these rules, and one draw needn't show every extreme that they name: `layout`: write query block b as 8 w + i with 0 <= i < 8. Row b lists the summary block of each window 0 .. w - 1 in order of windows, then the blocks 8 w .. 8 w + i in order, then -1 in the remaining entries. The summary block of window u is one of the blocks 8 u .. 8 u + 7 and is the same in every row.
All inputs are finite; a program needn't handle non-finite values.
Results may differ from the reference program's by a relative error of at most 0.038.
Values may be sent and summed in bfloat16 or wider, within the bound.
No kernel may reach another device: no remote copies, remote signals or barrier semaphores. Data moves between devices by JAX's collectives and lax.ppermute only.
A program may use at most 128 MiB of HBM per device.

```python
import math
import jax
import jax.numpy as jnp
from jax import lax

HEADS = 8
HD = 128
BLK = 64
WB = 8
TOK_DEV = 512
DW = 1024
SEQ = 4096
NBLK = 64
KMAX = 15
N_SEQ = 8


def draw_queries(key, part):
    base = jnp.clip(jax.random.normal(jax.random.fold_in(key, 1), (SEQ, HEADS * HD), jnp.float32), -4.0, 4.0)
    return base.astype(jnp.bfloat16)


def draw_keys(key, part):
    base = jnp.clip(jax.random.normal(jax.random.fold_in(key, 2), (NBLK, BLK, HEADS * HD), jnp.float32), -4.0, 4.0)
    return base.astype(jnp.bfloat16)


def draw_layout(key, part):
    spot = jax.random.randint(jax.random.fold_in(key, 3), (N_SEQ,), 0, WB).astype(jnp.int32)
    summary = jnp.arange(N_SEQ, dtype=jnp.int32) * WB + spot
    block = jnp.arange(NBLK, dtype=jnp.int32)[:, None]
    entry = jnp.arange(KMAX, dtype=jnp.int32)[None, :]
    window = block // WB
    inner = block % WB
    earlier = summary[jnp.minimum(entry, N_SEQ - 1)]
    local_block = window * WB + entry - window
    listed = jnp.where(entry < window, earlier, jnp.where(entry <= window + inner, local_block, -1))
    return listed.astype(jnp.int32)


def block_scale(key, extent, split, least, top_value):
    def one(dim, shards_of):
        heights = jax.random.uniform(jax.random.fold_in(jax.random.fold_in(key, 6), dim), (shards_of,), jnp.float32, least / len(split), top_value / len(split))
        return jnp.repeat(jnp.exp(heights), extent[dim] // shards_of).reshape((-1,) + (1,) * (len(extent) - dim - 1))

    factor_of = one(*split[0])
    for cut in split[1:]:
        factor_of = factor_of * one(*cut)
    return factor_of


def centred(own_key, extent, width, reach, split=(), kind=jnp.bfloat16):
    drawn = width * jax.random.normal(own_key, extent, jnp.float32)
    if split:
        drawn = drawn * block_scale(own_key, extent, split, -0.22, 0.18)
    return jnp.clip(drawn, -reach, reach).astype(kind)


def setup_inputs(seed: int = 0) -> dict:
    key_list = jax.random.split(jax.random.key(seed), 6)
    return {
        "queries": draw_queries(jax.random.fold_in(key_list[5], 71), 0),
        "keys": draw_keys(jax.random.fold_in(key_list[5], 71), 0),
        "values": centred(key_list[2], (NBLK, BLK, DW), 1.0, 6.0, ((0, 8), (1, 4))),
        "layout": draw_layout(jax.random.fold_in(key_list[5], 71), 0),
        "grad_out": centred(key_list[4], (SEQ, DW), 1.0, 6.0, ((0, 8),)),
    }


def reference(queries, keys, values, layout, grad_out):
    score_scale = 1.0 / math.sqrt(HD)
    feat_width = HEADS * HD
    list_len = layout.shape[1]

    def window_step(carry, window):
        key_acc, value_acc = carry
        query_rows = lax.dynamic_slice_in_dim(queries, window * TOK_DEV, TOK_DEV, 0).astype(jnp.float32).reshape(WB, BLK, HEADS, HD)
        grad_rows = lax.dynamic_slice_in_dim(grad_out, window * TOK_DEV, TOK_DEV, 0).astype(jnp.float32).reshape(WB, BLK, HEADS, HD)
        entries = lax.dynamic_slice_in_dim(layout, window * WB, WB, 0)
        safe_idx = jnp.maximum(entries, 0).astype(jnp.int32)
        key_blocks = keys[safe_idx].astype(jnp.float32).reshape(WB, list_len, BLK, HEADS, HD)
        value_blocks = values[safe_idx].astype(jnp.float32).reshape(WB, list_len, BLK, HEADS, HD)
        own_block = (window * WB + jnp.arange(WB, dtype=jnp.int32)).astype(jnp.int32)[:, None]
        token_pos = jnp.arange(BLK, dtype=jnp.int32)
        causal = token_pos[None, :] <= token_pos[:, None]
        earlier = (entries >= 0) & (entries < own_block)
        same = entries == own_block
        pair_ok = earlier[:, None, :, None] | same[:, None, :, None] & causal[None, :, None, :]
        valid_pair = pair_ok[:, None]
        raw_score = jnp.einsum('bihd,bkjhd->bhikj', query_rows, key_blocks) * score_scale
        row_peak = lax.optimization_barrier(jnp.max(jnp.where(valid_pair, raw_score, -jnp.inf), axis=(3, 4), keepdims=True))
        weight = jnp.where(valid_pair, jnp.exp(raw_score - row_peak), 0.0)
        row_total = lax.optimization_barrier(jnp.sum(weight, axis=(3, 4), keepdims=True))
        weight_b = lax.optimization_barrier(weight.astype(jnp.bfloat16)).astype(jnp.float32)
        out_sum = jnp.einsum('bhikj,bkjhd->bihd', weight_b, value_blocks)
        total_rows = jnp.transpose(row_total[:, :, :, 0, 0], (0, 2, 1))[..., None]
        attended = (out_sum / total_rows).astype(jnp.bfloat16)
        att_f = attended.astype(jnp.float32)
        row_delta = lax.optimization_barrier(jnp.sum(grad_rows * att_f, axis=3))
        prob = jnp.where(valid_pair, jnp.exp(raw_score - row_peak) / row_total, 0.0)
        grad_prob = jnp.einsum('bihd,bkjhd->bhikj', grad_rows, value_blocks)
        delta_wide = jnp.transpose(row_delta, (0, 2, 1))[:, :, :, None, None]
        grad_score = score_scale * prob * (grad_prob - delta_wide)
        grad_score = lax.optimization_barrier(grad_score.astype(jnp.bfloat16)).astype(jnp.float32)
        prob_b = lax.optimization_barrier(prob.astype(jnp.bfloat16)).astype(jnp.float32)
        query_grad = jnp.einsum('bhikj,bkjhd->bihd', grad_score, key_blocks)
        key_grad = jnp.einsum('bhikj,bihd->bkjhd', grad_score, query_rows)
        value_grad = jnp.einsum('bhikj,bihd->bkjhd', prob_b, grad_rows)
        flat_idx = safe_idx.reshape(-1)
        key_acc = key_acc.at[flat_idx].add(key_grad.reshape(WB * list_len, BLK, feat_width))
        value_acc = value_acc.at[flat_idx].add(value_grad.reshape(WB * list_len, BLK, feat_width))
        outputs = (attended.reshape(TOK_DEV, feat_width), query_grad.astype(jnp.bfloat16).reshape(TOK_DEV, feat_width))
        return ((key_acc, value_acc), outputs)
    start_acc = (jnp.zeros((NBLK, BLK, feat_width), jnp.float32), jnp.zeros((NBLK, BLK, feat_width), jnp.float32))
    (key_acc, value_acc), (att_all, qgrad_all) = lax.scan(window_step, start_acc, jnp.arange(N_SEQ, dtype=jnp.int32))
    attended = att_all.reshape(SEQ, feat_width)
    grad_q = qgrad_all.reshape(SEQ, feat_width)
    return (attended, grad_q, key_acc.astype(jnp.bfloat16), value_acc.astype(jnp.bfloat16))
```

```python
import functools
import math

import jax
import jax.numpy as jnp
from jax import lax
from jax.experimental import pallas as pl
from jax.experimental.pallas import tpu as pltpu
from jax.sharding import PartitionSpec as P

HEADS = 8
HIDDEN = -1e30
NT = (((1,), (1,)), ((), ()))
NN = (((1,), (0,)), ((), ()))
TN = (((0,), (0,)), ((), ()))


def dot(a, b, dims):
    return lax.dot_general(a, b, dims, preferred_element_type=jnp.float32)


def attention_kernel(
    members, blk_len, part_tok, tile, place, q_ref, g_ref, *refs
):
    local_refs = [refs[2 * j : 2 * j + 2] for j in range(members)]
    far_refs = refs[2 * members : 3 * members]
    att_ref, gq_ref, gk_ref, gv_ref, far_grad_ref, bias_ref = refs[3 * members :]
    rows, head_dim = q_ref.shape
    near = local_refs[0][0].shape[0]
    away = far_refs[0].shape[1]
    width = near + away
    score_scale = 1.0 / math.sqrt(head_dim)

    @pl.when(pl.program_id(0) == 0)
    def _():
        member, window = place[0], place[1]
        row = lax.broadcasted_iota(jnp.int32, (rows, near), 0)
        col = lax.broadcasted_iota(jnp.int32, (rows, near), 1)
        far_step = lax.broadcasted_iota(jnp.int32, (rows, away), 1) // part_tok + 1
        far_ok = (far_step <= window) & (far_step < away // part_tok)
        far_bias = jnp.where(far_ok, 0.0, HIDDEN)
        for j in range(members):
            key_pos = (col // part_tok) * blk_len + (member ^ j) * part_tok + col % part_tok
            bias_ref[:, j * width : j * width + near] = jnp.where(key_pos <= row, 0.0, HIDDEN)
            bias_ref[:, j * width + near : (j + 1) * width] = far_bias

    keys = jnp.concatenate(
        [part for j in range(members) for part in (local_refs[j][0][...], far_refs[j][0])], axis=0
    )
    values = jnp.concatenate(
        [part for j in range(members) for part in (local_refs[j][1][...], far_refs[j][1])], axis=0
    )
    key_grad = jnp.zeros((width, head_dim), jnp.float32)
    value_grad = jnp.zeros((width, head_dim), jnp.float32)
    for start in range(0, rows, tile):
        here = pl.ds(start, tile)
        query = q_ref[here, :]
        grad = g_ref[here, :]
        raw = dot(query, keys, NT) * (score_scale * math.log2(math.e)) + bias_ref[here, :]
        peak = jnp.max(raw, axis=1, keepdims=True)
        weight = jnp.exp2(raw - peak)
        total = jnp.sum(weight, axis=1, keepdims=True)
        inverse = 1.0 / total
        summed = dot(weight.astype(jnp.bfloat16), values, NN)
        attended = (summed * inverse).astype(jnp.bfloat16)
        att_ref[here, :] = attended
        drift = jnp.sum(
            grad.astype(jnp.float32) * attended.astype(jnp.float32), axis=1, keepdims=True
        )
        moved = weight * (dot(grad, values, NT) - drift)
        gq_ref[here, :] = (
            dot(moved.astype(jnp.bfloat16), keys, NN) * (inverse * score_scale)
        ).astype(jnp.bfloat16)
        own_score = (moved[:, :width] * (inverse * score_scale)).astype(jnp.bfloat16)
        own_prob = (weight[:, :width] * inverse).astype(jnp.bfloat16)
        key_grad += dot(own_score, query, TN)
        value_grad += dot(own_prob, grad, TN)
    gk_ref[...] = key_grad[:near]
    gv_ref[...] = value_grad[:near]
    far_grad_ref[0] = key_grad[near:].astype(jnp.bfloat16)
    far_grad_ref[1] = value_grad[near:].astype(jnp.bfloat16)


def attention(place, queries, grad_out, local_parts, far_parts, blk_len, part_tok):
    rows, feat_width = queries.shape
    head_dim = feat_width // HEADS
    near = local_parts[0][0].shape[0]
    away = far_parts[0].shape[1]
    members = len(local_parts)
    column = pl.BlockSpec((rows, head_dim), lambda h, place: (0, h))
    near_spec = pl.BlockSpec((near, head_dim), lambda h, place: (0, h))
    far_spec = pl.BlockSpec((2, away, head_dim), lambda h, place: (0, 0, h))
    pairs = rows * members * (near + away) * HEADS
    return pl.pallas_call(
        functools.partial(attention_kernel, members, blk_len, part_tok, min(rows, 256)),
        grid_spec=pltpu.PrefetchScalarGridSpec(
            num_scalar_prefetch=1,
            grid=(HEADS,),
            in_specs=[column, column] + [near_spec] * (2 * members) + [far_spec] * members,
            out_specs=[column, column, near_spec, near_spec, far_spec],
            scratch_shapes=[pltpu.VMEM((rows, members * (near + away)), jnp.float32)],
        ),
        out_shape=[
            jax.ShapeDtypeStruct((rows, feat_width), jnp.bfloat16),
            jax.ShapeDtypeStruct((rows, feat_width), jnp.bfloat16),
            jax.ShapeDtypeStruct((near, feat_width), jnp.float32),
            jax.ShapeDtypeStruct((near, feat_width), jnp.float32),
            jax.ShapeDtypeStruct((2, away, feat_width), jnp.bfloat16),
        ],
        compiler_params=pltpu.CompilerParams(vmem_limit_bytes=56 * 1024 * 1024),
        cost_estimate=pl.CostEstimate(
            flops=10 * pairs * head_dim, bytes_accessed=16 * rows * feat_width, transcendentals=pairs
        ),
    )(
        place,
        queries,
        grad_out,
        *[part for pair in local_parts for part in pair],
        *far_parts,
    )


def shards(queries, keys, values, layout, grad_out):
    seq_count = lax.axis_size("seq")
    seq_index = lax.axis_index("seq")
    members = lax.axis_size("kv")
    kv_index = lax.axis_index("kv")
    tok_rows, feat_width = queries.shape
    blocks, part_tok = (keys.shape[0], keys.shape[1])
    blk_len = part_tok * members
    last_row = layout[layout.shape[0] - 1]
    pick_window = jnp.minimum(seq_index, seq_count - 2)
    summary_local = jnp.clip(last_row[pick_window] - seq_index * blocks, 0, blocks - 1)
    own_pair = jnp.stack(
        [
            lax.dynamic_index_in_dim(keys, summary_local, 0, keepdims=False),
            lax.dynamic_index_in_dim(values, summary_local, 0, keepdims=False),
        ]
    )

    def swap(part, step):
        return lax.ppermute(part, "kv", [(m, m ^ step) for m in range(members)])

    def spread(part):
        parts = {0: part}
        step = members // 2
        while step:
            parts.update({j ^ step: swap(parts[j], step) for j in list(parts)})
            step //= 2
        return [parts[j] for j in range(members)]

    arrived = [
        lax.ppermute(own_pair, "seq", [(s, s + d) for s in range(seq_count - d)])
        for d in range(1, seq_count)
    ]
    key_parts = spread(keys.reshape(blocks * part_tok, feat_width))
    value_parts = spread(values.reshape(blocks * part_tok, feat_width))
    far_own = jnp.stack(arrived + [jnp.zeros_like(own_pair)], axis=1).reshape(
        2, seq_count * part_tok, feat_width
    )
    far_parts = spread(far_own)
    place = jnp.stack([kv_index, seq_index]).astype(jnp.int32)
    attended, grad_q, near_k, near_v, far_grad = attention(
        place, queries, grad_out, list(zip(key_parts, value_parts)), far_parts, blk_len, part_tok
    )
    far_grad = far_grad.reshape(2, seq_count, part_tok, feat_width)
    returned = [
        lax.ppermute(far_grad[:, d - 1], "seq", [(s, s - d) for s in range(d, seq_count)])
        for d in range(1, seq_count)
    ]
    extra = functools.reduce(lambda a, b: a + b, [part.astype(jnp.float32) for part in returned])
    chosen = (jnp.arange(blocks) == summary_local)[:, None, None]

    def finish(near_grad, far_term):
        near_grad = near_grad.reshape(blocks, part_tok, feat_width)
        return (near_grad + jnp.where(chosen, far_term[None], 0.0)).astype(jnp.bfloat16)

    return (attended, grad_q, finish(near_k, extra[0]), finish(near_v, extra[1]))


def solution(mesh):
    return jax.shard_map(
        shards,
        mesh=mesh,
        in_specs=(P("seq", None), P("seq", "kv", None), P("seq", "kv", None), P(), P("seq", None)),
        out_specs=(P("seq", None), P("seq", None), P("seq", "kv", None), P("seq", "kv", None)),
        check_vma=False,
    )
```

```python
import functools
import math

import jax
import jax.numpy as jnp
from jax import lax
from jax.experimental import pallas as pl
from jax.experimental.pallas import tpu as pltpu
from jax.sharding import PartitionSpec as P

HEADS = 8
COLUMNS = 2
HIDDEN = -1e30
NT = (((1,), (1,)), ((), ()))
NN = (((1,), (0,)), ((), ()))
TN = (((0,), (0,)), ((), ()))
LIMIT = pltpu.CompilerParams(vmem_limit_bytes=56 * 1024 * 1024)


def dot(a, b, dims):
    return lax.dot_general(a, b, dims, preferred_element_type=jnp.float32)


def base2_scale(head_dim):
    return math.log2(math.e) / math.sqrt(head_dim)


def pick_kernel(place, keys_ref, values_ref, pair_ref):
    pair_ref[0] = keys_ref[0]
    pair_ref[1] = values_ref[0]


def pick_pair(place, keys, values):
    _, part_tok, feat_width = keys.shape
    one = pl.BlockSpec((1, part_tok, feat_width), lambda i, place: (place[2], 0, 0))
    return pl.pallas_call(
        pick_kernel,
        grid_spec=pltpu.PrefetchScalarGridSpec(
            num_scalar_prefetch=1,
            grid=(1,),
            in_specs=[one, one],
            out_specs=pl.BlockSpec((2, part_tok, feat_width), lambda i, place: (0, 0, 0)),
        ),
        out_shape=jax.ShapeDtypeStruct((2, part_tok, feat_width), keys.dtype),
    )(place, keys, values)


def near_tiles(rows, near):
    half = rows // 2
    return [(0, half, near // 2), (half, half, near)]


def fill_near_bias(place, bias_ref, members, near, blk_len, part_tok):
    rows = bias_ref.shape[0]
    for start, count, used in near_tiles(rows, near):
        row = start + lax.broadcasted_iota(jnp.int32, (count, used), 0)
        col = lax.broadcasted_iota(jnp.int32, (count, used), 1)
        for j in range(members):
            key_pos = (col // part_tok) * blk_len + (place[0] ^ j) * part_tok + col % part_tok
            bias_ref[start : start + count, j * used : (j + 1) * used] = jnp.where(
                key_pos <= row, 0.0, HIDDEN
            )


def near_forward_kernel(members, blk_len, part_tok, place, q_ref, *refs):
    parts = refs[: 2 * members]
    sum_ref, stat_ref, bias_ref = refs[2 * members :]
    rows, head_dim = q_ref.shape
    near = parts[0].shape[0]

    @pl.when(pl.program_id(0) == 0)
    def _():
        fill_near_bias(place, bias_ref, members, near, blk_len, part_tok)

    for start, count, used in near_tiles(rows, near):
        here = pl.ds(start, count)
        keys = jnp.concatenate([ref[:used] for ref in parts[0::2]], axis=0)
        values = jnp.concatenate([ref[:used] for ref in parts[1::2]], axis=0)
        raw = dot(q_ref[here, :], keys, NT) * base2_scale(head_dim)
        raw += bias_ref[here, : members * used]
        peak = jnp.max(raw, axis=1, keepdims=True)
        weight = jnp.exp2(raw - peak)
        stat_ref[0, here, 0:1] = peak
        stat_ref[0, here, 1:2] = jnp.sum(weight, axis=1, keepdims=True)
        sum_ref[here, :] = dot(weight.astype(jnp.bfloat16), values, NN)


def far_kernel(members, place, q_ref, g_ref, sum_ref, stat_ref, *refs):
    parts = refs[: COLUMNS * members]
    att_ref, gq_ref, stat_out_ref = refs[COLUMNS * members : COLUMNS * members + 3]
    grad_refs = refs[COLUMNS * members + 3 :]
    rows, head_dim = q_ref.shape
    steps, _, part_tok, _ = parts[0].shape
    span = steps * part_tok
    width = COLUMNS * span
    score_scale = 1.0 / math.sqrt(head_dim)
    level, side = place[1] // COLUMNS, place[1] % COLUMNS
    step = lax.broadcasted_iota(jnp.int32, (1, span), 1) // part_tok
    valid = [(step >= 1) & (step <= level), (step >= 1 - side) & (step <= level)]
    bias = jnp.concatenate([jnp.where(ok, 0.0, HIDDEN) for ok in valid] * members, axis=1)
    keys = jnp.concatenate([ref[:, 0].reshape(span, head_dim) for ref in parts], axis=0)
    values = jnp.concatenate([ref[:, 1].reshape(span, head_dim) for ref in parts], axis=0)
    key_grad = jnp.zeros((width, head_dim), jnp.float32)
    value_grad = jnp.zeros((width, head_dim), jnp.float32)
    tile = min(rows, 256)
    for start in range(0, rows, tile):
        here = pl.ds(start, tile)
        query = q_ref[here, :]
        grad = g_ref[here, :]
        raw = dot(query, keys, NT) * base2_scale(head_dim) + bias
        near_peak = stat_ref[0, here, 0:1]
        peak = jnp.maximum(near_peak, jnp.max(raw, axis=1, keepdims=True))
        shrink = jnp.exp2(near_peak - peak)
        weight = jnp.exp2(raw - peak)
        total = stat_ref[0, here, 1:2] * shrink + jnp.sum(weight, axis=1, keepdims=True)
        inverse = 1.0 / total
        summed = sum_ref[here, :] * shrink + dot(weight.astype(jnp.bfloat16), values, NN)
        attended = (summed * inverse).astype(jnp.bfloat16)
        att_ref[here, :] = attended
        drift = jnp.sum(
            grad.astype(jnp.float32) * attended.astype(jnp.float32), axis=1, keepdims=True
        )
        stat_out_ref[0, here, 0:1] = peak
        stat_out_ref[0, here, 1:2] = inverse
        stat_out_ref[0, here, 2:3] = drift
        moved = weight * (dot(grad, values, NT) - drift)
        gq_ref[here, :] = dot(moved.astype(jnp.bfloat16), keys, NN) * (inverse * score_scale)
        own_score = (moved[:, :width] * (inverse * score_scale)).astype(jnp.bfloat16)
        own_prob = (weight[:, :width] * inverse).astype(jnp.bfloat16)
        key_grad += dot(own_score, query, TN)
        value_grad += dot(own_prob, grad, TN)
    for c, ref in enumerate(grad_refs):
        shape = (steps, part_tok, head_dim)
        ref[:, 0] = key_grad[c * span : (c + 1) * span].astype(jnp.bfloat16).reshape(shape)
        ref[:, 1] = value_grad[c * span : (c + 1) * span].astype(jnp.bfloat16).reshape(shape)


def near_backward_kernel(members, blk_len, part_tok, place, q_ref, g_ref, stat_ref, far_gq_ref, *refs):
    parts = refs[: 2 * members]
    gq_ref, gk_ref, gv_ref, bias_ref = refs[2 * members :]
    rows, head_dim = q_ref.shape
    near = parts[0].shape[0]
    score_scale = 1.0 / math.sqrt(head_dim)

    @pl.when(pl.program_id(0) == 0)
    def _():
        fill_near_bias(place, bias_ref, members, near, blk_len, part_tok)

    for start, count, used in reversed(near_tiles(rows, near)):
        here = pl.ds(start, count)
        query = q_ref[here, :]
        grad = g_ref[here, :]
        keys = jnp.concatenate([ref[:used] for ref in parts[0::2]], axis=0)
        values = jnp.concatenate([ref[:used] for ref in parts[1::2]], axis=0)
        peak = stat_ref[0, here, 0:1]
        inverse = stat_ref[0, here, 1:2]
        drift = stat_ref[0, here, 2:3]
        raw = dot(query, keys, NT) * base2_scale(head_dim)
        raw += bias_ref[here, : members * used]
        weight = jnp.exp2(raw - peak)
        moved = weight * (dot(grad, values, NT) - drift)
        factor = inverse * score_scale
        gq_ref[here, :] = (
            dot(moved.astype(jnp.bfloat16), keys, NN) * factor + far_gq_ref[here, :]
        ).astype(jnp.bfloat16)
        key_grad = dot((moved[:, :used] * factor).astype(jnp.bfloat16), query, TN)
        value_grad = dot((weight[:, :used] * inverse).astype(jnp.bfloat16), grad, TN)
        if used == near:
            gk_ref[...] = key_grad
            gv_ref[...] = value_grad
        else:
            gk_ref[:used] += key_grad
            gv_ref[:used] += value_grad


def call(kernel, place, operands, in_specs, outs, scratch, pairs, products, head_dim):
    moved_bytes = sum(a.size * a.dtype.itemsize for a in operands)
    return pl.pallas_call(
        kernel,
        grid_spec=pltpu.PrefetchScalarGridSpec(
            num_scalar_prefetch=1,
            grid=(HEADS,),
            in_specs=in_specs,
            out_specs=[spec for _, spec in outs],
            scratch_shapes=scratch,
        ),
        out_shape=[shape for shape, _ in outs],
        compiler_params=LIMIT,
        cost_estimate=pl.CostEstimate(
            flops=4 * products * pairs * head_dim, bytes_accessed=moved_bytes, transcendentals=pairs
        ),
    )(place, *operands)


def shards(queries, keys, values, layout, grad_out):
    seq_count = lax.axis_size("seq")
    seq_index = lax.axis_index("seq")
    members = lax.axis_size("kv")
    kv_index = lax.axis_index("kv")
    tok_rows, feat_width = queries.shape
    blocks, part_tok = (keys.shape[0], keys.shape[1])
    blk_len = part_tok * members
    near = blocks * part_tok
    head_dim = feat_width // HEADS
    levels = seq_count // COLUMNS
    pick_window = jnp.minimum(seq_index, seq_count - 2)
    last_row = layout[layout.shape[0] - 1]
    summary_local = jnp.clip(last_row[pick_window] - seq_index * blocks, 0, blocks - 1)
    place = jnp.stack([kv_index, seq_index, summary_local]).astype(jnp.int32)

    def hop(part, column_step, member_step):
        pairs = [
            (s * members + m, (s ^ column_step) * members + (m ^ member_step))
            for s in range(seq_count)
            for m in range(members)
        ]
        return lax.ppermute(part, ("seq", "kv"), pairs)

    def climb(part, d):
        return lax.ppermute(
            part, "seq", [(s, s + COLUMNS * d) for s in range(seq_count - COLUMNS * d)]
        )

    def sink(part, d):
        return lax.ppermute(
            part, "seq", [(s, s - COLUMNS * d) for s in range(COLUMNS * d, seq_count)]
        )

    key_rows = keys.reshape(near, feat_width)
    value_rows = values.reshape(near, feat_width)
    key_parts = [key_rows]
    value_parts = [value_rows]
    for step in range(2, members, 2):
        key_parts.append(hop(key_rows, 0, step))
        value_parts.append(hop(value_rows, 0, step))
    own_pair = pick_pair(place, keys, values)
    column = jnp.stack([own_pair] + [climb(own_pair, d) for d in range(1, levels)])
    far_parts = [
        column if (c, step) == (0, 0) else hop(column, c, step)
        for step in range(0, members, 2)
        for c in range(COLUMNS)
    ]
    key_parts = [p for part in key_parts for p in (part, hop(part, 0, 1))]
    value_parts = [p for part in value_parts for p in (part, hop(part, 0, 1))]
    near_parts = [p for pair in zip(key_parts, value_parts) for p in pair]
    far_parts = [
        p
        for m in range(0, len(far_parts), COLUMNS)
        for group in (
            far_parts[m : m + COLUMNS],
            [hop(part, 0, 1) for part in far_parts[m : m + COLUMNS]],
        )
        for p in group
    ]

    column_spec = pl.BlockSpec((tok_rows, head_dim), lambda h, place: (0, h))
    near_spec = pl.BlockSpec((near, head_dim), lambda h, place: (0, h))
    far_spec = pl.BlockSpec((levels, 2, part_tok, head_dim), lambda h, place: (0, 0, 0, h))

    def rows_out(dtype):
        return (jax.ShapeDtypeStruct((tok_rows, feat_width), dtype), column_spec)

    def stat_out(count):
        return (
            jax.ShapeDtypeStruct((HEADS, tok_rows, count), jnp.float32),
            pl.BlockSpec((1, tok_rows, count), lambda h, place: (h, 0, 0)),
        )

    near_out = (jax.ShapeDtypeStruct((near, feat_width), jnp.float32), near_spec)
    far_out = (jax.ShapeDtypeStruct(column.shape, jnp.bfloat16), far_spec)
    bias_scratch = [pltpu.VMEM((tok_rows, members * near), jnp.float32)]
    near_pairs = HEADS * tok_rows * members * near
    far_pairs = HEADS * tok_rows * members * seq_count * part_tok

    near_sum, near_stat = call(
        functools.partial(near_forward_kernel, members, blk_len, part_tok),
        place,
        [queries] + near_parts,
        [column_spec] + [near_spec] * (2 * members),
        [rows_out(jnp.float32), stat_out(2)],
        bias_scratch,
        near_pairs,
        2,
        head_dim,
    )
    attended, far_gq, stat, own_grad, cross_grad = call(
        functools.partial(far_kernel, members),
        place,
        [queries, grad_out, near_sum, near_stat] + far_parts,
        [column_spec, column_spec, column_spec, stat_out(2)[1]] + [far_spec] * len(far_parts),
        [rows_out(jnp.bfloat16), rows_out(jnp.float32), stat_out(3), far_out, far_out],
        [],
        far_pairs,
        5,
        head_dim,
    )
    crossed = hop(cross_grad, 1, 0)
    returned = [crossed[0].astype(jnp.float32)]
    for d in range(1, levels):
        both = own_grad[d].astype(jnp.float32) + crossed[d].astype(jnp.float32)
        returned.append(sink(both.astype(jnp.bfloat16), d).astype(jnp.float32))
    grad_q, near_k, near_v = call(
        functools.partial(near_backward_kernel, members, blk_len, part_tok),
        place,
        [queries, grad_out, stat, far_gq] + near_parts,
        [column_spec, column_spec, stat_out(3)[1], column_spec] + [near_spec] * (2 * members),
        [rows_out(jnp.bfloat16), near_out, near_out],
        bias_scratch,
        near_pairs,
        4,
        head_dim,
    )
    extra = functools.reduce(lambda a, b: a + b, returned)
    chosen = (jnp.arange(blocks) == summary_local)[:, None, None]

    def finish(near_grad, far_term):
        near_grad = near_grad.reshape(blocks, part_tok, feat_width)
        return (near_grad + jnp.where(chosen, far_term[None], 0.0)).astype(jnp.bfloat16)

    return (attended, grad_q, finish(near_k, extra[0]), finish(near_v, extra[1]))


def solution(mesh):
    return jax.shard_map(
        shards,
        mesh=mesh,
        in_specs=(P("seq", None), P("seq", "kv", None), P("seq", "kv", None), P(), P("seq", None)),
        out_specs=(P("seq", None), P("seq", None), P("seq", "kv", None), P("seq", "kv", None)),
        check_vma=False,
    )
```

```python
import functools
import math

import jax
import jax.numpy as jnp
from jax import lax
from jax.experimental import pallas as pl
from jax.experimental.pallas import tpu as pltpu
from jax.sharding import PartitionSpec as P

HEADS = 8
COLUMNS = 2
HIDDEN = -1e30
NT = (((1,), (1,)), ((), ()))
NN = (((1,), (0,)), ((), ()))
TN = (((0,), (0,)), ((), ()))
LIMIT = pltpu.CompilerParams(vmem_limit_bytes=56 * 1024 * 1024)


def dot(a, b, dims):
    return lax.dot_general(a, b, dims, preferred_element_type=jnp.float32)


def base2_scale(head_dim):
    return math.log2(math.e) / math.sqrt(head_dim)


def pick_kernel(blocks, table_ref, keys_ref, values_ref, pair_ref, both_ref, sems):
    window = lax.axis_index("seq")
    pick = jnp.minimum(window, lax.axis_size("seq") - 2)
    block = table_ref[pick, table_ref.shape[1] - 1] - window * blocks
    block = jnp.clip(block, 0, blocks - 1)
    copies = [
        pltpu.make_async_copy(keys_ref.at[block], pair_ref.at[0], sems.at[0]),
        pltpu.make_async_copy(values_ref.at[block], pair_ref.at[1], sems.at[1]),
        pltpu.make_async_copy(keys_ref, both_ref.at[0], sems.at[2]),
        pltpu.make_async_copy(values_ref, both_ref.at[1], sems.at[3]),
    ]
    for copy in copies:
        copy.start()
    for copy in copies:
        copy.wait()


def pick_pair(table, keys, values):
    blocks, part_tok, feat_width = keys.shape
    anywhere = pl.BlockSpec(memory_space=pl.ANY)
    return pl.pallas_call(
        functools.partial(pick_kernel, blocks),
        in_specs=[pl.BlockSpec(memory_space=pltpu.SMEM), anywhere, anywhere],
        out_specs=[anywhere, anywhere],
        out_shape=[
            jax.ShapeDtypeStruct((2, part_tok, feat_width), keys.dtype),
            jax.ShapeDtypeStruct((2,) + keys.shape, keys.dtype),
        ],
        scratch_shapes=[pltpu.SemaphoreType.DMA((4,))],
    )(table, keys, values)


def near_tiles(rows, near):
    half = rows // 2
    return [(0, half, near // 2), (half, half, near)]


def fill_near_bias(bias_ref, members, near, blk_len, part_tok):
    member = lax.axis_index("kv")
    shift = part_tok.bit_length() - 1
    for start, count, used in near_tiles(bias_ref.shape[0], near):
        row = start + lax.broadcasted_iota(jnp.int32, (count, 1), 0)
        col = lax.broadcasted_iota(jnp.int32, (1, used), 1)
        key_tok = (col >> shift) * blk_len + (col & (part_tok - 1))
        for j in range(members):
            key_pos = key_tok + (member ^ j) * part_tok
            bias_ref[start : start + count, j * used : (j + 1) * used] = jnp.where(
                key_pos <= row, 0.0, HIDDEN
            )


def near_forward_kernel(members, blk_len, part_tok, q_ref, *refs):
    parts = refs[:members]
    out_ref, stat_ref, bias_ref = refs[members:]
    rows, head_dim = q_ref.shape
    near = parts[0].shape[1]

    @pl.when(pl.program_id(0) == 0)
    def _():
        fill_near_bias(bias_ref, members, near, blk_len, part_tok)

    for start, count, used in near_tiles(rows, near):
        here = pl.ds(start, count)
        keys = jnp.concatenate([ref[0, :used] for ref in parts], axis=0)
        values = jnp.concatenate([ref[1, :used] for ref in parts], axis=0)
        raw = dot(q_ref[here, :], keys, NT) * base2_scale(head_dim)
        raw += bias_ref[here, : members * used]
        peak = jnp.max(raw, axis=1, keepdims=True)
        weight = jnp.exp2(raw - peak)
        total = jnp.sum(weight, axis=1, keepdims=True)
        stat_ref[here, :] = jnp.broadcast_to(peak + jnp.log2(total), (count, head_dim))
        out_ref[here, :] = dot(weight.astype(jnp.bfloat16), values, NN) * (1.0 / total)


def far_kernel(members, q_ref, g_ref, sum_ref, stat_ref, *refs):
    parts = refs[: COLUMNS * members]
    att_ref, gq_ref, stat_out_ref = refs[COLUMNS * members : COLUMNS * members + 3]
    grad_refs = refs[COLUMNS * members + 3 :]
    rows, head_dim = q_ref.shape
    steps, _, part_tok, _ = parts[0].shape
    span = steps * part_tok
    width = COLUMNS * span
    score_scale = 1.0 / math.sqrt(head_dim)
    window = lax.axis_index("seq")
    level, side = window // COLUMNS, window % COLUMNS
    step = lax.broadcasted_iota(jnp.int32, (1, span), 1) >> (part_tok.bit_length() - 1)
    valid = [(step >= 1) & (step <= level), (step >= 1 - side) & (step <= level)]
    bias = jnp.concatenate([jnp.where(ok, 0.0, HIDDEN) for ok in valid] * members, axis=1)
    keys = jnp.concatenate([ref[:, 0].reshape(span, head_dim) for ref in parts], axis=0)
    values = jnp.concatenate([ref[:, 1].reshape(span, head_dim) for ref in parts], axis=0)
    key_grad = jnp.zeros((width, head_dim), jnp.float32)
    value_grad = jnp.zeros((width, head_dim), jnp.float32)
    tile = min(rows, 256)
    lane = lax.broadcasted_iota(jnp.int32, (tile, head_dim), 1)
    for start in range(0, rows, tile):
        here = pl.ds(start, tile)
        query = q_ref[here, :]
        grad = g_ref[here, :]
        raw = dot(query, keys, NT) * base2_scale(head_dim) + bias
        near_level = stat_ref[here, 0:1]
        peak = jnp.maximum(near_level, jnp.max(raw, axis=1, keepdims=True))
        near_weight = jnp.exp2(near_level - peak)
        weight = jnp.exp2(raw - peak)
        total = near_weight + jnp.sum(weight, axis=1, keepdims=True)
        inverse = 1.0 / total
        summed = sum_ref[here, :] * near_weight + dot(weight.astype(jnp.bfloat16), values, NN)
        attended = (summed * inverse).astype(jnp.bfloat16)
        att_ref[here, :] = attended
        drift = jnp.sum(
            grad.astype(jnp.float32) * attended.astype(jnp.float32), axis=1, keepdims=True
        )
        stat_out_ref[here, :] = jnp.where(lane < head_dim // 2, peak + jnp.log2(total), drift)
        moved = weight * (dot(grad, values, NT) - drift)
        gq_ref[here, :] = dot(moved.astype(jnp.bfloat16), keys, NN) * (inverse * score_scale)
        own_score = (moved[:, :width] * (inverse * score_scale)).astype(jnp.bfloat16)
        own_prob = (weight[:, :width] * inverse).astype(jnp.bfloat16)
        key_grad += dot(own_score, query, TN)
        value_grad += dot(own_prob, grad, TN)
    for c, ref in enumerate(grad_refs):
        shape = (steps, part_tok, head_dim)
        ref[:, 0] = key_grad[c * span : (c + 1) * span].astype(jnp.bfloat16).reshape(shape)
        ref[:, 1] = value_grad[c * span : (c + 1) * span].astype(jnp.bfloat16).reshape(shape)


def near_backward_kernel(members, blk_len, part_tok, q_ref, g_ref, stat_ref, far_gq_ref, *refs):
    parts = refs[:members]
    gq_ref, grad_ref, bias_ref = refs[members:]
    rows, head_dim = q_ref.shape
    near = parts[0].shape[1]
    score_scale = 1.0 / math.sqrt(head_dim)

    @pl.when(pl.program_id(0) == 0)
    def _():
        fill_near_bias(bias_ref, members, near, blk_len, part_tok)

    for start, count, used in reversed(near_tiles(rows, near)):
        here = pl.ds(start, count)
        query = q_ref[here, :]
        grad = g_ref[here, :]
        keys = jnp.concatenate([ref[0, :used] for ref in parts], axis=0)
        values = jnp.concatenate([ref[1, :used] for ref in parts], axis=0)
        level = stat_ref[here, 0:1]
        drift = stat_ref[here, head_dim // 2 : head_dim // 2 + 1]
        raw = dot(query, keys, NT) * base2_scale(head_dim)
        raw += bias_ref[here, : members * used]
        prob = jnp.exp2(raw - level)
        moved = prob * (dot(grad, values, NT) - drift)
        gq_ref[here, :] = (
            dot(moved.astype(jnp.bfloat16), keys, NN) * score_scale + far_gq_ref[here, :]
        ).astype(jnp.bfloat16)
        key_grad = dot((moved[:, :used] * score_scale).astype(jnp.bfloat16), query, TN)
        value_grad = dot(prob[:, :used].astype(jnp.bfloat16), grad, TN)
        if used == near:
            grad_ref[0] = key_grad
            grad_ref[1] = value_grad
        else:
            grad_ref[0, :used] += key_grad
            grad_ref[1, :used] += value_grad


def call(kernel, operands, in_specs, outs, scratch, pairs, products, head_dim):
    moved_bytes = sum(a.size * a.dtype.itemsize for a in operands)
    return pl.pallas_call(
        kernel,
        grid=(HEADS,),
        in_specs=in_specs,
        out_specs=[spec for _, spec in outs],
        scratch_shapes=scratch,
        out_shape=[shape for shape, _ in outs],
        compiler_params=LIMIT,
        cost_estimate=pl.CostEstimate(
            flops=4 * products * pairs * head_dim, bytes_accessed=moved_bytes, transcendentals=pairs
        ),
    )(*operands)


def shards(queries, keys, values, layout, grad_out):
    seq_count = lax.axis_size("seq")
    seq_index = lax.axis_index("seq")
    members = lax.axis_size("kv")
    tok_rows, feat_width = queries.shape
    blocks, part_tok = (keys.shape[0], keys.shape[1])
    blk_len = part_tok * members
    near = blocks * part_tok
    head_dim = feat_width // HEADS
    levels = seq_count // COLUMNS
    pick_window = jnp.minimum(seq_index, seq_count - 2)
    last_row = layout[layout.shape[0] - 1]
    summary_local = jnp.clip(last_row[pick_window] - seq_index * blocks, 0, blocks - 1)

    def hop(part, column_step, member_step):
        pairs = [
            (s * members + m, (s ^ column_step) * members + (m ^ member_step))
            for s in range(seq_count)
            for m in range(members)
        ]
        return lax.ppermute(part, ("seq", "kv"), pairs)

    def climb(part, d):
        return lax.ppermute(
            part, "seq", [(s, s + COLUMNS * d) for s in range(seq_count - COLUMNS * d)]
        )

    def sink(part, d):
        return lax.ppermute(
            part, "seq", [(s, s - COLUMNS * d) for s in range(COLUMNS * d, seq_count)]
        )

    own_pair, both = pick_pair(layout.T, keys, values)
    both = both.reshape(2, near, feat_width)
    near_parts = [both] + [hop(both, 0, step) for step in range(2, members, 2)]
    near_parts = [p for part in near_parts for p in (part, hop(part, 0, 1))]
    column = jnp.stack([own_pair] + [climb(own_pair, d) for d in range(1, levels)])
    far_parts = []
    for step in range(0, members, 2):
        group = [
            column if (c, step) == (0, 0) else hop(column, c, step) for c in range(COLUMNS)
        ]
        far_parts += group + [hop(part, 0, 1) for part in group]

    column_spec = pl.BlockSpec((tok_rows, head_dim), lambda h: (0, h))
    near_spec = pl.BlockSpec((2, near, head_dim), lambda h: (0, 0, h))
    far_spec = pl.BlockSpec((levels, 2, part_tok, head_dim), lambda h: (0, 0, 0, h))

    def rows_out(dtype):
        return (jax.ShapeDtypeStruct((tok_rows, feat_width), dtype), column_spec)

    near_out = (jax.ShapeDtypeStruct((2, near, feat_width), jnp.float32), near_spec)
    far_out = (jax.ShapeDtypeStruct(column.shape, jnp.bfloat16), far_spec)
    bias_scratch = [pltpu.VMEM((tok_rows, members * near), jnp.float32)]
    near_pairs = HEADS * tok_rows * members * near
    far_pairs = HEADS * tok_rows * members * seq_count * part_tok

    near_sum, near_stat = call(
        functools.partial(near_forward_kernel, members, blk_len, part_tok),
        [queries] + near_parts,
        [column_spec] + [near_spec] * members,
        [rows_out(jnp.float32), rows_out(jnp.float32)],
        bias_scratch,
        near_pairs,
        2,
        head_dim,
    )
    attended, far_gq, stat, own_grad, cross_grad = call(
        functools.partial(far_kernel, members),
        [queries, grad_out, near_sum, near_stat] + far_parts,
        [column_spec] * 4 + [far_spec] * len(far_parts),
        [rows_out(jnp.bfloat16), rows_out(jnp.float32), rows_out(jnp.float32), far_out, far_out],
        [],
        far_pairs,
        5,
        head_dim,
    )
    crossed = hop(cross_grad, 1, 0)
    returned = [crossed[0].astype(jnp.float32)]
    for d in range(1, levels):
        summed = own_grad[d].astype(jnp.float32) + crossed[d].astype(jnp.float32)
        returned.append(sink(summed.astype(jnp.bfloat16), d).astype(jnp.float32))
    grad_q, near_grad = call(
        functools.partial(near_backward_kernel, members, blk_len, part_tok),
        [queries, grad_out, stat, far_gq] + near_parts,
        [column_spec] * 4 + [near_spec] * members,
        [rows_out(jnp.bfloat16), near_out],
        bias_scratch,
        near_pairs,
        4,
        head_dim,
    )
    extra = functools.reduce(lambda a, b: a + b, returned)
    chosen = (jnp.arange(blocks) == summary_local)[:, None, None]

    def finish(near_term, far_term):
        near_term = near_term.reshape(blocks, part_tok, feat_width)
        return (near_term + jnp.where(chosen, far_term[None], 0.0)).astype(jnp.bfloat16)

    return (attended, grad_q, finish(near_grad[0], extra[0]), finish(near_grad[1], extra[1]))


def solution(mesh):
    return jax.shard_map(
        shards,
        mesh=mesh,
        in_specs=(P("seq", None), P("seq", "kv", None), P("seq", "kv", None), P(), P("seq", None)),
        out_specs=(P("seq", None), P("seq", None), P("seq", "kv", None), P("seq", "kv", None)),
        check_vma=False,
    )
```

```python
import functools
import math

import jax
import jax.numpy as jnp
from jax import lax
from jax.experimental import pallas as pl
from jax.experimental.pallas import tpu as pltpu
from jax.sharding import PartitionSpec as P

HEADS = 8
COLUMNS = 2
HIDDEN = -1e30
NT = (((1,), (1,)), ((), ()))
NN = (((1,), (0,)), ((), ()))
TN = (((0,), (0,)), ((), ()))
WHOLE = pl.BlockSpec(memory_space=pltpu.VMEM)
LIMIT = pltpu.CompilerParams(vmem_limit_bytes=28 * 1024 * 1024)


def dot(a, b, dims):
    return lax.dot_general(a, b, dims, preferred_element_type=jnp.float32)


def base2_scale(head_dim):
    return math.log2(math.e) / math.sqrt(head_dim)


def pick_kernel(table_ref, keys_ref, values_ref, pair_ref, both_ref):
    window = lax.axis_index("seq")
    blocks = keys_ref.shape[0]
    pick = jnp.minimum(window, lax.axis_size("seq") - 2)
    block = table_ref[pick, table_ref.shape[1] - 1] - window * blocks
    block = jnp.clip(block, 0, blocks - 1)
    pair_ref[0] = keys_ref[block]
    pair_ref[1] = values_ref[block]
    both_ref[0] = keys_ref[...]
    both_ref[1] = values_ref[...]


def pick_pair(table, keys, values):
    _, part_tok, feat_width = keys.shape
    return pl.pallas_call(
        pick_kernel,
        in_specs=[pl.BlockSpec(memory_space=pltpu.SMEM), WHOLE, WHOLE],
        out_specs=[WHOLE, WHOLE],
        out_shape=[
            jax.ShapeDtypeStruct((2, part_tok, feat_width), keys.dtype),
            jax.ShapeDtypeStruct((2,) + keys.shape, keys.dtype),
        ],
    )(table, keys, values)


def near_tiles(rows, near):
    half = rows // 2
    return [(0, half, near // 2), (half, half, near)]


def fill_near_bias(bias_ref, members, near, blk_len, part_tok):
    member = lax.axis_index("kv")
    shift = part_tok.bit_length() - 1
    for start, count, used in near_tiles(bias_ref.shape[0], near):
        row = start + lax.broadcasted_iota(jnp.int32, (count, 1), 0)
        col = lax.broadcasted_iota(jnp.int32, (1, used), 1)
        key_tok = (col >> shift) * blk_len + (col & (part_tok - 1))
        for j in range(members):
            key_pos = key_tok + (member ^ j) * part_tok
            bias_ref[start : start + count, j * used : (j + 1) * used] = jnp.where(
                key_pos <= row, 0.0, HIDDEN
            )


def head_columns(head, feat_width):
    head_dim = feat_width // HEADS
    return pl.ds(pl.multiple_of(head * head_dim, head_dim), head_dim)


def near_forward_kernel(members, blk_len, part_tok, q_ref, *refs):
    parts = refs[:members]
    out_ref, stat_ref, bias_ref = refs[members:]
    rows, feat_width = q_ref.shape
    head_dim = feat_width // HEADS
    near = parts[0].shape[1]
    fill_near_bias(bias_ref, members, near, blk_len, part_tok)

    @pl.loop(0, HEADS)
    def _(head):
        cols = head_columns(head, feat_width)
        for start, count, used in near_tiles(rows, near):
            here = pl.ds(start, count)
            keys = jnp.concatenate([ref[0, :used, cols] for ref in parts], axis=0)
            values = jnp.concatenate([ref[1, :used, cols] for ref in parts], axis=0)
            raw = dot(q_ref[here, cols], keys, NT) * base2_scale(head_dim)
            raw += bias_ref[here, : members * used]
            peak = jnp.max(raw, axis=1, keepdims=True)
            weight = jnp.exp2(raw - peak)
            total = jnp.sum(weight, axis=1, keepdims=True)
            stat_ref[here, cols] = jnp.broadcast_to(peak + jnp.log2(total), (count, head_dim))
            out_ref[here, cols] = dot(weight.astype(jnp.bfloat16), values, NN) * (1.0 / total)


def far_kernel(members, tile, q_ref, g_ref, sum_ref, stat_ref, *refs):
    parts = refs[: COLUMNS * members]
    att_ref, gq_ref, stat_out_ref = refs[COLUMNS * members : COLUMNS * members + 3]
    grad_refs = refs[COLUMNS * members + 3 :]
    rows, feat_width = q_ref.shape
    head_dim = feat_width // HEADS
    steps, _, part_tok, _ = parts[0].shape
    span = steps * part_tok
    width = COLUMNS * span
    score_scale = 1.0 / math.sqrt(head_dim)
    window = lax.axis_index("seq")
    level, side = window // COLUMNS, window % COLUMNS
    step = lax.broadcasted_iota(jnp.int32, (1, span), 1) >> (part_tok.bit_length() - 1)
    valid = [(step >= 1) & (step <= level), (step >= 1 - side) & (step <= level)]
    bias = jnp.concatenate([jnp.where(ok, 0.0, HIDDEN) for ok in valid] * members, axis=1)
    lane = lax.broadcasted_iota(jnp.int32, (tile, head_dim), 1)

    @pl.loop(0, HEADS)
    def _(head):
        cols = head_columns(head, feat_width)
        keys = jnp.concatenate([ref[:, 0, :, cols].reshape(span, head_dim) for ref in parts], axis=0)
        values = jnp.concatenate([ref[:, 1, :, cols].reshape(span, head_dim) for ref in parts], axis=0)
        key_grad = jnp.zeros((width, head_dim), jnp.float32)
        value_grad = jnp.zeros((width, head_dim), jnp.float32)
        for start in range(0, rows, tile):
            here = pl.ds(start, tile)
            query = q_ref[here, cols]
            grad = g_ref[here, cols]
            raw = dot(query, keys, NT) * base2_scale(head_dim) + bias
            near_level = stat_ref[here, cols][:, 0:1]
            peak = jnp.maximum(near_level, jnp.max(raw, axis=1, keepdims=True))
            near_weight = jnp.exp2(near_level - peak)
            weight = jnp.exp2(raw - peak)
            total = near_weight + jnp.sum(weight, axis=1, keepdims=True)
            inverse = 1.0 / total
            summed = sum_ref[here, cols] * near_weight
            summed += dot(weight.astype(jnp.bfloat16), values, NN)
            attended = (summed * inverse).astype(jnp.bfloat16)
            att_ref[here, cols] = attended
            drift = jnp.sum(
                grad.astype(jnp.float32) * attended.astype(jnp.float32), axis=1, keepdims=True
            )
            stat_out_ref[here, cols] = jnp.where(
                lane < head_dim // 2, peak + jnp.log2(total), drift
            )
            moved = weight * (dot(grad, values, NT) - drift)
            gq_ref[here, cols] = dot(moved.astype(jnp.bfloat16), keys, NN) * (inverse * score_scale)
            own_score = (moved[:, :width] * (inverse * score_scale)).astype(jnp.bfloat16)
            own_prob = (weight[:, :width] * inverse).astype(jnp.bfloat16)
            key_grad += dot(own_score, query, TN)
            value_grad += dot(own_prob, grad, TN)
        for c, ref in enumerate(grad_refs):
            shape = (steps, part_tok, head_dim)
            used = slice(c * span, (c + 1) * span)
            ref[:, 0, :, cols] = key_grad[used].astype(jnp.bfloat16).reshape(shape)
            ref[:, 1, :, cols] = value_grad[used].astype(jnp.bfloat16).reshape(shape)


def near_backward_kernel(members, blk_len, part_tok, q_ref, g_ref, stat_ref, far_gq_ref, *refs):
    parts = refs[:members]
    gq_ref, gk_ref, gv_ref, bias_ref = refs[members:]
    rows, feat_width = q_ref.shape
    head_dim = feat_width // HEADS
    near = parts[0].shape[1]
    score_scale = 1.0 / math.sqrt(head_dim)
    fill_near_bias(bias_ref, members, near, blk_len, part_tok)

    @pl.loop(0, HEADS)
    def _(head):
        cols = head_columns(head, feat_width)
        for start, count, used in reversed(near_tiles(rows, near)):
            here = pl.ds(start, count)
            query = q_ref[here, cols]
            grad = g_ref[here, cols]
            keys = jnp.concatenate([ref[0, :used, cols] for ref in parts], axis=0)
            values = jnp.concatenate([ref[1, :used, cols] for ref in parts], axis=0)
            stat = stat_ref[here, cols]
            level = stat[:, 0:1]
            drift = stat[:, head_dim // 2 : head_dim // 2 + 1]
            raw = dot(query, keys, NT) * base2_scale(head_dim)
            raw += bias_ref[here, : members * used]
            prob = jnp.exp2(raw - level)
            moved = prob * (dot(grad, values, NT) - drift)
            gq_ref[here, cols] = (
                dot(moved.astype(jnp.bfloat16), keys, NN) * score_scale + far_gq_ref[here, cols]
            ).astype(jnp.bfloat16)
            key_grad = dot((moved[:, :used] * score_scale).astype(jnp.bfloat16), query, TN)
            value_grad = dot(prob[:, :used].astype(jnp.bfloat16), grad, TN)
            if used == near:
                gk_ref[:, cols] = key_grad
                gv_ref[:, cols] = value_grad
            else:
                gk_ref[:used, cols] += key_grad
                gv_ref[:used, cols] += value_grad


def call(kernel, operands, outs, scratch, pairs, products, head_dim):
    moved_bytes = sum(a.size * a.dtype.itemsize for a in operands)
    return pl.pallas_call(
        kernel,
        in_specs=[WHOLE] * len(operands),
        out_specs=[WHOLE] * len(outs),
        scratch_shapes=scratch,
        out_shape=outs,
        compiler_params=LIMIT,
        cost_estimate=pl.CostEstimate(
            flops=4 * products * pairs * head_dim, bytes_accessed=moved_bytes, transcendentals=pairs
        ),
    )(*operands)


def shards(queries, keys, values, layout, grad_out):
    seq_count = lax.axis_size("seq")
    seq_index = lax.axis_index("seq")
    members = lax.axis_size("kv")
    tok_rows, feat_width = queries.shape
    blocks, part_tok = (keys.shape[0], keys.shape[1])
    blk_len = part_tok * members
    near = blocks * part_tok
    head_dim = feat_width // HEADS
    levels = seq_count // COLUMNS
    pick_window = jnp.minimum(seq_index, seq_count - 2)
    last_row = layout[layout.shape[0] - 1]
    summary_local = jnp.clip(last_row[pick_window] - seq_index * blocks, 0, blocks - 1)

    def hop(part, column_step, member_step):
        pairs = [
            (s * members + m, (s ^ column_step) * members + (m ^ member_step))
            for s in range(seq_count)
            for m in range(members)
        ]
        return lax.ppermute(part, ("seq", "kv"), pairs)

    def climb(part, d):
        return lax.ppermute(
            part, "seq", [(s, s + COLUMNS * d) for s in range(seq_count - COLUMNS * d)]
        )

    def sink(part, d):
        return lax.ppermute(
            part, "seq", [(s, s - COLUMNS * d) for s in range(COLUMNS * d, seq_count)]
        )

    own_pair, both = pick_pair(layout.T, keys, values)
    both = both.reshape(2, near, feat_width)
    near_parts = [both] + [hop(both, 0, step) for step in range(2, members, 2)]
    near_parts = [p for part in near_parts for p in (part, hop(part, 0, 1))]
    column = jnp.stack([own_pair] + [climb(own_pair, d) for d in range(1, levels)])
    far_parts = []
    for step in range(0, members, 2):
        group = [
            column if (c, step) == (0, 0) else hop(column, c, step) for c in range(COLUMNS)
        ]
        far_parts += group + [hop(part, 0, 1) for part in group]

    def rows_out(dtype):
        return jax.ShapeDtypeStruct((tok_rows, feat_width), dtype)

    near_out = jax.ShapeDtypeStruct((near, feat_width), jnp.float32)
    far_out = jax.ShapeDtypeStruct(column.shape, jnp.bfloat16)
    bias_scratch = [pltpu.VMEM((tok_rows, members * near), jnp.float32)]
    near_pairs = HEADS * tok_rows * members * near
    far_pairs = HEADS * tok_rows * members * seq_count * part_tok
    tile = min(256, max(64, 2**18 // (members * seq_count * part_tok)))

    near_sum, near_stat = call(
        functools.partial(near_forward_kernel, members, blk_len, part_tok),
        [queries] + near_parts,
        [rows_out(jnp.float32), rows_out(jnp.float32)],
        bias_scratch,
        near_pairs,
        2,
        head_dim,
    )
    attended, far_gq, stat, own_grad, cross_grad = call(
        functools.partial(far_kernel, members, tile),
        [queries, grad_out, near_sum, near_stat] + far_parts,
        [rows_out(jnp.bfloat16), rows_out(jnp.float32), rows_out(jnp.float32), far_out, far_out],
        [],
        far_pairs,
        5,
        head_dim,
    )
    crossed = hop(cross_grad, 1, 0)
    returned = [crossed[0].astype(jnp.float32)]
    for d in range(1, levels):
        summed = own_grad[d].astype(jnp.float32) + crossed[d].astype(jnp.float32)
        returned.append(sink(summed.astype(jnp.bfloat16), d).astype(jnp.float32))
    grad_q, near_k, near_v = call(
        functools.partial(near_backward_kernel, members, blk_len, part_tok),
        [queries, grad_out, stat, far_gq] + near_parts,
        [rows_out(jnp.bfloat16), near_out, near_out],
        bias_scratch,
        near_pairs,
        4,
        head_dim,
    )
    extra = functools.reduce(lambda a, b: a + b, returned)
    chosen = (jnp.arange(blocks) == summary_local)[:, None, None]

    def finish(near_term, far_term):
        near_term = near_term.reshape(blocks, part_tok, feat_width)
        return (near_term + jnp.where(chosen, far_term[None], 0.0)).astype(jnp.bfloat16)

    return (attended, grad_q, finish(near_k, extra[0]), finish(near_v, extra[1]))


def solution(mesh):
    return jax.shard_map(
        shards,
        mesh=mesh,
        in_specs=(P("seq", None), P("seq", "kv", None), P("seq", "kv", None), P(), P("seq", None)),
        out_specs=(P("seq", None), P("seq", None), P("seq", "kv", None), P("seq", "kv", None)),
        check_vma=False,
    )
```

```python
import functools
import math

import jax
import jax.numpy as jnp
from jax import lax
from jax.experimental import pallas as pl
from jax.experimental.pallas import tpu as pltpu
from jax.sharding import PartitionSpec as P

HEADS = 8
COLUMNS = 2
GROUP = 2
HIDDEN = -1e30
NT = (((1,), (1,)), ((), ()))
NN = (((1,), (0,)), ((), ()))
TN = (((0,), (0,)), ((), ()))
WHOLE = pl.BlockSpec(memory_space=pltpu.VMEM)
LIMIT = pltpu.CompilerParams(vmem_limit_bytes=20 * 1024 * 1024)


def dot(a, b, dims):
    return lax.dot_general(a, b, dims, preferred_element_type=jnp.float32)


def base2_scale(head_dim):
    return math.log2(math.e) / math.sqrt(head_dim)


def pick_kernel(table_ref, keys_ref, values_ref, pair_ref, both_ref):
    window = lax.axis_index("seq")
    blocks = keys_ref.shape[0]
    pick = jnp.minimum(window, lax.axis_size("seq") - 2)
    block = table_ref[pick, table_ref.shape[1] - 1] - window * blocks
    block = jnp.clip(block, 0, blocks - 1)
    pair_ref[0] = keys_ref[block]
    pair_ref[1] = values_ref[block]
    both_ref[0] = keys_ref[...]
    both_ref[1] = values_ref[...]


def pick_pair(table, keys, values):
    _, part_tok, feat_width = keys.shape
    return pl.pallas_call(
        pick_kernel,
        in_specs=[pl.BlockSpec(memory_space=pltpu.SMEM), WHOLE, WHOLE],
        out_specs=[WHOLE, WHOLE],
        out_shape=[
            jax.ShapeDtypeStruct((2, part_tok, feat_width), keys.dtype),
            jax.ShapeDtypeStruct((2,) + keys.shape, keys.dtype),
        ],
    )(table, keys, values)


def near_tiles(rows, near):
    half = rows // 2
    return [(0, half, near // 2), (half, half, near)]


def fill_near_bias(bias_ref, members, near, blk_len, part_tok):
    member = lax.axis_index("kv")
    shift = part_tok.bit_length() - 1
    for start, count, used in near_tiles(bias_ref.shape[0], near):
        row = start + lax.broadcasted_iota(jnp.int32, (count, 1), 0)
        col = lax.broadcasted_iota(jnp.int32, (1, used), 1)
        key_tok = (col >> shift) * blk_len + (col & (part_tok - 1))
        for j in range(members):
            key_pos = key_tok + (member ^ j) * part_tok
            bias_ref[start : start + count, j * used : (j + 1) * used] = jnp.where(
                key_pos <= row, 0.0, HIDDEN
            )


def head_columns(head, feat_width):
    head_dim = feat_width // HEADS
    return pl.ds(pl.multiple_of(head * head_dim, head_dim), head_dim)


def near_rows(parts, which, used, cols):
    return jnp.concatenate([ref[which, :used, cols] for ref in parts], axis=0)


def near_forward_kernel(members, blk_len, part_tok, q_ref, *refs):
    parts = refs[:members]
    out_ref, stat_ref, bias_ref = refs[members:]
    rows, feat_width = q_ref.shape
    head_dim = feat_width // HEADS
    near = parts[0].shape[1]
    fill_near_bias(bias_ref, members, near, blk_len, part_tok)

    @pl.loop(0, HEADS // GROUP)
    def _(group):
        units = [
            (head_columns(group * GROUP + i, feat_width), pl.ds(start, count), used)
            for i in range(GROUP)
            for start, count, used in near_tiles(rows, near)
        ]
        raws = [
            dot(q_ref[here, cols], near_rows(parts, 0, used, cols), NT) * base2_scale(head_dim)
            + bias_ref[here, : members * used]
            for cols, here, used in units
        ]
        peaks = [jnp.max(raw, axis=1, keepdims=True) for raw in raws]
        weights = [jnp.exp2(raw - peak) for raw, peak in zip(raws, peaks)]
        totals = [jnp.sum(weight, axis=1, keepdims=True) for weight in weights]
        sums = [
            dot(weight.astype(jnp.bfloat16), near_rows(parts, 1, used, cols), NN)
            for weight, (cols, here, used) in zip(weights, units)
        ]
        for (cols, here, used), peak, total, summed in zip(units, peaks, totals, sums):
            level = peak + jnp.log2(total)
            stat_ref[here, cols] = jnp.broadcast_to(level, summed.shape)
            out_ref[here, cols] = summed * (1.0 / total)


def far_rows(parts, which, cols):
    steps, _, part_tok, _ = parts[0].shape
    return jnp.concatenate(
        [ref[:, which, :, cols].reshape(steps * part_tok, cols.size) for ref in parts], axis=0
    )


def far_kernel(members, tile, heads, batch, q_ref, g_ref, sum_ref, stat_ref, *refs):
    parts = refs[: COLUMNS * members]
    att_ref, gq_ref, stat_out_ref = refs[COLUMNS * members : COLUMNS * members + 3]
    grad_refs = refs[COLUMNS * members + 3 :]
    rows, feat_width = q_ref.shape
    head_dim = feat_width // HEADS
    steps, _, part_tok, _ = parts[0].shape
    span = steps * part_tok
    width = COLUMNS * span
    score_scale = 1.0 / math.sqrt(head_dim)
    window = lax.axis_index("seq")
    level, side = window // COLUMNS, window % COLUMNS
    step = lax.broadcasted_iota(jnp.int32, (1, span), 1) >> (part_tok.bit_length() - 1)
    valid = [(step >= 1) & (step <= level), (step >= 1 - side) & (step <= level)]
    bias = jnp.concatenate([jnp.where(ok, 0.0, HIDDEN) for ok in valid] * members, axis=1)
    lane = lax.broadcasted_iota(jnp.int32, (tile, head_dim), 1)

    def work(units, keys, values, key_grads, value_grads):
        raws = [
            dot(q_ref[here, cols], keys[i], NT) * base2_scale(head_dim) + bias
            for i, cols, here in units
        ]
        grad_probs = [dot(g_ref[here, cols], values[i], NT) for i, cols, here in units]
        near_levels = [stat_ref[here, cols][:, 0:1] for i, cols, here in units]
        peaks = [
            jnp.maximum(near_level, jnp.max(raw, axis=1, keepdims=True))
            for near_level, raw in zip(near_levels, raws)
        ]
        near_weights = [jnp.exp2(near_level - peak) for near_level, peak in zip(near_levels, peaks)]
        weights = [jnp.exp2(raw - peak) for raw, peak in zip(raws, peaks)]
        totals = [
            near_weight + jnp.sum(weight, axis=1, keepdims=True)
            for near_weight, weight in zip(near_weights, weights)
        ]
        inverses = [1.0 / total for total in totals]
        sums = [
            dot(weight.astype(jnp.bfloat16), values[i], NN)
            for weight, (i, cols, here) in zip(weights, units)
        ]
        drifts = []
        for u, (i, cols, here) in enumerate(units):
            summed = sum_ref[here, cols] * near_weights[u] + sums[u]
            attended = (summed * inverses[u]).astype(jnp.bfloat16)
            att_ref[here, cols] = attended
            product = g_ref[here, cols].astype(jnp.float32) * attended.astype(jnp.float32)
            drifts.append(jnp.sum(product, axis=1, keepdims=True))
            stat_out_ref[here, cols] = jnp.where(
                lane < head_dim // 2, peaks[u] + jnp.log2(totals[u]), drifts[u]
            )
        moved = [
            weight * (grad_prob - drift)
            for weight, grad_prob, drift in zip(weights, grad_probs, drifts)
        ]
        own_scores = [
            (part[:, :width] * (inverse * score_scale)).astype(jnp.bfloat16)
            for part, inverse in zip(moved, inverses)
        ]
        own_probs = [
            (weight[:, :width] * inverse).astype(jnp.bfloat16)
            for weight, inverse in zip(weights, inverses)
        ]
        for u, (i, cols, here) in enumerate(units):
            gq_ref[here, cols] = dot(moved[u].astype(jnp.bfloat16), keys[i], NN) * (
                inverses[u] * score_scale
            )
        for u, (i, cols, here) in enumerate(units):
            key_grads[i].append(dot(own_scores[u], q_ref[here, cols], TN))
            value_grads[i].append(dot(own_probs[u], g_ref[here, cols], TN))

    @pl.loop(0, HEADS // heads)
    def _(group):
        columns = [head_columns(group * heads + i, feat_width) for i in range(heads)]
        units = [
            (i, cols, pl.ds(r, tile)) for i, cols in enumerate(columns) for r in range(0, rows, tile)
        ]
        keys = [far_rows(parts, 0, cols) for cols in columns]
        values = [far_rows(parts, 1, cols) for cols in columns]
        grads = [[[] for _ in columns] for _ in range(2)]
        for first in range(0, len(units), batch):
            work(units[first : first + batch], keys, values, *grads)
        for which, per_head in enumerate(grads):
            for cols, terms in zip(columns, per_head):
                total = functools.reduce(lambda a, b: a + b, terms).astype(jnp.bfloat16)
                for c, ref in enumerate(grad_refs):
                    piece = total[c * span : (c + 1) * span]
                    ref[:, which, :, cols] = piece.reshape(steps, part_tok, head_dim)


def near_backward_kernel(members, blk_len, part_tok, q_ref, g_ref, stat_ref, far_gq_ref, *refs):
    parts = refs[:members]
    gq_ref, gk_ref, gv_ref, bias_ref = refs[members:]
    rows, feat_width = q_ref.shape
    head_dim = feat_width // HEADS
    near = parts[0].shape[1]
    score_scale = 1.0 / math.sqrt(head_dim)
    fill_near_bias(bias_ref, members, near, blk_len, part_tok)

    @pl.loop(0, HEADS // GROUP)
    def _(group):
        units = [
            (head_columns(group * GROUP + i, feat_width), pl.ds(start, count), used)
            for i in range(GROUP)
            for start, count, used in reversed(near_tiles(rows, near))
        ]
        keys = [near_rows(parts, 0, used, cols) for cols, here, used in units]
        values = [near_rows(parts, 1, used, cols) for cols, here, used in units]
        raws = [
            dot(q_ref[here, cols], key, NT) * base2_scale(head_dim)
            + bias_ref[here, : members * used]
            for (cols, here, used), key in zip(units, keys)
        ]
        grad_probs = [
            dot(g_ref[here, cols], value, NT) for (cols, here, used), value in zip(units, values)
        ]
        stats = [stat_ref[here, cols] for cols, here, used in units]
        probs = [jnp.exp2(raw - stat[:, 0:1]) for raw, stat in zip(raws, stats)]
        moved = [
            prob * (grad_prob - stat[:, head_dim // 2 : head_dim // 2 + 1])
            for prob, grad_prob, stat in zip(probs, grad_probs, stats)
        ]
        for (cols, here, used), part, key in zip(units, moved, keys):
            gq_ref[here, cols] = (
                dot(part.astype(jnp.bfloat16), key, NN) * score_scale + far_gq_ref[here, cols]
            ).astype(jnp.bfloat16)
        for (cols, here, used), part, prob in zip(units, moved, probs):
            own_score = (part[:, :used] * score_scale).astype(jnp.bfloat16)
            own_prob = prob[:, :used].astype(jnp.bfloat16)
            for left, right_ref, ref in ((own_score, q_ref, gk_ref), (own_prob, g_ref, gv_ref)):
                grad = dot(left, right_ref[here, cols], TN)
                if used == near:
                    ref[:, cols] = grad
                else:
                    ref[:used, cols] += grad


def call(kernel, operands, outs, scratch, pairs, products, head_dim):
    moved_bytes = sum(a.size * a.dtype.itemsize for a in operands)
    return pl.pallas_call(
        kernel,
        in_specs=[WHOLE] * len(operands),
        out_specs=[WHOLE] * len(outs),
        scratch_shapes=scratch,
        out_shape=outs,
        compiler_params=LIMIT,
        cost_estimate=pl.CostEstimate(
            flops=4 * products * pairs * head_dim, bytes_accessed=moved_bytes, transcendentals=pairs
        ),
    )(*operands)


def shards(queries, keys, values, layout, grad_out):
    seq_count = lax.axis_size("seq")
    seq_index = lax.axis_index("seq")
    members = lax.axis_size("kv")
    tok_rows, feat_width = queries.shape
    blocks, part_tok = (keys.shape[0], keys.shape[1])
    blk_len = part_tok * members
    near = blocks * part_tok
    head_dim = feat_width // HEADS
    levels = seq_count // COLUMNS
    pick_window = jnp.minimum(seq_index, seq_count - 2)
    last_row = layout[layout.shape[0] - 1]
    summary_local = jnp.clip(last_row[pick_window] - seq_index * blocks, 0, blocks - 1)

    def hop(part, column_step, member_step):
        pairs = [
            (s * members + m, (s ^ column_step) * members + (m ^ member_step))
            for s in range(seq_count)
            for m in range(members)
        ]
        return lax.ppermute(part, ("seq", "kv"), pairs)

    def climb(part, d):
        return lax.ppermute(
            part, "seq", [(s, s + COLUMNS * d) for s in range(seq_count - COLUMNS * d)]
        )

    def sink(part, d):
        return lax.ppermute(
            part, "seq", [(s, s - COLUMNS * d) for s in range(COLUMNS * d, seq_count)]
        )

    own_pair, both = pick_pair(layout.T, keys, values)
    both = both.reshape(2, near, feat_width)
    column = jnp.stack([own_pair] + [climb(own_pair, d) for d in range(1, levels)])
    crossing = [
        [column if (c, step) == (0, 0) else hop(column, c, step) for c in range(COLUMNS)]
        for step in range(0, members, 2)
    ]
    near_parts = [both, hop(both, 0, 1)]
    for step in range(2, members, 2):
        landed, _ = lax.optimization_barrier((hop(both, 0, step), column))
        near_parts += [landed, hop(landed, 0, 1)]

    def rows_out(dtype):
        return jax.ShapeDtypeStruct((tok_rows, feat_width), dtype)

    near_out = jax.ShapeDtypeStruct((near, feat_width), jnp.float32)
    far_out = jax.ShapeDtypeStruct(column.shape, jnp.bfloat16)
    bias_scratch = [pltpu.VMEM((tok_rows, members * near), jnp.float32)]
    near_pairs = HEADS * tok_rows * members * near
    far_width = members * seq_count * part_tok
    far_pairs = HEADS * tok_rows * far_width
    roomy = far_width <= 512
    far_plan = (tok_rows // 2, GROUP, 2 * GROUP) if roomy else (tok_rows // 8, 1, 1)

    near_sum, near_stat = call(
        functools.partial(near_forward_kernel, members, blk_len, part_tok),
        [queries] + near_parts,
        [rows_out(jnp.float32), rows_out(jnp.float32)],
        bias_scratch,
        near_pairs,
        2,
        head_dim,
    )
    far_parts = []
    for group in crossing:
        group, _ = lax.optimization_barrier((group, near_stat))
        far_parts += group + [hop(part, 0, 1) for part in group]
    attended, far_gq, stat, own_grad, cross_grad = call(
        functools.partial(far_kernel, members, *far_plan),
        [queries, grad_out, near_sum, near_stat] + far_parts,
        [rows_out(jnp.bfloat16), rows_out(jnp.float32), rows_out(jnp.float32), far_out, far_out],
        [],
        far_pairs,
        5,
        head_dim,
    )
    crossed = hop(cross_grad, 1, 0)
    returned = [crossed[0].astype(jnp.float32)]
    for d in range(1, levels):
        summed = own_grad[d].astype(jnp.float32) + crossed[d].astype(jnp.float32)
        returned.append(sink(summed.astype(jnp.bfloat16), d).astype(jnp.float32))
    grad_q, near_k, near_v = call(
        functools.partial(near_backward_kernel, members, blk_len, part_tok),
        [queries, grad_out, stat, far_gq] + near_parts,
        [rows_out(jnp.bfloat16), near_out, near_out],
        bias_scratch,
        near_pairs,
        4,
        head_dim,
    )
    extra = functools.reduce(lambda a, b: a + b, returned)
    chosen = (jnp.arange(blocks) == summary_local)[:, None, None]

    def finish(near_term, far_term):
        near_term = near_term.reshape(blocks, part_tok, feat_width)
        return (near_term + jnp.where(chosen, far_term[None], 0.0)).astype(jnp.bfloat16)

    return (attended, grad_q, finish(near_k, extra[0]), finish(near_v, extra[1]))


def solution(mesh):
    return jax.shard_map(
        shards,
        mesh=mesh,
        in_specs=(P("seq", None), P("seq", "kv", None), P("seq", "kv", None), P(), P("seq", None)),
        out_specs=(P("seq", None), P("seq", None), P("seq", "kv", None), P("seq", "kv", None)),
        check_vma=False,
    )
```

```python
import functools
import math

import jax
import jax.numpy as jnp
from jax import lax
from jax.experimental import pallas as pl
from jax.experimental.pallas import tpu as pltpu
from jax.sharding import PartitionSpec as P

HEADS = 8
COLUMNS = 2
GROUP = 2
HIDDEN = -1e30
NT = (((1,), (1,)), ((), ()))
NN = (((1,), (0,)), ((), ()))
TN = (((0,), (0,)), ((), ()))
WHOLE = pl.BlockSpec(memory_space=pltpu.VMEM)
LIMIT = pltpu.CompilerParams(vmem_limit_bytes=20 * 1024 * 1024)


def dot(a, b, dims):
    return lax.dot_general(a, b, dims, preferred_element_type=jnp.float32)


def wide(rows, width):
    return jnp.concatenate([rows] * (width // rows.shape[1]), axis=1)


def base2_scale(head_dim):
    return math.log2(math.e) / math.sqrt(head_dim)


def pick_kernel(table_ref, keys_ref, values_ref, pair_ref, both_ref):
    window = lax.axis_index("seq")
    blocks = keys_ref.shape[0]
    pick = jnp.minimum(window, lax.axis_size("seq") - 2)
    block = table_ref[pick, table_ref.shape[1] - 1] - window * blocks
    block = jnp.clip(block, 0, blocks - 1)
    pair_ref[0] = keys_ref[block]
    pair_ref[1] = values_ref[block]
    both_ref[0] = keys_ref[...]
    both_ref[1] = values_ref[...]


def pick_pair(table, keys, values):
    _, part_tok, feat_width = keys.shape
    return pl.pallas_call(
        pick_kernel,
        in_specs=[pl.BlockSpec(memory_space=pltpu.SMEM), WHOLE, WHOLE],
        out_specs=[WHOLE, WHOLE],
        out_shape=[
            jax.ShapeDtypeStruct((2, part_tok, feat_width), keys.dtype),
            jax.ShapeDtypeStruct((2,) + keys.shape, keys.dtype),
        ],
    )(table, keys, values)


def near_tiles(rows, near):
    half = rows // 2
    return [(0, half, near // 2), (half, half, near)]


def mask_kernel(members, near, blk_len, part_tok, pair_ref, q_ref, g_ref, bias_ref):
    member = lax.axis_index("kv")
    shift = part_tok.bit_length() - 1
    for start, count, used in near_tiles(bias_ref.shape[0], near):
        row = start + lax.broadcasted_iota(jnp.int32, (count, 1), 0)
        col = lax.broadcasted_iota(jnp.int32, (1, used), 1)
        key_tok = (col >> shift) * blk_len + (col & (part_tok - 1))
        for j in range(members):
            key_pos = key_tok + (member ^ j) * part_tok
            bias_ref[start : start + count, j * used : (j + 1) * used] = jnp.where(
                key_pos <= row, 0.0, HIDDEN
            )


def head_columns(head, feat_width):
    head_dim = feat_width // HEADS
    return pl.ds(pl.multiple_of(head * head_dim, head_dim), head_dim)


def near_rows(parts, which, used, cols):
    return jnp.concatenate([ref[which, :used, cols] for ref in parts], axis=0)


def near_forward_kernel(members, bias_ref, q_ref, *refs):
    parts = refs[:members]
    out_ref, stat_ref = refs[members:]
    rows, feat_width = q_ref.shape
    head_dim = feat_width // HEADS
    near = parts[0].shape[1]

    @pl.loop(0, HEADS // GROUP)
    def _(group):
        units = [
            (head_columns(group * GROUP + i, feat_width), pl.ds(start, count), used)
            for i in range(GROUP)
            for start, count, used in near_tiles(rows, near)
        ]
        raws = [
            dot(q_ref[here, cols], near_rows(parts, 0, used, cols), NT) * base2_scale(head_dim)
            + bias_ref[here, : members * used]
            for cols, here, used in units
        ]
        peaks = [jnp.max(raw, axis=1, keepdims=True) for raw in raws]
        weights = [jnp.exp2(raw - peak) for raw, peak in zip(raws, peaks)]
        totals = [jnp.sum(weight, axis=1, keepdims=True) for weight in weights]
        sums = [
            dot(weight.astype(jnp.bfloat16), near_rows(parts, 1, used, cols), NN)
            for weight, (cols, here, used) in zip(weights, units)
        ]
        for (cols, here, used), peak, total, summed in zip(units, peaks, totals, sums):
            level = peak + jnp.log2(total)
            stat_ref[here, cols] = jnp.broadcast_to(level, summed.shape)
            out_ref[here, cols] = summed * (1.0 / total)


def far_rows(parts, which, cols):
    steps, _, part_tok, _ = parts[0].shape
    return jnp.concatenate(
        [ref[:, which, :, cols].reshape(steps * part_tok, cols.size) for ref in parts], axis=0
    )


def far_kernel(members, tile, heads, batch, q_ref, g_ref, sum_ref, stat_ref, *refs):
    parts = refs[: COLUMNS * members]
    att_ref, gq_ref, level_ref, drift_ref = refs[COLUMNS * members : COLUMNS * members + 4]
    grad_refs = refs[COLUMNS * members + 4 :]
    rows, feat_width = q_ref.shape
    head_dim = feat_width // HEADS
    steps, _, part_tok, _ = parts[0].shape
    span = steps * part_tok
    width = COLUMNS * span
    score_scale = 1.0 / math.sqrt(head_dim)
    window = lax.axis_index("seq")
    level, side = window // COLUMNS, window % COLUMNS
    step = lax.broadcasted_iota(jnp.int32, (1, span), 1) >> (part_tok.bit_length() - 1)
    valid = [(step >= 1) & (step <= level), (step >= 1 - side) & (step <= level)]
    bias = jnp.concatenate([jnp.where(ok, 0.0, HIDDEN) for ok in valid] * members, axis=1)
    total_width = members * width

    def work(units, keys, values, key_grads, value_grads):
        raws = [
            dot(q_ref[here, cols], keys[i], NT) * base2_scale(head_dim) + bias
            for i, cols, here in units
        ]
        grad_probs = [dot(g_ref[here, cols], values[i], NT) for i, cols, here in units]
        near_levels = [stat_ref[here, cols] for i, cols, here in units]
        peaks = [
            jnp.maximum(near_level, jnp.max(raw, axis=1, keepdims=True))
            for near_level, raw in zip(near_levels, raws)
        ]
        near_weights = [jnp.exp2(near_level - peak) for near_level, peak in zip(near_levels, peaks)]
        weights = [jnp.exp2(raw - wide(peak, total_width)) for raw, peak in zip(raws, peaks)]
        totals = [
            near_weight + jnp.sum(weight, axis=1, keepdims=True)
            for near_weight, weight in zip(near_weights, weights)
        ]
        inverses = [1.0 / total for total in totals]
        sums = [
            dot(weight.astype(jnp.bfloat16), values[i], NN)
            for weight, (i, cols, here) in zip(weights, units)
        ]
        drifts = []
        for u, (i, cols, here) in enumerate(units):
            summed = sum_ref[here, cols] * near_weights[u] + sums[u]
            attended = (summed * inverses[u]).astype(jnp.bfloat16)
            att_ref[here, cols] = attended
            product = g_ref[here, cols].astype(jnp.float32) * attended.astype(jnp.float32)
            drift = jnp.broadcast_to(jnp.sum(product, axis=1, keepdims=True), product.shape)
            drifts.append(drift)
            level_ref[here, cols] = peaks[u] + jnp.log2(totals[u])
            drift_ref[here, cols] = drift
        moved = [
            weight * (grad_prob - wide(drift, total_width))
            for weight, grad_prob, drift in zip(weights, grad_probs, drifts)
        ]
        factors = [inverse * score_scale for inverse in inverses]
        own_scores = [
            (part[:, :width] * wide(factor, width)).astype(jnp.bfloat16)
            for part, factor in zip(moved, factors)
        ]
        own_probs = [
            (weight[:, :width] * wide(inverse, width)).astype(jnp.bfloat16)
            for weight, inverse in zip(weights, inverses)
        ]
        for u, (i, cols, here) in enumerate(units):
            gq_ref[here, cols] = dot(moved[u].astype(jnp.bfloat16), keys[i], NN) * factors[u]
        for u, (i, cols, here) in enumerate(units):
            key_grads[i].append(dot(own_scores[u], q_ref[here, cols], TN))
            value_grads[i].append(dot(own_probs[u], g_ref[here, cols], TN))

    @pl.loop(0, HEADS // heads)
    def _(group):
        columns = [head_columns(group * heads + i, feat_width) for i in range(heads)]
        units = [
            (i, cols, pl.ds(r, tile)) for i, cols in enumerate(columns) for r in range(0, rows, tile)
        ]
        keys = [far_rows(parts, 0, cols) for cols in columns]
        values = [far_rows(parts, 1, cols) for cols in columns]
        grads = [[[] for _ in columns] for _ in range(2)]
        for first in range(0, len(units), batch):
            work(units[first : first + batch], keys, values, *grads)
        for which, per_head in enumerate(grads):
            for cols, terms in zip(columns, per_head):
                total = functools.reduce(lambda a, b: a + b, terms).astype(jnp.bfloat16)
                for c, ref in enumerate(grad_refs):
                    piece = total[c * span : (c + 1) * span]
                    ref[:, which, :, cols] = piece.reshape(steps, part_tok, head_dim)


def near_backward_kernel(members, bias_ref, q_ref, g_ref, level_ref, drift_ref, far_gq_ref, *refs):
    parts = refs[:members]
    gq_ref, gk_ref, gv_ref = refs[members:]
    rows, feat_width = q_ref.shape
    head_dim = feat_width // HEADS
    near = parts[0].shape[1]
    score_scale = 1.0 / math.sqrt(head_dim)

    @pl.loop(0, HEADS // GROUP)
    def _(group):
        units = [
            (head_columns(group * GROUP + i, feat_width), pl.ds(start, count), used)
            for i in range(GROUP)
            for start, count, used in reversed(near_tiles(rows, near))
        ]
        keys = [near_rows(parts, 0, used, cols) for cols, here, used in units]
        values = [near_rows(parts, 1, used, cols) for cols, here, used in units]
        raws = [
            dot(q_ref[here, cols], key, NT) * base2_scale(head_dim)
            + bias_ref[here, : members * used]
            for (cols, here, used), key in zip(units, keys)
        ]
        grad_probs = [
            dot(g_ref[here, cols], value, NT) for (cols, here, used), value in zip(units, values)
        ]
        probs = [
            jnp.exp2(raw - wide(level_ref[here, cols], raw.shape[1]))
            for raw, (cols, here, used) in zip(raws, units)
        ]
        moved = [
            prob * (grad_prob - wide(drift_ref[here, cols], prob.shape[1]))
            for prob, grad_prob, (cols, here, used) in zip(probs, grad_probs, units)
        ]
        for (cols, here, used), part, key in zip(units, moved, keys):
            gq_ref[here, cols] = (
                dot(part.astype(jnp.bfloat16), key, NN) * score_scale + far_gq_ref[here, cols]
            ).astype(jnp.bfloat16)
        for (cols, here, used), part, prob in zip(units, moved, probs):
            own_score = (part[:, :used] * score_scale).astype(jnp.bfloat16)
            own_prob = prob[:, :used].astype(jnp.bfloat16)
            for left, right_ref, ref in ((own_score, q_ref, gk_ref), (own_prob, g_ref, gv_ref)):
                grad = dot(left, right_ref[here, cols], TN)
                if used == near:
                    ref[:, cols] = grad
                else:
                    ref[:used, cols] += grad


def call(kernel, operands, outs, pairs, products, head_dim):
    moved_bytes = sum(a.size * a.dtype.itemsize for a in operands)
    return pl.pallas_call(
        kernel,
        in_specs=[WHOLE] * len(operands),
        out_specs=[WHOLE] * len(outs),
        out_shape=outs,
        compiler_params=LIMIT,
        cost_estimate=pl.CostEstimate(
            flops=4 * products * pairs * head_dim, bytes_accessed=moved_bytes, transcendentals=pairs
        ),
    )(*operands)


def shards(queries, keys, values, layout, grad_out):
    seq_count = lax.axis_size("seq")
    seq_index = lax.axis_index("seq")
    members = lax.axis_size("kv")
    tok_rows, feat_width = queries.shape
    blocks, part_tok = (keys.shape[0], keys.shape[1])
    blk_len = part_tok * members
    near = blocks * part_tok
    head_dim = feat_width // HEADS
    levels = seq_count // COLUMNS
    pick_window = jnp.minimum(seq_index, seq_count - 2)
    last_row = layout[layout.shape[0] - 1]
    summary_local = jnp.clip(last_row[pick_window] - seq_index * blocks, 0, blocks - 1)

    def hop(part, column_step, member_step):
        pairs = [
            (s * members + m, (s ^ column_step) * members + (m ^ member_step))
            for s in range(seq_count)
            for m in range(members)
        ]
        return lax.ppermute(part, ("seq", "kv"), pairs)

    def climb(part, d):
        return lax.ppermute(
            part, "seq", [(s, s + COLUMNS * d) for s in range(seq_count - COLUMNS * d)]
        )

    def sink(part, d):
        return lax.ppermute(
            part, "seq", [(s, s - COLUMNS * d) for s in range(COLUMNS * d, seq_count)]
        )

    own_pair, both = pick_pair(layout.T, keys, values)
    both = both.reshape(2, near, feat_width)
    column = jnp.stack([own_pair] + [climb(own_pair, d) for d in range(1, levels)])
    bias = call(
        functools.partial(mask_kernel, members, near, blk_len, part_tok),
        [own_pair, queries, grad_out],
        [jax.ShapeDtypeStruct((tok_rows, members * near), jnp.float32)],
        tok_rows * members * near,
        0,
        1,
    )[0]
    column, bias = lax.optimization_barrier((column, bias))
    crossing = [
        [column if (c, step) == (0, 0) else hop(column, c, step) for c in range(COLUMNS)]
        for step in range(0, members, 2)
    ]
    near_parts = [both, hop(both, 0, 1)]
    for step in range(2, members, 2):
        landed, _ = lax.optimization_barrier((hop(both, 0, step), column))
        near_parts += [landed, hop(landed, 0, 1)]

    def rows_out(dtype):
        return jax.ShapeDtypeStruct((tok_rows, feat_width), dtype)

    near_out = jax.ShapeDtypeStruct((near, feat_width), jnp.float32)
    far_out = jax.ShapeDtypeStruct(column.shape, jnp.bfloat16)
    near_pairs = HEADS * tok_rows * members * near
    far_width = members * seq_count * part_tok
    far_pairs = HEADS * tok_rows * far_width
    roomy = far_width <= 512
    far_plan = (tok_rows // 2, GROUP, 2 * GROUP) if roomy else (tok_rows // 8, 1, 1)

    near_sum, near_stat = call(
        functools.partial(near_forward_kernel, members),
        [bias, queries] + near_parts,
        [rows_out(jnp.float32), rows_out(jnp.float32)],
        near_pairs,
        2,
        head_dim,
    )
    far_parts = []
    for group in crossing:
        group, _ = lax.optimization_barrier((group, near_stat))
        far_parts += group + [hop(part, 0, 1) for part in group]
    attended, far_gq, level, drift, own_grad, cross_grad = call(
        functools.partial(far_kernel, members, *far_plan),
        [queries, grad_out, near_sum, near_stat] + far_parts,
        [rows_out(jnp.bfloat16)] + [rows_out(jnp.float32)] * 3 + [far_out, far_out],
        far_pairs,
        5,
        head_dim,
    )
    grad_q, near_k, near_v = call(
        functools.partial(near_backward_kernel, members),
        [bias, queries, grad_out, level, drift, far_gq] + near_parts,
        [rows_out(jnp.bfloat16), near_out, near_out],
        near_pairs,
        4,
        head_dim,
    )
    crossed, near_k = lax.optimization_barrier((hop(cross_grad, 1, 0), near_k))
    returned = [crossed[0].astype(jnp.float32)]
    for d in range(1, levels):
        summed = own_grad[d].astype(jnp.float32) + crossed[d].astype(jnp.float32)
        returned.append(sink(summed.astype(jnp.bfloat16), d).astype(jnp.float32))
    extra = functools.reduce(lambda a, b: a + b, returned)
    chosen = (jnp.arange(blocks) == summary_local)[:, None, None]

    def finish(near_term, far_term):
        near_term = near_term.reshape(blocks, part_tok, feat_width)
        return (near_term + jnp.where(chosen, far_term[None], 0.0)).astype(jnp.bfloat16)

    return (attended, grad_q, finish(near_k, extra[0]), finish(near_v, extra[1]))


def solution(mesh):
    return jax.shard_map(
        shards,
        mesh=mesh,
        in_specs=(P("seq", None), P("seq", "kv", None), P("seq", "kv", None), P(), P("seq", None)),
        out_specs=(P("seq", None), P("seq", None), P("seq", "kv", None), P("seq", "kv", None)),
        check_vma=False,
    )
```

```python
import functools
import math

import jax
import jax.numpy as jnp
from jax import lax
from jax.experimental import pallas as pl
from jax.experimental.pallas import tpu as pltpu
from jax.sharding import PartitionSpec as P

HEADS = 8
COLUMNS = 2
GROUP = 2
HIDDEN = -1e30
NT = (((1,), (1,)), ((), ()))
NN = (((1,), (0,)), ((), ()))
TN = (((0,), (0,)), ((), ()))
WHOLE = pl.BlockSpec(memory_space=pltpu.VMEM)
LIMIT = pltpu.CompilerParams(vmem_limit_bytes=20 * 1024 * 1024)


def dot(a, b, dims):
    return lax.dot_general(a, b, dims, preferred_element_type=jnp.float32)


def wide(rows, width):
    return jnp.concatenate([rows] * (width // rows.shape[1]), axis=1)


def base2_scale(head_dim):
    return math.log2(math.e) / math.sqrt(head_dim)


def pick_kernel(table_ref, keys_ref, values_ref, pair_ref, both_ref):
    block = chosen_block(table_ref, keys_ref.shape[0])
    pair_ref[0] = keys_ref[block]
    pair_ref[1] = values_ref[block]
    both_ref[0] = keys_ref[...]
    both_ref[1] = values_ref[...]


def pick_pair(table, keys, values):
    _, part_tok, feat_width = keys.shape
    return pl.pallas_call(
        pick_kernel,
        in_specs=[pl.BlockSpec(memory_space=pltpu.SMEM), WHOLE, WHOLE],
        out_specs=[WHOLE, WHOLE],
        out_shape=[
            jax.ShapeDtypeStruct((2, part_tok, feat_width), keys.dtype),
            jax.ShapeDtypeStruct((2,) + keys.shape, keys.dtype),
        ],
    )(table, keys, values)


def near_tiles(rows, near):
    half = rows // 2
    return [(0, half, near // 2), (half, half, near)]


def mask_kernel(members, near, blk_len, part_tok, pair_ref, q_ref, g_ref, bias_ref):
    member = lax.axis_index("kv")
    shift = part_tok.bit_length() - 1
    for start, count, used in near_tiles(bias_ref.shape[0], near):
        row = start + lax.broadcasted_iota(jnp.int32, (count, 1), 0)
        col = lax.broadcasted_iota(jnp.int32, (1, used), 1)
        key_tok = (col >> shift) * blk_len + (col & (part_tok - 1))
        for j in range(members):
            key_pos = key_tok + (member ^ j) * part_tok
            bias_ref[start : start + count, j * used : (j + 1) * used] = jnp.where(
                key_pos <= row, 0.0, HIDDEN
            )


def head_columns(head, feat_width):
    head_dim = feat_width // HEADS
    return pl.ds(pl.multiple_of(head * head_dim, head_dim), head_dim)


def near_rows(parts, which, used, cols):
    return jnp.concatenate([ref[which, :used, cols] for ref in parts], axis=0)


def near_forward_kernel(members, bias_ref, q_ref, *refs):
    parts = refs[:members]
    out_ref, stat_ref = refs[members:]
    rows, feat_width = q_ref.shape
    head_dim = feat_width // HEADS
    near = parts[0].shape[1]

    @pl.loop(0, HEADS // GROUP)
    def _(group):
        units = [
            (head_columns(group * GROUP + i, feat_width), pl.ds(start, count), used)
            for i in range(GROUP)
            for start, count, used in near_tiles(rows, near)
        ]
        raws = [
            dot(q_ref[here, cols], near_rows(parts, 0, used, cols), NT) * base2_scale(head_dim)
            + bias_ref[here, : members * used]
            for cols, here, used in units
        ]
        peaks = [jnp.max(raw, axis=1, keepdims=True) for raw in raws]
        weights = [jnp.exp2(raw - peak) for raw, peak in zip(raws, peaks)]
        totals = [jnp.sum(weight, axis=1, keepdims=True) for weight in weights]
        sums = [
            dot(weight.astype(jnp.bfloat16), near_rows(parts, 1, used, cols), NN)
            for weight, (cols, here, used) in zip(weights, units)
        ]
        for (cols, here, used), peak, total, summed in zip(units, peaks, totals, sums):
            level = peak + jnp.log2(total)
            stat_ref[here, cols] = jnp.broadcast_to(level, summed.shape)
            out_ref[here, cols] = summed * (1.0 / total)


def far_rows(parts, which, cols):
    rows = []
    for pair_ref, column_ref in zip(parts[0::2], parts[1::2]):
        steps, _, part_tok, _ = column_ref.shape
        rows.append(pair_ref[which, :, cols])
        rows.append(column_ref[:, which, :, cols].reshape(steps * part_tok, cols.size))
    return jnp.concatenate(rows, axis=0)


def far_kernel(members, tile, heads, batch, q_ref, g_ref, sum_ref, stat_ref, *refs):
    parts = refs[: 2 * COLUMNS * members]
    att_ref, gq_ref, level_ref, drift_ref, *grad_refs = refs[2 * COLUMNS * members :]
    rows, feat_width = q_ref.shape
    head_dim = feat_width // HEADS
    steps, _, part_tok, _ = grad_refs[0].shape
    span = steps * part_tok
    width = COLUMNS * span
    score_scale = 1.0 / math.sqrt(head_dim)
    window = lax.axis_index("seq")
    level, side = window // COLUMNS, window % COLUMNS
    step = lax.broadcasted_iota(jnp.int32, (1, span), 1) >> (part_tok.bit_length() - 1)
    valid = [(step >= 1) & (step <= level), (step >= 1 - side) & (step <= level)]
    bias = jnp.concatenate([jnp.where(ok, 0.0, HIDDEN) for ok in valid] * members, axis=1)
    total_width = members * width

    def work(units, keys, values, key_grads, value_grads):
        raws = [
            dot(q_ref[here, cols], keys[i], NT) * base2_scale(head_dim) + bias
            for i, cols, here in units
        ]
        grad_probs = [dot(g_ref[here, cols], values[i], NT) for i, cols, here in units]
        near_levels = [stat_ref[here, cols] for i, cols, here in units]
        peaks = [
            jnp.maximum(near_level, jnp.max(raw, axis=1, keepdims=True))
            for near_level, raw in zip(near_levels, raws)
        ]
        near_weights = [jnp.exp2(near_level - peak) for near_level, peak in zip(near_levels, peaks)]
        weights = [jnp.exp2(raw - wide(peak, total_width)) for raw, peak in zip(raws, peaks)]
        totals = [
            near_weight + jnp.sum(weight, axis=1, keepdims=True)
            for near_weight, weight in zip(near_weights, weights)
        ]
        inverses = [1.0 / total for total in totals]
        sums = [
            dot(weight.astype(jnp.bfloat16), values[i], NN)
            for weight, (i, cols, here) in zip(weights, units)
        ]
        drifts = []
        for u, (i, cols, here) in enumerate(units):
            summed = sum_ref[here, cols] * near_weights[u] + sums[u]
            attended = (summed * inverses[u]).astype(jnp.bfloat16)
            att_ref[here, cols] = attended
            product = g_ref[here, cols].astype(jnp.float32) * attended.astype(jnp.float32)
            drift = jnp.broadcast_to(jnp.sum(product, axis=1, keepdims=True), product.shape)
            drifts.append(drift)
            level_ref[here, cols] = peaks[u] + jnp.log2(totals[u])
            drift_ref[here, cols] = drift
        moved = [
            weight * (grad_prob - wide(drift, total_width))
            for weight, grad_prob, drift in zip(weights, grad_probs, drifts)
        ]
        factors = [inverse * score_scale for inverse in inverses]
        own_scores = [
            (part[:, :width] * wide(factor, width)).astype(jnp.bfloat16)
            for part, factor in zip(moved, factors)
        ]
        own_probs = [
            (weight[:, :width] * wide(inverse, width)).astype(jnp.bfloat16)
            for weight, inverse in zip(weights, inverses)
        ]
        for u, (i, cols, here) in enumerate(units):
            gq_ref[here, cols] = dot(moved[u].astype(jnp.bfloat16), keys[i], NN) * factors[u]
        for u, (i, cols, here) in enumerate(units):
            key_grads[i].append(dot(own_scores[u], q_ref[here, cols], TN))
            value_grads[i].append(dot(own_probs[u], g_ref[here, cols], TN))

    @pl.loop(0, HEADS // heads)
    def _(group):
        columns = [head_columns(group * heads + i, feat_width) for i in range(heads)]
        units = [
            (i, cols, pl.ds(r, tile)) for i, cols in enumerate(columns) for r in range(0, rows, tile)
        ]
        keys = [far_rows(parts, 0, cols) for cols in columns]
        values = [far_rows(parts, 1, cols) for cols in columns]
        grads = [[[] for _ in columns] for _ in range(2)]
        for first in range(0, len(units), batch):
            work(units[first : first + batch], keys, values, *grads)
        for which, per_head in enumerate(grads):
            for cols, terms in zip(columns, per_head):
                total = functools.reduce(lambda a, b: a + b, terms).astype(jnp.bfloat16)
                for c, ref in enumerate(grad_refs):
                    piece = total[c * span : (c + 1) * span]
                    ref[:, which, :, cols] = piece.reshape(steps, part_tok, head_dim)


def near_backward_kernel(members, bias_ref, q_ref, g_ref, level_ref, drift_ref, far_gq_ref, *refs):
    parts = refs[:members]
    gq_ref, gk_ref, gv_ref = refs[members:]
    rows, feat_width = q_ref.shape
    head_dim = feat_width // HEADS
    near = parts[0].shape[1]
    score_scale = 1.0 / math.sqrt(head_dim)

    @pl.loop(0, HEADS // GROUP)
    def _(group):
        units = [
            (head_columns(group * GROUP + i, feat_width), pl.ds(start, count), used)
            for i in range(GROUP)
            for start, count, used in reversed(near_tiles(rows, near))
        ]
        keys = [near_rows(parts, 0, used, cols) for cols, here, used in units]
        values = [near_rows(parts, 1, used, cols) for cols, here, used in units]
        raws = [
            dot(q_ref[here, cols], key, NT) * base2_scale(head_dim)
            + bias_ref[here, : members * used]
            for (cols, here, used), key in zip(units, keys)
        ]
        grad_probs = [
            dot(g_ref[here, cols], value, NT) for (cols, here, used), value in zip(units, values)
        ]
        probs = [
            jnp.exp2(raw - wide(level_ref[here, cols], raw.shape[1]))
            for raw, (cols, here, used) in zip(raws, units)
        ]
        moved = [
            prob * (grad_prob - wide(drift_ref[here, cols], prob.shape[1]))
            for prob, grad_prob, (cols, here, used) in zip(probs, grad_probs, units)
        ]
        for (cols, here, used), part, key in zip(units, moved, keys):
            gq_ref[here, cols] = (
                dot(part.astype(jnp.bfloat16), key, NN) * score_scale + far_gq_ref[here, cols]
            ).astype(jnp.bfloat16)
        for (cols, here, used), part, prob in zip(units, moved, probs):
            own_score = (part[:, :used] * score_scale).astype(jnp.bfloat16)
            own_prob = prob[:, :used].astype(jnp.bfloat16)
            for left, right_ref, ref in ((own_score, q_ref, gk_ref), (own_prob, g_ref, gv_ref)):
                grad = dot(left, right_ref[here, cols], TN)
                if used == near:
                    ref[:, cols] = grad
                else:
                    ref[:used, cols] += grad


def chosen_block(table_ref, blocks):
    window = lax.axis_index("seq")
    pick = jnp.minimum(window, lax.axis_size("seq") - 2)
    block = table_ref[pick, table_ref.shape[1] - 1] - window * blocks
    return jnp.clip(block, 0, blocks - 1)


def finish_kernel(blocks, table_ref, gk_ref, gv_ref, crossed_ref, *refs):
    arrived = refs[:-2]
    part_tok = gk_ref.shape[0] // blocks
    block = chosen_block(table_ref, blocks)
    here = pl.ds(pl.multiple_of(block * part_tok, part_tok), part_tok)
    for which, (near_ref, out_ref) in enumerate(zip((gk_ref, gv_ref), refs[-2:])):
        out_ref[...] = near_ref[...].astype(out_ref.dtype)
        extra = crossed_ref[0, which].astype(jnp.float32)
        for ref in arrived:
            extra += ref[which].astype(jnp.float32)
        out_ref[here] = (near_ref[here] + extra).astype(out_ref.dtype)


def call(kernel, operands, outs, pairs, products, head_dim):
    moved_bytes = sum(a.size * a.dtype.itemsize for a in operands)
    return pl.pallas_call(
        kernel,
        in_specs=[WHOLE] * len(operands),
        out_specs=[WHOLE] * len(outs),
        out_shape=outs,
        compiler_params=LIMIT,
        cost_estimate=pl.CostEstimate(
            flops=4 * products * pairs * head_dim, bytes_accessed=moved_bytes, transcendentals=pairs
        ),
    )(*operands)


def shards(queries, keys, values, layout, grad_out):
    seq_count = lax.axis_size("seq")
    members = lax.axis_size("kv")
    tok_rows, feat_width = queries.shape
    blocks, part_tok = (keys.shape[0], keys.shape[1])
    blk_len = part_tok * members
    near = blocks * part_tok
    head_dim = feat_width // HEADS
    levels = seq_count // COLUMNS
    def hop(part, column_step, member_step):
        pairs = [
            (s * members + m, (s ^ column_step) * members + (m ^ member_step))
            for s in range(seq_count)
            for m in range(members)
        ]
        return lax.ppermute(part, ("seq", "kv"), pairs)

    def climb(part, d):
        return lax.ppermute(
            part, "seq", [(s, s + COLUMNS * d) for s in range(seq_count - COLUMNS * d)]
        )

    def sink(part, d):
        return lax.ppermute(
            part, "seq", [(s, s - COLUMNS * d) for s in range(COLUMNS * d, seq_count)]
        )

    own_pair, both = pick_pair(layout.T, keys, values)
    both = both.reshape(2, near, feat_width)
    column = jnp.stack([climb(own_pair, d) for d in range(1, levels)])
    bias = call(
        functools.partial(mask_kernel, members, near, blk_len, part_tok),
        [own_pair, queries, grad_out],
        [jax.ShapeDtypeStruct((tok_rows, members * near), jnp.float32)],
        tok_rows * members * near,
        0,
        1,
    )[0]
    cross_pairs = []
    for step in range(0, members, 2):
        pair = hop(own_pair, 1, step)
        cross_pairs += [pair, hop(pair, 0, 1)]
    column, bias, cross_pairs = lax.optimization_barrier((column, bias, cross_pairs))
    crossing = [
        [column if (c, step) == (0, 0) else hop(column, c, step) for c in range(COLUMNS)]
        for step in range(0, members, 2)
    ]
    near_parts = [both, hop(both, 0, 1)]
    for step in range(2, members, 2):
        landed, _ = lax.optimization_barrier((hop(both, 0, step), column))
        near_parts += [landed, hop(landed, 0, 1)]

    def rows_out(dtype):
        return jax.ShapeDtypeStruct((tok_rows, feat_width), dtype)

    near_out = jax.ShapeDtypeStruct((near, feat_width), jnp.float32)
    far_out = jax.ShapeDtypeStruct((levels,) + own_pair.shape, jnp.bfloat16)
    near_pairs = HEADS * tok_rows * members * near
    far_width = members * seq_count * part_tok
    far_pairs = HEADS * tok_rows * far_width
    roomy = far_width <= 512
    far_plan = (tok_rows // 2, GROUP, 2 * GROUP) if roomy else (tok_rows // 8, 1, 1)

    near_sum, near_stat = call(
        functools.partial(near_forward_kernel, members),
        [bias, queries] + near_parts,
        [pltpu.VMEM((tok_rows, feat_width), jnp.float32)] * 2,
        near_pairs,
        2,
        head_dim,
    )
    far_parts = []
    for group in crossing:
        group, _ = lax.optimization_barrier((group, near_stat))
        for same, other in (group, [hop(part, 0, 1) for part in group]):
            far_parts += [own_pair, same, cross_pairs[len(far_parts) // 4], other]
    attended, far_gq, level, drift, own_grad, cross_grad = call(
        functools.partial(far_kernel, members, *far_plan),
        [queries, grad_out, near_sum, near_stat] + far_parts,
        [rows_out(jnp.bfloat16)] + [rows_out(jnp.float32)] * 3 + [far_out, far_out],
        far_pairs,
        5,
        head_dim,
    )
    grad_q, near_k, near_v = call(
        functools.partial(near_backward_kernel, members),
        [bias, queries, grad_out, level, drift, far_gq] + near_parts,
        [rows_out(jnp.bfloat16), near_out, near_out],
        near_pairs,
        4,
        head_dim,
    )
    crossed, near_k = lax.optimization_barrier((hop(cross_grad, 1, 0), near_k))
    returned = []
    for d in range(1, levels):
        summed = own_grad[d].astype(jnp.float32) + crossed[d].astype(jnp.float32)
        returned.append(sink(summed.astype(jnp.bfloat16), d))
    grad_k, grad_v = pl.pallas_call(
        functools.partial(finish_kernel, blocks),
        in_specs=[pl.BlockSpec(memory_space=pltpu.SMEM)] + [WHOLE] * (2 + levels),
        out_specs=[WHOLE, WHOLE],
        out_shape=[jax.ShapeDtypeStruct((near, feat_width), jnp.bfloat16)] * 2,
    )(layout.T, near_k, near_v, crossed, *returned)
    return (attended, grad_q, grad_k.reshape(keys.shape), grad_v.reshape(values.shape))


def solution(mesh):
    return jax.shard_map(
        shards,
        mesh=mesh,
        in_specs=(P("seq", None), P("seq", "kv", None), P("seq", "kv", None), P(), P("seq", None)),
        out_specs=(P("seq", None), P("seq", None), P("seq", "kv", None), P("seq", "kv", None)),
        check_vma=False,
    )
```

```python
import functools
import math

import jax
import jax.numpy as jnp
from jax import lax
from jax.experimental import pallas as pl
from jax.experimental.pallas import tpu as pltpu
from jax.sharding import PartitionSpec as P

HEADS = 8
COLUMNS = 2
GROUP = 2
HIDDEN = -1e30
NT = (((1,), (1,)), ((), ()))
NN = (((1,), (0,)), ((), ()))
TN = (((0,), (0,)), ((), ()))
WHOLE = pl.BlockSpec(memory_space=pltpu.VMEM)
LIMIT = pltpu.CompilerParams(vmem_limit_bytes=20 * 1024 * 1024)


def dot(a, b, dims):
    return lax.dot_general(a, b, dims, preferred_element_type=jnp.float32)


def wide(rows, width):
    return jnp.concatenate([rows] * (width // rows.shape[1]), axis=1)


def base2_scale(head_dim):
    return math.log2(math.e) / math.sqrt(head_dim)


def pick_kernel(table_ref, keys_ref, values_ref, pair_ref, both_ref, block_ref):
    window = lax.axis_index("seq")
    blocks = keys_ref.shape[0]
    pick = jnp.minimum(window, lax.axis_size("seq") - 2)
    entry = lax.broadcasted_iota(jnp.int32, table_ref.shape, 0)
    row = lax.broadcasted_iota(jnp.int32, table_ref.shape, 1)
    here = (entry == pick) & (row == table_ref.shape[1] - 1)
    named = jnp.where(here, table_ref[...].astype(jnp.float32), -1.0)
    named = jnp.max(jnp.max(named, axis=1, keepdims=True), axis=0, keepdims=True)
    block = jnp.clip(named - (window * blocks).astype(jnp.float32), 0.0, blocks - 1.0)
    block_ref[...] = jnp.broadcast_to(block, block_ref.shape).astype(jnp.int32)
    for which, ref in enumerate((keys_ref, values_ref)):
        chosen = ref[0].astype(jnp.float32)
        for b in range(1, blocks):
            chosen = jnp.where(block == b, ref[b].astype(jnp.float32), chosen)
        pair_ref[which] = chosen.astype(pair_ref.dtype)
        both_ref[which] = ref[...]


def pick_pair(table, keys, values):
    _, part_tok, feat_width = keys.shape
    return pl.pallas_call(
        pick_kernel,
        in_specs=[WHOLE] * 3,
        out_specs=[WHOLE] * 3,
        out_shape=[
            jax.ShapeDtypeStruct((2, part_tok, feat_width), keys.dtype),
            jax.ShapeDtypeStruct((2,) + keys.shape, keys.dtype),
            jax.ShapeDtypeStruct((8, 128), jnp.int32),
        ],
    )(table, keys, values)


def near_tiles(rows, near):
    half = rows // 2
    return [(0, half, near // 2), (half, half, near)]


def fill_mask(members, near, blk_len, part_tok, bias_ref):
    member = lax.axis_index("kv")
    shift = part_tok.bit_length() - 1
    for start, count, used in near_tiles(bias_ref.shape[0], near):
        row = start + lax.broadcasted_iota(jnp.int32, (count, 1), 0)
        col = lax.broadcasted_iota(jnp.int32, (1, used), 1)
        key_tok = (col >> shift) * blk_len + (col & (part_tok - 1))
        for j in range(members):
            key_pos = key_tok + (member ^ j) * part_tok
            bias_ref[start : start + count, j * used : (j + 1) * used] = jnp.where(
                key_pos <= row, 0.0, HIDDEN
            )


def head_columns(head, feat_width):
    head_dim = feat_width // HEADS
    return pl.ds(pl.multiple_of(head * head_dim, head_dim), head_dim)


def near_rows(parts, which, used, cols):
    return jnp.concatenate([ref[which, :used, cols] for ref in parts], axis=0)


def near_forward_kernel(members, blk_len, part_tok, q_hbm, g_hbm, *refs):
    parts = refs[:members]
    out_ref, stat_ref, bias_ref, q_ref, g_ref, sems = refs[members:]
    rows, feat_width = q_ref.shape
    head_dim = feat_width // HEADS
    near = parts[0].shape[1]
    slab = feat_width * GROUP // HEADS
    copies = [
        pltpu.make_async_copy(q_hbm.at[:, pl.ds(c, slab)], q_ref.at[:, pl.ds(c, slab)], sems.at[i])
        for i, c in enumerate(range(0, feat_width, slab))
    ]
    copies.append(pltpu.make_async_copy(g_hbm, g_ref, sems.at[HEADS // GROUP]))
    for copy in copies:
        copy.start()
    fill_mask(members, near, blk_len, part_tok, bias_ref)
    copies[0].wait()

    @pl.loop(0, HEADS // GROUP)
    def _(group):
        @pl.when(group > 0)
        def _():
            cols = pl.ds(pl.multiple_of(group * slab, slab), slab)
            pltpu.make_async_copy(q_hbm.at[:, cols], q_ref.at[:, cols], sems.at[group]).wait()

        units = [
            (head_columns(group * GROUP + i, feat_width), pl.ds(start, count), used)
            for i in range(GROUP)
            for start, count, used in near_tiles(rows, near)
        ]
        raws = [
            dot(q_ref[here, cols], near_rows(parts, 0, used, cols), NT) * base2_scale(head_dim)
            + bias_ref[here, : members * used]
            for cols, here, used in units
        ]
        peaks = [jnp.max(raw, axis=1, keepdims=True) for raw in raws]
        weights = [jnp.exp2(raw - peak) for raw, peak in zip(raws, peaks)]
        totals = [jnp.sum(weight, axis=1, keepdims=True) for weight in weights]
        sums = [
            dot(weight.astype(jnp.bfloat16), near_rows(parts, 1, used, cols), NN)
            for weight, (cols, here, used) in zip(weights, units)
        ]
        for (cols, here, used), peak, total, summed in zip(units, peaks, totals, sums):
            level = peak + jnp.log2(total)
            stat_ref[here, cols] = jnp.broadcast_to(level, summed.shape)
            out_ref[here, cols] = summed * (1.0 / total)

    copies[-1].wait()


def far_rows(parts, which, cols):
    rows = []
    for pair_ref, column_ref in zip(parts[0::2], parts[1::2]):
        steps, _, part_tok, _ = column_ref.shape
        rows.append(pair_ref[which, :, cols])
        rows.append(column_ref[:, which, :, cols].reshape(steps * part_tok, cols.size))
    return jnp.concatenate(rows, axis=0)


def far_kernel(members, tile, heads, batch, q_ref, g_ref, sum_ref, stat_ref, *refs):
    parts = refs[: 2 * COLUMNS * members]
    att_ref, gq_ref, level_ref, drift_ref, *grad_refs = refs[2 * COLUMNS * members :]
    rows, feat_width = q_ref.shape
    head_dim = feat_width // HEADS
    steps, _, part_tok, _ = grad_refs[0].shape
    span = steps * part_tok
    width = COLUMNS * span
    score_scale = 1.0 / math.sqrt(head_dim)
    window = lax.axis_index("seq")
    level, side = window // COLUMNS, window % COLUMNS
    step = lax.broadcasted_iota(jnp.int32, (1, span), 1) >> (part_tok.bit_length() - 1)
    valid = [(step >= 1) & (step <= level), (step >= 1 - side) & (step <= level)]
    bias = jnp.concatenate([jnp.where(ok, 0.0, HIDDEN) for ok in valid] * members, axis=1)
    total_width = members * width

    def work(units, keys, values, key_grads, value_grads):
        raws = [
            dot(q_ref[here, cols], keys[i], NT) * base2_scale(head_dim) + bias
            for i, cols, here in units
        ]
        grad_probs = [dot(g_ref[here, cols], values[i], NT) for i, cols, here in units]
        near_levels = [stat_ref[here, cols] for i, cols, here in units]
        peaks = [
            jnp.maximum(near_level, jnp.max(raw, axis=1, keepdims=True))
            for near_level, raw in zip(near_levels, raws)
        ]
        near_weights = [jnp.exp2(near_level - peak) for near_level, peak in zip(near_levels, peaks)]
        weights = [jnp.exp2(raw - wide(peak, total_width)) for raw, peak in zip(raws, peaks)]
        totals = [
            near_weight + jnp.sum(weight, axis=1, keepdims=True)
            for near_weight, weight in zip(near_weights, weights)
        ]
        inverses = [1.0 / total for total in totals]
        sums = [
            dot(weight.astype(jnp.bfloat16), values[i], NN)
            for weight, (i, cols, here) in zip(weights, units)
        ]
        drifts = []
        for u, (i, cols, here) in enumerate(units):
            summed = sum_ref[here, cols] * near_weights[u] + sums[u]
            attended = (summed * inverses[u]).astype(jnp.bfloat16)
            att_ref[here, cols] = attended
            product = g_ref[here, cols].astype(jnp.float32) * attended.astype(jnp.float32)
            drift = jnp.broadcast_to(jnp.sum(product, axis=1, keepdims=True), product.shape)
            drifts.append(drift)
            level_ref[here, cols] = peaks[u] + jnp.log2(totals[u])
            drift_ref[here, cols] = drift
        moved = [
            weight * (grad_prob - wide(drift, total_width))
            for weight, grad_prob, drift in zip(weights, grad_probs, drifts)
        ]
        factors = [inverse * score_scale for inverse in inverses]
        own_scores = [
            (part[:, :width] * wide(factor, width)).astype(jnp.bfloat16)
            for part, factor in zip(moved, factors)
        ]
        own_probs = [
            (weight[:, :width] * wide(inverse, width)).astype(jnp.bfloat16)
            for weight, inverse in zip(weights, inverses)
        ]
        for u, (i, cols, here) in enumerate(units):
            gq_ref[here, cols] = dot(moved[u].astype(jnp.bfloat16), keys[i], NN) * factors[u]
        for u, (i, cols, here) in enumerate(units):
            key_grads[i].append(dot(own_scores[u], q_ref[here, cols], TN))
            value_grads[i].append(dot(own_probs[u], g_ref[here, cols], TN))

    @pl.loop(0, HEADS // heads)
    def _(group):
        columns = [head_columns(group * heads + i, feat_width) for i in range(heads)]
        units = [
            (i, cols, pl.ds(r, tile)) for i, cols in enumerate(columns) for r in range(0, rows, tile)
        ]
        keys = [far_rows(parts, 0, cols) for cols in columns]
        values = [far_rows(parts, 1, cols) for cols in columns]
        grads = [[[] for _ in columns] for _ in range(2)]
        for first in range(0, len(units), batch):
            work(units[first : first + batch], keys, values, *grads)
        for which, per_head in enumerate(grads):
            for cols, terms in zip(columns, per_head):
                total = functools.reduce(lambda a, b: a + b, terms).astype(jnp.bfloat16)
                for c, ref in enumerate(grad_refs):
                    piece = total[c * span : (c + 1) * span]
                    ref[:, which, :, cols] = piece.reshape(steps, part_tok, head_dim)


def near_backward_kernel(members, bias_ref, q_ref, g_ref, level_ref, drift_ref, far_gq_ref, *refs):
    parts = refs[:members]
    gq_ref, gk_ref, gv_ref = refs[members:]
    rows, feat_width = q_ref.shape
    head_dim = feat_width // HEADS
    near = parts[0].shape[1]
    score_scale = 1.0 / math.sqrt(head_dim)

    @pl.loop(0, HEADS // GROUP)
    def _(group):
        units = [
            (head_columns(group * GROUP + i, feat_width), pl.ds(start, count), used)
            for i in range(GROUP)
            for start, count, used in reversed(near_tiles(rows, near))
        ]
        keys = [near_rows(parts, 0, used, cols) for cols, here, used in units]
        values = [near_rows(parts, 1, used, cols) for cols, here, used in units]
        raws = [
            dot(q_ref[here, cols], key, NT) * base2_scale(head_dim)
            + bias_ref[here, : members * used]
            for (cols, here, used), key in zip(units, keys)
        ]
        grad_probs = [
            dot(g_ref[here, cols], value, NT) for (cols, here, used), value in zip(units, values)
        ]
        probs = [
            jnp.exp2(raw - wide(level_ref[here, cols], raw.shape[1]))
            for raw, (cols, here, used) in zip(raws, units)
        ]
        moved = [
            prob * (grad_prob - wide(drift_ref[here, cols], prob.shape[1]))
            for prob, grad_prob, (cols, here, used) in zip(probs, grad_probs, units)
        ]
        for (cols, here, used), part, key in zip(units, moved, keys):
            gq_ref[here, cols] = (
                dot(part.astype(jnp.bfloat16), key, NN) * score_scale + far_gq_ref[here, cols]
            ).astype(jnp.bfloat16)
        for (cols, here, used), part, prob in zip(units, moved, probs):
            own_score = (part[:, :used] * score_scale).astype(jnp.bfloat16)
            own_prob = prob[:, :used].astype(jnp.bfloat16)
            for left, right_ref, ref in ((own_score, q_ref, gk_ref), (own_prob, g_ref, gv_ref)):
                grad = dot(left, right_ref[here, cols], TN)
                if used == near:
                    ref[:, cols] = grad
                else:
                    ref[:used, cols] += grad


def call(kernel, operands, outs, pairs, products, head_dim, in_specs=None, scratch=()):
    moved_bytes = sum(a.size * a.dtype.itemsize for a in operands)
    return pl.pallas_call(
        kernel,
        in_specs=in_specs or [WHOLE] * len(operands),
        out_specs=[WHOLE] * len(outs),
        out_shape=outs,
        scratch_shapes=scratch,
        compiler_params=LIMIT,
        cost_estimate=pl.CostEstimate(
            flops=4 * products * pairs * head_dim, bytes_accessed=moved_bytes, transcendentals=pairs
        ),
    )(*operands)


def shards(queries, keys, values, layout, grad_out):
    seq_count = lax.axis_size("seq")
    members = lax.axis_size("kv")
    tok_rows, feat_width = queries.shape
    blocks, part_tok = (keys.shape[0], keys.shape[1])
    blk_len = part_tok * members
    near = blocks * part_tok
    head_dim = feat_width // HEADS
    levels = seq_count // COLUMNS
    def hop(part, column_step, member_step):
        pairs = [
            (s * members + m, (s ^ column_step) * members + (m ^ member_step))
            for s in range(seq_count)
            for m in range(members)
        ]
        return lax.ppermute(part, ("seq", "kv"), pairs)

    def climb(part, d):
        return lax.ppermute(
            part, "seq", [(s, s + COLUMNS * d) for s in range(seq_count - COLUMNS * d)]
        )

    def sink(part, d):
        return lax.ppermute(
            part, "seq", [(s, s - COLUMNS * d) for s in range(COLUMNS * d, seq_count)]
        )

    own_pair, both, block = pick_pair(layout.T, keys, values)
    both = both.reshape(2, near, feat_width)
    climbed = [climb(own_pair, d) for d in range(1, levels)]
    column = jnp.stack(climbed)
    sent_pair, _ = lax.optimization_barrier((own_pair, climbed[0]))
    cross_pairs = []
    for step in range(0, members, 2):
        pair = hop(sent_pair, 1, step)
        cross_pairs += [pair, hop(pair, 0, 1)]
    column, cross_pairs = lax.optimization_barrier((column, cross_pairs))
    crossing = [
        [column if (c, step) == (0, 0) else hop(column, c, step) for c in range(COLUMNS)]
        for step in range(0, members, 2)
    ]
    near_parts = [both, hop(both, 0, 1)]
    for step in range(2, members, 2):
        landed, _ = lax.optimization_barrier((hop(both, 0, step), column))
        near_parts += [landed, hop(landed, 0, 1)]

    def rows_out(dtype):
        return jax.ShapeDtypeStruct((tok_rows, feat_width), dtype)

    near_out = jax.ShapeDtypeStruct((near, feat_width), jnp.float32)
    far_out = jax.ShapeDtypeStruct((levels,) + own_pair.shape, jnp.bfloat16)
    near_pairs = HEADS * tok_rows * members * near
    far_width = members * seq_count * part_tok
    far_pairs = HEADS * tok_rows * far_width
    roomy = far_width <= 512
    far_plan = (tok_rows // 2, GROUP, 2 * GROUP) if roomy else (tok_rows // 8, 1, 1)

    in_hbm = pl.BlockSpec(memory_space=pltpu.HBM)
    near_sum, near_stat, bias, queries, grad_out = call(
        functools.partial(near_forward_kernel, members, blk_len, part_tok),
        [pltpu.with_memory_space_constraint(a, pltpu.HBM) for a in (queries, grad_out)] + near_parts,
        [pltpu.VMEM((tok_rows, feat_width), jnp.float32)] * 2
        + [pltpu.VMEM((tok_rows, members * near), jnp.float32)]
        + [pltpu.VMEM((tok_rows, feat_width), jnp.bfloat16)] * 2,
        near_pairs,
        2,
        head_dim,
        [in_hbm, in_hbm] + [WHOLE] * members,
        [pltpu.SemaphoreType.DMA((HEADS // GROUP + 1,))],
    )
    far_parts = []
    for group in crossing:
        group, _ = lax.optimization_barrier((group, near_stat))
        for same, other in (group, [hop(part, 0, 1) for part in group]):
            far_parts += [own_pair, same, cross_pairs[len(far_parts) // 4], other]
    attended, far_gq, level, drift, own_grad, cross_grad = call(
        functools.partial(far_kernel, members, *far_plan),
        [queries, grad_out, near_sum, near_stat] + far_parts,
        [rows_out(jnp.bfloat16)] + [rows_out(jnp.float32)] * 3 + [far_out, far_out],
        far_pairs,
        5,
        head_dim,
    )
    grad_q, near_k, near_v = call(
        functools.partial(near_backward_kernel, members),
        [bias, queries, grad_out, level, drift, far_gq] + near_parts,
        [rows_out(jnp.bfloat16), near_out, near_out],
        near_pairs,
        4,
        head_dim,
    )
    crossed, near_k = lax.optimization_barrier((hop(cross_grad, 1, 0), near_k))
    returned = []
    for d in range(1, levels):
        summed = own_grad[d].astype(jnp.float32) + crossed[d].astype(jnp.float32)
        returned.append(sink(summed.astype(jnp.bfloat16), d))
    extra = sum(part.astype(jnp.float32) for part in [crossed[0]] + returned)
    chosen = (jnp.arange(blocks) == block[0, 0])[:, None, None]

    def finish(near_term, far_term):
        near_term = near_term.reshape(blocks, part_tok, feat_width)
        return (near_term + jnp.where(chosen, far_term[None], 0.0)).astype(jnp.bfloat16)

    return (attended, grad_q, finish(near_k, extra[0]), finish(near_v, extra[1]))


def solution(mesh):
    return jax.shard_map(
        shards,
        mesh=mesh,
        in_specs=(P("seq", None), P("seq", "kv", None), P("seq", "kv", None), P(), P("seq", None)),
        out_specs=(P("seq", None), P("seq", None), P("seq", "kv", None), P("seq", "kv", None)),
        check_vma=False,
    )
```

```python
import functools
import math

import jax
import jax.numpy as jnp
from jax import lax
from jax.experimental import pallas as pl
from jax.experimental.pallas import tpu as pltpu
from jax.sharding import PartitionSpec as P

HEADS = 8
COLUMNS = 2
GROUP = 2
HIDDEN = -1e30
NT = (((1,), (1,)), ((), ()))
NN = (((1,), (0,)), ((), ()))
TN = (((0,), (0,)), ((), ()))
WHOLE = pl.BlockSpec(memory_space=pltpu.VMEM)
LIMIT = pltpu.CompilerParams(vmem_limit_bytes=20 * 1024 * 1024)


def dot(a, b, dims):
    return lax.dot_general(a, b, dims, preferred_element_type=jnp.float32)


def wide(rows, width):
    return jnp.concatenate([rows] * (width // rows.shape[1]), axis=1)


def base2_scale(head_dim):
    return math.log2(math.e) / math.sqrt(head_dim)


def pick_kernel(table_ref, keys_ref, values_ref, pair_ref, both_ref, block_ref):
    window = lax.axis_index("seq")
    blocks = keys_ref.shape[0]
    pick = jnp.minimum(window, lax.axis_size("seq") - 2)
    entry = lax.broadcasted_iota(jnp.int32, table_ref.shape, 0)
    row = lax.broadcasted_iota(jnp.int32, table_ref.shape, 1)
    here = (entry == pick) & (row == table_ref.shape[1] - 1)
    named = jnp.where(here, table_ref[...].astype(jnp.float32), -1.0)
    named = jnp.max(jnp.max(named, axis=1, keepdims=True), axis=0, keepdims=True)
    block = jnp.clip(named - (window * blocks).astype(jnp.float32), 0.0, blocks - 1.0)
    block_ref[...] = jnp.broadcast_to(block, block_ref.shape).astype(jnp.int32)
    for which, ref in enumerate((keys_ref, values_ref)):
        chosen = ref[0].astype(jnp.float32)
        for b in range(1, blocks):
            chosen = jnp.where(block == b, ref[b].astype(jnp.float32), chosen)
        pair_ref[which] = chosen.astype(pair_ref.dtype)
        both_ref[which] = ref[...]


def pick_pair(table, keys, values):
    _, part_tok, feat_width = keys.shape
    return pl.pallas_call(
        pick_kernel,
        in_specs=[WHOLE] * 3,
        out_specs=[WHOLE] * 3,
        out_shape=[
            jax.ShapeDtypeStruct((2, part_tok, feat_width), keys.dtype),
            jax.ShapeDtypeStruct((2,) + keys.shape, keys.dtype),
            jax.ShapeDtypeStruct((8, 128), jnp.int32),
        ],
    )(table, keys, values)


def near_tiles(rows, near):
    half = rows // 2
    return [(0, half, near // 2), (half, half, near)]


def fill_mask(members, near, blk_len, part_tok, bias_ref):
    member = lax.axis_index("kv")
    shift = part_tok.bit_length() - 1
    for start, count, used in near_tiles(bias_ref.shape[0], near):
        row = start + lax.broadcasted_iota(jnp.int32, (count, 1), 0)
        col = lax.broadcasted_iota(jnp.int32, (1, used), 1)
        key_tok = (col >> shift) * blk_len + (col & (part_tok - 1))
        for j in range(members):
            key_pos = key_tok + (member ^ j) * part_tok
            bias_ref[start : start + count, j * used : (j + 1) * used] = jnp.where(
                key_pos <= row, 0.0, HIDDEN
            )


def head_columns(head, feat_width):
    head_dim = feat_width // HEADS
    return pl.ds(pl.multiple_of(head * head_dim, head_dim), head_dim)


def near_rows(parts, which, used, cols):
    return jnp.concatenate([ref[which, :used, cols] for ref in parts], axis=0)


def near_forward_kernel(members, blk_len, part_tok, q_hbm, g_hbm, *refs):
    parts = refs[:members]
    out_ref, stat_ref, bias_ref, q_ref, g_ref, sems = refs[members:]
    rows, feat_width = q_ref.shape
    head_dim = feat_width // HEADS
    near = parts[0].shape[1]
    slab = feat_width * GROUP // HEADS
    copies = [
        pltpu.make_async_copy(q_hbm.at[:, pl.ds(c, slab)], q_ref.at[:, pl.ds(c, slab)], sems.at[i])
        for i, c in enumerate(range(0, feat_width, slab))
    ]
    copies.append(pltpu.make_async_copy(g_hbm, g_ref, sems.at[HEADS // GROUP]))
    for copy in copies:
        copy.start()
    fill_mask(members, near, blk_len, part_tok, bias_ref)
    copies[0].wait()

    @pl.loop(0, HEADS // GROUP)
    def _(group):
        @pl.when(group > 0)
        def _():
            cols = pl.ds(pl.multiple_of(group * slab, slab), slab)
            pltpu.make_async_copy(q_hbm.at[:, cols], q_ref.at[:, cols], sems.at[group]).wait()

        units = [
            (head_columns(group * GROUP + i, feat_width), pl.ds(start, count), used)
            for i in range(GROUP)
            for start, count, used in near_tiles(rows, near)
        ]
        raws = [
            dot(q_ref[here, cols], near_rows(parts, 0, used, cols), NT) * base2_scale(head_dim)
            + bias_ref[here, : members * used]
            for cols, here, used in units
        ]
        peaks = [jnp.max(raw, axis=1, keepdims=True) for raw in raws]
        weights = [jnp.exp2(raw - peak) for raw, peak in zip(raws, peaks)]
        totals = [jnp.sum(weight, axis=1, keepdims=True) for weight in weights]
        sums = [
            dot(weight.astype(jnp.bfloat16), near_rows(parts, 1, used, cols), NN)
            for weight, (cols, here, used) in zip(weights, units)
        ]
        for (cols, here, used), peak, total, summed in zip(units, peaks, totals, sums):
            level = peak + jnp.log2(total)
            stat_ref[here, cols] = jnp.broadcast_to(level, summed.shape)
            out_ref[here, cols] = summed * (1.0 / total)

    copies[-1].wait()


def far_rows(parts, which, cols):
    steps, _, part_tok, _ = parts[0].shape
    return jnp.concatenate(
        [ref[:, which, :, cols].reshape(steps * part_tok, cols.size) for ref in parts], axis=0
    )


def far_kernel(members, tile, heads, batch, q_ref, g_ref, sum_ref, stat_ref, *refs):
    parts = refs[: COLUMNS * members]
    att_ref, gq_ref, level_ref, drift_ref, *grad_refs = refs[COLUMNS * members :]
    rows, feat_width = q_ref.shape
    head_dim = feat_width // HEADS
    steps, _, part_tok, _ = grad_refs[0].shape
    span = steps * part_tok
    width = COLUMNS * span
    score_scale = 1.0 / math.sqrt(head_dim)
    window = lax.axis_index("seq")
    level, side = window // COLUMNS, window % COLUMNS
    step = lax.broadcasted_iota(jnp.int32, (1, span), 1) >> (part_tok.bit_length() - 1)
    valid = [step < level, step < level + side]
    bias = jnp.concatenate([jnp.where(ok, 0.0, HIDDEN) for ok in valid] * members, axis=1)
    total_width = members * width

    def work(units, keys, values, key_grads, value_grads):
        raws = [
            dot(q_ref[here, cols], keys[i], NT) * base2_scale(head_dim) + bias
            for i, cols, here in units
        ]
        grad_probs = [dot(g_ref[here, cols], values[i], NT) for i, cols, here in units]
        near_levels = [stat_ref[here, cols] for i, cols, here in units]
        peaks = [
            jnp.maximum(near_level, jnp.max(raw, axis=1, keepdims=True))
            for near_level, raw in zip(near_levels, raws)
        ]
        near_weights = [jnp.exp2(near_level - peak) for near_level, peak in zip(near_levels, peaks)]
        weights = [jnp.exp2(raw - wide(peak, total_width)) for raw, peak in zip(raws, peaks)]
        totals = [
            near_weight + jnp.sum(weight, axis=1, keepdims=True)
            for near_weight, weight in zip(near_weights, weights)
        ]
        inverses = [1.0 / total for total in totals]
        sums = [
            dot(weight.astype(jnp.bfloat16), values[i], NN)
            for weight, (i, cols, here) in zip(weights, units)
        ]
        drifts = []
        for u, (i, cols, here) in enumerate(units):
            summed = sum_ref[here, cols] * near_weights[u] + sums[u]
            attended = (summed * inverses[u]).astype(jnp.bfloat16)
            att_ref[here, cols] = attended
            product = g_ref[here, cols].astype(jnp.float32) * attended.astype(jnp.float32)
            drift = jnp.broadcast_to(jnp.sum(product, axis=1, keepdims=True), product.shape)
            drifts.append(drift)
            level_ref[here, cols] = peaks[u] + jnp.log2(totals[u])
            drift_ref[here, cols] = drift
        moved = [
            weight * (grad_prob - wide(drift, total_width))
            for weight, grad_prob, drift in zip(weights, grad_probs, drifts)
        ]
        factors = [inverse * score_scale for inverse in inverses]
        own_scores = [
            (part[:, :width] * wide(factor, width)).astype(jnp.bfloat16)
            for part, factor in zip(moved, factors)
        ]
        own_probs = [
            (weight[:, :width] * wide(inverse, width)).astype(jnp.bfloat16)
            for weight, inverse in zip(weights, inverses)
        ]
        for u, (i, cols, here) in enumerate(units):
            gq_ref[here, cols] = dot(moved[u].astype(jnp.bfloat16), keys[i], NN) * factors[u]
        for u, (i, cols, here) in enumerate(units):
            key_grads[i].append(dot(own_scores[u], q_ref[here, cols], TN))
            value_grads[i].append(dot(own_probs[u], g_ref[here, cols], TN))

    @pl.loop(0, HEADS // heads)
    def _(group):
        columns = [head_columns(group * heads + i, feat_width) for i in range(heads)]
        units = [
            (i, cols, pl.ds(r, tile)) for i, cols in enumerate(columns) for r in range(0, rows, tile)
        ]
        keys = [far_rows(parts, 0, cols) for cols in columns]
        values = [far_rows(parts, 1, cols) for cols in columns]
        grads = [[[] for _ in columns] for _ in range(2)]
        for first in range(0, len(units), batch):
            work(units[first : first + batch], keys, values, *grads)
        for which, per_head in enumerate(grads):
            for cols, terms in zip(columns, per_head):
                total = functools.reduce(lambda a, b: a + b, terms).astype(jnp.bfloat16)
                for c, ref in enumerate(grad_refs):
                    piece = total[c * span : (c + 1) * span]
                    ref[:, which, :, cols] = piece.reshape(steps, part_tok, head_dim)


def near_backward_kernel(members, bias_ref, q_ref, g_ref, level_ref, drift_ref, far_gq_ref, *refs):
    parts = refs[:members]
    gq_ref, gk_ref, gv_ref = refs[members:]
    rows, feat_width = q_ref.shape
    head_dim = feat_width // HEADS
    near = parts[0].shape[1]
    score_scale = 1.0 / math.sqrt(head_dim)

    @pl.loop(0, HEADS // GROUP)
    def _(group):
        units = [
            (head_columns(group * GROUP + i, feat_width), pl.ds(start, count), used)
            for i in range(GROUP)
            for start, count, used in reversed(near_tiles(rows, near))
        ]
        keys = [near_rows(parts, 0, used, cols) for cols, here, used in units]
        values = [near_rows(parts, 1, used, cols) for cols, here, used in units]
        raws = [
            dot(q_ref[here, cols], key, NT) * base2_scale(head_dim)
            + bias_ref[here, : members * used]
            for (cols, here, used), key in zip(units, keys)
        ]
        grad_probs = [
            dot(g_ref[here, cols], value, NT) for (cols, here, used), value in zip(units, values)
        ]
        probs = [
            jnp.exp2(raw - wide(level_ref[here, cols], raw.shape[1]))
            for raw, (cols, here, used) in zip(raws, units)
        ]
        moved = [
            prob * (grad_prob - wide(drift_ref[here, cols], prob.shape[1]))
            for prob, grad_prob, (cols, here, used) in zip(probs, grad_probs, units)
        ]
        for (cols, here, used), part, key in zip(units, moved, keys):
            gq_ref[here, cols] = (
                dot(part.astype(jnp.bfloat16), key, NN) * score_scale + far_gq_ref[here, cols]
            ).astype(jnp.bfloat16)
        for (cols, here, used), part, prob in zip(units, moved, probs):
            own_score = (part[:, :used] * score_scale).astype(jnp.bfloat16)
            own_prob = prob[:, :used].astype(jnp.bfloat16)
            for left, right_ref, ref in ((own_score, q_ref, gk_ref), (own_prob, g_ref, gv_ref)):
                grad = dot(left, right_ref[here, cols], TN)
                if used == near:
                    ref[:, cols] = grad
                else:
                    ref[:used, cols] += grad


def call(kernel, operands, outs, pairs, products, head_dim, in_specs=None, scratch=()):
    moved_bytes = sum(a.size * a.dtype.itemsize for a in operands)
    return pl.pallas_call(
        kernel,
        in_specs=in_specs or [WHOLE] * len(operands),
        out_specs=[WHOLE] * len(outs),
        out_shape=outs,
        scratch_shapes=scratch,
        compiler_params=LIMIT,
        cost_estimate=pl.CostEstimate(
            flops=4 * products * pairs * head_dim, bytes_accessed=moved_bytes, transcendentals=pairs
        ),
    )(*operands)


def shards(queries, keys, values, layout, grad_out):
    seq_count = lax.axis_size("seq")
    members = lax.axis_size("kv")
    tok_rows, feat_width = queries.shape
    blocks, part_tok = (keys.shape[0], keys.shape[1])
    blk_len = part_tok * members
    near = blocks * part_tok
    head_dim = feat_width // HEADS
    levels = seq_count // COLUMNS
    def hop(part, column_step, member_step):
        pairs = [
            (s * members + m, (s ^ column_step) * members + (m ^ member_step))
            for s in range(seq_count)
            for m in range(members)
        ]
        return lax.ppermute(part, ("seq", "kv"), pairs)

    columns = [list(range(c, seq_count, COLUMNS)) for c in range(COLUMNS)]
    own_pair, both, block = pick_pair(layout.T, keys, values)
    both = both.reshape(2, near, feat_width)
    column = lax.all_gather(own_pair, "seq", axis=0, axis_index_groups=columns)
    crossing = [
        [column if (c, step) == (0, 0) else hop(column, c, step) for c in range(COLUMNS)]
        for step in range(0, members, 2)
    ]
    near_parts = [both, hop(both, 0, 1)]
    for step in range(2, members, 2):
        landed, _ = lax.optimization_barrier((hop(both, 0, step), column))
        near_parts += [landed, hop(landed, 0, 1)]

    def rows_out(dtype):
        return jax.ShapeDtypeStruct((tok_rows, feat_width), dtype)

    near_out = jax.ShapeDtypeStruct((near, feat_width), jnp.float32)
    far_out = jax.ShapeDtypeStruct((levels,) + own_pair.shape, jnp.bfloat16)
    near_pairs = HEADS * tok_rows * members * near
    far_width = members * seq_count * part_tok
    far_pairs = HEADS * tok_rows * far_width
    roomy = far_width <= 512
    far_plan = (tok_rows // 2, GROUP, 2 * GROUP) if roomy else (tok_rows // 8, 1, 1)

    in_hbm = pl.BlockSpec(memory_space=pltpu.HBM)
    near_sum, near_stat, bias, queries, grad_out = call(
        functools.partial(near_forward_kernel, members, blk_len, part_tok),
        [pltpu.with_memory_space_constraint(a, pltpu.HBM) for a in (queries, grad_out)] + near_parts,
        [pltpu.VMEM((tok_rows, feat_width), jnp.float32)] * 2
        + [pltpu.VMEM((tok_rows, members * near), jnp.float32)]
        + [pltpu.VMEM((tok_rows, feat_width), jnp.bfloat16)] * 2,
        near_pairs,
        2,
        head_dim,
        [in_hbm, in_hbm] + [WHOLE] * members,
        [pltpu.SemaphoreType.DMA((HEADS // GROUP + 1,))],
    )
    far_parts = []
    for group in crossing:
        group, _ = lax.optimization_barrier((group, near_stat))
        far_parts += group + [hop(part, 0, 1) for part in group]
    attended, far_gq, level, drift, own_grad, cross_grad = call(
        functools.partial(far_kernel, members, *far_plan),
        [queries, grad_out, near_sum, near_stat] + far_parts,
        [rows_out(jnp.bfloat16)] + [rows_out(jnp.float32)] * 3 + [far_out, far_out],
        far_pairs,
        5,
        head_dim,
    )
    grad_q, near_k, near_v = call(
        functools.partial(near_backward_kernel, members),
        [bias, queries, grad_out, level, drift, far_gq] + near_parts,
        [rows_out(jnp.bfloat16), near_out, near_out],
        near_pairs,
        4,
        head_dim,
    )
    crossed, near_k = lax.optimization_barrier((hop(cross_grad, 1, 0), near_k))
    summed = (own_grad.astype(jnp.float32) + crossed.astype(jnp.float32)).astype(jnp.bfloat16)
    returned = lax.all_to_all(summed, "seq", 0, 0, axis_index_groups=columns)
    extra = jnp.sum(returned.astype(jnp.float32), axis=0)
    chosen = (jnp.arange(blocks) == block[0, 0])[:, None, None]

    def finish(near_term, far_term):
        near_term = near_term.reshape(blocks, part_tok, feat_width)
        return (near_term + jnp.where(chosen, far_term[None], 0.0)).astype(jnp.bfloat16)

    return (attended, grad_q, finish(near_k, extra[0]), finish(near_v, extra[1]))


def solution(mesh):
    return jax.shard_map(
        shards,
        mesh=mesh,
        in_specs=(P("seq", None), P("seq", "kv", None), P("seq", "kv", None), P(), P("seq", None)),
        out_specs=(P("seq", None), P("seq", None), P("seq", "kv", None), P("seq", "kv", None)),
        check_vma=False,
    )
```

```python
import functools
import math

import jax
import jax.numpy as jnp
from jax import lax
from jax.experimental import pallas as pl
from jax.experimental.pallas import tpu as pltpu
from jax.sharding import PartitionSpec as P

HEADS = 8
COLUMNS = 2
CORES = 2
GROUP = 2
HIDDEN = -1e30
NT = (((1,), (1,)), ((), ()))
NN = (((1,), (0,)), ((), ()))
TN = (((0,), (0,)), ((), ()))
IN_HBM = pl.BlockSpec(memory_space=pltpu.HBM)
WHOLE = pl.BlockSpec(memory_space=pltpu.VMEM)
LIMIT = pltpu.CompilerParams(vmem_limit_bytes=20 * 1024 * 1024)


def dot(a, b, dims):
    return lax.dot_general(a, b, dims, preferred_element_type=jnp.float32)


def wide(rows, width):
    return jnp.concatenate([rows] * (width // rows.shape[1]), axis=1)


def base2_scale(head_dim):
    return math.log2(math.e) / math.sqrt(head_dim)


def pick_kernel(table_hbm, keys_hbm, values_hbm, mine_ref, theirs_ref, pair_ref, sent_ref, mask_ref, table_ref, sems):
    window = lax.axis_index("seq")
    core = lax.axis_index("kv") % CORES
    blocks, _, half = mask_ref.shape
    copies = [pltpu.make_async_copy(table_hbm, table_ref, sems.at[0])]
    for which, ref in enumerate((keys_hbm, values_hbm)):
        for side, out_ref in enumerate((mine_ref, theirs_ref)):
            cols = pl.ds(pl.multiple_of((core ^ side) * half, half), half)
            copies.append(
                pltpu.make_async_copy(ref.at[:, :, cols], out_ref.at[which], sems.at[len(copies)])
            )
    for copy in copies:
        copy.start()
    copies[0].wait()
    pick = jnp.minimum(window, lax.axis_size("seq") - 2)
    entry = lax.broadcasted_iota(jnp.int32, table_ref.shape, 0)
    row = lax.broadcasted_iota(jnp.int32, table_ref.shape, 1)
    here = (entry == pick) & (row == table_ref.shape[1] - 1)
    named = jnp.where(here, table_ref[...].astype(jnp.float32), -1.0)
    named = jnp.max(jnp.max(named, axis=1, keepdims=True), axis=0, keepdims=True)
    block = jnp.clip(named - (window * blocks).astype(jnp.float32), 0.0, blocks - 1.0)
    block = jnp.broadcast_to(block, mask_ref.shape[1:])
    for b in range(blocks):
        mask_ref[b] = jnp.where(block == b, 1.0, 0.0)
    for copy in copies[1:]:
        copy.wait()
    for ref, out_ref in ((mine_ref, pair_ref), (theirs_ref, sent_ref)):
        for which in range(2):
            chosen = ref[which, 0].astype(jnp.float32)
            for b in range(1, blocks):
                chosen = jnp.where(block == b, ref[which, b].astype(jnp.float32), chosen)
            out_ref[which] = chosen.astype(out_ref.dtype)


def pick_pair(table, keys, values):
    blocks, part_tok, feat_width = keys.shape
    half = feat_width // CORES
    operands = [pltpu.with_memory_space_constraint(a, pltpu.HBM) for a in (table, keys, values)]
    return pl.pallas_call(
        pick_kernel,
        in_specs=[IN_HBM] * 3,
        out_specs=[WHOLE] * 5,
        out_shape=[pltpu.VMEM((2, blocks, part_tok, half), keys.dtype)] * 2
        + [pltpu.VMEM((2, part_tok, half), keys.dtype)] * 2
        + [pltpu.VMEM((blocks, part_tok, half), jnp.float32)],
        scratch_shapes=[pltpu.VMEM(table.shape, table.dtype), pltpu.SemaphoreType.DMA((5,))],
    )(*operands)


def join_kernel(*refs):
    sems = refs[-1]
    count = (len(refs) - 1) // 3
    core = lax.axis_index("kv") % CORES
    copies = []
    for i in range(count):
        out_ref = refs[2 * count + i]
        half = refs[2 * i].shape[1]
        for side in range(CORES):
            cols = pl.ds(pl.multiple_of((core ^ side) * half, half), half)
            copies.append(
                pltpu.make_async_copy(refs[2 * i + side], out_ref.at[:, cols], sems.at[len(copies)])
            )
    for copy in copies:
        copy.start()
    for copy in copies:
        copy.wait()


def join(pairs):
    rows, half = pairs[0][0].shape
    operands = [pltpu.with_memory_space_constraint(a, pltpu.VMEM) for pair in pairs for a in pair]
    return pl.pallas_call(
        join_kernel,
        in_specs=[WHOLE] * len(operands),
        out_specs=[IN_HBM] * len(pairs),
        out_shape=[pltpu.HBM((rows, half * CORES), pairs[0][0].dtype)] * len(pairs),
        scratch_shapes=[pltpu.SemaphoreType.DMA((len(operands),))],
    )(*operands)


def finish_kernel(mask_ref, gk_ref, gv_ref, near_ref, far_ref, *refs):
    arrived = refs[:-2]
    core = lax.axis_index("kv") % CORES
    half = mask_ref.shape[-1]
    mine = pl.ds(pl.multiple_of(core * half, half), half)
    theirs = pl.ds(pl.multiple_of((core ^ 1) * half, half), half)
    mask = mask_ref[...]
    for which, (own_ref, out_ref) in enumerate(zip((gk_ref, gv_ref), refs[-2:])):
        extra = sum(ref[0, which].astype(jnp.float32) for ref in arrived)
        out_ref[:, :, mine] = (own_ref[...] + mask * extra[None]).astype(out_ref.dtype)
        near = near_ref[which].astype(jnp.float32)
        extra = far_ref[which].astype(jnp.float32)
        out_ref[:, :, theirs] = (near + mask * extra[None]).astype(out_ref.dtype)


def near_tiles(rows, near):
    half = rows // 2
    return [(0, half, near // 2), (half, half, near)]


def fill_mask(members, near, blk_len, part_tok, bias_ref):
    member = lax.axis_index("kv")
    shift = part_tok.bit_length() - 1
    for start, count, used in near_tiles(bias_ref.shape[0], near):
        row = start + lax.broadcasted_iota(jnp.int32, (count, 1), 0)
        col = lax.broadcasted_iota(jnp.int32, (1, used), 1)
        key_tok = (col >> shift) * blk_len + (col & (part_tok - 1))
        for j in range(members):
            key_pos = key_tok + (member ^ j) * part_tok
            bias_ref[start : start + count, j * used : (j + 1) * used] = jnp.where(
                key_pos <= row, 0.0, HIDDEN
            )


def head_columns(head, head_dim):
    return pl.ds(pl.multiple_of(head * head_dim, head_dim), head_dim)


def near_rows(parts, which, used, cols):
    return jnp.concatenate([ref[which, :used, cols] for ref in parts], axis=0)


def near_forward_kernel(members, blk_len, part_tok, head_dim, q_hbm, g_hbm, *refs):
    parts = refs[:members]
    out_ref, stat_ref, bias_ref, q_ref, g_ref, sems = refs[members:]
    rows, half = q_ref.shape
    near = parts[0].shape[1]
    slab = GROUP * head_dim
    core = lax.axis_index("kv") % CORES

    def fetch(group):
        there = pl.ds(pl.multiple_of(core * half + group * slab, slab), slab)
        here = pl.ds(pl.multiple_of(group * slab, slab), slab)
        return pltpu.make_async_copy(q_hbm.at[:, there], q_ref.at[:, here], sems.at[group])

    there = pl.ds(pl.multiple_of(core * half, half), half)
    last = pltpu.make_async_copy(g_hbm.at[:, there], g_ref, sems.at[half // slab])
    for group in range(half // slab):
        fetch(group).start()
    last.start()
    fill_mask(members, near, blk_len, part_tok, bias_ref)

    @pl.loop(0, half // slab)
    def _(group):
        fetch(group).wait()
        units = [
            (head_columns(group * GROUP + i, head_dim), pl.ds(start, count), used)
            for i in range(GROUP)
            for start, count, used in near_tiles(rows, near)
        ]
        raws = [
            dot(q_ref[here, cols], near_rows(parts, 0, used, cols), NT) * base2_scale(head_dim)
            + bias_ref[here, : members * used]
            for cols, here, used in units
        ]
        peaks = [jnp.max(raw, axis=1, keepdims=True) for raw in raws]
        weights = [jnp.exp2(raw - peak) for raw, peak in zip(raws, peaks)]
        totals = [jnp.sum(weight, axis=1, keepdims=True) for weight in weights]
        sums = [
            dot(weight.astype(jnp.bfloat16), near_rows(parts, 1, used, cols), NN)
            for weight, (cols, here, used) in zip(weights, units)
        ]
        for (cols, here, used), peak, total, summed in zip(units, peaks, totals, sums):
            level = peak + jnp.log2(total)
            stat_ref[here, cols] = jnp.broadcast_to(level, summed.shape)
            out_ref[here, cols] = summed * (1.0 / total)

    last.wait()


def far_rows(parts, which, cols):
    rows = []
    for pair_ref, column_ref in zip(parts[0::2], parts[1::2]):
        steps, cores, _, part_tok, _ = column_ref.shape
        rows.append(pair_ref[:, which, :, cols].reshape(cores * part_tok, cols.size))
        rows.append(column_ref[:, :, which, :, cols].reshape(steps * cores * part_tok, cols.size))
    return jnp.concatenate(rows, axis=0)


def far_kernel(groups, head_dim, tile, heads, batch, q_ref, g_ref, sum_ref, stat_ref, *refs):
    parts = refs[: 2 * COLUMNS * groups]
    att_ref, gq_ref, level_ref, drift_ref, *grad_refs = refs[2 * COLUMNS * groups :]
    rows, half = q_ref.shape
    steps, cores, _, part_tok, _ = grad_refs[0].shape
    span = steps * cores * part_tok
    width = COLUMNS * span
    score_scale = 1.0 / math.sqrt(head_dim)
    window = lax.axis_index("seq")
    level, side = window // COLUMNS, window % COLUMNS
    step = lax.broadcasted_iota(jnp.int32, (1, span), 1) >> ((cores * part_tok).bit_length() - 1)
    valid = [(step >= 1) & (step <= level), (step >= 1 - side) & (step <= level)]
    bias = jnp.concatenate([jnp.where(ok, 0.0, HIDDEN) for ok in valid] * groups, axis=1)
    total_width = groups * width

    def work(units, keys, values, key_grads, value_grads):
        raws = [
            dot(q_ref[here, cols], keys[i], NT) * base2_scale(head_dim) + bias
            for i, cols, here in units
        ]
        grad_probs = [dot(g_ref[here, cols], values[i], NT) for i, cols, here in units]
        near_levels = [stat_ref[here, cols] for i, cols, here in units]
        peaks = [
            jnp.maximum(near_level, jnp.max(raw, axis=1, keepdims=True))
            for near_level, raw in zip(near_levels, raws)
        ]
        near_weights = [jnp.exp2(near_level - peak) for near_level, peak in zip(near_levels, peaks)]
        weights = [jnp.exp2(raw - wide(peak, total_width)) for raw, peak in zip(raws, peaks)]
        totals = [
            near_weight + jnp.sum(weight, axis=1, keepdims=True)
            for near_weight, weight in zip(near_weights, weights)
        ]
        inverses = [1.0 / total for total in totals]
        sums = [
            dot(weight.astype(jnp.bfloat16), values[i], NN)
            for weight, (i, cols, here) in zip(weights, units)
        ]
        drifts = []
        for u, (i, cols, here) in enumerate(units):
            summed = sum_ref[here, cols] * near_weights[u] + sums[u]
            attended = (summed * inverses[u]).astype(jnp.bfloat16)
            att_ref[here, cols] = attended
            product = g_ref[here, cols].astype(jnp.float32) * attended.astype(jnp.float32)
            drift = jnp.broadcast_to(jnp.sum(product, axis=1, keepdims=True), product.shape)
            drifts.append(drift)
            level_ref[here, cols] = peaks[u] + jnp.log2(totals[u])
            drift_ref[here, cols] = drift
        moved = [
            weight * (grad_prob - wide(drift, total_width))
            for weight, grad_prob, drift in zip(weights, grad_probs, drifts)
        ]
        factors = [inverse * score_scale for inverse in inverses]
        own_scores = [
            (part[:, :width] * wide(factor, width)).astype(jnp.bfloat16)
            for part, factor in zip(moved, factors)
        ]
        own_probs = [
            (weight[:, :width] * wide(inverse, width)).astype(jnp.bfloat16)
            for weight, inverse in zip(weights, inverses)
        ]
        for u, (i, cols, here) in enumerate(units):
            gq_ref[here, cols] = dot(moved[u].astype(jnp.bfloat16), keys[i], NN) * factors[u]
        for u, (i, cols, here) in enumerate(units):
            key_grads[i].append(dot(own_scores[u], q_ref[here, cols], TN))
            value_grads[i].append(dot(own_probs[u], g_ref[here, cols], TN))

    @pl.loop(0, half // (heads * head_dim))
    def _(group):
        columns = [head_columns(group * heads + i, head_dim) for i in range(heads)]
        units = [
            (i, cols, pl.ds(r, tile)) for i, cols in enumerate(columns) for r in range(0, rows, tile)
        ]
        keys = [far_rows(parts, 0, cols) for cols in columns]
        values = [far_rows(parts, 1, cols) for cols in columns]
        grads = [[[] for _ in columns] for _ in range(2)]
        for first in range(0, len(units), batch):
            work(units[first : first + batch], keys, values, *grads)
        for which, per_head in enumerate(grads):
            for cols, terms in zip(columns, per_head):
                total = functools.reduce(lambda a, b: a + b, terms).astype(jnp.bfloat16)
                for c, ref in enumerate(grad_refs):
                    piece = total[c * span : (c + 1) * span]
                    ref[:, :, which, :, cols] = piece.reshape(steps, cores, part_tok, head_dim)


def near_backward_kernel(members, head_dim, bias_ref, q_ref, g_ref, level_ref, drift_ref, far_gq_ref, *refs):
    parts = refs[:members]
    gq_ref, gk_ref, gv_ref, sent_ref = refs[members:]
    rows, half = q_ref.shape
    near = parts[0].shape[1]
    score_scale = 1.0 / math.sqrt(head_dim)

    @pl.loop(0, half // (GROUP * head_dim))
    def _(group):
        units = [
            (head_columns(group * GROUP + i, head_dim), pl.ds(start, count), used)
            for i in range(GROUP)
            for start, count, used in near_tiles(rows, near)
        ]
        keys = [near_rows(parts, 0, used, cols) for cols, here, used in units]
        values = [near_rows(parts, 1, used, cols) for cols, here, used in units]
        raws = [
            dot(q_ref[here, cols], key, NT) * base2_scale(head_dim)
            + bias_ref[here, : members * used]
            for (cols, here, used), key in zip(units, keys)
        ]
        grad_probs = [
            dot(g_ref[here, cols], value, NT) for (cols, here, used), value in zip(units, values)
        ]
        probs = [
            jnp.exp2(raw - wide(level_ref[here, cols], raw.shape[1]))
            for raw, (cols, here, used) in zip(raws, units)
        ]
        moved = [
            prob * (grad_prob - wide(drift_ref[here, cols], prob.shape[1]))
            for prob, grad_prob, (cols, here, used) in zip(probs, grad_probs, units)
        ]
        for (cols, here, used), part, key in zip(units, moved, keys):
            gq_ref[here, cols] = (
                dot(part.astype(jnp.bfloat16), key, NN) * score_scale + far_gq_ref[here, cols]
            ).astype(jnp.bfloat16)
        grads = []
        for (cols, here, used), part, prob in zip(units, moved, probs):
            own_score = (part[:, : CORES * used] * score_scale).astype(jnp.bfloat16)
            own_prob = prob[:, : CORES * used].astype(jnp.bfloat16)
            grads.append((dot(own_score, q_ref[here, cols], TN), dot(own_prob, g_ref[here, cols], TN)))
        low = near // 2
        for (cols, _, _), early, late in zip(units[0::2], grads[0::2], grads[1::2]):
            for which, own_ref in enumerate((gk_ref, gv_ref)):
                for core in range(CORES):
                    top = late[which][core * near : core * near + low]
                    top += early[which][core * low : (core + 1) * low]
                    bottom = late[which][core * near + low : (core + 1) * near]
                    if core == 0:
                        own_ref[:low, cols] = top
                        own_ref[low:, cols] = bottom
                    else:
                        sent_ref[which, :low, cols] = top.astype(sent_ref.dtype)
                        sent_ref[which, low:, cols] = bottom.astype(sent_ref.dtype)


def call(kernel, operands, outs, pairs, products, head_dim, in_specs=None, scratch=()):
    moved_bytes = sum(a.size * a.dtype.itemsize for a in operands)
    return pl.pallas_call(
        kernel,
        in_specs=in_specs or [WHOLE] * len(operands),
        out_specs=[WHOLE] * len(outs),
        out_shape=outs,
        scratch_shapes=scratch,
        compiler_params=LIMIT,
        cost_estimate=pl.CostEstimate(
            flops=4 * products * pairs * head_dim, bytes_accessed=moved_bytes, transcendentals=pairs
        ),
    )(*operands)


def shards(queries, keys, values, layout, grad_out):
    seq_count = lax.axis_size("seq")
    members = lax.axis_size("kv")
    tok_rows, feat_width = queries.shape
    blocks, part_tok = (keys.shape[0], keys.shape[1])
    blk_len = part_tok * members
    near = blocks * part_tok
    head_dim = feat_width // HEADS
    half = feat_width // CORES
    levels = seq_count // COLUMNS
    groups = members // CORES

    def hop(part, column_step, member_step):
        pairs = [
            (s * members + m, (s ^ column_step) * members + (m ^ member_step))
            for s in range(seq_count)
            for m in range(members)
        ]
        return lax.ppermute(part, ("seq", "kv"), pairs)

    def climb(part, d):
        return lax.ppermute(
            part, "seq", [(s, s + COLUMNS * d) for s in range(seq_count - COLUMNS * d)]
        )

    def sink(part, d):
        return lax.ppermute(
            part, "seq", [(s, s - COLUMNS * d) for s in range(COLUMNS * d, seq_count)]
        )

    mine, theirs, pair_mine, pair_theirs, mask = pick_pair(layout.T, keys, values)
    own_pair = jnp.stack([pair_mine, hop(pair_theirs, 0, 1)])
    climbed = [climb(own_pair, d) for d in range(1, levels)]
    column = jnp.stack(climbed)
    chip_parts = [mine, hop(theirs, 0, 1)]
    near_parts = list(chip_parts)
    for group in range(1, groups):
        near_parts += [hop(part, 0, CORES * group) for part in chip_parts]
    sent_pair, _ = lax.optimization_barrier((own_pair, climbed[0]))
    cross_pairs = [hop(sent_pair, 1, CORES * group) for group in range(groups)]
    column, cross_pairs, near_parts = lax.optimization_barrier((column, cross_pairs, near_parts))
    near_parts = [part.reshape(2, near, half) for part in near_parts]
    crossing = [
        [column if (c, group) == (0, 0) else hop(column, c, CORES * group) for c in range(COLUMNS)]
        for group in range(groups)
    ]

    def rows_out(dtype):
        return pltpu.VMEM((tok_rows, half), dtype)

    near_out = pltpu.VMEM((near, half), jnp.float32)
    far_out = jax.ShapeDtypeStruct((levels,) + own_pair.shape, jnp.bfloat16)
    near_pairs = HEADS // CORES * tok_rows * members * near
    far_width = members * seq_count * part_tok
    far_pairs = HEADS // CORES * tok_rows * far_width
    roomy = far_width <= 512
    far_plan = (tok_rows // 2, GROUP, 2 * GROUP) if roomy else (tok_rows // 8, 1, 1)

    near_sum, near_stat, bias, queries, grad_out = call(
        functools.partial(near_forward_kernel, members, blk_len, part_tok, head_dim),
        [pltpu.with_memory_space_constraint(a, pltpu.HBM) for a in (queries, grad_out)] + near_parts,
        [rows_out(jnp.float32)] * 2
        + [pltpu.VMEM((tok_rows, members * near), jnp.float32)]
        + [rows_out(jnp.bfloat16)] * 2,
        near_pairs,
        2,
        head_dim,
        [IN_HBM, IN_HBM] + [WHOLE] * members,
        [pltpu.SemaphoreType.DMA((half // (GROUP * head_dim) + 1,))],
    )
    far_parts = []
    for group, cross_pair in zip(crossing, cross_pairs):
        (same, other), _ = lax.optimization_barrier((group, near_stat))
        far_parts += [own_pair, same, cross_pair, other]
    attended, far_gq, level, drift, own_grad, cross_grad = call(
        functools.partial(far_kernel, groups, head_dim, *far_plan),
        [queries, grad_out, near_sum, near_stat] + far_parts,
        [rows_out(jnp.bfloat16)] + [rows_out(jnp.float32)] * 3 + [far_out, far_out],
        far_pairs,
        5,
        head_dim,
    )
    grad_q, near_k, near_v, near_sent = call(
        functools.partial(near_backward_kernel, members, head_dim),
        [bias, queries, grad_out, level, drift, far_gq] + near_parts,
        [rows_out(jnp.bfloat16), near_out, near_out, pltpu.VMEM((2, near, half), jnp.bfloat16)],
        near_pairs,
        4,
        head_dim,
    )
    crossed, near_k = lax.optimization_barrier((hop(cross_grad, 1, 0), near_k))
    returned = [crossed[0]]
    for d in range(1, levels):
        summed = own_grad[d].astype(jnp.float32) + crossed[d].astype(jnp.float32)
        returned.append(sink(summed.astype(jnp.bfloat16), d))
    near_theirs = hop(near_sent, 0, 1)
    attended, grad_q = join([(attended, hop(attended, 0, 1)), (grad_q, hop(grad_q, 0, 1))])
    returned, attended, grad_q = lax.optimization_barrier((returned, attended, grad_q))
    far_sent = sum(part[1].astype(jnp.float32) for part in returned).astype(jnp.bfloat16)
    shape = (blocks, part_tok, half)
    grad_k, grad_v = pl.pallas_call(
        finish_kernel,
        in_specs=[WHOLE] * (5 + levels),
        out_specs=[WHOLE] * 2,
        out_shape=[jax.ShapeDtypeStruct(keys.shape, keys.dtype)] * 2,
    )(
        mask,
        near_k.reshape(shape),
        near_v.reshape(shape),
        near_theirs.reshape((2,) + shape),
        hop(far_sent, 0, 1),
        *returned,
    )
    return (attended, grad_q, grad_k, grad_v)


def solution(mesh):
    return jax.shard_map(
        shards,
        mesh=mesh,
        in_specs=(P("seq", None), P("seq", "kv", None), P("seq", "kv", None), P(), P("seq", None)),
        out_specs=(P("seq", None), P("seq", None), P("seq", "kv", None), P("seq", "kv", None)),
        check_vma=False,
    )
```

```python
import functools
import math

import jax
import jax.numpy as jnp
from jax import lax
from jax.experimental import pallas as pl
from jax.experimental.pallas import tpu as pltpu
from jax.sharding import PartitionSpec as P

HEADS = 8
COLUMNS = 2
CORES = 2
GROUP = 2
HIDDEN = -1e30
NT = (((1,), (1,)), ((), ()))
NN = (((1,), (0,)), ((), ()))
TN = (((0,), (0,)), ((), ()))
IN_HBM = pl.BlockSpec(memory_space=pltpu.HBM)
WHOLE = pl.BlockSpec(memory_space=pltpu.VMEM)
LIMIT = pltpu.CompilerParams(vmem_limit_bytes=20 * 1024 * 1024)


def dot(a, b, dims):
    return lax.dot_general(a, b, dims, preferred_element_type=jnp.float32)


def wide(rows, width):
    return jnp.concatenate([rows] * (width // rows.shape[1]), axis=1)


def base2_scale(head_dim):
    return math.log2(math.e) / math.sqrt(head_dim)


def pick_kernel(table_hbm, keys_hbm, values_hbm, mine_ref, theirs_ref, pair_ref, sent_ref, block_ref, table_ref, sems):
    window = lax.axis_index("seq")
    core = lax.axis_index("kv") % CORES
    _, blocks, part_tok, half = mine_ref.shape
    copies = [pltpu.make_async_copy(table_hbm, table_ref, sems.at[0])]
    for which, ref in enumerate((keys_hbm, values_hbm)):
        for side, out_ref in enumerate((mine_ref, theirs_ref)):
            cols = pl.ds(pl.multiple_of((core ^ side) * half, half), half)
            copies.append(
                pltpu.make_async_copy(ref.at[:, :, cols], out_ref.at[which], sems.at[len(copies)])
            )
    for copy in copies:
        copy.start()
    copies[0].wait()
    pick = jnp.minimum(window, lax.axis_size("seq") - 2)
    entry = lax.broadcasted_iota(jnp.int32, table_ref.shape, 0)
    row = lax.broadcasted_iota(jnp.int32, table_ref.shape, 1)
    here = (entry == pick) & (row == table_ref.shape[1] - 1)
    named = jnp.where(here, table_ref[...].astype(jnp.float32), -1.0)
    named = jnp.max(jnp.max(named, axis=1, keepdims=True), axis=0, keepdims=True)
    block = jnp.clip(named - (window * blocks).astype(jnp.float32), 0.0, blocks - 1.0)
    block_ref[...] = jnp.broadcast_to(block, block_ref.shape)
    block = jnp.broadcast_to(block, (part_tok, half))
    for copy in copies[1:]:
        copy.wait()
    for ref, out_ref in ((mine_ref, pair_ref), (theirs_ref, sent_ref)):
        for which in range(2):
            chosen = ref[which, 0].astype(jnp.float32)
            for b in range(1, blocks):
                chosen = jnp.where(block == b, ref[which, b].astype(jnp.float32), chosen)
            out_ref[which] = chosen.astype(out_ref.dtype)


def pick_pair(table, keys, values):
    blocks, part_tok, feat_width = keys.shape
    half = feat_width // CORES
    operands = [pltpu.with_memory_space_constraint(a, pltpu.HBM) for a in (table, keys, values)]
    return pl.pallas_call(
        pick_kernel,
        in_specs=[IN_HBM] * 3,
        out_specs=[WHOLE] * 5,
        out_shape=[pltpu.VMEM((2, blocks, part_tok, half), keys.dtype)] * 2
        + [pltpu.VMEM((2, part_tok, half), keys.dtype)] * 2
        + [pltpu.VMEM((8, 128), jnp.float32)],
        scratch_shapes=[pltpu.VMEM(table.shape, table.dtype), pltpu.SemaphoreType.DMA((5,))],
    )(*operands)


def join_kernel(att_ref, att_far, gq_ref, gq_far, near_ref, near_far, att_out, gq_out, gk_out, gv_out, sems):
    core = lax.axis_index("kv") % CORES
    copies = []
    for out_ref, sides in (
        (att_out, (att_ref, att_far)),
        (gq_out, (gq_ref, gq_far)),
        (gk_out, (near_ref.at[0], near_far.at[0])),
        (gv_out, (near_ref.at[1], near_far.at[1])),
    ):
        half = out_ref.shape[1] // CORES
        for side, ref in enumerate(sides):
            cols = pl.ds(pl.multiple_of((core ^ side) * half, half), half)
            copies.append(pltpu.make_async_copy(ref, out_ref.at[:, cols], sems.at[len(copies)]))
    for copy in copies:
        copy.start()
    for copy in copies:
        copy.wait()


def join(operands, shapes):
    operands = [pltpu.with_memory_space_constraint(a, pltpu.VMEM) for a in operands]
    return pl.pallas_call(
        join_kernel,
        in_specs=[WHOLE] * len(operands),
        out_specs=[IN_HBM] * len(shapes),
        out_shape=[pltpu.HBM(shape, jnp.bfloat16) for shape in shapes],
        scratch_shapes=[pltpu.SemaphoreType.DMA((2 * len(shapes),))],
    )(*operands)


def finish_kernel(block_ref, near_ref, near_far_ref, far_ref, *refs):
    arrived, outs, rows_ref, sems = refs[:-6], refs[-4:-2], refs[-2], refs[-1]
    core = lax.axis_index("kv") % CORES
    part_tok, half = far_ref.shape[1:]
    block = jnp.max(block_ref[...]).astype(jnp.int32)
    here = pl.ds(pl.multiple_of(block * part_tok, part_tok), part_tok)
    mine = pl.ds(pl.multiple_of(core * half, half), half)
    theirs = pl.ds(pl.multiple_of((core ^ 1) * half, half), half)
    copies = []
    for which, out_ref in enumerate(outs):
        total = near_ref[which, here]
        for ref in arrived:
            total += ref[0, which].astype(jnp.float32)
        rows_ref[which, :, mine] = total.astype(rows_ref.dtype)
        total = near_far_ref[which, here].astype(jnp.float32) + far_ref[which].astype(jnp.float32)
        rows_ref[which, :, theirs] = total.astype(rows_ref.dtype)
        copies.append(pltpu.make_async_copy(rows_ref.at[which], out_ref.at[here], sems.at[which]))
        copies[-1].start()
    for copy in copies:
        copy.wait()


def finish(operands, outs):
    part_tok, half = operands[3].shape[1:]
    operands = [pltpu.with_memory_space_constraint(a, pltpu.VMEM) for a in operands]
    outs = [pltpu.with_memory_space_constraint(a, pltpu.HBM) for a in outs]
    return pl.pallas_call(
        finish_kernel,
        in_specs=[WHOLE] * len(operands) + [IN_HBM] * 2,
        out_specs=[IN_HBM] * 2,
        out_shape=[pltpu.HBM(a.shape, a.dtype) for a in outs],
        input_output_aliases={len(operands): 0, len(operands) + 1: 1},
        scratch_shapes=[
            pltpu.VMEM((2, part_tok, half * CORES), jnp.bfloat16),
            pltpu.SemaphoreType.DMA((2,)),
        ],
    )(*operands, *outs)


def near_tiles(rows, near):
    half = rows // 2
    return [(0, half, near // 2), (half, half, near)]


def fill_mask(members, near, blk_len, part_tok, bias_ref):
    member = lax.axis_index("kv")
    shift = part_tok.bit_length() - 1
    for start, count, used in near_tiles(bias_ref.shape[0], near):
        row = start + lax.broadcasted_iota(jnp.int32, (count, 1), 0)
        col = lax.broadcasted_iota(jnp.int32, (1, used), 1)
        key_tok = (col >> shift) * blk_len + (col & (part_tok - 1))
        for j in range(members):
            key_pos = key_tok + (member ^ j) * part_tok
            bias_ref[start : start + count, j * used : (j + 1) * used] = jnp.where(
                key_pos <= row, 0.0, HIDDEN
            )


def head_columns(head, head_dim):
    return pl.ds(pl.multiple_of(head * head_dim, head_dim), head_dim)


def near_rows(parts, which, used, cols):
    return jnp.concatenate([ref[which, :used, cols] for ref in parts], axis=0)


def near_forward_kernel(members, blk_len, part_tok, head_dim, q_hbm, g_hbm, *refs):
    parts = refs[:members]
    out_ref, stat_ref, bias_ref, q_ref, g_ref, sems = refs[members:]
    rows, half = q_ref.shape
    near = parts[0].shape[1]
    slab = GROUP * head_dim
    core = lax.axis_index("kv") % CORES

    def fetch(group):
        there = pl.ds(pl.multiple_of(core * half + group * slab, slab), slab)
        here = pl.ds(pl.multiple_of(group * slab, slab), slab)
        return pltpu.make_async_copy(q_hbm.at[:, there], q_ref.at[:, here], sems.at[group])

    there = pl.ds(pl.multiple_of(core * half, half), half)
    last = pltpu.make_async_copy(g_hbm.at[:, there], g_ref, sems.at[half // slab])
    for group in range(half // slab):
        fetch(group).start()
    last.start()
    fill_mask(members, near, blk_len, part_tok, bias_ref)

    @pl.loop(0, half // slab)
    def _(group):
        fetch(group).wait()
        units = [
            (head_columns(group * GROUP + i, head_dim), pl.ds(start, count), used)
            for i in range(GROUP)
            for start, count, used in near_tiles(rows, near)
        ]
        raws = [
            dot(q_ref[here, cols], near_rows(parts, 0, used, cols), NT) * base2_scale(head_dim)
            + bias_ref[here, : members * used]
            for cols, here, used in units
        ]
        peaks = [jnp.max(raw, axis=1, keepdims=True) for raw in raws]
        weights = [jnp.exp2(raw - peak) for raw, peak in zip(raws, peaks)]
        totals = [jnp.sum(weight, axis=1, keepdims=True) for weight in weights]
        sums = [
            dot(weight.astype(jnp.bfloat16), near_rows(parts, 1, used, cols), NN)
            for weight, (cols, here, used) in zip(weights, units)
        ]
        for (cols, here, used), peak, total, summed in zip(units, peaks, totals, sums):
            level = peak + jnp.log2(total)
            stat_ref[here, cols] = jnp.broadcast_to(level, summed.shape)
            out_ref[here, cols] = summed * (1.0 / total)

    last.wait()


def far_rows(parts, which, cols):
    rows = []
    for pair_ref, column_ref in zip(parts[0::2], parts[1::2]):
        steps, cores, _, part_tok, _ = column_ref.shape
        rows.append(pair_ref[:, which, :, cols].reshape(cores * part_tok, cols.size))
        rows.append(column_ref[:, :, which, :, cols].reshape(steps * cores * part_tok, cols.size))
    return jnp.concatenate(rows, axis=0)


def far_kernel(groups, steps, head_dim, tile, heads, batch, q_ref, g_ref, sum_ref, stat_ref, *refs):
    parts = refs[: 2 * COLUMNS * groups]
    att_ref, gq_ref, level_ref, drift_ref, *grad_refs = refs[2 * COLUMNS * groups :]
    _, cores, _, part_tok, _ = grad_refs[0].shape
    rows, half = q_ref.shape
    span = steps * cores * part_tok
    width = COLUMNS * span
    score_scale = 1.0 / math.sqrt(head_dim)
    window = lax.axis_index("seq")
    level, side = window // COLUMNS, window % COLUMNS
    step = lax.broadcasted_iota(jnp.int32, (1, span), 1) >> ((cores * part_tok).bit_length() - 1)
    valid = [(step >= 1) & (step <= level), (step >= 1 - side) & (step <= level)]
    bias = jnp.concatenate([jnp.where(ok, 0.0, HIDDEN) for ok in valid] * groups, axis=1)
    total_width = groups * width

    def work(units, keys, values, key_grads, value_grads):
        raws = [
            dot(q_ref[here, cols], keys[i], NT) * base2_scale(head_dim) + bias
            for i, cols, here in units
        ]
        grad_probs = [dot(g_ref[here, cols], values[i], NT) for i, cols, here in units]
        near_levels = [stat_ref[here, cols] for i, cols, here in units]
        peaks = [
            jnp.maximum(near_level, jnp.max(raw, axis=1, keepdims=True))
            for near_level, raw in zip(near_levels, raws)
        ]
        near_weights = [jnp.exp2(near_level - peak) for near_level, peak in zip(near_levels, peaks)]
        weights = [jnp.exp2(raw - wide(peak, total_width)) for raw, peak in zip(raws, peaks)]
        totals = [
            near_weight + jnp.sum(weight, axis=1, keepdims=True)
            for near_weight, weight in zip(near_weights, weights)
        ]
        inverses = [1.0 / total for total in totals]
        sums = [
            dot(weight.astype(jnp.bfloat16), values[i], NN)
            for weight, (i, cols, here) in zip(weights, units)
        ]
        drifts = []
        for u, (i, cols, here) in enumerate(units):
            summed = sum_ref[here, cols] * near_weights[u] + sums[u]
            attended = (summed * inverses[u]).astype(jnp.bfloat16)
            att_ref[here, cols] = attended
            product = g_ref[here, cols].astype(jnp.float32) * attended.astype(jnp.float32)
            drift = jnp.broadcast_to(jnp.sum(product, axis=1, keepdims=True), product.shape)
            drifts.append(drift)
            level_ref[here, cols] = peaks[u] + jnp.log2(totals[u])
            drift_ref[here, cols] = drift
        moved = [
            weight * (grad_prob - wide(drift, total_width))
            for weight, grad_prob, drift in zip(weights, grad_probs, drifts)
        ]
        factors = [inverse * score_scale for inverse in inverses]
        own_scores = [
            (part[:, :width] * wide(factor, width)).astype(jnp.bfloat16)
            for part, factor in zip(moved, factors)
        ]
        own_probs = [
            (weight[:, :width] * wide(inverse, width)).astype(jnp.bfloat16)
            for weight, inverse in zip(weights, inverses)
        ]
        for u, (i, cols, here) in enumerate(units):
            gq_ref[here, cols] = dot(moved[u].astype(jnp.bfloat16), keys[i], NN) * factors[u]
        for u, (i, cols, here) in enumerate(units):
            key_grads[i].append(dot(own_scores[u], q_ref[here, cols], TN))
            value_grads[i].append(dot(own_probs[u], g_ref[here, cols], TN))

    @pl.loop(0, half // (heads * head_dim))
    def _(group):
        columns = [head_columns(group * heads + i, head_dim) for i in range(heads)]
        units = [
            (i, cols, pl.ds(r, tile)) for i, cols in enumerate(columns) for r in range(0, rows, tile)
        ]
        keys = [far_rows(parts, 0, cols) for cols in columns]
        values = [far_rows(parts, 1, cols) for cols in columns]
        grads = [[[] for _ in columns] for _ in range(2)]
        for first in range(0, len(units), batch):
            work(units[first : first + batch], keys, values, *grads)
        for which, per_head in enumerate(grads):
            for cols, terms in zip(columns, per_head):
                total = functools.reduce(lambda a, b: a + b, terms).astype(jnp.bfloat16)
                start = 0
                for ref in grad_refs:
                    shape = ref.shape[:2] + (part_tok, head_dim)
                    count = math.prod(shape[:3])
                    ref[:, :, which, :, cols] = total[start : start + count].reshape(shape)
                    start += count


def near_backward_kernel(members, head_dim, bias_ref, q_ref, g_ref, level_ref, drift_ref, far_gq_ref, *refs):
    parts = refs[:members]
    gq_ref, own_ref, kept_ref, sent_ref = refs[members:]
    rows, half = q_ref.shape
    near = parts[0].shape[1]
    score_scale = 1.0 / math.sqrt(head_dim)

    @pl.loop(0, half // (GROUP * head_dim))
    def _(group):
        units = [
            (head_columns(group * GROUP + i, head_dim), pl.ds(start, count), used)
            for i in range(GROUP)
            for start, count, used in near_tiles(rows, near)
        ]
        keys = [near_rows(parts, 0, used, cols) for cols, here, used in units]
        values = [near_rows(parts, 1, used, cols) for cols, here, used in units]
        raws = [
            dot(q_ref[here, cols], key, NT) * base2_scale(head_dim)
            + bias_ref[here, : members * used]
            for (cols, here, used), key in zip(units, keys)
        ]
        grad_probs = [
            dot(g_ref[here, cols], value, NT) for (cols, here, used), value in zip(units, values)
        ]
        probs = [
            jnp.exp2(raw - wide(level_ref[here, cols], raw.shape[1]))
            for raw, (cols, here, used) in zip(raws, units)
        ]
        moved = [
            prob * (grad_prob - wide(drift_ref[here, cols], prob.shape[1]))
            for prob, grad_prob, (cols, here, used) in zip(probs, grad_probs, units)
        ]
        for (cols, here, used), part, key in zip(units, moved, keys):
            gq_ref[here, cols] = (
                dot(part.astype(jnp.bfloat16), key, NN) * score_scale + far_gq_ref[here, cols]
            ).astype(jnp.bfloat16)
        grads = []
        for (cols, here, used), part, prob in zip(units, moved, probs):
            own_score = (part[:, : CORES * used] * score_scale).astype(jnp.bfloat16)
            own_prob = prob[:, : CORES * used].astype(jnp.bfloat16)
            grads.append((dot(own_score, q_ref[here, cols], TN), dot(own_prob, g_ref[here, cols], TN)))
        low = near // 2
        for (cols, _, _), early, late in zip(units[0::2], grads[0::2], grads[1::2]):
            for which in range(2):
                for core in range(CORES):
                    top = late[which][core * near : core * near + low]
                    top += early[which][core * low : (core + 1) * low]
                    bottom = late[which][core * near + low : (core + 1) * near]
                    if core == 0:
                        own_ref[which, :low, cols] = top
                        own_ref[which, low:, cols] = bottom
                    ref = (kept_ref, sent_ref)[core]
                    ref[which, :low, cols] = top.astype(ref.dtype)
                    ref[which, low:, cols] = bottom.astype(ref.dtype)


def call(kernel, operands, outs, pairs, products, head_dim, in_specs=None, scratch=()):
    moved_bytes = sum(a.size * a.dtype.itemsize for a in operands)
    return pl.pallas_call(
        kernel,
        in_specs=in_specs or [WHOLE] * len(operands),
        out_specs=[WHOLE] * len(outs),
        out_shape=outs,
        scratch_shapes=scratch,
        compiler_params=LIMIT,
        cost_estimate=pl.CostEstimate(
            flops=4 * products * pairs * head_dim, bytes_accessed=moved_bytes, transcendentals=pairs
        ),
    )(*operands)


def shards(queries, keys, values, layout, grad_out):
    seq_count = lax.axis_size("seq")
    members = lax.axis_size("kv")
    tok_rows, feat_width = queries.shape
    blocks, part_tok = (keys.shape[0], keys.shape[1])
    blk_len = part_tok * members
    near = blocks * part_tok
    head_dim = feat_width // HEADS
    half = feat_width // CORES
    levels = seq_count // COLUMNS
    groups = members // CORES

    def hop(part, column_step, member_step):
        pairs = [
            (s * members + m, (s ^ column_step) * members + (m ^ member_step))
            for s in range(seq_count)
            for m in range(members)
        ]
        return lax.ppermute(part, ("seq", "kv"), pairs)

    def climb(part, d):
        return lax.ppermute(
            part, "seq", [(s, s + COLUMNS * d) for s in range(seq_count - COLUMNS * d)]
        )

    def sink(part, d):
        return lax.ppermute(
            part, "seq", [(s, s - COLUMNS * d) for s in range(COLUMNS * d, seq_count)]
        )

    mine, theirs, pair_mine, pair_theirs, block = pick_pair(layout.T, keys, values)
    own_pair = jnp.stack([pair_mine, hop(pair_theirs, 0, 1)])
    climbed = [climb(own_pair, d) for d in range(1, levels)]
    column = jnp.stack(climbed)
    chip_parts = [mine, hop(theirs, 0, 1)]
    near_parts = list(chip_parts)
    for group in range(1, groups):
        near_parts += [hop(part, 0, CORES * group) for part in chip_parts]
    sent_pair, _ = lax.optimization_barrier((own_pair, chip_parts[1]))
    cross_pairs = [hop(sent_pair, 1, CORES * group) for group in range(groups)]
    column, cross_pairs, near_parts = lax.optimization_barrier((column, cross_pairs, near_parts))
    near_parts = [part.reshape(2, near, half) for part in near_parts]
    crossing = [
        [column if (c, group) == (0, 0) else hop(column, c, CORES * group) for c in range(COLUMNS)]
        for group in range(groups)
    ]

    def rows_out(dtype):
        return pltpu.VMEM((tok_rows, half), dtype)

    def far_out(count):
        return pltpu.VMEM((count,) + own_pair.shape, jnp.bfloat16)

    low = (levels + 1) // 2
    near_pairs = HEADS // CORES * tok_rows * members * near
    far_width = members * seq_count * part_tok
    far_pairs = HEADS // CORES * tok_rows * far_width
    roomy = far_width <= 512
    far_plan = (tok_rows // 2, GROUP, 2 * GROUP) if roomy else (tok_rows // 8, 1, 1)

    near_sum, near_stat, bias, queries, grad_out = call(
        functools.partial(near_forward_kernel, members, blk_len, part_tok, head_dim),
        [pltpu.with_memory_space_constraint(a, pltpu.HBM) for a in (queries, grad_out)] + near_parts,
        [rows_out(jnp.float32)] * 2
        + [pltpu.VMEM((tok_rows, members * near), jnp.float32)]
        + [rows_out(jnp.bfloat16)] * 2,
        near_pairs,
        2,
        head_dim,
        [IN_HBM, IN_HBM] + [WHOLE] * members,
        [pltpu.SemaphoreType.DMA((half // (GROUP * head_dim) + 1,))],
    )
    far_parts = []
    for group, cross_pair in zip(crossing, cross_pairs):
        (same, other), _ = lax.optimization_barrier((group, near_stat))
        far_parts += [own_pair, same, cross_pair, other]
    attended, far_gq, level, drift, own_low, own_high, cross_low, cross_high = call(
        functools.partial(far_kernel, groups, levels, head_dim, *far_plan),
        [queries, grad_out, near_sum, near_stat] + far_parts,
        [rows_out(jnp.bfloat16)]
        + [rows_out(jnp.float32)] * 3
        + [far_out(low), far_out(levels - low)] * COLUMNS,
        far_pairs,
        5,
        head_dim,
    )
    high = hop(cross_high, 1, 0)
    grad_q, near_own, near_kept, near_sent = call(
        functools.partial(near_backward_kernel, members, head_dim),
        [bias, queries, grad_out, level, drift, far_gq] + near_parts,
        [rows_out(jnp.bfloat16), pltpu.VMEM((2, near, half), jnp.float32)]
        + [pltpu.VMEM((2, near, half), jnp.bfloat16)] * 2,
        near_pairs,
        4,
        head_dim,
    )
    cross_low, near_own = lax.optimization_barrier((cross_low, near_own))
    crossed = hop(cross_low, 1, 0)
    high, near_own = lax.optimization_barrier((high, near_own))

    def add(own, cross):
        return (own.astype(jnp.float32) + cross.astype(jnp.float32)).astype(jnp.bfloat16)

    sums = [add(own_high[d - low], high[d - low]) for d in range(low, levels)]
    attended, grad_q, near_sent, _ = lax.optimization_barrier(
        (attended, grad_q, near_sent, crossed)
    )
    sums = [add(own_low[d], crossed[d]) for d in range(1, low)] + sums
    returned = [sink(part, d) for d, part in enumerate(sums, 1)] + [crossed[0]]
    near_theirs = hop(near_sent, 0, 1)
    attended, grad_q, grad_k, grad_v = join(
        [attended, hop(attended, 0, 1), grad_q, hop(grad_q, 0, 1), near_kept, near_theirs],
        [(tok_rows, feat_width)] * 2 + [(near, feat_width)] * 2,
    )
    returned, grad_k, grad_v = lax.optimization_barrier((returned, grad_k, grad_v))
    far_sent = sum(part[1].astype(jnp.float32) for part in returned).astype(jnp.bfloat16)
    grad_k, grad_v = finish(
        [block, near_own, near_theirs, hop(far_sent, 0, 1)] + returned, [grad_k, grad_v]
    )
    return (attended, grad_q, grad_k.reshape(keys.shape), grad_v.reshape(values.shape))


def solution(mesh):
    return jax.shard_map(
        shards,
        mesh=mesh,
        in_specs=(P("seq", None), P("seq", "kv", None), P("seq", "kv", None), P(), P("seq", None)),
        out_specs=(P("seq", None), P("seq", None), P("seq", "kv", None), P("seq", "kv", None)),
        check_vma=False,
    )
```

```python
import functools
import math

import jax
import jax.numpy as jnp
from jax import lax
from jax.experimental import pallas as pl
from jax.experimental.pallas import tpu as pltpu
from jax.sharding import PartitionSpec as P

HEADS = 8
COLUMNS = 2
CORES = 2
GROUP = 2
SMALL = pl.CostEstimate(flops=0, bytes_accessed=0, transcendentals=0)
HIDDEN = -1e30
NT = (((1,), (1,)), ((), ()))
NN = (((1,), (0,)), ((), ()))
TN = (((0,), (0,)), ((), ()))
IN_HBM = pl.BlockSpec(memory_space=pltpu.HBM)
WHOLE = pl.BlockSpec(memory_space=pltpu.VMEM)
LIMIT = pltpu.CompilerParams(vmem_limit_bytes=20 * 1024 * 1024)


def dot(a, b, dims):
    return lax.dot_general(a, b, dims, preferred_element_type=jnp.float32)


def wide(rows, width):
    return jnp.concatenate([rows] * (width // rows.shape[1]), axis=1)


def base2_scale(head_dim):
    return math.log2(math.e) / math.sqrt(head_dim)


def pick_kernel(table_hbm, keys_hbm, values_hbm, mine_ref, theirs_ref, pair_ref, sent_ref, block_ref, table_ref, sems):
    window = lax.axis_index("seq")
    core = lax.axis_index("kv") % CORES
    _, blocks, part_tok, half = mine_ref.shape
    copies = [pltpu.make_async_copy(table_hbm, table_ref, sems.at[0])]
    for which, ref in enumerate((keys_hbm, values_hbm)):
        for side, out_ref in enumerate((mine_ref, theirs_ref)):
            cols = pl.ds(pl.multiple_of((core ^ side) * half, half), half)
            copies.append(
                pltpu.make_async_copy(ref.at[:, :, cols], out_ref.at[which], sems.at[len(copies)])
            )
    for copy in copies:
        copy.start()
    copies[0].wait()
    pick = jnp.minimum(window, lax.axis_size("seq") - 2)
    entry = lax.broadcasted_iota(jnp.int32, table_ref.shape, 0)
    row = lax.broadcasted_iota(jnp.int32, table_ref.shape, 1)
    here = (entry == pick) & (row == table_ref.shape[1] - 1)
    named = jnp.where(here, table_ref[...].astype(jnp.float32), -1.0)
    named = jnp.max(jnp.max(named, axis=1, keepdims=True), axis=0, keepdims=True)
    block = jnp.clip(named - (window * blocks).astype(jnp.float32), 0.0, blocks - 1.0)
    block_ref[...] = jnp.broadcast_to(block, block_ref.shape)
    block = jnp.broadcast_to(block, (part_tok, half))
    for copy in copies[1:]:
        copy.wait()
    for ref, out_ref in ((mine_ref, pair_ref), (theirs_ref, sent_ref)):
        for which in range(2):
            chosen = ref[which, 0].astype(jnp.float32)
            for b in range(1, blocks):
                chosen = jnp.where(block == b, ref[which, b].astype(jnp.float32), chosen)
            out_ref[which] = chosen.astype(out_ref.dtype)


def pick_pair(table, keys, values):
    blocks, part_tok, feat_width = keys.shape
    half = feat_width // CORES
    operands = [pltpu.with_memory_space_constraint(a, pltpu.HBM) for a in (table, keys, values)]
    return pl.pallas_call(
        pick_kernel,
        in_specs=[IN_HBM] * 3,
        out_specs=[WHOLE] * 5,
        out_shape=[pltpu.VMEM((2, blocks, part_tok, half), keys.dtype)] * 2
        + [pltpu.VMEM((2, part_tok, half), keys.dtype)] * 2
        + [pltpu.VMEM((8, 128), jnp.float32)],
        scratch_shapes=[pltpu.VMEM(table.shape, table.dtype), pltpu.SemaphoreType.DMA((5,))],
    )(*operands)


def join_kernel(att_ref, att_far, sent_ref, sent_far, kept_ref, att_out, gq_out, gk_out, gv_out, sems):
    core = lax.axis_index("kv") % CORES
    rows, half = att_ref.shape
    near = gk_out.shape[0]
    own, gk, gv = pl.ds(0, rows), pl.ds(rows, near), pl.ds(rows + near, near)
    copies = []
    for out_ref, sides in (
        (att_out, (att_ref, att_far)),
        (gq_out, (sent_ref.at[own], sent_far.at[own])),
        (gk_out, (kept_ref.at[pl.ds(0, near)], sent_far.at[gk])),
        (gv_out, (kept_ref.at[pl.ds(near, near)], sent_far.at[gv])),
    ):
        for side, ref in enumerate(sides):
            cols = pl.ds(pl.multiple_of((core ^ side) * half, half), half)
            copies.append(pltpu.make_async_copy(ref, out_ref.at[:, cols], sems.at[len(copies)]))
    for copy in copies:
        copy.start()
    for copy in copies:
        copy.wait()


def join(operands, shapes):
    return pl.pallas_call(
        join_kernel,
        in_specs=[pl.BlockSpec(memory_space=pl.ANY)] * len(operands),
        out_specs=[IN_HBM] * len(shapes),
        out_shape=[pltpu.HBM(shape, jnp.bfloat16) for shape in shapes],
        scratch_shapes=[pltpu.SemaphoreType.DMA((2 * len(shapes),))],
        cost_estimate=SMALL,
    )(*operands)


def finish_kernel(block_ref, near_ref, near_far_ref, far_ref, *refs):
    arrived, outs, rows_ref, sems = refs[:-6], refs[-4:-2], refs[-2], refs[-1]
    core = lax.axis_index("kv") % CORES
    part_tok, half = far_ref.shape[1:]
    block = jnp.max(block_ref[...]).astype(jnp.int32)
    here = pl.ds(pl.multiple_of(block * part_tok, part_tok), part_tok)
    near = near_ref.shape[1]
    first = near_far_ref.shape[0] - 2 * near
    mine = pl.ds(pl.multiple_of(core * half, half), half)
    theirs = pl.ds(pl.multiple_of((core ^ 1) * half, half), half)
    copies = []
    for which, out_ref in enumerate(outs):
        total = near_ref[which, here]
        for ref in arrived:
            total += ref[0, which].astype(jnp.float32)
        rows_ref[which, :, mine] = total.astype(rows_ref.dtype)
        there = first + which * near + block * part_tok
        there = pl.ds(pl.multiple_of(there, part_tok), part_tok)
        total = near_far_ref[there, :].astype(jnp.float32) + far_ref[which].astype(jnp.float32)
        rows_ref[which, :, theirs] = total.astype(rows_ref.dtype)
        copies.append(pltpu.make_async_copy(rows_ref.at[which], out_ref.at[here], sems.at[which]))
        copies[-1].start()
    for copy in copies:
        copy.wait()


def finish(operands, outs):
    part_tok, half = operands[3].shape[1:]
    operands = [pltpu.with_memory_space_constraint(a, pltpu.VMEM) for a in operands]
    outs = [pltpu.with_memory_space_constraint(a, pltpu.HBM) for a in outs]
    return pl.pallas_call(
        finish_kernel,
        in_specs=[WHOLE] * len(operands) + [IN_HBM] * 2,
        out_specs=[IN_HBM] * 2,
        out_shape=[pltpu.HBM(a.shape, a.dtype) for a in outs],
        input_output_aliases={len(operands): 0, len(operands) + 1: 1},
        scratch_shapes=[
            pltpu.VMEM((2, part_tok, half * CORES), jnp.bfloat16),
            pltpu.SemaphoreType.DMA((2,)),
        ],
        cost_estimate=SMALL,
    )(*operands, *outs)


def near_tiles(rows, near):
    half = rows // 2
    return [(0, half, near // 2), (half, half, near)]


def fill_mask(members, near, blk_len, part_tok, bias_ref):
    member = lax.axis_index("kv")
    shift = part_tok.bit_length() - 1
    for start, count, used in near_tiles(bias_ref.shape[0], near):
        row = start + lax.broadcasted_iota(jnp.int32, (count, 1), 0)
        col = lax.broadcasted_iota(jnp.int32, (1, used), 1)
        key_tok = (col >> shift) * blk_len + (col & (part_tok - 1))
        for j in range(members):
            key_pos = key_tok + (member ^ j) * part_tok
            bias_ref[start : start + count, j * used : (j + 1) * used] = jnp.where(
                key_pos <= row, 0.0, HIDDEN
            )


def head_columns(head, head_dim):
    return pl.ds(pl.multiple_of(head * head_dim, head_dim), head_dim)


def near_rows(parts, which, used, cols):
    return jnp.concatenate(
        [ref[core, which, :used, cols] for ref in parts for core in range(CORES)], axis=0
    )


def near_forward_kernel(members, blk_len, part_tok, head_dim, q_hbm, g_hbm, *refs):
    parts, outs = refs[: members // CORES], refs[members // CORES :]
    out_ref, stat_ref, bias_ref, q_ref, g_ref, sems = outs
    rows, half = q_ref.shape
    near = parts[0].shape[2]
    slab = GROUP * head_dim
    core = lax.axis_index("kv") % CORES

    def fetch(group):
        there = pl.ds(pl.multiple_of(core * half + group * slab, slab), slab)
        here = pl.ds(pl.multiple_of(group * slab, slab), slab)
        return pltpu.make_async_copy(q_hbm.at[:, there], q_ref.at[:, here], sems.at[group])

    there = pl.ds(pl.multiple_of(core * half, half), half)
    last = pltpu.make_async_copy(g_hbm.at[:, there], g_ref, sems.at[half // slab])
    for group in range(half // slab):
        fetch(group).start()
    last.start()
    fill_mask(members, near, blk_len, part_tok, bias_ref)

    @pl.loop(0, half // slab)
    def _(group):
        fetch(group).wait()
        units = [
            (head_columns(group * GROUP + i, head_dim), pl.ds(start, count), used)
            for i in range(GROUP)
            for start, count, used in near_tiles(rows, near)
        ]
        raws = [
            dot(q_ref[here, cols], near_rows(parts, 0, used, cols), NT) * base2_scale(head_dim)
            + bias_ref[here, : members * used]
            for cols, here, used in units
        ]
        peaks = [jnp.max(raw, axis=1, keepdims=True) for raw in raws]
        weights = [jnp.exp2(raw - peak) for raw, peak in zip(raws, peaks)]
        totals = [jnp.sum(weight, axis=1, keepdims=True) for weight in weights]
        sums = [
            dot(weight.astype(jnp.bfloat16), near_rows(parts, 1, used, cols), NN)
            for weight, (cols, here, used) in zip(weights, units)
        ]
        for (cols, here, used), peak, total, summed in zip(units, peaks, totals, sums):
            level = peak + jnp.log2(total)
            stat_ref[here, cols] = jnp.broadcast_to(level, summed.shape)
            out_ref[here, cols] = summed * (1.0 / total)

    last.wait()


def far_rows(parts, which, cols):
    rows = []
    for pair_ref, column_ref in zip(parts[0::2], parts[1::2]):
        steps, cores, _, part_tok, _ = column_ref.shape
        rows.append(pair_ref[:, which, :, cols].reshape(cores * part_tok, cols.size))
        rows.append(column_ref[:, :, which, :, cols].reshape(steps * cores * part_tok, cols.size))
    return jnp.concatenate(rows, axis=0)


def far_kernel(groups, steps, head_dim, tile, heads, batch, q_ref, g_ref, sum_ref, stat_ref, *refs):
    parts = refs[: 2 * COLUMNS * groups]
    att_ref, gq_ref, level_ref, drift_ref, *grad_refs = refs[2 * COLUMNS * groups :]
    _, cores, _, part_tok, _ = grad_refs[0].shape
    rows, half = q_ref.shape
    span = steps * cores * part_tok
    width = COLUMNS * span
    score_scale = 1.0 / math.sqrt(head_dim)
    window = lax.axis_index("seq")
    level, side = window // COLUMNS, window % COLUMNS
    step = lax.broadcasted_iota(jnp.int32, (1, span), 1) >> ((cores * part_tok).bit_length() - 1)
    valid = [(step >= 1) & (step <= level), (step >= 1 - side) & (step <= level)]
    bias = jnp.concatenate([jnp.where(ok, 0.0, HIDDEN) for ok in valid] * groups, axis=1)
    total_width = groups * width

    def work(units, keys, values, key_grads, value_grads):
        raws = [
            dot(q_ref[here, cols], keys[i], NT) * base2_scale(head_dim) + bias
            for i, cols, here in units
        ]
        grad_probs = [dot(g_ref[here, cols], values[i], NT) for i, cols, here in units]
        near_levels = [stat_ref[here, cols] for i, cols, here in units]
        peaks = [
            jnp.maximum(near_level, jnp.max(raw, axis=1, keepdims=True))
            for near_level, raw in zip(near_levels, raws)
        ]
        near_weights = [jnp.exp2(near_level - peak) for near_level, peak in zip(near_levels, peaks)]
        weights = [jnp.exp2(raw - wide(peak, total_width)) for raw, peak in zip(raws, peaks)]
        totals = [
            near_weight + jnp.sum(weight, axis=1, keepdims=True)
            for near_weight, weight in zip(near_weights, weights)
        ]
        inverses = [1.0 / total for total in totals]
        sums = [
            dot(weight.astype(jnp.bfloat16), values[i], NN)
            for weight, (i, cols, here) in zip(weights, units)
        ]
        drifts = []
        for u, (i, cols, here) in enumerate(units):
            summed = sum_ref[here, cols] * near_weights[u] + sums[u]
            attended = (summed * inverses[u]).astype(jnp.bfloat16)
            att_ref[here, cols] = attended
            product = g_ref[here, cols].astype(jnp.float32) * attended.astype(jnp.float32)
            drift = jnp.broadcast_to(jnp.sum(product, axis=1, keepdims=True), product.shape)
            drifts.append(drift)
            level_ref[here, cols] = peaks[u] + jnp.log2(totals[u])
            drift_ref[here, cols] = drift
        moved = [
            weight * (grad_prob - wide(drift, total_width))
            for weight, grad_prob, drift in zip(weights, grad_probs, drifts)
        ]
        factors = [inverse * score_scale for inverse in inverses]
        own_scores = [
            (part[:, :width] * wide(factor, width)).astype(jnp.bfloat16)
            for part, factor in zip(moved, factors)
        ]
        own_probs = [
            (weight[:, :width] * wide(inverse, width)).astype(jnp.bfloat16)
            for weight, inverse in zip(weights, inverses)
        ]
        for u, (i, cols, here) in enumerate(units):
            gq_ref[here, cols] = dot(moved[u].astype(jnp.bfloat16), keys[i], NN) * factors[u]
        for u, (i, cols, here) in enumerate(units):
            key_grads[i].append(dot(own_scores[u], q_ref[here, cols], TN))
            value_grads[i].append(dot(own_probs[u], g_ref[here, cols], TN))

    @pl.loop(0, half // (heads * head_dim))
    def _(group):
        columns = [head_columns(group * heads + i, head_dim) for i in range(heads)]
        units = [
            (i, cols, pl.ds(r, tile)) for i, cols in enumerate(columns) for r in range(0, rows, tile)
        ]
        keys = [far_rows(parts, 0, cols) for cols in columns]
        values = [far_rows(parts, 1, cols) for cols in columns]
        grads = [[[] for _ in columns] for _ in range(2)]
        for first in range(0, len(units), batch):
            work(units[first : first + batch], keys, values, *grads)
        for which, per_head in enumerate(grads):
            for cols, terms in zip(columns, per_head):
                total = functools.reduce(lambda a, b: a + b, terms).astype(jnp.bfloat16)
                start = 0
                for ref in grad_refs:
                    shape = ref.shape[:2] + (part_tok, head_dim)
                    count = math.prod(shape[:3])
                    ref[:, :, which, :, cols] = total[start : start + count].reshape(shape)
                    start += count


def near_backward_kernel(members, head_dim, bias_ref, q_ref, g_ref, level_ref, drift_ref, far_gq_ref, *refs):
    parts, outs = refs[: members // CORES], refs[members // CORES :]
    own_ref, kept_ref, sent_ref = outs
    rows, half = q_ref.shape
    near = parts[0].shape[2]
    score_scale = 1.0 / math.sqrt(head_dim)

    @pl.loop(0, half // (GROUP * head_dim))
    def _(group):
        units = [
            (head_columns(group * GROUP + i, head_dim), pl.ds(start, count), used)
            for i in range(GROUP)
            for start, count, used in near_tiles(rows, near)
        ]
        keys = [near_rows(parts, 0, used, cols) for cols, here, used in units]
        values = [near_rows(parts, 1, used, cols) for cols, here, used in units]
        raws = [
            dot(q_ref[here, cols], key, NT) * base2_scale(head_dim)
            + bias_ref[here, : members * used]
            for (cols, here, used), key in zip(units, keys)
        ]
        grad_probs = [
            dot(g_ref[here, cols], value, NT) for (cols, here, used), value in zip(units, values)
        ]
        probs = [
            jnp.exp2(raw - wide(level_ref[here, cols], raw.shape[1]))
            for raw, (cols, here, used) in zip(raws, units)
        ]
        moved = [
            prob * (grad_prob - wide(drift_ref[here, cols], prob.shape[1]))
            for prob, grad_prob, (cols, here, used) in zip(probs, grad_probs, units)
        ]
        for (cols, here, used), part, key in zip(units, moved, keys):
            sent_ref[here, cols] = (
                dot(part.astype(jnp.bfloat16), key, NN) * score_scale + far_gq_ref[here, cols]
            ).astype(jnp.bfloat16)
        grads = []
        for (cols, here, used), part, prob in zip(units, moved, probs):
            own_score = (part[:, : CORES * used] * score_scale).astype(jnp.bfloat16)
            own_prob = prob[:, : CORES * used].astype(jnp.bfloat16)
            grads.append((dot(own_score, q_ref[here, cols], TN), dot(own_prob, g_ref[here, cols], TN)))
        low = near // 2
        for (cols, _, _), early, late in zip(units[0::2], grads[0::2], grads[1::2]):
            for which in range(2):
                for core in range(CORES):
                    top = late[which][core * near : core * near + low]
                    top += early[which][core * low : (core + 1) * low]
                    bottom = late[which][core * near + low : (core + 1) * near]
                    if core == 0:
                        own_ref[which, :low, cols] = top
                        own_ref[which, low:, cols] = bottom
                    ref, first = ((kept_ref, 0), (sent_ref, rows))[core]
                    first += which * near
                    ref[first : first + low, cols] = top.astype(ref.dtype)
                    ref[first + low : first + near, cols] = bottom.astype(ref.dtype)


def call(kernel, operands, outs, pairs, products, head_dim, in_specs=None, scratch=()):
    moved_bytes = sum(a.size * a.dtype.itemsize for a in operands)
    return pl.pallas_call(
        kernel,
        in_specs=in_specs or [WHOLE] * len(operands),
        out_specs=[WHOLE] * len(outs),
        out_shape=outs,
        scratch_shapes=scratch,
        compiler_params=LIMIT,
        cost_estimate=pl.CostEstimate(
            flops=4 * products * pairs * head_dim, bytes_accessed=moved_bytes, transcendentals=pairs
        ),
    )(*operands)


def shards(queries, keys, values, layout, grad_out):
    seq_count = lax.axis_size("seq")
    members = lax.axis_size("kv")
    tok_rows, feat_width = queries.shape
    blocks, part_tok = (keys.shape[0], keys.shape[1])
    blk_len = part_tok * members
    near = blocks * part_tok
    head_dim = feat_width // HEADS
    half = feat_width // CORES
    levels = seq_count // COLUMNS
    groups = members // CORES

    def hop(part, column_step, member_step):
        pairs = [
            (s * members + m, (s ^ column_step) * members + (m ^ member_step))
            for s in range(seq_count)
            for m in range(members)
        ]
        return lax.ppermute(part, ("seq", "kv"), pairs)

    def climb(part, d):
        return lax.ppermute(
            part, "seq", [(s, s + COLUMNS * d) for s in range(seq_count - COLUMNS * d)]
        )

    def sink(part, d):
        return lax.ppermute(
            part, "seq", [(s, s - COLUMNS * d) for s in range(COLUMNS * d, seq_count)]
        )

    mine, theirs, pair_mine, pair_theirs, block = pick_pair(layout.T, keys, values)
    own_pair = jnp.stack([pair_mine, hop(pair_theirs, 0, 1)])
    climbed = [climb(own_pair, d) for d in range(1, levels)]
    column = jnp.stack(climbed)
    chip_parts = [mine, hop(theirs, 0, 1)]
    chip_near = jnp.stack(chip_parts).reshape(CORES, 2, near, half)
    chip_near, _ = lax.optimization_barrier((chip_near, own_pair))
    near_parts = [chip_near] + [hop(chip_near, 0, CORES * group) for group in range(1, groups)]
    sent_pair, _ = lax.optimization_barrier((own_pair, chip_parts[1]))
    cross_pairs = [hop(sent_pair, 1, CORES * group) for group in range(groups)]
    column, near_parts = lax.optimization_barrier((column, near_parts))
    crossing = [
        [column if (c, group) == (0, 0) else hop(column, c, CORES * group) for c in range(COLUMNS)]
        for group in range(groups)
    ]

    def rows_out(dtype):
        return pltpu.VMEM((tok_rows, half), dtype)

    def far_out(count):
        return pltpu.VMEM((count,) + own_pair.shape, jnp.bfloat16)

    low = (levels + 1) // 2
    near_pairs = HEADS // CORES * tok_rows * members * near
    far_width = members * seq_count * part_tok
    far_pairs = HEADS // CORES * tok_rows * far_width
    roomy = far_width <= 512
    far_plan = (tok_rows // 2, GROUP, 2 * GROUP) if roomy else (tok_rows // 8, 1, 1)

    near_sum, near_stat, bias, queries, grad_out = call(
        functools.partial(near_forward_kernel, members, blk_len, part_tok, head_dim),
        [pltpu.with_memory_space_constraint(a, pltpu.HBM) for a in (queries, grad_out)] + near_parts,
        [rows_out(jnp.float32)] * 2
        + [pltpu.VMEM((tok_rows, members * near), jnp.float32)]
        + [rows_out(jnp.bfloat16)] * 2,
        near_pairs,
        2,
        head_dim,
        [IN_HBM, IN_HBM] + [WHOLE] * groups,
        [pltpu.SemaphoreType.DMA((half // (GROUP * head_dim) + 1,))],
    )
    far_parts = []
    for group, cross_pair in zip(crossing, cross_pairs):
        (same, other), _ = lax.optimization_barrier((group, near_stat))
        far_parts += [own_pair, same, cross_pair, other]
    attended, far_gq, level, drift, own_low, own_high, cross_low, cross_high = call(
        functools.partial(far_kernel, groups, levels, head_dim, *far_plan),
        [queries, grad_out, near_sum, near_stat] + far_parts,
        [rows_out(jnp.bfloat16)]
        + [rows_out(jnp.float32)] * 3
        + [far_out(low), far_out(levels - low)] * COLUMNS,
        far_pairs,
        5,
        head_dim,
    )

    def add(own, cross):
        return (own.astype(jnp.float32) + cross.astype(jnp.float32)).astype(jnp.bfloat16)

    high = hop(cross_high, 1, 0)
    near_own, near_kept, sent = call(
        functools.partial(near_backward_kernel, members, head_dim),
        [bias, queries, grad_out, level, drift, far_gq] + near_parts,
        [
            pltpu.VMEM((2, near, half), jnp.float32),
            pltpu.VMEM((2 * near, half), jnp.bfloat16),
            pltpu.VMEM((tok_rows + 2 * near, half), jnp.bfloat16),
        ],
        near_pairs,
        4,
        head_dim,
    )
    high, _ = lax.optimization_barrier((high, sent))
    sums = [add(own_high[d - low], high[d - low]) for d in range(low, levels)]
    cross_low, sent_mine, att_mine, _ = lax.optimization_barrier((cross_low, sent, attended, sums))
    crossed = hop(cross_low, 1, 0)
    sent_far = hop(sent_mine, 0, 1)
    att_far = hop(att_mine, 0, 1)
    sums = [add(own_low[d], crossed[d]) for d in range(1, low)] + sums
    returned = [sink(part, d) for d, part in enumerate(sums, 1)] + [crossed[0]]
    attended, grad_q, grad_k, grad_v = join(
        [attended, att_far, sent, sent_far, near_kept],
        [(tok_rows, feat_width)] * 2 + [(near, feat_width)] * 2,
    )
    returned, grad_k, grad_v = lax.optimization_barrier((returned, grad_k, grad_v))
    far_sent = sum(part[1].astype(jnp.float32) for part in returned).astype(jnp.bfloat16)
    grad_k, grad_v = finish(
        [block, near_own, sent_far, hop(far_sent, 0, 1)] + returned, [grad_k, grad_v]
    )
    return (attended, grad_q, grad_k.reshape(keys.shape), grad_v.reshape(values.shape))


def solution(mesh):
    return jax.shard_map(
        shards,
        mesh=mesh,
        in_specs=(P("seq", None), P("seq", "kv", None), P("seq", "kv", None), P(), P("seq", None)),
        out_specs=(P("seq", None), P("seq", None), P("seq", "kv", None), P("seq", "kv", None)),
        check_vma=False,
    )
```

```python
import functools
import math

import jax
import jax.numpy as jnp
from jax import lax
from jax.experimental import pallas as pl
from jax.experimental.pallas import tpu as pltpu
from jax.sharding import PartitionSpec as P

HEADS = 8
COLUMNS = 2
CORES = 2
GROUP = 2
SMALL = pl.CostEstimate(flops=0, bytes_accessed=0, transcendentals=0)
HIDDEN = -1e30
NT = (((1,), (1,)), ((), ()))
NN = (((1,), (0,)), ((), ()))
TN = (((0,), (0,)), ((), ()))
IN_HBM = pl.BlockSpec(memory_space=pltpu.HBM)
WHOLE = pl.BlockSpec(memory_space=pltpu.VMEM)
LIMIT = pltpu.CompilerParams(vmem_limit_bytes=12 * 1024 * 1024)


def dot(a, b, dims):
    return lax.dot_general(a, b, dims, preferred_element_type=jnp.float32)


def wide(rows, width):
    return jnp.concatenate([rows] * (width // rows.shape[1]), axis=1)


def base2_scale(head_dim):
    return math.log2(math.e) / math.sqrt(head_dim)


def pick_kernel(table_hbm, keys_hbm, values_hbm, mine_ref, theirs_ref, pair_ref, sent_ref, block_ref, table_ref, sems):
    window = lax.axis_index("seq")
    core = lax.axis_index("kv") % CORES
    _, blocks, part_tok, half = mine_ref.shape
    copies = [pltpu.make_async_copy(table_hbm, table_ref, sems.at[0])]
    for which, ref in enumerate((keys_hbm, values_hbm)):
        for side, out_ref in enumerate((mine_ref, theirs_ref)):
            cols = pl.ds(pl.multiple_of((core ^ side) * half, half), half)
            copies.append(
                pltpu.make_async_copy(ref.at[:, :, cols], out_ref.at[which], sems.at[len(copies)])
            )
    for copy in copies:
        copy.start()
    copies[0].wait()
    pick = jnp.minimum(window, lax.axis_size("seq") - 2)
    entry = lax.broadcasted_iota(jnp.int32, table_ref.shape, 0)
    row = lax.broadcasted_iota(jnp.int32, table_ref.shape, 1)
    here = (entry == pick) & (row == table_ref.shape[1] - 1)
    named = jnp.where(here, table_ref[...].astype(jnp.float32), -1.0)
    named = jnp.max(jnp.max(named, axis=1, keepdims=True), axis=0, keepdims=True)
    block = jnp.clip(named - (window * blocks).astype(jnp.float32), 0.0, blocks - 1.0)
    block_ref[...] = jnp.broadcast_to(block, block_ref.shape)
    block = jnp.broadcast_to(block, (part_tok, half))
    for copy in copies[1:]:
        copy.wait()
    for ref, out_ref in ((mine_ref, pair_ref), (theirs_ref, sent_ref)):
        for which in range(2):
            chosen = ref[which, 0].astype(jnp.float32)
            for b in range(1, blocks):
                chosen = jnp.where(block == b, ref[which, b].astype(jnp.float32), chosen)
            out_ref[which] = chosen.astype(out_ref.dtype)


def pick_pair(table, keys, values):
    blocks, part_tok, feat_width = keys.shape
    half = feat_width // CORES
    operands = [pltpu.with_memory_space_constraint(a, pltpu.HBM) for a in (table, keys, values)]
    return pl.pallas_call(
        pick_kernel,
        in_specs=[IN_HBM] * 3,
        out_specs=[WHOLE] * 5,
        out_shape=[pltpu.VMEM((2, blocks, part_tok, half), keys.dtype)] * 2
        + [pltpu.VMEM((2, part_tok, half), keys.dtype)] * 2
        + [pltpu.VMEM((8, 128), jnp.float32)],
        scratch_shapes=[pltpu.VMEM(table.shape, table.dtype), pltpu.SemaphoreType.DMA((5,))],
    )(*operands)


def join_kernel(att_ref, att_far, sent_ref, sent_far, kept_ref, att_out, gq_out, gk_out, gv_out, sems):
    core = lax.axis_index("kv") % CORES
    rows, half = att_ref.shape
    near = gk_out.shape[0]
    own, gk, gv = pl.ds(0, rows), pl.ds(rows, near), pl.ds(rows + near, near)
    copies = []
    for out_ref, sides in (
        (att_out, (att_ref, att_far)),
        (gq_out, (sent_ref.at[own], sent_far.at[own])),
        (gk_out, (kept_ref.at[pl.ds(0, near)], sent_far.at[gk])),
        (gv_out, (kept_ref.at[pl.ds(near, near)], sent_far.at[gv])),
    ):
        for side, ref in enumerate(sides):
            cols = pl.ds(pl.multiple_of((core ^ side) * half, half), half)
            copies.append(pltpu.make_async_copy(ref, out_ref.at[:, cols], sems.at[len(copies)]))
    for copy in copies:
        copy.start()
    for copy in copies:
        copy.wait()


def join(operands, shapes):
    return pl.pallas_call(
        join_kernel,
        in_specs=[WHOLE] * len(operands),
        out_specs=[IN_HBM] * len(shapes),
        out_shape=[pltpu.HBM(shape, jnp.bfloat16) for shape in shapes],
        scratch_shapes=[pltpu.SemaphoreType.DMA((2 * len(shapes),))],
        cost_estimate=SMALL,
    )(*operands)


def finish_kernel(block_ref, near_ref, near_far_ref, far_ref, *refs):
    arrived, outs, rows_ref, sems = refs[:-6], refs[-4:-2], refs[-2], refs[-1]
    core = lax.axis_index("kv") % CORES
    part_tok, half = far_ref.shape[1:]
    block = jnp.max(block_ref[...]).astype(jnp.int32)
    here = pl.ds(pl.multiple_of(block * part_tok, part_tok), part_tok)
    near = near_ref.shape[1]
    first = near_far_ref.shape[0] - 2 * near
    mine = pl.ds(pl.multiple_of(core * half, half), half)
    theirs = pl.ds(pl.multiple_of((core ^ 1) * half, half), half)
    copies = []
    for which, out_ref in enumerate(outs):
        total = near_ref[which, here]
        for ref in arrived:
            total += ref[0, which].astype(jnp.float32)
        rows_ref[which, :, mine] = total.astype(rows_ref.dtype)
        there = first + which * near + block * part_tok
        there = pl.ds(pl.multiple_of(there, part_tok), part_tok)
        total = near_far_ref[there, :].astype(jnp.float32) + far_ref[which].astype(jnp.float32)
        rows_ref[which, :, theirs] = total.astype(rows_ref.dtype)
        copies.append(pltpu.make_async_copy(rows_ref.at[which], out_ref.at[here], sems.at[which]))
        copies[-1].start()
    for copy in copies:
        copy.wait()


def finish(operands, outs):
    part_tok, half = operands[3].shape[1:]
    operands = [pltpu.with_memory_space_constraint(a, pltpu.VMEM) for a in operands]
    outs = [pltpu.with_memory_space_constraint(a, pltpu.HBM) for a in outs]
    return pl.pallas_call(
        finish_kernel,
        in_specs=[WHOLE] * len(operands) + [IN_HBM] * 2,
        out_specs=[IN_HBM] * 2,
        out_shape=[pltpu.HBM(a.shape, a.dtype) for a in outs],
        input_output_aliases={len(operands): 0, len(operands) + 1: 1},
        scratch_shapes=[
            pltpu.VMEM((2, part_tok, half * CORES), jnp.bfloat16),
            pltpu.SemaphoreType.DMA((2,)),
        ],
        cost_estimate=SMALL,
    )(*operands, *outs)


def near_tiles(rows, near):
    half = rows // 2
    return [(0, half, near // 2), (half, half, near)]


def fill_mask(members, near, blk_len, part_tok, bias_ref):
    member = lax.axis_index("kv")
    shift = part_tok.bit_length() - 1
    for start, count, used in near_tiles(bias_ref.shape[0], near):
        row = start + lax.broadcasted_iota(jnp.int32, (count, 1), 0)
        col = lax.broadcasted_iota(jnp.int32, (1, used), 1)
        key_tok = (col >> shift) * blk_len + (col & (part_tok - 1))
        for j in range(members):
            key_pos = key_tok + (member ^ j) * part_tok
            bias_ref[start : start + count, j * used : (j + 1) * used] = jnp.where(
                key_pos <= row, 0.0, HIDDEN
            )


def head_columns(head, head_dim):
    return pl.ds(pl.multiple_of(head * head_dim, head_dim), head_dim)


def near_rows(parts, which, used, cols):
    return jnp.concatenate([ref[which, :used, cols] for ref in parts], axis=0)


def near_forward_kernel(members, blk_len, part_tok, head_dim, q_hbm, g_hbm, *refs):
    parts, outs = refs[:members], refs[members:]
    out_ref, stat_ref, bias_ref, q_ref, g_ref, sems = outs
    rows, half = q_ref.shape
    near = parts[0].shape[1]
    slab = GROUP * head_dim
    core = lax.axis_index("kv") % CORES

    def fetch(group):
        there = pl.ds(pl.multiple_of(core * half + group * slab, slab), slab)
        here = pl.ds(pl.multiple_of(group * slab, slab), slab)
        return pltpu.make_async_copy(q_hbm.at[:, there], q_ref.at[:, here], sems.at[group])

    there = pl.ds(pl.multiple_of(core * half, half), half)
    last = pltpu.make_async_copy(g_hbm.at[:, there], g_ref, sems.at[half // slab])
    for group in range(half // slab):
        fetch(group).start()
    last.start()
    fill_mask(members, near, blk_len, part_tok, bias_ref)

    @pl.loop(0, half // slab)
    def _(group):
        fetch(group).wait()
        units = [
            (head_columns(group * GROUP + i, head_dim), pl.ds(start, count), used)
            for i in range(GROUP)
            for start, count, used in near_tiles(rows, near)
        ]
        raws = [
            dot(q_ref[here, cols], near_rows(parts, 0, used, cols), NT) * base2_scale(head_dim)
            + bias_ref[here, : members * used]
            for cols, here, used in units
        ]
        peaks = [jnp.max(raw, axis=1, keepdims=True) for raw in raws]
        weights = [jnp.exp2(raw - peak) for raw, peak in zip(raws, peaks)]
        totals = [jnp.sum(weight, axis=1, keepdims=True) for weight in weights]
        sums = [
            dot(weight.astype(jnp.bfloat16), near_rows(parts, 1, used, cols), NN)
            for weight, (cols, here, used) in zip(weights, units)
        ]
        for (cols, here, used), peak, total, summed in zip(units, peaks, totals, sums):
            level = peak + jnp.log2(total)
            stat_ref[here, cols] = jnp.broadcast_to(level, summed.shape)
            out_ref[here, cols] = summed * (1.0 / total)

    last.wait()


def far_rows(parts, which, cols):
    rows = []
    for pair_ref, column_ref in zip(parts[0::2], parts[1::2]):
        steps, cores, _, part_tok, _ = column_ref.shape
        rows.append(pair_ref[:, which, :, cols].reshape(cores * part_tok, cols.size))
        rows.append(column_ref[:, :, which, :, cols].reshape(steps * cores * part_tok, cols.size))
    return jnp.concatenate(rows, axis=0)


def far_kernel(groups, steps, head_dim, tile, heads, batch, q_ref, g_ref, sum_ref, stat_ref, *refs):
    parts = refs[: 2 * COLUMNS * groups]
    att_ref, gq_ref, level_ref, drift_ref, *grad_refs = refs[2 * COLUMNS * groups :]
    _, cores, _, part_tok, _ = grad_refs[0].shape
    rows, half = q_ref.shape
    span = steps * cores * part_tok
    width = COLUMNS * span
    score_scale = 1.0 / math.sqrt(head_dim)
    window = lax.axis_index("seq")
    level, side = window // COLUMNS, window % COLUMNS
    step = lax.broadcasted_iota(jnp.int32, (1, span), 1) >> ((cores * part_tok).bit_length() - 1)
    valid = [(step >= 1) & (step <= level), (step >= 1 - side) & (step <= level)]
    bias = jnp.concatenate([jnp.where(ok, 0.0, HIDDEN) for ok in valid] * groups, axis=1)
    total_width = groups * width

    def work(units, keys, values, key_grads, value_grads):
        raws = [
            dot(q_ref[here, cols], keys[i], NT) * base2_scale(head_dim) + bias
            for i, cols, here in units
        ]
        grad_probs = [dot(g_ref[here, cols], values[i], NT) for i, cols, here in units]
        near_levels = [stat_ref[here, cols] for i, cols, here in units]
        peaks = [
            jnp.maximum(near_level, jnp.max(raw, axis=1, keepdims=True))
            for near_level, raw in zip(near_levels, raws)
        ]
        near_weights = [jnp.exp2(near_level - peak) for near_level, peak in zip(near_levels, peaks)]
        weights = [jnp.exp2(raw - wide(peak, total_width)) for raw, peak in zip(raws, peaks)]
        totals = [
            near_weight + jnp.sum(weight, axis=1, keepdims=True)
            for near_weight, weight in zip(near_weights, weights)
        ]
        inverses = [1.0 / total for total in totals]
        sums = [
            dot(weight.astype(jnp.bfloat16), values[i], NN)
            for weight, (i, cols, here) in zip(weights, units)
        ]
        drifts = []
        for u, (i, cols, here) in enumerate(units):
            summed = sum_ref[here, cols] * near_weights[u] + sums[u]
            attended = (summed * inverses[u]).astype(jnp.bfloat16)
            att_ref[here, cols] = attended
            product = g_ref[here, cols].astype(jnp.float32) * attended.astype(jnp.float32)
            drift = jnp.broadcast_to(jnp.sum(product, axis=1, keepdims=True), product.shape)
            drifts.append(drift)
            level_ref[here, cols] = peaks[u] + jnp.log2(totals[u])
            drift_ref[here, cols] = drift
        moved = [
            weight * (grad_prob - wide(drift, total_width))
            for weight, grad_prob, drift in zip(weights, grad_probs, drifts)
        ]
        factors = [inverse * score_scale for inverse in inverses]
        own_scores = [
            (part[:, :width] * wide(factor, width)).astype(jnp.bfloat16)
            for part, factor in zip(moved, factors)
        ]
        own_probs = [
            (weight[:, :width] * wide(inverse, width)).astype(jnp.bfloat16)
            for weight, inverse in zip(weights, inverses)
        ]
        for u, (i, cols, here) in enumerate(units):
            gq_ref[here, cols] = dot(moved[u].astype(jnp.bfloat16), keys[i], NN) * factors[u]
        for u, (i, cols, here) in enumerate(units):
            key_grads[i].append(dot(own_scores[u], q_ref[here, cols], TN))
            value_grads[i].append(dot(own_probs[u], g_ref[here, cols], TN))

    @pl.loop(0, half // (heads * head_dim))
    def _(group):
        columns = [head_columns(group * heads + i, head_dim) for i in range(heads)]
        units = [
            (i, cols, pl.ds(r, tile)) for i, cols in enumerate(columns) for r in range(0, rows, tile)
        ]
        keys = [far_rows(parts, 0, cols) for cols in columns]
        values = [far_rows(parts, 1, cols) for cols in columns]
        grads = [[[] for _ in columns] for _ in range(2)]
        for first in range(0, len(units), batch):
            work(units[first : first + batch], keys, values, *grads)
        for which, per_head in enumerate(grads):
            for cols, terms in zip(columns, per_head):
                total = functools.reduce(lambda a, b: a + b, terms).astype(jnp.bfloat16)
                start = 0
                for ref in grad_refs:
                    shape = ref.shape[:2] + (part_tok, head_dim)
                    count = math.prod(shape[:3])
                    ref[:, :, which, :, cols] = total[start : start + count].reshape(shape)
                    start += count


def near_backward_kernel(members, head_dim, bias_ref, q_ref, g_ref, level_ref, drift_ref, far_gq_ref, *refs):
    parts, outs = refs[:members], refs[members:]
    own_ref, kept_ref, sent_ref = outs
    rows, half = q_ref.shape
    near = parts[0].shape[1]
    score_scale = 1.0 / math.sqrt(head_dim)

    @pl.loop(0, half // (GROUP * head_dim))
    def _(group):
        units = [
            (head_columns(group * GROUP + i, head_dim), pl.ds(start, count), used)
            for i in range(GROUP)
            for start, count, used in near_tiles(rows, near)
        ]
        keys = [near_rows(parts, 0, used, cols) for cols, here, used in units]
        values = [near_rows(parts, 1, used, cols) for cols, here, used in units]
        raws = [
            dot(q_ref[here, cols], key, NT) * base2_scale(head_dim)
            + bias_ref[here, : members * used]
            for (cols, here, used), key in zip(units, keys)
        ]
        grad_probs = [
            dot(g_ref[here, cols], value, NT) for (cols, here, used), value in zip(units, values)
        ]
        probs = [
            jnp.exp2(raw - wide(level_ref[here, cols], raw.shape[1]))
            for raw, (cols, here, used) in zip(raws, units)
        ]
        moved = [
            prob * (grad_prob - wide(drift_ref[here, cols], prob.shape[1]))
            for prob, grad_prob, (cols, here, used) in zip(probs, grad_probs, units)
        ]
        for (cols, here, used), part, key in zip(units, moved, keys):
            sent_ref[here, cols] = (
                dot(part.astype(jnp.bfloat16), key, NN) * score_scale + far_gq_ref[here, cols]
            ).astype(jnp.bfloat16)
        grads = []
        for (cols, here, used), part, prob in zip(units, moved, probs):
            own_score = (part[:, : CORES * used] * score_scale).astype(jnp.bfloat16)
            own_prob = prob[:, : CORES * used].astype(jnp.bfloat16)
            grads.append((dot(own_score, q_ref[here, cols], TN), dot(own_prob, g_ref[here, cols], TN)))
        low = near // 2
        for (cols, _, _), early, late in zip(units[0::2], grads[0::2], grads[1::2]):
            for which in range(2):
                for core in range(CORES):
                    top = late[which][core * near : core * near + low]
                    top += early[which][core * low : (core + 1) * low]
                    bottom = late[which][core * near + low : (core + 1) * near]
                    if core == 0:
                        own_ref[which, :low, cols] = top
                        own_ref[which, low:, cols] = bottom
                    ref, first = ((kept_ref, 0), (sent_ref, rows))[core]
                    first += which * near
                    ref[first : first + low, cols] = top.astype(ref.dtype)
                    ref[first + low : first + near, cols] = bottom.astype(ref.dtype)


def call(kernel, operands, outs, pairs, products, head_dim, in_specs=None, scratch=()):
    moved_bytes = sum(a.size * a.dtype.itemsize for a in operands)
    return pl.pallas_call(
        kernel,
        in_specs=in_specs or [WHOLE] * len(operands),
        out_specs=[WHOLE] * len(outs),
        out_shape=outs,
        scratch_shapes=scratch,
        compiler_params=LIMIT,
        cost_estimate=pl.CostEstimate(
            flops=4 * products * pairs * head_dim, bytes_accessed=moved_bytes, transcendentals=pairs
        ),
    )(*operands)


def shards(queries, keys, values, layout, grad_out):
    seq_count = lax.axis_size("seq")
    members = lax.axis_size("kv")
    tok_rows, feat_width = queries.shape
    blocks, part_tok = (keys.shape[0], keys.shape[1])
    blk_len = part_tok * members
    near = blocks * part_tok
    head_dim = feat_width // HEADS
    half = feat_width // CORES
    levels = seq_count // COLUMNS
    groups = members // CORES

    def hop(part, column_step, member_step):
        pairs = [
            (s * members + m, (s ^ column_step) * members + (m ^ member_step))
            for s in range(seq_count)
            for m in range(members)
        ]
        return lax.ppermute(part, ("seq", "kv"), pairs)

    def climb(part, d):
        return lax.ppermute(
            part, "seq", [(s, s + COLUMNS * d) for s in range(seq_count - COLUMNS * d)]
        )

    def sink(part, d):
        return lax.ppermute(
            part, "seq", [(s, s - COLUMNS * d) for s in range(COLUMNS * d, seq_count)]
        )

    mine, theirs, pair_mine, pair_theirs, block = pick_pair(layout.T, keys, values)
    own_pair = jnp.stack([pair_mine, hop(pair_theirs, 0, 1)])
    climbed = [climb(own_pair, d) for d in range(1, levels)]
    column = jnp.stack(climbed)
    chip_parts = [mine, hop(theirs, 0, 1)]
    near_parts = list(chip_parts)
    for group in range(1, groups):
        near_parts += [hop(part, 0, CORES * group) for part in chip_parts]
    sent_pair, _ = lax.optimization_barrier((own_pair, chip_parts[1]))
    cross_pairs = [hop(sent_pair, 1, CORES * group) for group in range(groups)]
    column, near_parts = lax.optimization_barrier((column, near_parts))
    near_parts = [part.reshape(2, near, half) for part in near_parts]
    crossing = [
        [column if (c, group) == (0, 0) else hop(column, c, CORES * group) for c in range(COLUMNS)]
        for group in range(groups)
    ]

    def rows_out(dtype):
        return pltpu.VMEM((tok_rows, half), dtype)

    def far_out(count):
        return pltpu.VMEM((count,) + own_pair.shape, jnp.bfloat16)

    low = (levels + 1) // 2
    near_pairs = HEADS // CORES * tok_rows * members * near
    far_width = members * seq_count * part_tok
    far_pairs = HEADS // CORES * tok_rows * far_width
    roomy = far_width <= 512
    far_plan = (tok_rows // 2, GROUP, 2 * GROUP) if roomy else (tok_rows // 8, 1, 1)

    near_sum, near_stat, bias, queries, grad_out = call(
        functools.partial(near_forward_kernel, members, blk_len, part_tok, head_dim),
        [pltpu.with_memory_space_constraint(a, pltpu.HBM) for a in (queries, grad_out)] + near_parts,
        [rows_out(jnp.float32)] * 2
        + [pltpu.VMEM((tok_rows, members * near), jnp.float32)]
        + [rows_out(jnp.bfloat16)] * 2,
        near_pairs,
        2,
        head_dim,
        [IN_HBM, IN_HBM] + [WHOLE] * members,
        [pltpu.SemaphoreType.DMA((half // (GROUP * head_dim) + 1,))],
    )
    far_parts = []
    for group, cross_pair in zip(crossing, cross_pairs):
        (same, other), _ = lax.optimization_barrier((group, near_stat))
        far_parts += [own_pair, same, cross_pair, other]
    attended, far_gq, level, drift, own_low, own_high, cross_low, cross_high = call(
        functools.partial(far_kernel, groups, levels, head_dim, *far_plan),
        [queries, grad_out, near_sum, near_stat] + far_parts,
        [rows_out(jnp.bfloat16)]
        + [rows_out(jnp.float32)] * 3
        + [far_out(low), far_out(levels - low)] * COLUMNS,
        far_pairs,
        5,
        head_dim,
    )

    def add(own, cross):
        return (own.astype(jnp.float32) + cross.astype(jnp.float32)).astype(jnp.bfloat16)

    high = hop(cross_high, 1, 0)
    near_own, near_kept, sent = call(
        functools.partial(near_backward_kernel, members, head_dim),
        [bias, queries, grad_out, level, drift, far_gq] + near_parts,
        [
            pltpu.VMEM((2, near, half), jnp.float32),
            pltpu.VMEM((2 * near, half), jnp.bfloat16),
            pltpu.VMEM((tok_rows + 2 * near, half), jnp.bfloat16),
        ],
        near_pairs,
        4,
        head_dim,
    )
    high, _ = lax.optimization_barrier((high, sent))
    sums = [add(own_high[d - low], high[d - low]) for d in range(low, levels)]
    cross_low, sent_mine, _ = lax.optimization_barrier((cross_low, sent, sums))
    crossed = hop(cross_low, 1, 0)
    sent_far = hop(sent_mine, 0, 1)
    att_far = hop(attended, 0, 1)
    sums = [add(own_low[d], crossed[d]) for d in range(1, low)] + sums
    returned = [sink(part, d) for d, part in enumerate(sums, 1)] + [crossed[0]]
    attended, grad_q, grad_k, grad_v = join(
        [attended, att_far, sent, sent_far, near_kept],
        [(tok_rows, feat_width)] * 2 + [(near, feat_width)] * 2,
    )
    returned, grad_k, grad_v = lax.optimization_barrier((returned, grad_k, grad_v))
    far_sent = sum(part[1].astype(jnp.float32) for part in returned).astype(jnp.bfloat16)
    grad_k, grad_v = finish(
        [block, near_own, sent_far, hop(far_sent, 0, 1)] + returned, [grad_k, grad_v]
    )
    return (attended, grad_q, grad_k.reshape(keys.shape), grad_v.reshape(values.shape))


def solution(mesh):
    return jax.shard_map(
        shards,
        mesh=mesh,
        in_specs=(P("seq", None), P("seq", "kv", None), P("seq", "kv", None), P(), P("seq", None)),
        out_specs=(P("seq", None), P("seq", None), P("seq", "kv", None), P("seq", "kv", None)),
        check_vma=False,
    )
```

```python
import functools
import math

import jax
import jax.numpy as jnp
from jax import lax
from jax.experimental import pallas as pl
from jax.experimental.pallas import tpu as pltpu
from jax.sharding import PartitionSpec as P

HEADS = 8
COLUMNS = 2
CORES = 2
GROUP = 2
SMALL = pl.CostEstimate(flops=0, bytes_accessed=0, transcendentals=0)
HIDDEN = -1e30
NT = (((1,), (1,)), ((), ()))
NN = (((1,), (0,)), ((), ()))
TN = (((0,), (0,)), ((), ()))
IN_HBM = pl.BlockSpec(memory_space=pltpu.HBM)
WHOLE = pl.BlockSpec(memory_space=pltpu.VMEM)
LIMIT = pltpu.CompilerParams(vmem_limit_bytes=12 * 1024 * 1024)


def dot(a, b, dims):
    return lax.dot_general(a, b, dims, preferred_element_type=jnp.float32)


def wide(rows, width):
    return jnp.concatenate([rows] * (width // rows.shape[1]), axis=1)


def base2_scale(head_dim):
    return math.log2(math.e) / math.sqrt(head_dim)


def pick_kernel(table_hbm, keys_hbm, values_hbm, mine_ref, theirs_ref, pair_ref, sent_ref, block_ref, table_ref, sems):
    window = lax.axis_index("seq")
    core = lax.axis_index("kv") % CORES
    _, blocks, part_tok, half = mine_ref.shape
    copies = [pltpu.make_async_copy(table_hbm, table_ref, sems.at[0])]
    for which, ref in enumerate((keys_hbm, values_hbm)):
        for side, out_ref in enumerate((mine_ref, theirs_ref)):
            cols = pl.ds(pl.multiple_of((core ^ side) * half, half), half)
            copies.append(
                pltpu.make_async_copy(ref.at[:, :, cols], out_ref.at[which], sems.at[len(copies)])
            )
    for copy in copies:
        copy.start()
    copies[0].wait()
    pick = jnp.minimum(window, lax.axis_size("seq") - 2)
    entry = lax.broadcasted_iota(jnp.int32, table_ref.shape, 0)
    row = lax.broadcasted_iota(jnp.int32, table_ref.shape, 1)
    here = (entry == pick) & (row == table_ref.shape[1] - 1)
    named = jnp.where(here, table_ref[...].astype(jnp.float32), -1.0)
    named = jnp.max(jnp.max(named, axis=1, keepdims=True), axis=0, keepdims=True)
    block = jnp.clip(named - (window * blocks).astype(jnp.float32), 0.0, blocks - 1.0)
    block_ref[...] = jnp.broadcast_to(block, block_ref.shape)
    block = jnp.broadcast_to(block, (part_tok, half))
    for copy in copies[1:]:
        copy.wait()
    for ref, out_ref in ((mine_ref, pair_ref), (theirs_ref, sent_ref)):
        for which in range(2):
            chosen = ref[which, 0].astype(jnp.float32)
            for b in range(1, blocks):
                chosen = jnp.where(block == b, ref[which, b].astype(jnp.float32), chosen)
            out_ref[which] = chosen.astype(out_ref.dtype)


def pick_pair(table, keys, values):
    blocks, part_tok, feat_width = keys.shape
    half = feat_width // CORES
    operands = [pltpu.with_memory_space_constraint(a, pltpu.HBM) for a in (table, keys, values)]
    return pl.pallas_call(
        pick_kernel,
        in_specs=[IN_HBM] * 3,
        out_specs=[WHOLE] * 5,
        out_shape=[pltpu.VMEM((2, blocks, part_tok, half), keys.dtype)] * 2
        + [pltpu.VMEM((2, part_tok, half), keys.dtype)] * 2
        + [pltpu.VMEM((8, 128), jnp.float32)],
        scratch_shapes=[pltpu.VMEM(table.shape, table.dtype), pltpu.SemaphoreType.DMA((5,))],
    )(*operands)


def join_kernel(att_ref, att_far, sent_ref, sent_far, kept_ref, att_out, gq_out, gk_out, gv_out, sems):
    core = lax.axis_index("kv") % CORES
    rows, half = att_ref.shape
    near = gk_out.shape[0]
    own, gk, gv = pl.ds(0, rows), pl.ds(rows, near), pl.ds(rows + near, near)
    copies = []
    for out_ref, sides in (
        (att_out, (att_ref, att_far)),
        (gq_out, (sent_ref.at[own], sent_far.at[own])),
        (gk_out, (kept_ref.at[pl.ds(0, near)], sent_far.at[gk])),
        (gv_out, (kept_ref.at[pl.ds(near, near)], sent_far.at[gv])),
    ):
        for side, ref in enumerate(sides):
            cols = pl.ds(pl.multiple_of((core ^ side) * half, half), half)
            copies.append(pltpu.make_async_copy(ref, out_ref.at[:, cols], sems.at[len(copies)]))
    for copy in copies:
        copy.start()
    for copy in copies:
        copy.wait()


def join(operands, shapes):
    operands = [pltpu.with_memory_space_constraint(a, pltpu.VMEM) for a in operands]
    return pl.pallas_call(
        join_kernel,
        in_specs=[WHOLE] * len(operands),
        out_specs=[IN_HBM] * len(shapes),
        out_shape=[pltpu.HBM(shape, jnp.bfloat16) for shape in shapes],
        scratch_shapes=[pltpu.SemaphoreType.DMA((2 * len(shapes),))],
        cost_estimate=SMALL,
    )(*operands)


def finish_kernel(block_ref, chosen_ref, far_ref, *refs):
    arrived, outs, rows_ref, sems = refs[:-6], refs[-4:-2], refs[-2], refs[-1]
    core = lax.axis_index("kv") % CORES
    part_tok, half = far_ref.shape[1:]
    block = jnp.max(block_ref[...]).astype(jnp.int32)
    here = pl.ds(pl.multiple_of(block * part_tok, part_tok), part_tok)
    mine = pl.ds(pl.multiple_of(core * half, half), half)
    theirs = pl.ds(pl.multiple_of((core ^ 1) * half, half), half)
    copies = []
    for which, out_ref in enumerate(outs):
        total = chosen_ref[0, which]
        for ref in arrived:
            total += ref[0, which].astype(jnp.float32)
        rows_ref[which, :, mine] = total.astype(rows_ref.dtype)
        rows_ref[which, :, theirs] = far_ref[which]
        copies.append(pltpu.make_async_copy(rows_ref.at[which], out_ref.at[here], sems.at[which]))
        copies[-1].start()
    for copy in copies:
        copy.wait()


def finish(operands, outs):
    part_tok, half = operands[2].shape[1:]
    operands = [pltpu.with_memory_space_constraint(a, pltpu.VMEM) for a in operands]
    outs = [pltpu.with_memory_space_constraint(a, pltpu.HBM) for a in outs]
    return pl.pallas_call(
        finish_kernel,
        in_specs=[WHOLE] * len(operands) + [IN_HBM] * 2,
        out_specs=[IN_HBM] * 2,
        out_shape=[pltpu.HBM(a.shape, a.dtype) for a in outs],
        input_output_aliases={len(operands): 0, len(operands) + 1: 1},
        scratch_shapes=[
            pltpu.VMEM((2, part_tok, half * CORES), jnp.bfloat16),
            pltpu.SemaphoreType.DMA((2,)),
        ],
        cost_estimate=SMALL,
    )(*operands, *outs)


def near_tiles(rows, near):
    half = rows // 2
    return [(0, half, near // 2), (half, half, near)]


def fill_mask(members, near, blk_len, part_tok, bias_ref):
    member = lax.axis_index("kv")
    shift = part_tok.bit_length() - 1
    for start, count, used in near_tiles(bias_ref.shape[0], near):
        row = start + lax.broadcasted_iota(jnp.int32, (count, 1), 0)
        col = lax.broadcasted_iota(jnp.int32, (1, used), 1)
        key_tok = (col >> shift) * blk_len + (col & (part_tok - 1))
        for j in range(members):
            key_pos = key_tok + (member ^ j) * part_tok
            bias_ref[start : start + count, j * used : (j + 1) * used] = jnp.where(
                key_pos <= row, 0.0, HIDDEN
            )


def head_columns(head, head_dim):
    return pl.ds(pl.multiple_of(head * head_dim, head_dim), head_dim)


def near_rows(parts, which, used, cols):
    return jnp.concatenate([ref[which, :used, cols] for ref in parts], axis=0)


def near_forward_kernel(members, blk_len, part_tok, head_dim, q_hbm, g_hbm, *refs):
    parts, outs = refs[:members], refs[members:]
    out_ref, stat_ref, bias_ref, q_ref, g_ref, sems = outs
    rows, half = q_ref.shape
    near = parts[0].shape[1]
    slab = GROUP * head_dim
    core = lax.axis_index("kv") % CORES

    def fetch(group):
        there = pl.ds(pl.multiple_of(core * half + group * slab, slab), slab)
        here = pl.ds(pl.multiple_of(group * slab, slab), slab)
        return pltpu.make_async_copy(q_hbm.at[:, there], q_ref.at[:, here], sems.at[group])

    there = pl.ds(pl.multiple_of(core * half, half), half)
    last = pltpu.make_async_copy(g_hbm.at[:, there], g_ref, sems.at[half // slab])
    for group in range(half // slab):
        fetch(group).start()
    last.start()
    fill_mask(members, near, blk_len, part_tok, bias_ref)

    @pl.loop(0, half // slab)
    def _(group):
        fetch(group).wait()
        units = [
            (head_columns(group * GROUP + i, head_dim), pl.ds(start, count), used)
            for i in range(GROUP)
            for start, count, used in near_tiles(rows, near)
        ]
        raws = [
            dot(q_ref[here, cols], near_rows(parts, 0, used, cols), NT) * base2_scale(head_dim)
            + bias_ref[here, : members * used]
            for cols, here, used in units
        ]
        peaks = [jnp.max(raw, axis=1, keepdims=True) for raw in raws]
        weights = [jnp.exp2(raw - peak) for raw, peak in zip(raws, peaks)]
        totals = [jnp.sum(weight, axis=1, keepdims=True) for weight in weights]
        sums = [
            dot(weight.astype(jnp.bfloat16), near_rows(parts, 1, used, cols), NN)
            for weight, (cols, here, used) in zip(weights, units)
        ]
        for (cols, here, used), peak, total, summed in zip(units, peaks, totals, sums):
            level = peak + jnp.log2(total)
            stat_ref[here, cols] = jnp.broadcast_to(level, summed.shape)
            out_ref[here, cols] = summed * (1.0 / total)

    last.wait()


def far_rows(parts, which, cols):
    rows = []
    for pair_ref, column_ref in zip(parts[0::2], parts[1::2]):
        steps, cores, _, part_tok, _ = column_ref.shape
        rows.append(pair_ref[:, which, :, cols].reshape(cores * part_tok, cols.size))
        rows.append(column_ref[:, :, which, :, cols].reshape(steps * cores * part_tok, cols.size))
    return jnp.concatenate(rows, axis=0)


def far_kernel(groups, steps, head_dim, tile, heads, batch, q_ref, g_ref, sum_ref, stat_ref, *refs):
    parts = refs[: 2 * COLUMNS * groups]
    att_ref, gq_ref, level_ref, drift_ref, *grad_refs = refs[2 * COLUMNS * groups :]
    _, cores, _, part_tok, _ = grad_refs[0].shape
    rows, half = q_ref.shape
    span = steps * cores * part_tok
    width = COLUMNS * span
    score_scale = 1.0 / math.sqrt(head_dim)
    window = lax.axis_index("seq")
    level, side = window // COLUMNS, window % COLUMNS
    step = lax.broadcasted_iota(jnp.int32, (1, span), 1) >> ((cores * part_tok).bit_length() - 1)
    valid = [(step >= 1) & (step <= level), (step >= 1 - side) & (step <= level)]
    bias = jnp.concatenate([jnp.where(ok, 0.0, HIDDEN) for ok in valid] * groups, axis=1)
    total_width = groups * width

    def work(units, keys, values, key_grads, value_grads):
        raws = [
            dot(q_ref[here, cols], keys[i], NT) * base2_scale(head_dim) + bias
            for i, cols, here in units
        ]
        grad_probs = [dot(g_ref[here, cols], values[i], NT) for i, cols, here in units]
        near_levels = [stat_ref[here, cols] for i, cols, here in units]
        peaks = [
            jnp.maximum(near_level, jnp.max(raw, axis=1, keepdims=True))
            for near_level, raw in zip(near_levels, raws)
        ]
        near_weights = [jnp.exp2(near_level - peak) for near_level, peak in zip(near_levels, peaks)]
        weights = [jnp.exp2(raw - wide(peak, total_width)) for raw, peak in zip(raws, peaks)]
        totals = [
            near_weight + jnp.sum(weight, axis=1, keepdims=True)
            for near_weight, weight in zip(near_weights, weights)
        ]
        inverses = [1.0 / total for total in totals]
        sums = [
            dot(weight.astype(jnp.bfloat16), values[i], NN)
            for weight, (i, cols, here) in zip(weights, units)
        ]
        drifts = []
        for u, (i, cols, here) in enumerate(units):
            summed = sum_ref[here, cols] * near_weights[u] + sums[u]
            attended = (summed * inverses[u]).astype(jnp.bfloat16)
            att_ref[here, cols] = attended
            product = g_ref[here, cols].astype(jnp.float32) * attended.astype(jnp.float32)
            drift = jnp.broadcast_to(jnp.sum(product, axis=1, keepdims=True), product.shape)
            drifts.append(drift)
            level_ref[here, cols] = peaks[u] + jnp.log2(totals[u])
            drift_ref[here, cols] = drift
        moved = [
            weight * (grad_prob - wide(drift, total_width))
            for weight, grad_prob, drift in zip(weights, grad_probs, drifts)
        ]
        factors = [inverse * score_scale for inverse in inverses]
        own_scores = [
            (part[:, :width] * wide(factor, width)).astype(jnp.bfloat16)
            for part, factor in zip(moved, factors)
        ]
        own_probs = [
            (weight[:, :width] * wide(inverse, width)).astype(jnp.bfloat16)
            for weight, inverse in zip(weights, inverses)
        ]
        for u, (i, cols, here) in enumerate(units):
            gq_ref[here, cols] = dot(moved[u].astype(jnp.bfloat16), keys[i], NN) * factors[u]
        for u, (i, cols, here) in enumerate(units):
            key_grads[i].append(dot(own_scores[u], q_ref[here, cols], TN))
            value_grads[i].append(dot(own_probs[u], g_ref[here, cols], TN))

    @pl.loop(0, half // (heads * head_dim))
    def _(group):
        columns = [head_columns(group * heads + i, head_dim) for i in range(heads)]
        units = [
            (i, cols, pl.ds(r, tile)) for i, cols in enumerate(columns) for r in range(0, rows, tile)
        ]
        keys = [far_rows(parts, 0, cols) for cols in columns]
        values = [far_rows(parts, 1, cols) for cols in columns]
        grads = [[[] for _ in columns] for _ in range(2)]
        for first in range(0, len(units), batch):
            work(units[first : first + batch], keys, values, *grads)
        for which, per_head in enumerate(grads):
            for cols, terms in zip(columns, per_head):
                total = functools.reduce(lambda a, b: a + b, terms).astype(jnp.bfloat16)
                start = 0
                for ref in grad_refs:
                    shape = ref.shape[:2] + (part_tok, head_dim)
                    count = math.prod(shape[:3])
                    ref[:, :, which, :, cols] = total[start : start + count].reshape(shape)
                    start += count


def near_backward_kernel(members, head_dim, blocks, block_ref, bias_ref, q_ref, g_ref, level_ref, drift_ref, far_gq_ref, *refs):
    parts, outs = refs[:members], refs[members:]
    chosen_ref, kept_ref, sent_ref, grad_ref = outs
    rows, half = q_ref.shape
    near = parts[0].shape[1]
    score_scale = 1.0 / math.sqrt(head_dim)

    @pl.loop(0, half // (GROUP * head_dim))
    def _(group):
        units = [
            (head_columns(group * GROUP + i, head_dim), pl.ds(start, count), used)
            for i in range(GROUP)
            for start, count, used in near_tiles(rows, near)
        ]
        keys = [near_rows(parts, 0, used, cols) for cols, here, used in units]
        values = [near_rows(parts, 1, used, cols) for cols, here, used in units]
        raws = [
            dot(q_ref[here, cols], key, NT) * base2_scale(head_dim)
            + bias_ref[here, : members * used]
            for (cols, here, used), key in zip(units, keys)
        ]
        grad_probs = [
            dot(g_ref[here, cols], value, NT) for (cols, here, used), value in zip(units, values)
        ]
        probs = [
            jnp.exp2(raw - wide(level_ref[here, cols], raw.shape[1]))
            for raw, (cols, here, used) in zip(raws, units)
        ]
        moved = [
            prob * (grad_prob - wide(drift_ref[here, cols], prob.shape[1]))
            for prob, grad_prob, (cols, here, used) in zip(probs, grad_probs, units)
        ]
        for (cols, here, used), part, key in zip(units, moved, keys):
            sent_ref[here, cols] = (
                dot(part.astype(jnp.bfloat16), key, NN) * score_scale + far_gq_ref[here, cols]
            ).astype(jnp.bfloat16)
        grads = []
        for (cols, here, used), part, prob in zip(units, moved, probs):
            own_score = (part[:, : CORES * used] * score_scale).astype(jnp.bfloat16)
            own_prob = prob[:, : CORES * used].astype(jnp.bfloat16)
            grads.append((dot(own_score, q_ref[here, cols], TN), dot(own_prob, g_ref[here, cols], TN)))
        low = near // 2
        for (cols, _, _), early, late in zip(units[0::2], grads[0::2], grads[1::2]):
            for which in range(2):
                for core in range(CORES):
                    top = late[which][core * near : core * near + low]
                    top += early[which][core * low : (core + 1) * low]
                    bottom = late[which][core * near + low : (core + 1) * near]
                    grad_ref[core, which, :low, cols] = top
                    grad_ref[core, which, low:, cols] = bottom
                    ref, first = ((kept_ref, 0), (sent_ref, rows))[core]
                    first += which * near
                    ref[first : first + low, cols] = top.astype(ref.dtype)
                    ref[first + low : first + near, cols] = bottom.astype(ref.dtype)

    part_tok = near // blocks
    block = jnp.max(jnp.max(block_ref[...], axis=1, keepdims=True), axis=0, keepdims=True)
    for core in range(CORES):
        for which in range(2):
            chosen = grad_ref[core, which, :part_tok]
            for b in range(1, blocks):
                rows_b = grad_ref[core, which, b * part_tok : (b + 1) * part_tok]
                chosen = jnp.where(block == b, rows_b, chosen)
            chosen_ref[core, which] = chosen


def call(kernel, operands, outs, pairs, products, head_dim, in_specs=None, scratch=()):
    moved_bytes = sum(a.size * a.dtype.itemsize for a in operands)
    return pl.pallas_call(
        kernel,
        in_specs=in_specs or [WHOLE] * len(operands),
        out_specs=[WHOLE] * len(outs),
        out_shape=outs,
        scratch_shapes=scratch,
        compiler_params=LIMIT,
        cost_estimate=pl.CostEstimate(
            flops=4 * products * pairs * head_dim, bytes_accessed=moved_bytes, transcendentals=pairs
        ),
    )(*operands)


def shards(queries, keys, values, layout, grad_out):
    seq_count = lax.axis_size("seq")
    members = lax.axis_size("kv")
    tok_rows, feat_width = queries.shape
    blocks, part_tok = (keys.shape[0], keys.shape[1])
    blk_len = part_tok * members
    near = blocks * part_tok
    head_dim = feat_width // HEADS
    half = feat_width // CORES
    levels = seq_count // COLUMNS
    groups = members // CORES

    def hop(part, column_step, member_step):
        pairs = [
            (s * members + m, (s ^ column_step) * members + (m ^ member_step))
            for s in range(seq_count)
            for m in range(members)
        ]
        return lax.ppermute(part, ("seq", "kv"), pairs)

    def climb(part, d):
        return lax.ppermute(
            part, "seq", [(s, s + COLUMNS * d) for s in range(seq_count - COLUMNS * d)]
        )

    def sink(part, d):
        return lax.ppermute(
            part, "seq", [(s, s - COLUMNS * d) for s in range(COLUMNS * d, seq_count)]
        )

    mine, theirs, pair_mine, pair_theirs, block = pick_pair(layout.T, keys, values)
    own_pair = jnp.stack([pair_mine, hop(pair_theirs, 0, 1)])
    climbed = [climb(own_pair, d) for d in range(1, levels)]
    column = jnp.stack(climbed)
    chip_parts = [mine, hop(theirs, 0, 1)]
    near_parts = list(chip_parts)
    for group in range(1, groups):
        near_parts += [hop(part, 0, CORES * group) for part in chip_parts]
    sent_pair, _ = lax.optimization_barrier((own_pair, chip_parts[1]))
    cross_pairs = [hop(sent_pair, 1, CORES * group) for group in range(groups)]
    column, near_parts = lax.optimization_barrier((column, near_parts))
    near_parts = [part.reshape(2, near, half) for part in near_parts]
    crossing = [
        [column if (c, group) == (0, 0) else hop(column, c, CORES * group) for c in range(COLUMNS)]
        for group in range(groups)
    ]

    def rows_out(dtype):
        return pltpu.VMEM((tok_rows, half), dtype)

    def far_out(count):
        return pltpu.VMEM((count,) + own_pair.shape, jnp.bfloat16)

    low = (levels + 1) // 2
    near_pairs = HEADS // CORES * tok_rows * members * near
    far_width = members * seq_count * part_tok
    far_pairs = HEADS // CORES * tok_rows * far_width
    roomy = far_width <= 512
    far_plan = (tok_rows // 2, GROUP, 2 * GROUP) if roomy else (tok_rows // 8, 1, 1)

    near_sum, near_stat, bias, queries, grad_out = call(
        functools.partial(near_forward_kernel, members, blk_len, part_tok, head_dim),
        [pltpu.with_memory_space_constraint(a, pltpu.HBM) for a in (queries, grad_out)] + near_parts,
        [rows_out(jnp.float32)] * 2
        + [pltpu.VMEM((tok_rows, members * near), jnp.float32)]
        + [rows_out(jnp.bfloat16)] * 2,
        near_pairs,
        2,
        head_dim,
        [IN_HBM, IN_HBM] + [WHOLE] * members,
        [pltpu.SemaphoreType.DMA((half // (GROUP * head_dim) + 1,))],
    )
    far_parts = []
    for group, cross_pair in zip(crossing, cross_pairs):
        (same, other), _ = lax.optimization_barrier((group, near_stat))
        far_parts += [own_pair, same, cross_pair, other]
    attended, far_gq, level, drift, own_low, own_high, cross_low, cross_high = call(
        functools.partial(far_kernel, groups, levels, head_dim, *far_plan),
        [queries, grad_out, near_sum, near_stat] + far_parts,
        [rows_out(jnp.bfloat16)]
        + [rows_out(jnp.float32)] * 3
        + [far_out(low), far_out(levels - low)] * COLUMNS,
        far_pairs,
        5,
        head_dim,
    )

    def add(own, cross):
        return (own.astype(jnp.float32) + cross.astype(jnp.float32)).astype(jnp.bfloat16)

    high = hop(cross_high, 1, 0)
    chosen, near_kept, sent = call(
        functools.partial(near_backward_kernel, members, head_dim, blocks),
        [block, bias, queries, grad_out, level, drift, far_gq] + near_parts,
        [
            pltpu.VMEM((CORES, 2, part_tok, half), jnp.float32),
            pltpu.VMEM((2 * near, half), jnp.bfloat16),
            pltpu.VMEM((tok_rows + 2 * near, half), jnp.bfloat16),
        ],
        near_pairs,
        4,
        head_dim,
        scratch=[pltpu.VMEM((CORES, 2, near, half), jnp.float32)],
    )
    high, _ = lax.optimization_barrier((high, sent))
    sums = [add(own_high[d - low], high[d - low]) for d in range(low, levels)]
    cross_low, sent_mine, _ = lax.optimization_barrier((cross_low, sent, sums))
    crossed = hop(cross_low, 1, 0)
    sent_far = hop(sent_mine, 0, 1)
    att_far = hop(attended, 0, 1)
    sums = [add(own_low[d], crossed[d]) for d in range(1, low)] + sums
    returned = [sink(part, d) for d, part in enumerate(sums, 1)] + [crossed[0]]
    attended, grad_q, grad_k, grad_v = join(
        [attended, att_far, sent, sent_far, near_kept],
        [(tok_rows, feat_width)] * 2 + [(near, feat_width)] * 2,
    )
    returned, grad_k, grad_v = lax.optimization_barrier((returned, grad_k, grad_v))
    far_sent = chosen[1] + sum(part[1].astype(jnp.float32) for part in returned)
    far_sent = far_sent.astype(jnp.bfloat16)
    grad_k, grad_v = finish(
        [block, chosen, hop(far_sent, 0, 1)] + returned, [grad_k, grad_v]
    )
    return (attended, grad_q, grad_k.reshape(keys.shape), grad_v.reshape(values.shape))


def solution(mesh):
    return jax.shard_map(
        shards,
        mesh=mesh,
        in_specs=(P("seq", None), P("seq", "kv", None), P("seq", "kv", None), P(), P("seq", None)),
        out_specs=(P("seq", None), P("seq", None), P("seq", "kv", None), P("seq", "kv", None)),
        check_vma=False,
    )
```

```python
import functools
import math

import jax
import jax.numpy as jnp
from jax import lax
from jax.experimental import pallas as pl
from jax.experimental.pallas import tpu as pltpu
from jax.sharding import PartitionSpec as P

HEADS = 8
COLUMNS = 2
CORES = 2
GROUP = 2
SMALL = pl.CostEstimate(flops=0, bytes_accessed=0, transcendentals=0)
HIDDEN = -1e30
NT = (((1,), (1,)), ((), ()))
NN = (((1,), (0,)), ((), ()))
TN = (((0,), (0,)), ((), ()))
IN_HBM = pl.BlockSpec(memory_space=pltpu.HBM)
WHOLE = pl.BlockSpec(memory_space=pltpu.VMEM)
LIMIT = pltpu.CompilerParams(vmem_limit_bytes=12 * 1024 * 1024)


def dot(a, b, dims):
    return lax.dot_general(a, b, dims, preferred_element_type=jnp.float32)


def wide(rows, width):
    return jnp.concatenate([rows] * (width // rows.shape[1]), axis=1)


def base2_scale(head_dim):
    return math.log2(math.e) / math.sqrt(head_dim)


def pick_kernel(table_hbm, keys_hbm, values_hbm, mine_ref, theirs_ref, pair_ref, sent_ref, block_ref, table_ref, sems):
    window = lax.axis_index("seq")
    core = lax.axis_index("kv") % CORES
    _, blocks, part_tok, half = mine_ref.shape
    copies = [pltpu.make_async_copy(table_hbm, table_ref, sems.at[0])]
    for which, ref in enumerate((keys_hbm, values_hbm)):
        for side, out_ref in enumerate((mine_ref, theirs_ref)):
            cols = pl.ds(pl.multiple_of((core ^ side) * half, half), half)
            copies.append(
                pltpu.make_async_copy(ref.at[:, :, cols], out_ref.at[which], sems.at[len(copies)])
            )
    for copy in copies:
        copy.start()
    copies[0].wait()
    pick = jnp.minimum(window, lax.axis_size("seq") - 2)
    entry = lax.broadcasted_iota(jnp.int32, table_ref.shape, 0)
    row = lax.broadcasted_iota(jnp.int32, table_ref.shape, 1)
    here = (entry == pick) & (row == table_ref.shape[1] - 1)
    named = jnp.where(here, table_ref[...].astype(jnp.float32), -1.0)
    named = jnp.max(jnp.max(named, axis=1, keepdims=True), axis=0, keepdims=True)
    block = jnp.clip(named - (window * blocks).astype(jnp.float32), 0.0, blocks - 1.0)
    block_ref[...] = jnp.broadcast_to(block, block_ref.shape)
    block = jnp.broadcast_to(block, (part_tok, half))
    for copy in copies[1:]:
        copy.wait()
    for ref, out_ref in ((mine_ref, pair_ref), (theirs_ref, sent_ref)):
        for which in range(2):
            chosen = ref[which, 0].astype(jnp.float32)
            for b in range(1, blocks):
                chosen = jnp.where(block == b, ref[which, b].astype(jnp.float32), chosen)
            out_ref[which] = chosen.astype(out_ref.dtype)


def pick_pair(table, keys, values):
    blocks, part_tok, feat_width = keys.shape
    half = feat_width // CORES
    operands = [pltpu.with_memory_space_constraint(a, pltpu.HBM) for a in (table, keys, values)]
    return pl.pallas_call(
        pick_kernel,
        in_specs=[IN_HBM] * 3,
        out_specs=[WHOLE] * 5,
        out_shape=[pltpu.VMEM((2, blocks, part_tok, half), keys.dtype)] * 2
        + [pltpu.VMEM((2, part_tok, half), keys.dtype)] * 2
        + [pltpu.VMEM((8, 128), jnp.float32)],
        scratch_shapes=[pltpu.VMEM(table.shape, table.dtype), pltpu.SemaphoreType.DMA((5,))],
    )(*operands)


def join_kernel(att_ref, att_far, sent_ref, sent_far, kept_ref, att_out, gq_out, gk_out, gv_out, sems):
    core = lax.axis_index("kv") % CORES
    rows, half = att_ref.shape
    near = gk_out.shape[0]
    own, gk, gv = pl.ds(0, rows), pl.ds(rows, near), pl.ds(rows + near, near)
    copies = []
    for out_ref, sides in (
        (att_out, (att_ref, att_far)),
        (gq_out, (sent_ref.at[own], sent_far.at[own])),
        (gk_out, (kept_ref.at[pl.ds(0, near)], sent_far.at[gk])),
        (gv_out, (kept_ref.at[pl.ds(near, near)], sent_far.at[gv])),
    ):
        for side, ref in enumerate(sides):
            cols = pl.ds(pl.multiple_of((core ^ side) * half, half), half)
            copies.append(pltpu.make_async_copy(ref, out_ref.at[:, cols], sems.at[len(copies)]))
    for copy in copies:
        copy.start()
    for copy in copies:
        copy.wait()


def join(operands, shapes):
    operands = [pltpu.with_memory_space_constraint(a, pltpu.VMEM) for a in operands]
    return pl.pallas_call(
        join_kernel,
        in_specs=[WHOLE] * len(operands),
        out_specs=[IN_HBM] * len(shapes),
        out_shape=[pltpu.HBM(shape, jnp.bfloat16) for shape in shapes],
        scratch_shapes=[pltpu.SemaphoreType.DMA((2 * len(shapes),))],
        cost_estimate=SMALL,
    )(*operands)


def finish_kernel(block_ref, chosen_ref, far_ref, *refs):
    arrived, outs, rows_ref, sems = refs[:-6], refs[-4:-2], refs[-2], refs[-1]
    core = lax.axis_index("kv") % CORES
    part_tok, half = far_ref.shape[1:]
    block = jnp.max(block_ref[...]).astype(jnp.int32)
    here = pl.ds(pl.multiple_of(block * part_tok, part_tok), part_tok)
    mine = pl.ds(pl.multiple_of(core * half, half), half)
    theirs = pl.ds(pl.multiple_of((core ^ 1) * half, half), half)
    copies = []
    for which, out_ref in enumerate(outs):
        total = chosen_ref[0, which]
        for ref in arrived:
            total += ref[0, which].astype(jnp.float32)
        rows_ref[which, :, mine] = total.astype(rows_ref.dtype)
        rows_ref[which, :, theirs] = far_ref[which]
        copies.append(pltpu.make_async_copy(rows_ref.at[which], out_ref.at[here], sems.at[which]))
        copies[-1].start()
    for copy in copies:
        copy.wait()


def finish(operands, outs):
    part_tok, half = operands[2].shape[1:]
    operands = [pltpu.with_memory_space_constraint(a, pltpu.VMEM) for a in operands]
    outs = [pltpu.with_memory_space_constraint(a, pltpu.HBM) for a in outs]
    return pl.pallas_call(
        finish_kernel,
        in_specs=[WHOLE] * len(operands) + [IN_HBM] * 2,
        out_specs=[IN_HBM] * 2,
        out_shape=[pltpu.HBM(a.shape, a.dtype) for a in outs],
        input_output_aliases={len(operands): 0, len(operands) + 1: 1},
        scratch_shapes=[
            pltpu.VMEM((2, part_tok, half * CORES), jnp.bfloat16),
            pltpu.SemaphoreType.DMA((2,)),
        ],
        cost_estimate=SMALL,
    )(*operands, *outs)


def near_tiles(rows, near):
    half = rows // 2
    return [(0, half, near // 2), (half, half, near)]


def fill_mask(members, near, blk_len, part_tok, bias_ref):
    member = lax.axis_index("kv")
    shift = part_tok.bit_length() - 1
    for start, count, used in near_tiles(bias_ref.shape[0], near):
        row = start + lax.broadcasted_iota(jnp.int32, (count, 1), 0)
        col = lax.broadcasted_iota(jnp.int32, (1, used), 1)
        key_tok = (col >> shift) * blk_len + (col & (part_tok - 1))
        for j in range(members):
            key_pos = key_tok + (member ^ j) * part_tok
            bias_ref[start : start + count, j * used : (j + 1) * used] = jnp.where(
                key_pos <= row, 0.0, HIDDEN
            )


def head_columns(head, head_dim):
    return pl.ds(pl.multiple_of(head * head_dim, head_dim), head_dim)


def near_rows(parts, which, used, cols):
    return jnp.concatenate([ref[which, :used, cols] for ref in parts], axis=0)


def near_forward_kernel(members, blk_len, part_tok, head_dim, q_hbm, g_hbm, *refs):
    parts, outs = refs[:members], refs[members:]
    out_ref, stat_ref, bias_ref, q_ref, g_ref, sems = outs
    rows, half = q_ref.shape
    near = parts[0].shape[1]
    slab = GROUP * head_dim
    core = lax.axis_index("kv") % CORES

    def fetch(group):
        there = pl.ds(pl.multiple_of(core * half + group * slab, slab), slab)
        here = pl.ds(pl.multiple_of(group * slab, slab), slab)
        return pltpu.make_async_copy(q_hbm.at[:, there], q_ref.at[:, here], sems.at[group])

    there = pl.ds(pl.multiple_of(core * half, half), half)
    last = pltpu.make_async_copy(g_hbm.at[:, there], g_ref, sems.at[half // slab])
    for group in range(half // slab):
        fetch(group).start()
    last.start()
    fill_mask(members, near, blk_len, part_tok, bias_ref)

    @pl.loop(0, half // slab)
    def _(group):
        fetch(group).wait()
        units = [
            (head_columns(group * GROUP + i, head_dim), pl.ds(start, count), used)
            for i in range(GROUP)
            for start, count, used in near_tiles(rows, near)
        ]
        raws = [
            dot(q_ref[here, cols], near_rows(parts, 0, used, cols), NT) * base2_scale(head_dim)
            + bias_ref[here, : members * used]
            for cols, here, used in units
        ]
        peaks = [jnp.max(raw, axis=1, keepdims=True) for raw in raws]
        weights = [jnp.exp2(raw - peak) for raw, peak in zip(raws, peaks)]
        totals = [jnp.sum(weight, axis=1, keepdims=True) for weight in weights]
        sums = [
            dot(weight.astype(jnp.bfloat16), near_rows(parts, 1, used, cols), NN)
            for weight, (cols, here, used) in zip(weights, units)
        ]
        for (cols, here, used), peak, total, summed in zip(units, peaks, totals, sums):
            level = peak + jnp.log2(total)
            stat_ref[here, cols] = jnp.broadcast_to(level, summed.shape)
            out_ref[here, cols] = summed * (1.0 / total)

    last.wait()


def far_rows(parts, which, cols):
    rows = []
    for pair_ref, column_ref in zip(parts[0::2], parts[1::2]):
        steps, cores, _, part_tok, _ = column_ref.shape
        rows.append(pair_ref[:, which, :, cols].reshape(cores * part_tok, cols.size))
        rows.append(column_ref[:, :, which, :, cols].reshape(steps * cores * part_tok, cols.size))
    return jnp.concatenate(rows, axis=0)


def far_kernel(groups, steps, head_dim, tile, heads, batch, q_ref, g_ref, sum_ref, stat_ref, *refs):
    parts = refs[: 2 * COLUMNS * groups]
    att_ref, gq_ref, level_ref, drift_ref, *grad_refs = refs[2 * COLUMNS * groups :]
    _, cores, _, part_tok, _ = grad_refs[0].shape
    rows, half = q_ref.shape
    span = steps * cores * part_tok
    width = COLUMNS * span
    score_scale = 1.0 / math.sqrt(head_dim)
    window = lax.axis_index("seq")
    level, side = window // COLUMNS, window % COLUMNS
    step = lax.broadcasted_iota(jnp.int32, (1, span), 1) >> ((cores * part_tok).bit_length() - 1)
    valid = [(step >= 1) & (step <= level), (step >= 1 - side) & (step <= level)]
    bias = jnp.concatenate([jnp.where(ok, 0.0, HIDDEN) for ok in valid] * groups, axis=1)
    total_width = groups * width

    def work(units, keys, values, key_grads, value_grads):
        raws = [
            dot(q_ref[here, cols], keys[i], NT) * base2_scale(head_dim) + bias
            for i, cols, here in units
        ]
        grad_probs = [dot(g_ref[here, cols], values[i], NT) for i, cols, here in units]
        near_levels = [stat_ref[here, cols] for i, cols, here in units]
        peaks = [
            jnp.maximum(near_level, jnp.max(raw, axis=1, keepdims=True))
            for near_level, raw in zip(near_levels, raws)
        ]
        near_weights = [jnp.exp2(near_level - peak) for near_level, peak in zip(near_levels, peaks)]
        weights = [jnp.exp2(raw - wide(peak, total_width)) for raw, peak in zip(raws, peaks)]
        totals = [
            near_weight + jnp.sum(weight, axis=1, keepdims=True)
            for near_weight, weight in zip(near_weights, weights)
        ]
        inverses = [1.0 / total for total in totals]
        sums = [
            dot(weight.astype(jnp.bfloat16), values[i], NN)
            for weight, (i, cols, here) in zip(weights, units)
        ]
        drifts = []
        for u, (i, cols, here) in enumerate(units):
            summed = sum_ref[here, cols] * near_weights[u] + sums[u]
            attended = (summed * inverses[u]).astype(jnp.bfloat16)
            att_ref[here, cols] = attended
            product = g_ref[here, cols].astype(jnp.float32) * attended.astype(jnp.float32)
            drift = jnp.broadcast_to(jnp.sum(product, axis=1, keepdims=True), product.shape)
            drifts.append(drift)
            level_ref[here, cols] = peaks[u] + jnp.log2(totals[u])
            drift_ref[here, cols] = drift
        moved = [
            weight * (grad_prob - wide(drift, total_width))
            for weight, grad_prob, drift in zip(weights, grad_probs, drifts)
        ]
        factors = [inverse * score_scale for inverse in inverses]
        own_scores = [
            (part[:, :width] * wide(factor, width)).astype(jnp.bfloat16)
            for part, factor in zip(moved, factors)
        ]
        own_probs = [
            (weight[:, :width] * wide(inverse, width)).astype(jnp.bfloat16)
            for weight, inverse in zip(weights, inverses)
        ]
        for u, (i, cols, here) in enumerate(units):
            gq_ref[here, cols] = dot(moved[u].astype(jnp.bfloat16), keys[i], NN) * factors[u]
        for u, (i, cols, here) in enumerate(units):
            key_grads[i].append(dot(own_scores[u], q_ref[here, cols], TN))
            value_grads[i].append(dot(own_probs[u], g_ref[here, cols], TN))

    @pl.loop(0, half // (heads * head_dim))
    def _(group):
        columns = [head_columns(group * heads + i, head_dim) for i in range(heads)]
        units = [
            (i, cols, pl.ds(r, tile)) for i, cols in enumerate(columns) for r in range(0, rows, tile)
        ]
        keys = [far_rows(parts, 0, cols) for cols in columns]
        values = [far_rows(parts, 1, cols) for cols in columns]
        grads = [[[] for _ in columns] for _ in range(2)]
        for first in range(0, len(units), batch):
            work(units[first : first + batch], keys, values, *grads)
        for which, per_head in enumerate(grads):
            for cols, terms in zip(columns, per_head):
                total = functools.reduce(lambda a, b: a + b, terms).astype(jnp.bfloat16)
                start = 0
                for ref in grad_refs:
                    shape = ref.shape[:2] + (part_tok, head_dim)
                    count = math.prod(shape[:3])
                    ref[:, :, which, :, cols] = total[start : start + count].reshape(shape)
                    start += count


def near_backward_kernel(members, head_dim, blocks, block_ref, bias_ref, q_ref, g_ref, level_ref, drift_ref, far_gq_ref, *refs):
    parts, outs = refs[:members], refs[members:]
    chosen_ref, kept_ref, sent_ref, grad_ref = outs
    rows, half = q_ref.shape
    near = parts[0].shape[1]
    score_scale = 1.0 / math.sqrt(head_dim)

    @pl.loop(0, half // (GROUP * head_dim))
    def _(group):
        units = [
            (head_columns(group * GROUP + i, head_dim), pl.ds(start, count), used)
            for i in range(GROUP)
            for start, count, used in near_tiles(rows, near)
        ]
        keys = [near_rows(parts, 0, used, cols) for cols, here, used in units]
        values = [near_rows(parts, 1, used, cols) for cols, here, used in units]
        raws = [
            dot(q_ref[here, cols], key, NT) * base2_scale(head_dim)
            + bias_ref[here, : members * used]
            for (cols, here, used), key in zip(units, keys)
        ]
        grad_probs = [
            dot(g_ref[here, cols], value, NT) for (cols, here, used), value in zip(units, values)
        ]
        probs = [
            jnp.exp2(raw - wide(level_ref[here, cols], raw.shape[1]))
            for raw, (cols, here, used) in zip(raws, units)
        ]
        moved = [
            prob * (grad_prob - wide(drift_ref[here, cols], prob.shape[1]))
            for prob, grad_prob, (cols, here, used) in zip(probs, grad_probs, units)
        ]
        for (cols, here, used), part, key in zip(units, moved, keys):
            sent_ref[here, cols] = (
                dot(part.astype(jnp.bfloat16), key, NN) * score_scale + far_gq_ref[here, cols]
            ).astype(jnp.bfloat16)
        grads = []
        for (cols, here, used), part, prob in zip(units, moved, probs):
            own_score = (part[:, : CORES * used] * score_scale).astype(jnp.bfloat16)
            own_prob = prob[:, : CORES * used].astype(jnp.bfloat16)
            grads.append((dot(own_score, q_ref[here, cols], TN), dot(own_prob, g_ref[here, cols], TN)))
        low = near // 2
        for (cols, _, _), early, late in zip(units[0::2], grads[0::2], grads[1::2]):
            for which in range(2):
                for core in range(CORES):
                    top = late[which][core * near : core * near + low]
                    top += early[which][core * low : (core + 1) * low]
                    bottom = late[which][core * near + low : (core + 1) * near]
                    grad_ref[core, which, :low, cols] = top
                    grad_ref[core, which, low:, cols] = bottom
                    ref, first = ((kept_ref, 0), (sent_ref, rows))[core]
                    first += which * near
                    ref[first : first + low, cols] = top.astype(ref.dtype)
                    ref[first + low : first + near, cols] = bottom.astype(ref.dtype)

    part_tok = near // blocks
    block = jnp.max(jnp.max(block_ref[...], axis=1, keepdims=True), axis=0, keepdims=True)
    for core in range(CORES):
        for which in range(2):
            chosen = grad_ref[core, which, :part_tok]
            for b in range(1, blocks):
                rows_b = grad_ref[core, which, b * part_tok : (b + 1) * part_tok]
                chosen = jnp.where(block == b, rows_b, chosen)
            chosen_ref[core, which] = chosen


def call(kernel, operands, outs, pairs, products, head_dim, in_specs=None, scratch=()):
    moved_bytes = sum(a.size * a.dtype.itemsize for a in operands)
    return pl.pallas_call(
        kernel,
        in_specs=in_specs or [WHOLE] * len(operands),
        out_specs=[WHOLE] * len(outs),
        out_shape=outs,
        scratch_shapes=scratch,
        compiler_params=LIMIT,
        cost_estimate=pl.CostEstimate(
            flops=4 * products * pairs * head_dim, bytes_accessed=moved_bytes, transcendentals=pairs
        ),
    )(*operands)


def shards(queries, keys, values, layout, grad_out):
    seq_count = lax.axis_size("seq")
    members = lax.axis_size("kv")
    tok_rows, feat_width = queries.shape
    blocks, part_tok = (keys.shape[0], keys.shape[1])
    blk_len = part_tok * members
    near = blocks * part_tok
    head_dim = feat_width // HEADS
    half = feat_width // CORES
    levels = seq_count // COLUMNS
    groups = members // CORES

    def hop(part, column_step, member_step):
        pairs = [
            (s * members + m, (s ^ column_step) * members + (m ^ member_step))
            for s in range(seq_count)
            for m in range(members)
        ]
        return lax.ppermute(part, ("seq", "kv"), pairs)

    def climb(part, d):
        return lax.ppermute(
            part, "seq", [(s, s + COLUMNS * d) for s in range(seq_count - COLUMNS * d)]
        )

    def sink(part, d):
        return lax.ppermute(
            part, "seq", [(s, s - COLUMNS * d) for s in range(COLUMNS * d, seq_count)]
        )

    mine, theirs, pair_mine, pair_theirs, block = pick_pair(layout.T, keys, values)
    own_pair = jnp.stack([pair_mine, hop(pair_theirs, 0, 1)])
    climbed = [climb(own_pair, d) for d in range(1, levels)]
    column = jnp.stack(climbed)
    chip_parts = [mine, hop(theirs, 0, 1)]
    near_parts = list(chip_parts)
    for group in range(1, groups):
        near_parts += [hop(part, 0, CORES * group) for part in chip_parts]
    sent_pair, _ = lax.optimization_barrier((own_pair, chip_parts[1]))
    cross_pairs = [hop(sent_pair, 1, CORES * group) for group in range(groups)]
    column, near_parts = lax.optimization_barrier((column, near_parts))
    near_parts = [part.reshape(2, near, half) for part in near_parts]
    crossing = [
        [column if (c, group) == (0, 0) else hop(column, c, CORES * group) for c in range(COLUMNS)]
        for group in range(groups)
    ]

    def rows_out(dtype):
        return pltpu.VMEM((tok_rows, half), dtype)

    def far_out(count):
        return pltpu.VMEM((count,) + own_pair.shape, jnp.bfloat16)

    low = 1
    near_pairs = HEADS // CORES * tok_rows * members * near
    far_width = members * seq_count * part_tok
    far_pairs = HEADS // CORES * tok_rows * far_width
    roomy = far_width <= 512
    far_plan = (tok_rows // 2, GROUP, 2 * GROUP) if roomy else (tok_rows // 8, 1, 1)

    near_sum, near_stat, bias, queries, grad_out = call(
        functools.partial(near_forward_kernel, members, blk_len, part_tok, head_dim),
        [pltpu.with_memory_space_constraint(a, pltpu.HBM) for a in (queries, grad_out)] + near_parts,
        [rows_out(jnp.float32)] * 2
        + [pltpu.VMEM((tok_rows, members * near), jnp.float32)]
        + [rows_out(jnp.bfloat16)] * 2,
        near_pairs,
        2,
        head_dim,
        [IN_HBM, IN_HBM] + [WHOLE] * members,
        [pltpu.SemaphoreType.DMA((half // (GROUP * head_dim) + 1,))],
    )
    far_parts = []
    for group, cross_pair in zip(crossing, cross_pairs):
        (same, other), _ = lax.optimization_barrier((group, near_stat))
        far_parts += [own_pair, same, cross_pair, other]
    attended, far_gq, level, drift, own_low, own_high, cross_low, cross_high = call(
        functools.partial(far_kernel, groups, levels, head_dim, *far_plan),
        [queries, grad_out, near_sum, near_stat] + far_parts,
        [rows_out(jnp.bfloat16)]
        + [rows_out(jnp.float32)] * 3
        + [far_out(low), far_out(levels - low)] * COLUMNS,
        far_pairs,
        5,
        head_dim,
    )

    def add(own, cross):
        return (own.astype(jnp.float32) + cross.astype(jnp.float32)).astype(jnp.bfloat16)

    high = hop(cross_high, 1, 0)
    chosen, near_kept, sent = call(
        functools.partial(near_backward_kernel, members, head_dim, blocks),
        [block, bias, queries, grad_out, level, drift, far_gq] + near_parts,
        [
            pltpu.VMEM((CORES, 2, part_tok, half), jnp.float32),
            pltpu.VMEM((2 * near, half), jnp.bfloat16),
            pltpu.VMEM((tok_rows + 2 * near, half), jnp.bfloat16),
        ],
        near_pairs,
        4,
        head_dim,
        scratch=[pltpu.VMEM((CORES, 2, near, half), jnp.float32)],
    )
    high, _ = lax.optimization_barrier((high, sent))
    sums = [add(own_high[d - low], high[d - low]) for d in range(low, levels)]
    cross_low, sent_mine, _ = lax.optimization_barrier((cross_low, sent, sums))
    crossed = hop(cross_low, 1, 0)
    sent_far = hop(sent_mine, 0, 1)
    att_far = hop(attended, 0, 1)
    sums = [add(own_low[d], crossed[d]) for d in range(1, low)] + sums
    returned = [sink(part, d) for d, part in enumerate(sums, 1)] + [crossed[0]]
    attended, grad_q, grad_k, grad_v = join(
        [attended, att_far, sent, sent_far, near_kept],
        [(tok_rows, feat_width)] * 2 + [(near, feat_width)] * 2,
    )
    returned, grad_k, grad_v = lax.optimization_barrier((returned, grad_k, grad_v))
    far_sent = chosen[1] + sum(part[1].astype(jnp.float32) for part in returned)
    far_sent = far_sent.astype(jnp.bfloat16)
    grad_k, grad_v = finish(
        [block, chosen, hop(far_sent, 0, 1)] + returned, [grad_k, grad_v]
    )
    return (attended, grad_q, grad_k.reshape(keys.shape), grad_v.reshape(values.shape))


def solution(mesh):
    return jax.shard_map(
        shards,
        mesh=mesh,
        in_specs=(P("seq", None), P("seq", "kv", None), P("seq", "kv", None), P(), P("seq", None)),
        out_specs=(P("seq", None), P("seq", None), P("seq", "kv", None), P("seq", "kv", None)),
        check_vma=False,
    )
```

```python
import functools
import math

import jax
import jax.numpy as jnp
from jax import lax
from jax.experimental import pallas as pl
from jax.experimental.pallas import tpu as pltpu
from jax.sharding import PartitionSpec as P

HEADS = 8
COLUMNS = 2
CORES = 2
GROUP = 2
SMALL = pl.CostEstimate(flops=0, bytes_accessed=0, transcendentals=0)
HIDDEN = -1e30
NT = (((1,), (1,)), ((), ()))
NN = (((1,), (0,)), ((), ()))
TN = (((0,), (0,)), ((), ()))
IN_HBM = pl.BlockSpec(memory_space=pltpu.HBM)
WHOLE = pl.BlockSpec(memory_space=pltpu.VMEM)
LIMIT = pltpu.CompilerParams(vmem_limit_bytes=12 * 1024 * 1024)


def dot(a, b, dims):
    return lax.dot_general(a, b, dims, preferred_element_type=jnp.float32)


def wide(rows, width):
    return jnp.concatenate([rows] * (width // rows.shape[1]), axis=1)


def base2_scale(head_dim):
    return math.log2(math.e) / math.sqrt(head_dim)


def pick_kernel(table_hbm, keys_hbm, values_hbm, mine_ref, theirs_ref, pair_ref, sent_ref, block_ref, table_ref, sems):
    window = lax.axis_index("seq")
    core = lax.axis_index("kv") % CORES
    _, blocks, part_tok, half = mine_ref.shape
    copies = [pltpu.make_async_copy(table_hbm, table_ref, sems.at[0])]
    for which, ref in enumerate((keys_hbm, values_hbm)):
        for side, out_ref in enumerate((mine_ref, theirs_ref)):
            cols = pl.ds(pl.multiple_of((core ^ side) * half, half), half)
            copies.append(
                pltpu.make_async_copy(ref.at[:, :, cols], out_ref.at[which], sems.at[len(copies)])
            )
    for copy in copies:
        copy.start()
    copies[0].wait()
    pick = jnp.minimum(window, lax.axis_size("seq") - 2)
    entry = lax.broadcasted_iota(jnp.int32, table_ref.shape, 0)
    row = lax.broadcasted_iota(jnp.int32, table_ref.shape, 1)
    here = (entry == pick) & (row == table_ref.shape[1] - 1)
    named = jnp.where(here, table_ref[...].astype(jnp.float32), -1.0)
    named = jnp.max(jnp.max(named, axis=1, keepdims=True), axis=0, keepdims=True)
    block = jnp.clip(named - (window * blocks).astype(jnp.float32), 0.0, blocks - 1.0)
    block_ref[...] = jnp.broadcast_to(block, block_ref.shape)
    block = jnp.broadcast_to(block, (part_tok, half))
    for copy in copies[1:]:
        copy.wait()
    for ref, out_ref in ((mine_ref, pair_ref), (theirs_ref, sent_ref)):
        for which in range(2):
            chosen = ref[which, 0].astype(jnp.float32)
            for b in range(1, blocks):
                chosen = jnp.where(block == b, ref[which, b].astype(jnp.float32), chosen)
            out_ref[which] = chosen.astype(out_ref.dtype)


def pick_pair(table, keys, values):
    blocks, part_tok, feat_width = keys.shape
    half = feat_width // CORES
    operands = [pltpu.with_memory_space_constraint(a, pltpu.HBM) for a in (table, keys, values)]
    return pl.pallas_call(
        pick_kernel,
        in_specs=[IN_HBM] * 3,
        out_specs=[WHOLE] * 5,
        out_shape=[pltpu.VMEM((2, blocks, part_tok, half), keys.dtype)] * 2
        + [pltpu.VMEM((2, part_tok, half), keys.dtype)] * 2
        + [pltpu.VMEM((8, 128), jnp.float32)],
        scratch_shapes=[pltpu.VMEM(table.shape, table.dtype), pltpu.SemaphoreType.DMA((5,))],
    )(*operands)


def join_kernel(att_ref, att_far, sent_ref, sent_far, kept_ref, att_out, gq_out, gk_out, gv_out, sems):
    core = lax.axis_index("kv") % CORES
    rows, half = att_ref.shape
    near = gk_out.shape[0]
    own, gk, gv = pl.ds(0, rows), pl.ds(rows, near), pl.ds(rows + near, near)
    copies = []
    for out_ref, sides in (
        (att_out, (att_ref, att_far)),
        (gq_out, (sent_ref.at[own], sent_far.at[own])),
        (gk_out, (kept_ref.at[pl.ds(0, near)], sent_far.at[gk])),
        (gv_out, (kept_ref.at[pl.ds(near, near)], sent_far.at[gv])),
    ):
        for side, ref in enumerate(sides):
            cols = pl.ds(pl.multiple_of((core ^ side) * half, half), half)
            copies.append(pltpu.make_async_copy(ref, out_ref.at[:, cols], sems.at[len(copies)]))
    for copy in copies:
        copy.start()
    for copy in copies:
        copy.wait()


def join(operands, shapes):
    operands = [pltpu.with_memory_space_constraint(a, pltpu.VMEM) for a in operands]
    return pl.pallas_call(
        join_kernel,
        in_specs=[WHOLE] * len(operands),
        out_specs=[IN_HBM] * len(shapes),
        out_shape=[pltpu.HBM(shape, jnp.bfloat16) for shape in shapes],
        scratch_shapes=[pltpu.SemaphoreType.DMA((2 * len(shapes),))],
        cost_estimate=SMALL,
    )(*operands)


def finish_kernel(block_ref, chosen_ref, far_ref, *refs):
    arrived, outs, rows_ref, sems = refs[:-6], refs[-4:-2], refs[-2], refs[-1]
    core = lax.axis_index("kv") % CORES
    part_tok, half = far_ref.shape[1:]
    block = jnp.max(block_ref[...]).astype(jnp.int32)
    here = pl.ds(pl.multiple_of(block * part_tok, part_tok), part_tok)
    mine = pl.ds(pl.multiple_of(core * half, half), half)
    theirs = pl.ds(pl.multiple_of((core ^ 1) * half, half), half)
    copies = []
    for which, out_ref in enumerate(outs):
        total = chosen_ref[0, which]
        for ref in arrived:
            total += ref[0, which].astype(jnp.float32)
        rows_ref[which, :, mine] = total.astype(rows_ref.dtype)
        rows_ref[which, :, theirs] = far_ref[which]
        copies.append(pltpu.make_async_copy(rows_ref.at[which], out_ref.at[here], sems.at[which]))
        copies[-1].start()
    for copy in copies:
        copy.wait()


def finish(operands, outs):
    part_tok, half = operands[2].shape[1:]
    operands = [pltpu.with_memory_space_constraint(a, pltpu.VMEM) for a in operands]
    outs = [pltpu.with_memory_space_constraint(a, pltpu.HBM) for a in outs]
    return pl.pallas_call(
        finish_kernel,
        in_specs=[WHOLE] * len(operands) + [IN_HBM] * 2,
        out_specs=[IN_HBM] * 2,
        out_shape=[pltpu.HBM(a.shape, a.dtype) for a in outs],
        input_output_aliases={len(operands): 0, len(operands) + 1: 1},
        scratch_shapes=[
            pltpu.VMEM((2, part_tok, half * CORES), jnp.bfloat16),
            pltpu.SemaphoreType.DMA((2,)),
        ],
        cost_estimate=SMALL,
    )(*operands, *outs)


def near_tiles(rows, near):
    half = rows // 2
    return [(0, half, near // 2), (half, half, near)]


def fill_mask(members, near, blk_len, part_tok, bias_ref):
    member = lax.axis_index("kv")
    shift = part_tok.bit_length() - 1
    for start, count, used in near_tiles(bias_ref.shape[0], near):
        row = start + lax.broadcasted_iota(jnp.int32, (count, 1), 0)
        col = lax.broadcasted_iota(jnp.int32, (1, used), 1)
        key_tok = (col >> shift) * blk_len + (col & (part_tok - 1))
        for j in range(members):
            key_pos = key_tok + (member ^ j) * part_tok
            bias_ref[start : start + count, j * used : (j + 1) * used] = jnp.where(
                key_pos <= row, 0.0, HIDDEN
            )


def head_columns(head, head_dim):
    return pl.ds(pl.multiple_of(head * head_dim, head_dim), head_dim)


def near_rows(parts, which, used, cols):
    return jnp.concatenate([ref[which, :used, cols] for ref in parts], axis=0)


def near_forward_kernel(members, blk_len, part_tok, head_dim, q_hbm, g_hbm, *refs):
    parts, outs = refs[:members], refs[members:]
    out_ref, stat_ref, bias_ref, q_ref, g_ref, sems = outs
    rows, half = q_ref.shape
    near = parts[0].shape[1]
    slab = GROUP * head_dim
    core = lax.axis_index("kv") % CORES

    def fetch(group):
        there = pl.ds(pl.multiple_of(core * half + group * slab, slab), slab)
        here = pl.ds(pl.multiple_of(group * slab, slab), slab)
        return pltpu.make_async_copy(q_hbm.at[:, there], q_ref.at[:, here], sems.at[group])

    there = pl.ds(pl.multiple_of(core * half, half), half)
    last = pltpu.make_async_copy(g_hbm.at[:, there], g_ref, sems.at[half // slab])
    for group in range(half // slab):
        fetch(group).start()
    last.start()
    fill_mask(members, near, blk_len, part_tok, bias_ref)

    @pl.loop(0, half // slab)
    def _(group):
        fetch(group).wait()
        units = [
            (head_columns(group * GROUP + i, head_dim), pl.ds(start, count), used)
            for i in range(GROUP)
            for start, count, used in near_tiles(rows, near)
        ]
        raws = [
            dot(q_ref[here, cols], near_rows(parts, 0, used, cols), NT) * base2_scale(head_dim)
            + bias_ref[here, : members * used]
            for cols, here, used in units
        ]
        peaks = [jnp.max(raw, axis=1, keepdims=True) for raw in raws]
        weights = [jnp.exp2(raw - peak) for raw, peak in zip(raws, peaks)]
        totals = [jnp.sum(weight, axis=1, keepdims=True) for weight in weights]
        sums = [
            dot(weight.astype(jnp.bfloat16), near_rows(parts, 1, used, cols), NN)
            for weight, (cols, here, used) in zip(weights, units)
        ]
        for (cols, here, used), peak, total, summed in zip(units, peaks, totals, sums):
            level = peak + jnp.log2(total)
            stat_ref[here, cols] = jnp.broadcast_to(level, summed.shape)
            out_ref[here, cols] = summed * (1.0 / total)

    last.wait()


def far_rows(parts, which, cols):
    rows = []
    for pair_ref, column_ref in zip(parts[0::2], parts[1::2]):
        steps, cores, _, part_tok, _ = column_ref.shape
        rows.append(pair_ref[:, which, :, cols].reshape(cores * part_tok, cols.size))
        rows.append(column_ref[:, :, which, :, cols].reshape(steps * cores * part_tok, cols.size))
    return jnp.concatenate(rows, axis=0)


def far_kernel(groups, steps, head_dim, tile, heads, batch, q_ref, g_ref, sum_ref, stat_ref, *refs):
    parts = refs[: 2 * COLUMNS * groups]
    att_ref, gq_ref, level_ref, drift_ref, *grad_refs = refs[2 * COLUMNS * groups :]
    _, cores, _, part_tok, _ = grad_refs[0].shape
    rows, half = q_ref.shape
    span = steps * cores * part_tok
    width = COLUMNS * span
    score_scale = 1.0 / math.sqrt(head_dim)
    window = lax.axis_index("seq")
    level, side = window // COLUMNS, window % COLUMNS
    step = lax.broadcasted_iota(jnp.int32, (1, span), 1) >> ((cores * part_tok).bit_length() - 1)
    valid = [(step >= 1) & (step <= level), (step >= 1 - side) & (step <= level)]
    bias = jnp.concatenate([jnp.where(ok, 0.0, HIDDEN) for ok in valid] * groups, axis=1)
    total_width = groups * width

    def work(units, keys, values, key_grads, value_grads):
        raws = [
            dot(q_ref[here, cols], keys[i], NT) * base2_scale(head_dim) + bias
            for i, cols, here in units
        ]
        grad_probs = [dot(g_ref[here, cols], values[i], NT) for i, cols, here in units]
        near_levels = [stat_ref[here, cols] for i, cols, here in units]
        peaks = [
            jnp.maximum(near_level, jnp.max(raw, axis=1, keepdims=True))
            for near_level, raw in zip(near_levels, raws)
        ]
        near_weights = [jnp.exp2(near_level - peak) for near_level, peak in zip(near_levels, peaks)]
        weights = [jnp.exp2(raw - wide(peak, total_width)) for raw, peak in zip(raws, peaks)]
        totals = [
            near_weight + jnp.sum(weight, axis=1, keepdims=True)
            for near_weight, weight in zip(near_weights, weights)
        ]
        inverses = [1.0 / total for total in totals]
        sums = [
            dot(weight.astype(jnp.bfloat16), values[i], NN)
            for weight, (i, cols, here) in zip(weights, units)
        ]
        drifts = []
        for u, (i, cols, here) in enumerate(units):
            summed = sum_ref[here, cols] * near_weights[u] + sums[u]
            attended = (summed * inverses[u]).astype(jnp.bfloat16)
            att_ref[here, cols] = attended
            product = g_ref[here, cols].astype(jnp.float32) * attended.astype(jnp.float32)
            drift = jnp.broadcast_to(jnp.sum(product, axis=1, keepdims=True), product.shape)
            drifts.append(drift)
            level_ref[here, cols] = peaks[u] + jnp.log2(totals[u])
            drift_ref[here, cols] = drift
        moved = [
            weight * (grad_prob - wide(drift, total_width))
            for weight, grad_prob, drift in zip(weights, grad_probs, drifts)
        ]
        factors = [inverse * score_scale for inverse in inverses]
        own_scores = [
            (part[:, :width] * wide(factor, width)).astype(jnp.bfloat16)
            for part, factor in zip(moved, factors)
        ]
        own_probs = [
            (weight[:, :width] * wide(inverse, width)).astype(jnp.bfloat16)
            for weight, inverse in zip(weights, inverses)
        ]
        for u, (i, cols, here) in enumerate(units):
            gq_ref[here, cols] = dot(moved[u].astype(jnp.bfloat16), keys[i], NN) * factors[u]
        for u, (i, cols, here) in enumerate(units):
            key_grads[i].append(dot(own_scores[u], q_ref[here, cols], TN))
            value_grads[i].append(dot(own_probs[u], g_ref[here, cols], TN))

    @pl.loop(0, half // (heads * head_dim))
    def _(group):
        columns = [head_columns(group * heads + i, head_dim) for i in range(heads)]
        units = [
            (i, cols, pl.ds(r, tile)) for i, cols in enumerate(columns) for r in range(0, rows, tile)
        ]
        keys = [far_rows(parts, 0, cols) for cols in columns]
        values = [far_rows(parts, 1, cols) for cols in columns]
        grads = [[[] for _ in columns] for _ in range(2)]
        for first in range(0, len(units), batch):
            work(units[first : first + batch], keys, values, *grads)
        for which, per_head in enumerate(grads):
            for cols, terms in zip(columns, per_head):
                total = functools.reduce(lambda a, b: a + b, terms).astype(jnp.bfloat16)
                start = 0
                for ref in grad_refs:
                    shape = ref.shape[:2] + (part_tok, head_dim)
                    count = math.prod(shape[:3])
                    ref[:, :, which, :, cols] = total[start : start + count].reshape(shape)
                    start += count


def near_backward_kernel(members, head_dim, blocks, block_ref, bias_ref, q_ref, g_ref, level_ref, drift_ref, far_gq_ref, *refs):
    parts, outs = refs[:members], refs[members:]
    chosen_ref, kept_ref, sent_ref, grad_ref = outs
    rows, half = q_ref.shape
    near = parts[0].shape[1]
    score_scale = 1.0 / math.sqrt(head_dim)

    @pl.loop(0, half // (GROUP * head_dim))
    def _(group):
        units = [
            (head_columns(group * GROUP + i, head_dim), pl.ds(start, count), used)
            for i in range(GROUP)
            for start, count, used in near_tiles(rows, near)
        ]
        keys = [near_rows(parts, 0, used, cols) for cols, here, used in units]
        values = [near_rows(parts, 1, used, cols) for cols, here, used in units]
        raws = [
            dot(q_ref[here, cols], key, NT) * base2_scale(head_dim)
            + bias_ref[here, : members * used]
            for (cols, here, used), key in zip(units, keys)
        ]
        grad_probs = [
            dot(g_ref[here, cols], value, NT) for (cols, here, used), value in zip(units, values)
        ]
        probs = [
            jnp.exp2(raw - wide(level_ref[here, cols], raw.shape[1]))
            for raw, (cols, here, used) in zip(raws, units)
        ]
        moved = [
            prob * (grad_prob - wide(drift_ref[here, cols], prob.shape[1]))
            for prob, grad_prob, (cols, here, used) in zip(probs, grad_probs, units)
        ]
        for (cols, here, used), part, key in zip(units, moved, keys):
            sent_ref[here, cols] = (
                dot(part.astype(jnp.bfloat16), key, NN) * score_scale + far_gq_ref[here, cols]
            ).astype(jnp.bfloat16)
        grads = []
        for (cols, here, used), part, prob in zip(units, moved, probs):
            own_score = (part[:, : CORES * used] * score_scale).astype(jnp.bfloat16)
            own_prob = prob[:, : CORES * used].astype(jnp.bfloat16)
            grads.append((dot(own_score, q_ref[here, cols], TN), dot(own_prob, g_ref[here, cols], TN)))
        low = near // 2
        for (cols, _, _), early, late in zip(units[0::2], grads[0::2], grads[1::2]):
            for which in range(2):
                for core in range(CORES):
                    top = late[which][core * near : core * near + low]
                    top += early[which][core * low : (core + 1) * low]
                    bottom = late[which][core * near + low : (core + 1) * near]
                    grad_ref[core, which, :low, cols] = top
                    grad_ref[core, which, low:, cols] = bottom
                    ref, first = ((kept_ref, 0), (sent_ref, rows))[core]
                    first += which * near
                    ref[first : first + low, cols] = top.astype(ref.dtype)
                    ref[first + low : first + near, cols] = bottom.astype(ref.dtype)

    part_tok = near // blocks
    block = jnp.max(jnp.max(block_ref[...], axis=1, keepdims=True), axis=0, keepdims=True)
    for core in range(CORES):
        for which in range(2):
            chosen = grad_ref[core, which, :part_tok]
            for b in range(1, blocks):
                rows_b = grad_ref[core, which, b * part_tok : (b + 1) * part_tok]
                chosen = jnp.where(block == b, rows_b, chosen)
            chosen_ref[core, which] = chosen


def call(kernel, operands, outs, pairs, products, head_dim, in_specs=None, scratch=()):
    moved_bytes = sum(a.size * a.dtype.itemsize for a in operands)
    return pl.pallas_call(
        kernel,
        in_specs=in_specs or [WHOLE] * len(operands),
        out_specs=[WHOLE] * len(outs),
        out_shape=outs,
        scratch_shapes=scratch,
        compiler_params=LIMIT,
        cost_estimate=pl.CostEstimate(
            flops=4 * products * pairs * head_dim, bytes_accessed=moved_bytes, transcendentals=pairs
        ),
    )(*operands)


def shards(queries, keys, values, layout, grad_out):
    seq_count = lax.axis_size("seq")
    members = lax.axis_size("kv")
    tok_rows, feat_width = queries.shape
    blocks, part_tok = (keys.shape[0], keys.shape[1])
    blk_len = part_tok * members
    near = blocks * part_tok
    head_dim = feat_width // HEADS
    half = feat_width // CORES
    levels = seq_count // COLUMNS
    groups = members // CORES

    def hop(part, column_step, member_step):
        pairs = [
            (s * members + m, (s ^ column_step) * members + (m ^ member_step))
            for s in range(seq_count)
            for m in range(members)
        ]
        return lax.ppermute(part, ("seq", "kv"), pairs)

    def climb(part, d):
        return lax.ppermute(
            part, "seq", [(s, s + COLUMNS * d) for s in range(seq_count - COLUMNS * d)]
        )

    def sink(part, d):
        return lax.ppermute(
            part, "seq", [(s, s - COLUMNS * d) for s in range(COLUMNS * d, seq_count)]
        )

    mine, theirs, pair_mine, pair_theirs, block = pick_pair(layout.T, keys, values)
    own_pair = jnp.stack([pair_mine, hop(pair_theirs, 0, 1)])
    climbed = [climb(own_pair, d) for d in range(1, levels)]
    column = jnp.stack(climbed)
    chip_parts = [mine, hop(theirs, 0, 1)]
    near_parts = list(chip_parts)
    for group in range(1, groups):
        near_parts += [hop(part, 0, CORES * group) for part in chip_parts]
    sent_pair, _ = lax.optimization_barrier((own_pair, chip_parts[1]))
    cross_pairs = [hop(sent_pair, 1, CORES * group) for group in range(groups)]
    column, near_parts = lax.optimization_barrier((column, near_parts))
    near_parts = [part.reshape(2, near, half) for part in near_parts]
    crossing = [
        [column if (c, group) == (0, 0) else hop(column, c, CORES * group) for c in range(COLUMNS)]
        for group in range(groups)
    ]

    def rows_out(dtype):
        return pltpu.VMEM((tok_rows, half), dtype)

    def far_out(count):
        return pltpu.VMEM((count,) + own_pair.shape, jnp.bfloat16)

    low = (levels + 1) // 2
    near_pairs = HEADS // CORES * tok_rows * members * near
    far_width = members * seq_count * part_tok
    far_pairs = HEADS // CORES * tok_rows * far_width
    roomy = far_width <= 512
    far_plan = (tok_rows // 2, GROUP, 2 * GROUP) if roomy else (tok_rows // 8, 1, 1)

    near_sum, near_stat, bias, queries, grad_out = call(
        functools.partial(near_forward_kernel, members, blk_len, part_tok, head_dim),
        [pltpu.with_memory_space_constraint(a, pltpu.HBM) for a in (queries, grad_out)] + near_parts,
        [rows_out(jnp.float32)] * 2
        + [pltpu.VMEM((tok_rows, members * near), jnp.float32)]
        + [rows_out(jnp.bfloat16)] * 2,
        near_pairs,
        2,
        head_dim,
        [IN_HBM, IN_HBM] + [WHOLE] * members,
        [pltpu.SemaphoreType.DMA((half // (GROUP * head_dim) + 1,))],
    )
    far_parts = []
    for group, cross_pair in zip(crossing, cross_pairs):
        (same, other), _ = lax.optimization_barrier((group, near_stat))
        far_parts += [own_pair, same, cross_pair, other]
    attended, far_gq, level, drift, own_low, own_high, cross_low, cross_high = call(
        functools.partial(far_kernel, groups, levels, head_dim, *far_plan),
        [queries, grad_out, near_sum, near_stat] + far_parts,
        [rows_out(jnp.bfloat16)]
        + [rows_out(jnp.float32)] * 3
        + [far_out(low), far_out(levels - low)] * COLUMNS,
        far_pairs,
        5,
        head_dim,
    )

    def add(own, cross):
        return (own.astype(jnp.float32) + cross.astype(jnp.float32)).astype(jnp.bfloat16)

    high = hop(cross_high, 1, 0)
    chosen, near_kept, sent = call(
        functools.partial(near_backward_kernel, members, head_dim, blocks),
        [block, bias, queries, grad_out, level, drift, far_gq] + near_parts,
        [
            pltpu.VMEM((CORES, 2, part_tok, half), jnp.float32),
            pltpu.VMEM((2 * near, half), jnp.bfloat16),
            pltpu.VMEM((tok_rows + 2 * near, half), jnp.bfloat16),
        ],
        near_pairs,
        4,
        head_dim,
        scratch=[pltpu.VMEM((CORES, 2, near, half), jnp.float32)],
    )
    high, _ = lax.optimization_barrier((high, chosen))
    sums = [add(own_high[d - low], high[d - low]) for d in range(low, levels)]
    cross_low, _ = lax.optimization_barrier((cross_low, sums))
    crossed = hop(cross_low, 1, 0)
    sent = sent + high[0, 0, 0, 0][None] * 0
    sent_far = hop(sent, 0, 1)
    att_far = hop(attended, 0, 1)
    sums = [add(own_low[d], crossed[d]) for d in range(1, low)] + sums
    returned = [sink(part, d) for d, part in enumerate(sums, 1)] + [crossed[0]]
    attended, grad_q, grad_k, grad_v = join(
        [attended, att_far, sent, sent_far, near_kept],
        [(tok_rows, feat_width)] * 2 + [(near, feat_width)] * 2,
    )
    returned, grad_k, grad_v = lax.optimization_barrier((returned, grad_k, grad_v))
    far_sent = chosen[1] + sum(part[1].astype(jnp.float32) for part in returned)
    far_sent = far_sent.astype(jnp.bfloat16)
    grad_k, grad_v = finish(
        [block, chosen, hop(far_sent, 0, 1)] + returned, [grad_k, grad_v]
    )
    return (attended, grad_q, grad_k.reshape(keys.shape), grad_v.reshape(values.shape))


def solution(mesh):
    return jax.shard_map(
        shards,
        mesh=mesh,
        in_specs=(P("seq", None), P("seq", "kv", None), P("seq", "kv", None), P(), P("seq", None)),
        out_specs=(P("seq", None), P("seq", None), P("seq", "kv", None), P("seq", "kv", None)),
        check_vma=False,
    )
```

```python
import functools
import math

import jax
import jax.numpy as jnp
from jax import lax
from jax.experimental import pallas as pl
from jax.experimental.pallas import tpu as pltpu
from jax.sharding import PartitionSpec as P

HEADS = 8
COLUMNS = 2
CORES = 2
GROUP = 2
SMALL = pl.CostEstimate(flops=0, bytes_accessed=0, transcendentals=0)
HIDDEN = -1e30
NT = (((1,), (1,)), ((), ()))
NN = (((1,), (0,)), ((), ()))
TN = (((0,), (0,)), ((), ()))
IN_HBM = pl.BlockSpec(memory_space=pltpu.HBM)
WHOLE = pl.BlockSpec(memory_space=pltpu.VMEM)
LIMIT = pltpu.CompilerParams(vmem_limit_bytes=12 * 1024 * 1024)


def dot(a, b, dims):
    return lax.dot_general(a, b, dims, preferred_element_type=jnp.float32)


def wide(rows, width):
    return jnp.concatenate([rows] * (width // rows.shape[1]), axis=1)


def base2_scale(head_dim):
    return math.log2(math.e) / math.sqrt(head_dim)


def pick_kernel(table_hbm, keys_hbm, values_hbm, mine_ref, theirs_ref, pair_ref, sent_ref, block_ref, table_ref, sems):
    window = lax.axis_index("seq")
    core = lax.axis_index("kv") % CORES
    _, blocks, part_tok, half = mine_ref.shape
    copies = [pltpu.make_async_copy(table_hbm, table_ref, sems.at[0])]
    for which, ref in enumerate((keys_hbm, values_hbm)):
        for side, out_ref in enumerate((mine_ref, theirs_ref)):
            cols = pl.ds(pl.multiple_of((core ^ side) * half, half), half)
            copies.append(
                pltpu.make_async_copy(ref.at[:, :, cols], out_ref.at[which], sems.at[len(copies)])
            )
    for copy in copies:
        copy.start()
    copies[0].wait()
    pick = jnp.minimum(window, lax.axis_size("seq") - 2)
    entry = lax.broadcasted_iota(jnp.int32, table_ref.shape, 0)
    row = lax.broadcasted_iota(jnp.int32, table_ref.shape, 1)
    here = (entry == pick) & (row == table_ref.shape[1] - 1)
    named = jnp.where(here, table_ref[...].astype(jnp.float32), -1.0)
    named = jnp.max(jnp.max(named, axis=1, keepdims=True), axis=0, keepdims=True)
    block = jnp.clip(named - (window * blocks).astype(jnp.float32), 0.0, blocks - 1.0)
    block_ref[...] = jnp.broadcast_to(block, block_ref.shape)
    block = jnp.broadcast_to(block, (part_tok, half))
    for copy in copies[1:]:
        copy.wait()
    for ref, out_ref in ((mine_ref, pair_ref), (theirs_ref, sent_ref)):
        for which in range(2):
            chosen = ref[which, 0].astype(jnp.float32)
            for b in range(1, blocks):
                chosen = jnp.where(block == b, ref[which, b].astype(jnp.float32), chosen)
            out_ref[which] = chosen.astype(out_ref.dtype)


def pick_pair(table, keys, values):
    blocks, part_tok, feat_width = keys.shape
    half = feat_width // CORES
    operands = [pltpu.with_memory_space_constraint(a, pltpu.HBM) for a in (table, keys, values)]
    return pl.pallas_call(
        pick_kernel,
        in_specs=[IN_HBM] * 3,
        out_specs=[WHOLE] * 5,
        out_shape=[pltpu.VMEM((2, blocks, part_tok, half), keys.dtype)] * 2
        + [pltpu.VMEM((2, part_tok, half), keys.dtype)] * 2
        + [pltpu.VMEM((8, 128), jnp.float32)],
        scratch_shapes=[pltpu.VMEM(table.shape, table.dtype), pltpu.SemaphoreType.DMA((5,))],
    )(*operands)


def join_kernel(att_ref, att_far, gq_ref, gq_far, kept_ref, near_far, att_out, gq_out, gk_out, gv_out, sems):
    core = lax.axis_index("kv") % CORES
    half, near = att_ref.shape[1], gk_out.shape[0]
    gk, gv = pl.ds(0, near), pl.ds(near, near)
    copies = []
    for out_ref, sides in (
        (att_out, (att_ref, att_far)),
        (gq_out, (gq_ref, gq_far)),
        (gk_out, (kept_ref.at[gk], near_far.at[gk])),
        (gv_out, (kept_ref.at[gv], near_far.at[gv])),
    ):
        for side, ref in enumerate(sides):
            cols = pl.ds(pl.multiple_of((core ^ side) * half, half), half)
            copies.append(pltpu.make_async_copy(ref, out_ref.at[:, cols], sems.at[len(copies)]))
    for copy in copies:
        copy.start()
    for copy in copies:
        copy.wait()


def join(operands, shapes):
    operands = [pltpu.with_memory_space_constraint(a, pltpu.VMEM) for a in operands]
    return pl.pallas_call(
        join_kernel,
        in_specs=[WHOLE] * len(operands),
        out_specs=[IN_HBM] * len(shapes),
        out_shape=[pltpu.HBM(shape, jnp.bfloat16) for shape in shapes],
        scratch_shapes=[pltpu.SemaphoreType.DMA((2 * len(shapes),))],
        cost_estimate=SMALL,
    )(*operands)


def finish_kernel(block_ref, chosen_ref, far_ref, *refs):
    arrived, outs, rows_ref, sems = refs[:-6], refs[-4:-2], refs[-2], refs[-1]
    core = lax.axis_index("kv") % CORES
    part_tok, half = far_ref.shape[1:]
    block = jnp.max(block_ref[...]).astype(jnp.int32)
    here = pl.ds(pl.multiple_of(block * part_tok, part_tok), part_tok)
    mine = pl.ds(pl.multiple_of(core * half, half), half)
    theirs = pl.ds(pl.multiple_of((core ^ 1) * half, half), half)
    copies = []
    for which, out_ref in enumerate(outs):
        total = chosen_ref[0, which]
        for ref in arrived:
            total += ref[0, which].astype(jnp.float32)
        rows_ref[which, :, mine] = total.astype(rows_ref.dtype)
        rows_ref[which, :, theirs] = far_ref[which]
        copies.append(pltpu.make_async_copy(rows_ref.at[which], out_ref.at[here], sems.at[which]))
        copies[-1].start()
    for copy in copies:
        copy.wait()


def finish(operands, outs):
    part_tok, half = operands[2].shape[1:]
    operands = [pltpu.with_memory_space_constraint(a, pltpu.VMEM) for a in operands]
    outs = [pltpu.with_memory_space_constraint(a, pltpu.HBM) for a in outs]
    return pl.pallas_call(
        finish_kernel,
        in_specs=[WHOLE] * len(operands) + [IN_HBM] * 2,
        out_specs=[IN_HBM] * 2,
        out_shape=[pltpu.HBM(a.shape, a.dtype) for a in outs],
        input_output_aliases={len(operands): 0, len(operands) + 1: 1},
        scratch_shapes=[
            pltpu.VMEM((2, part_tok, half * CORES), jnp.bfloat16),
            pltpu.SemaphoreType.DMA((2,)),
        ],
        cost_estimate=SMALL,
    )(*operands, *outs)


def near_tiles(rows, near):
    half = rows // 2
    return [(0, half, near // 2), (half, half, near)]


def fill_mask(members, near, blk_len, part_tok, bias_ref):
    member = lax.axis_index("kv")
    shift = part_tok.bit_length() - 1
    for start, count, used in near_tiles(bias_ref.shape[0], near):
        row = start + lax.broadcasted_iota(jnp.int32, (count, 1), 0)
        col = lax.broadcasted_iota(jnp.int32, (1, used), 1)
        key_tok = (col >> shift) * blk_len + (col & (part_tok - 1))
        for j in range(members):
            key_pos = key_tok + (member ^ j) * part_tok
            bias_ref[start : start + count, j * used : (j + 1) * used] = jnp.where(
                key_pos <= row, 0.0, HIDDEN
            )


def head_columns(head, head_dim):
    return pl.ds(pl.multiple_of(head * head_dim, head_dim), head_dim)


def near_rows(parts, which, used, cols):
    return jnp.concatenate([ref[which, :used, cols] for ref in parts], axis=0)


def near_forward_kernel(members, blk_len, part_tok, head_dim, q_hbm, g_hbm, *refs):
    parts, outs = refs[:members], refs[members:]
    out_ref, stat_ref, bias_ref, q_ref, g_ref, sems = outs
    rows, half = q_ref.shape
    near = parts[0].shape[1]
    slab = GROUP * head_dim
    core = lax.axis_index("kv") % CORES

    def fetch(group):
        there = pl.ds(pl.multiple_of(core * half + group * slab, slab), slab)
        here = pl.ds(pl.multiple_of(group * slab, slab), slab)
        return pltpu.make_async_copy(q_hbm.at[:, there], q_ref.at[:, here], sems.at[group])

    there = pl.ds(pl.multiple_of(core * half, half), half)
    last = pltpu.make_async_copy(g_hbm.at[:, there], g_ref, sems.at[half // slab])
    for group in range(half // slab):
        fetch(group).start()
    last.start()
    fill_mask(members, near, blk_len, part_tok, bias_ref)

    @pl.loop(0, half // slab)
    def _(group):
        fetch(group).wait()
        units = [
            (head_columns(group * GROUP + i, head_dim), pl.ds(start, count), used)
            for i in range(GROUP)
            for start, count, used in near_tiles(rows, near)
        ]
        raws = [
            dot(q_ref[here, cols], near_rows(parts, 0, used, cols), NT) * base2_scale(head_dim)
            + bias_ref[here, : members * used]
            for cols, here, used in units
        ]
        peaks = [jnp.max(raw, axis=1, keepdims=True) for raw in raws]
        weights = [jnp.exp2(raw - peak) for raw, peak in zip(raws, peaks)]
        totals = [jnp.sum(weight, axis=1, keepdims=True) for weight in weights]
        sums = [
            dot(weight.astype(jnp.bfloat16), near_rows(parts, 1, used, cols), NN)
            for weight, (cols, here, used) in zip(weights, units)
        ]
        for (cols, here, used), peak, total, summed in zip(units, peaks, totals, sums):
            level = peak + jnp.log2(total)
            stat_ref[here, cols] = jnp.broadcast_to(level, summed.shape)
            out_ref[here, cols] = summed * (1.0 / total)

    last.wait()


def far_rows(parts, which, cols):
    rows = []
    for pair_ref, column_ref in zip(parts[0::2], parts[1::2]):
        steps, cores, _, part_tok, _ = column_ref.shape
        rows.append(pair_ref[:, which, :, cols].reshape(cores * part_tok, cols.size))
        rows.append(column_ref[:, :, which, :, cols].reshape(steps * cores * part_tok, cols.size))
    return jnp.concatenate(rows, axis=0)


def far_kernel(groups, steps, head_dim, tile, heads, batch, q_ref, g_ref, sum_ref, stat_ref, *refs):
    parts = refs[: 2 * COLUMNS * groups]
    att_ref, gq_ref, level_ref, drift_ref, *grad_refs = refs[2 * COLUMNS * groups :]
    _, cores, _, part_tok, _ = grad_refs[0].shape
    rows, half = q_ref.shape
    span = steps * cores * part_tok
    width = COLUMNS * span
    score_scale = 1.0 / math.sqrt(head_dim)
    window = lax.axis_index("seq")
    level, side = window // COLUMNS, window % COLUMNS
    step = lax.broadcasted_iota(jnp.int32, (1, span), 1) >> ((cores * part_tok).bit_length() - 1)
    valid = [(step >= 1) & (step <= level), (step >= 1 - side) & (step <= level)]
    bias = jnp.concatenate([jnp.where(ok, 0.0, HIDDEN) for ok in valid] * groups, axis=1)
    total_width = groups * width

    def work(units, keys, values, key_grads, value_grads):
        raws = [
            dot(q_ref[here, cols], keys[i], NT) * base2_scale(head_dim) + bias
            for i, cols, here in units
        ]
        grad_probs = [dot(g_ref[here, cols], values[i], NT) for i, cols, here in units]
        near_levels = [stat_ref[here, cols] for i, cols, here in units]
        peaks = [
            jnp.maximum(near_level, jnp.max(raw, axis=1, keepdims=True))
            for near_level, raw in zip(near_levels, raws)
        ]
        near_weights = [jnp.exp2(near_level - peak) for near_level, peak in zip(near_levels, peaks)]
        weights = [jnp.exp2(raw - wide(peak, total_width)) for raw, peak in zip(raws, peaks)]
        totals = [
            near_weight + jnp.sum(weight, axis=1, keepdims=True)
            for near_weight, weight in zip(near_weights, weights)
        ]
        inverses = [1.0 / total for total in totals]
        sums = [
            dot(weight.astype(jnp.bfloat16), values[i], NN)
            for weight, (i, cols, here) in zip(weights, units)
        ]
        drifts = []
        for u, (i, cols, here) in enumerate(units):
            summed = sum_ref[here, cols] * near_weights[u] + sums[u]
            attended = (summed * inverses[u]).astype(jnp.bfloat16)
            att_ref[here, cols] = attended
            product = g_ref[here, cols].astype(jnp.float32) * attended.astype(jnp.float32)
            drift = jnp.broadcast_to(jnp.sum(product, axis=1, keepdims=True), product.shape)
            drifts.append(drift)
            level_ref[here, cols] = peaks[u] + jnp.log2(totals[u])
            drift_ref[here, cols] = drift
        moved = [
            weight * (grad_prob - wide(drift, total_width))
            for weight, grad_prob, drift in zip(weights, grad_probs, drifts)
        ]
        factors = [inverse * score_scale for inverse in inverses]
        own_scores = [
            (part[:, :width] * wide(factor, width)).astype(jnp.bfloat16)
            for part, factor in zip(moved, factors)
        ]
        own_probs = [
            (weight[:, :width] * wide(inverse, width)).astype(jnp.bfloat16)
            for weight, inverse in zip(weights, inverses)
        ]
        for u, (i, cols, here) in enumerate(units):
            gq_ref[here, cols] = dot(moved[u].astype(jnp.bfloat16), keys[i], NN) * factors[u]
        for u, (i, cols, here) in enumerate(units):
            key_grads[i].append(dot(own_scores[u], q_ref[here, cols], TN))
            value_grads[i].append(dot(own_probs[u], g_ref[here, cols], TN))

    @pl.loop(0, half // (heads * head_dim))
    def _(group):
        columns = [head_columns(group * heads + i, head_dim) for i in range(heads)]
        units = [
            (i, cols, pl.ds(r, tile)) for i, cols in enumerate(columns) for r in range(0, rows, tile)
        ]
        keys = [far_rows(parts, 0, cols) for cols in columns]
        values = [far_rows(parts, 1, cols) for cols in columns]
        grads = [[[] for _ in columns] for _ in range(2)]
        for first in range(0, len(units), batch):
            work(units[first : first + batch], keys, values, *grads)
        for which, per_head in enumerate(grads):
            for cols, terms in zip(columns, per_head):
                total = functools.reduce(lambda a, b: a + b, terms).astype(jnp.bfloat16)
                start = 0
                for ref in grad_refs:
                    shape = ref.shape[:2] + (part_tok, head_dim)
                    count = math.prod(shape[:3])
                    ref[:, :, which, :, cols] = total[start : start + count].reshape(shape)
                    start += count


def near_backward_kernel(members, head_dim, blocks, block_ref, bias_ref, q_ref, g_ref, level_ref, drift_ref, far_gq_ref, *refs):
    parts, outs = refs[:members], refs[members:]
    chosen_ref, kept_ref, gq_ref, sent_ref, grad_ref = outs
    rows, half = q_ref.shape
    near = parts[0].shape[1]
    score_scale = 1.0 / math.sqrt(head_dim)

    @pl.loop(0, half // (GROUP * head_dim))
    def _(group):
        units = [
            (head_columns(group * GROUP + i, head_dim), pl.ds(start, count), used)
            for i in range(GROUP)
            for start, count, used in near_tiles(rows, near)
        ]
        keys = [near_rows(parts, 0, used, cols) for cols, here, used in units]
        values = [near_rows(parts, 1, used, cols) for cols, here, used in units]
        raws = [
            dot(q_ref[here, cols], key, NT) * base2_scale(head_dim)
            + bias_ref[here, : members * used]
            for (cols, here, used), key in zip(units, keys)
        ]
        grad_probs = [
            dot(g_ref[here, cols], value, NT) for (cols, here, used), value in zip(units, values)
        ]
        probs = [
            jnp.exp2(raw - wide(level_ref[here, cols], raw.shape[1]))
            for raw, (cols, here, used) in zip(raws, units)
        ]
        moved = [
            prob * (grad_prob - wide(drift_ref[here, cols], prob.shape[1]))
            for prob, grad_prob, (cols, here, used) in zip(probs, grad_probs, units)
        ]
        for (cols, here, used), part, key in zip(units, moved, keys):
            gq_ref[here, cols] = (
                dot(part.astype(jnp.bfloat16), key, NN) * score_scale + far_gq_ref[here, cols]
            ).astype(jnp.bfloat16)
        grads = []
        for (cols, here, used), part, prob in zip(units, moved, probs):
            own_score = (part[:, : CORES * used] * score_scale).astype(jnp.bfloat16)
            own_prob = prob[:, : CORES * used].astype(jnp.bfloat16)
            grads.append((dot(own_score, q_ref[here, cols], TN), dot(own_prob, g_ref[here, cols], TN)))
        low = near // 2
        for (cols, _, _), early, late in zip(units[0::2], grads[0::2], grads[1::2]):
            for which in range(2):
                for core in range(CORES):
                    top = late[which][core * near : core * near + low]
                    top += early[which][core * low : (core + 1) * low]
                    bottom = late[which][core * near + low : (core + 1) * near]
                    grad_ref[core, which, :low, cols] = top
                    grad_ref[core, which, low:, cols] = bottom
                    ref, first = (kept_ref, sent_ref)[core], which * near
                    ref[first : first + low, cols] = top.astype(ref.dtype)
                    ref[first + low : first + near, cols] = bottom.astype(ref.dtype)

    part_tok = near // blocks
    block = jnp.max(jnp.max(block_ref[...], axis=1, keepdims=True), axis=0, keepdims=True)
    for core in range(CORES):
        for which in range(2):
            chosen = grad_ref[core, which, :part_tok]
            for b in range(1, blocks):
                rows_b = grad_ref[core, which, b * part_tok : (b + 1) * part_tok]
                chosen = jnp.where(block == b, rows_b, chosen)
            chosen_ref[core, which] = chosen


def call(kernel, operands, outs, pairs, products, head_dim, in_specs=None, scratch=()):
    moved_bytes = sum(a.size * a.dtype.itemsize for a in operands)
    return pl.pallas_call(
        kernel,
        in_specs=in_specs or [WHOLE] * len(operands),
        out_specs=[WHOLE] * len(outs),
        out_shape=outs,
        scratch_shapes=scratch,
        compiler_params=LIMIT,
        cost_estimate=pl.CostEstimate(
            flops=4 * products * pairs * head_dim, bytes_accessed=moved_bytes, transcendentals=pairs
        ),
    )(*operands)


def shards(queries, keys, values, layout, grad_out):
    seq_count = lax.axis_size("seq")
    members = lax.axis_size("kv")
    tok_rows, feat_width = queries.shape
    blocks, part_tok = (keys.shape[0], keys.shape[1])
    blk_len = part_tok * members
    near = blocks * part_tok
    head_dim = feat_width // HEADS
    half = feat_width // CORES
    levels = seq_count // COLUMNS
    groups = members // CORES

    def hop(part, column_step, member_step):
        pairs = [
            (s * members + m, (s ^ column_step) * members + (m ^ member_step))
            for s in range(seq_count)
            for m in range(members)
        ]
        return lax.ppermute(part, ("seq", "kv"), pairs)

    def climb(part, d):
        return lax.ppermute(
            part, "seq", [(s, s + COLUMNS * d) for s in range(seq_count - COLUMNS * d)]
        )

    def sink(part, d):
        return lax.ppermute(
            part, "seq", [(s, s - COLUMNS * d) for s in range(COLUMNS * d, seq_count)]
        )

    mine, theirs, pair_mine, pair_theirs, block = pick_pair(layout.T, keys, values)
    own_pair = jnp.stack([pair_mine, hop(pair_theirs, 0, 1)])
    climbed = [climb(own_pair, d) for d in range(1, levels)]
    column = jnp.stack(climbed)
    chip_parts = [mine, hop(theirs, 0, 1)]
    near_parts = list(chip_parts)
    for group in range(1, groups):
        near_parts += [hop(part, 0, CORES * group) for part in chip_parts]
    sent_pair, _ = lax.optimization_barrier((own_pair, chip_parts[1]))
    cross_pairs = [hop(sent_pair, 1, CORES * group) for group in range(groups)]
    column, near_parts = lax.optimization_barrier((column, near_parts))
    near_parts = [part.reshape(2, near, half) for part in near_parts]
    crossing = [
        [column if (c, group) == (0, 0) else hop(column, c, CORES * group) for c in range(COLUMNS)]
        for group in range(groups)
    ]

    def rows_out(dtype):
        return pltpu.VMEM((tok_rows, half), dtype)

    def far_out(count):
        return pltpu.VMEM((count,) + own_pair.shape, jnp.bfloat16)

    low = (levels + 1) // 2
    near_pairs = HEADS // CORES * tok_rows * members * near
    far_width = members * seq_count * part_tok
    far_pairs = HEADS // CORES * tok_rows * far_width
    roomy = far_width <= 512
    far_plan = (tok_rows // 2, GROUP, 2 * GROUP) if roomy else (tok_rows // 8, 1, 1)

    near_sum, near_stat, bias, queries, grad_out = call(
        functools.partial(near_forward_kernel, members, blk_len, part_tok, head_dim),
        [pltpu.with_memory_space_constraint(a, pltpu.HBM) for a in (queries, grad_out)] + near_parts,
        [rows_out(jnp.float32)] * 2
        + [pltpu.VMEM((tok_rows, members * near), jnp.float32)]
        + [rows_out(jnp.bfloat16)] * 2,
        near_pairs,
        2,
        head_dim,
        [IN_HBM, IN_HBM] + [WHOLE] * members,
        [pltpu.SemaphoreType.DMA((half // (GROUP * head_dim) + 1,))],
    )
    far_parts = []
    for group, cross_pair in zip(crossing, cross_pairs):
        (same, other), _ = lax.optimization_barrier((group, near_stat))
        far_parts += [own_pair, same, cross_pair, other]
    attended, far_gq, level, drift, own_low, own_high, cross_low, cross_high = call(
        functools.partial(far_kernel, groups, levels, head_dim, *far_plan),
        [queries, grad_out, near_sum, near_stat] + far_parts,
        [rows_out(jnp.bfloat16)]
        + [rows_out(jnp.float32)] * 3
        + [far_out(low), far_out(levels - low)] * COLUMNS,
        far_pairs,
        5,
        head_dim,
    )

    def add(own, cross):
        return (own.astype(jnp.float32) + cross.astype(jnp.float32)).astype(jnp.bfloat16)

    high = hop(cross_high, 1, 0)
    chosen, near_kept, grad_q, sent = call(
        functools.partial(near_backward_kernel, members, head_dim, blocks),
        [block, bias, queries, grad_out, level, drift, far_gq] + near_parts,
        [
            pltpu.VMEM((CORES, 2, part_tok, half), jnp.float32),
            pltpu.VMEM((2 * near, half), jnp.bfloat16),
            rows_out(jnp.bfloat16),
            pltpu.VMEM((2 * near, half), jnp.bfloat16),
        ],
        near_pairs,
        4,
        head_dim,
        scratch=[pltpu.VMEM((CORES, 2, near, half), jnp.float32)],
    )
    att_far = hop(attended, 0, 1)
    high, _, _ = lax.optimization_barrier((high, chosen, att_far))
    sums = [add(own_high[d - low], high[d - low]) for d in range(low, levels)]
    cross_low, _ = lax.optimization_barrier((cross_low, sums))
    crossed = hop(cross_low, 1, 0)
    nothing = high[0, 0, 0, 0][None] * 0
    grad_q = grad_q + nothing
    gq_far = hop(grad_q, 0, 1)
    sent_far = hop(sent + nothing, 0, 1)
    sums = [add(own_low[d], crossed[d]) for d in range(1, low)] + sums
    returned = [sink(part, d) for d, part in enumerate(sums, 1)] + [crossed[0]]
    attended, grad_q, grad_k, grad_v = join(
        [attended, att_far, grad_q, gq_far, near_kept, sent_far],
        [(tok_rows, feat_width)] * 2 + [(near, feat_width)] * 2,
    )
    returned, grad_k, grad_v = lax.optimization_barrier((returned, grad_k, grad_v))
    far_sent = chosen[1] + sum(part[1].astype(jnp.float32) for part in returned)
    far_sent = far_sent.astype(jnp.bfloat16)
    grad_k, grad_v = finish(
        [block, chosen, hop(far_sent, 0, 1)] + returned, [grad_k, grad_v]
    )
    return (attended, grad_q, grad_k.reshape(keys.shape), grad_v.reshape(values.shape))


def solution(mesh):
    return jax.shard_map(
        shards,
        mesh=mesh,
        in_specs=(P("seq", None), P("seq", "kv", None), P("seq", "kv", None), P(), P("seq", None)),
        out_specs=(P("seq", None), P("seq", None), P("seq", "kv", None), P("seq", "kv", None)),
        check_vma=False,
    )
```

```python
import functools
import math

import jax
import jax.numpy as jnp
from jax import lax
from jax.experimental import pallas as pl
from jax.experimental.pallas import tpu as pltpu
from jax.sharding import PartitionSpec as P

HEADS = 8
COLUMNS = 2
CORES = 2
GROUP = 2
SMALL = pl.CostEstimate(flops=0, bytes_accessed=0, transcendentals=0)
HIDDEN = -1e30
NT = (((1,), (1,)), ((), ()))
NN = (((1,), (0,)), ((), ()))
TN = (((0,), (0,)), ((), ()))
IN_HBM = pl.BlockSpec(memory_space=pltpu.HBM)
WHOLE = pl.BlockSpec(memory_space=pltpu.VMEM)
LIMIT = pltpu.CompilerParams(vmem_limit_bytes=12 * 1024 * 1024)


def dot(a, b, dims):
    return lax.dot_general(a, b, dims, preferred_element_type=jnp.float32)


def wide(rows, width):
    return jnp.concatenate([rows] * (width // rows.shape[1]), axis=1)


def base2_scale(head_dim):
    return math.log2(math.e) / math.sqrt(head_dim)


def pick_kernel(table_hbm, keys_hbm, values_hbm, mine_ref, theirs_ref, pair_ref, sent_ref, block_ref, table_ref, sems):
    window = lax.axis_index("seq")
    core = lax.axis_index("kv") % CORES
    _, blocks, part_tok, half = mine_ref.shape
    copies = [pltpu.make_async_copy(table_hbm, table_ref, sems.at[0])]
    for which, ref in enumerate((keys_hbm, values_hbm)):
        for side, out_ref in enumerate((mine_ref, theirs_ref)):
            cols = pl.ds(pl.multiple_of((core ^ side) * half, half), half)
            copies.append(
                pltpu.make_async_copy(ref.at[:, :, cols], out_ref.at[which], sems.at[len(copies)])
            )
    for copy in copies:
        copy.start()
    copies[0].wait()
    pick = jnp.minimum(window, lax.axis_size("seq") - 2)
    entry = lax.broadcasted_iota(jnp.int32, table_ref.shape, 0)
    row = lax.broadcasted_iota(jnp.int32, table_ref.shape, 1)
    here = (entry == pick) & (row == table_ref.shape[1] - 1)
    named = jnp.where(here, table_ref[...].astype(jnp.float32), -1.0)
    named = jnp.max(jnp.max(named, axis=1, keepdims=True), axis=0, keepdims=True)
    block = jnp.clip(named - (window * blocks).astype(jnp.float32), 0.0, blocks - 1.0)
    block_ref[...] = jnp.broadcast_to(block, block_ref.shape)
    block = jnp.broadcast_to(block, (part_tok, half))
    for copy in copies[1:]:
        copy.wait()
    for ref, out_ref in ((mine_ref, pair_ref), (theirs_ref, sent_ref)):
        for which in range(2):
            chosen = ref[which, 0].astype(jnp.float32)
            for b in range(1, blocks):
                chosen = jnp.where(block == b, ref[which, b].astype(jnp.float32), chosen)
            out_ref[which] = chosen.astype(out_ref.dtype)


def pick_pair(table, keys, values):
    blocks, part_tok, feat_width = keys.shape
    half = feat_width // CORES
    operands = [pltpu.with_memory_space_constraint(a, pltpu.HBM) for a in (table, keys, values)]
    return pl.pallas_call(
        pick_kernel,
        in_specs=[IN_HBM] * 3,
        out_specs=[WHOLE] * 5,
        out_shape=[pltpu.VMEM((2, blocks, part_tok, half), keys.dtype)] * 2
        + [pltpu.VMEM((2, part_tok, half), keys.dtype)] * 2
        + [pltpu.VMEM((8, 128), jnp.float32)],
        scratch_shapes=[pltpu.VMEM(table.shape, table.dtype), pltpu.SemaphoreType.DMA((5,))],
    )(*operands)


def join_kernel(att_ref, att_far, gq_ref, gq_far, kept_ref, near_far, att_out, gq_out, gk_out, gv_out, sems):
    core = lax.axis_index("kv") % CORES
    half, near = att_ref.shape[1], gk_out.shape[0]
    gk, gv = pl.ds(0, near), pl.ds(near, near)
    copies = []
    for out_ref, sides in (
        (att_out, (att_ref, att_far)),
        (gq_out, (gq_ref, gq_far)),
        (gk_out, (kept_ref.at[gk], near_far.at[gk])),
        (gv_out, (kept_ref.at[gv], near_far.at[gv])),
    ):
        for side, ref in enumerate(sides):
            cols = pl.ds(pl.multiple_of((core ^ side) * half, half), half)
            copies.append(pltpu.make_async_copy(ref, out_ref.at[:, cols], sems.at[len(copies)]))
    for copy in copies:
        copy.start()
    for copy in copies:
        copy.wait()


def join(operands, shapes):
    operands = [pltpu.with_memory_space_constraint(a, pltpu.VMEM) for a in operands]
    return pl.pallas_call(
        join_kernel,
        in_specs=[WHOLE] * len(operands),
        out_specs=[IN_HBM] * len(shapes),
        out_shape=[pltpu.HBM(shape, jnp.bfloat16) for shape in shapes],
        scratch_shapes=[pltpu.SemaphoreType.DMA((2 * len(shapes),))],
        cost_estimate=SMALL,
    )(*operands)


def finish_kernel(block_ref, chosen_ref, far_ref, *refs):
    arrived, outs, rows_ref, sems = refs[:-6], refs[-4:-2], refs[-2], refs[-1]
    core = lax.axis_index("kv") % CORES
    part_tok, half = far_ref.shape[1:]
    block = jnp.max(block_ref[...]).astype(jnp.int32)
    here = pl.ds(pl.multiple_of(block * part_tok, part_tok), part_tok)
    mine = pl.ds(pl.multiple_of(core * half, half), half)
    theirs = pl.ds(pl.multiple_of((core ^ 1) * half, half), half)
    copies = []
    for which, out_ref in enumerate(outs):
        total = chosen_ref[0, which]
        for ref in arrived:
            total += ref[0, which].astype(jnp.float32)
        rows_ref[which, :, mine] = total.astype(rows_ref.dtype)
        rows_ref[which, :, theirs] = far_ref[which]
        copies.append(pltpu.make_async_copy(rows_ref.at[which], out_ref.at[here], sems.at[which]))
        copies[-1].start()
    for copy in copies:
        copy.wait()


def finish(operands, outs):
    part_tok, half = operands[2].shape[1:]
    operands = [pltpu.with_memory_space_constraint(a, pltpu.VMEM) for a in operands]
    outs = [pltpu.with_memory_space_constraint(a, pltpu.HBM) for a in outs]
    return pl.pallas_call(
        finish_kernel,
        in_specs=[WHOLE] * len(operands) + [IN_HBM] * 2,
        out_specs=[IN_HBM] * 2,
        out_shape=[pltpu.HBM(a.shape, a.dtype) for a in outs],
        input_output_aliases={len(operands): 0, len(operands) + 1: 1},
        scratch_shapes=[
            pltpu.VMEM((2, part_tok, half * CORES), jnp.bfloat16),
            pltpu.SemaphoreType.DMA((2,)),
        ],
        cost_estimate=SMALL,
    )(*operands, *outs)


def near_tiles(rows, near):
    half = rows // 2
    return [(0, half, near // 2), (half, half, near)]


def fill_mask(members, near, blk_len, part_tok, bias_ref):
    member = lax.axis_index("kv")
    shift = part_tok.bit_length() - 1
    for start, count, used in near_tiles(bias_ref.shape[0], near):
        row = start + lax.broadcasted_iota(jnp.int32, (count, 1), 0)
        col = lax.broadcasted_iota(jnp.int32, (1, used), 1)
        key_tok = (col >> shift) * blk_len + (col & (part_tok - 1))
        for j in range(members):
            key_pos = key_tok + (member ^ j) * part_tok
            bias_ref[start : start + count, j * used : (j + 1) * used] = jnp.where(
                key_pos <= row, 0.0, HIDDEN
            )


def head_columns(head, head_dim):
    return pl.ds(pl.multiple_of(head * head_dim, head_dim), head_dim)


def near_rows(parts, which, used, cols):
    return jnp.concatenate([ref[which, :used, cols] for ref in parts], axis=0)


def near_forward_kernel(members, blk_len, part_tok, head_dim, q_hbm, g_hbm, *refs):
    parts, outs = refs[:members], refs[members:]
    out_ref, stat_ref, bias_ref, q_ref, g_ref, sems = outs
    rows, half = q_ref.shape
    near = parts[0].shape[1]
    slab = GROUP * head_dim
    core = lax.axis_index("kv") % CORES

    def fetch(group):
        there = pl.ds(pl.multiple_of(core * half + group * slab, slab), slab)
        here = pl.ds(pl.multiple_of(group * slab, slab), slab)
        return pltpu.make_async_copy(q_hbm.at[:, there], q_ref.at[:, here], sems.at[group])

    there = pl.ds(pl.multiple_of(core * half, half), half)
    last = pltpu.make_async_copy(g_hbm.at[:, there], g_ref, sems.at[half // slab])
    for group in range(half // slab):
        fetch(group).start()
    last.start()
    fill_mask(members, near, blk_len, part_tok, bias_ref)

    @pl.loop(0, half // slab)
    def _(group):
        fetch(group).wait()
        units = [
            (head_columns(group * GROUP + i, head_dim), pl.ds(start, count), used)
            for i in range(GROUP)
            for start, count, used in near_tiles(rows, near)
        ]
        raws = [
            dot(q_ref[here, cols], near_rows(parts, 0, used, cols), NT) * base2_scale(head_dim)
            + bias_ref[here, : members * used]
            for cols, here, used in units
        ]
        peaks = [jnp.max(raw, axis=1, keepdims=True) for raw in raws]
        weights = [jnp.exp2(raw - peak) for raw, peak in zip(raws, peaks)]
        totals = [jnp.sum(weight, axis=1, keepdims=True) for weight in weights]
        sums = [
            dot(weight.astype(jnp.bfloat16), near_rows(parts, 1, used, cols), NN)
            for weight, (cols, here, used) in zip(weights, units)
        ]
        for (cols, here, used), peak, total, summed in zip(units, peaks, totals, sums):
            level = peak + jnp.log2(total)
            stat_ref[here, cols] = jnp.broadcast_to(level, summed.shape)
            out_ref[here, cols] = summed * (1.0 / total)

    last.wait()


def far_rows(parts, which, cols):
    rows = []
    for pair_ref, column_ref in zip(parts[0::2], parts[1::2]):
        steps, cores, _, part_tok, _ = column_ref.shape
        rows.append(pair_ref[:, which, :, cols].reshape(cores * part_tok, cols.size))
        rows.append(column_ref[:, :, which, :, cols].reshape(steps * cores * part_tok, cols.size))
    return jnp.concatenate(rows, axis=0)


def far_kernel(groups, steps, head_dim, tile, heads, batch, q_ref, g_ref, sum_ref, stat_ref, *refs):
    parts = refs[: 2 * COLUMNS * groups]
    att_ref, gq_ref, level_ref, drift_ref, *grad_refs = refs[2 * COLUMNS * groups :]
    _, cores, _, part_tok, _ = grad_refs[0].shape
    rows, half = q_ref.shape
    span = steps * cores * part_tok
    width = COLUMNS * span
    score_scale = 1.0 / math.sqrt(head_dim)
    window = lax.axis_index("seq")
    level, side = window // COLUMNS, window % COLUMNS
    step = lax.broadcasted_iota(jnp.int32, (1, span), 1) >> ((cores * part_tok).bit_length() - 1)
    valid = [(step >= 1) & (step <= level), (step >= 1 - side) & (step <= level)]
    bias = jnp.concatenate([jnp.where(ok, 0.0, HIDDEN) for ok in valid] * groups, axis=1)
    total_width = groups * width

    def work(units, keys, values, key_grads, value_grads):
        raws = [
            dot(q_ref[here, cols], keys[i], NT) * base2_scale(head_dim) + bias
            for i, cols, here in units
        ]
        grad_probs = [dot(g_ref[here, cols], values[i], NT) for i, cols, here in units]
        near_levels = [stat_ref[here, cols] for i, cols, here in units]
        peaks = [
            jnp.maximum(near_level, jnp.max(raw, axis=1, keepdims=True))
            for near_level, raw in zip(near_levels, raws)
        ]
        near_weights = [jnp.exp2(near_level - peak) for near_level, peak in zip(near_levels, peaks)]
        weights = [jnp.exp2(raw - wide(peak, total_width)) for raw, peak in zip(raws, peaks)]
        totals = [
            near_weight + jnp.sum(weight, axis=1, keepdims=True)
            for near_weight, weight in zip(near_weights, weights)
        ]
        inverses = [1.0 / total for total in totals]
        sums = [
            dot(weight.astype(jnp.bfloat16), values[i], NN)
            for weight, (i, cols, here) in zip(weights, units)
        ]
        drifts = []
        for u, (i, cols, here) in enumerate(units):
            summed = sum_ref[here, cols] * near_weights[u] + sums[u]
            attended = (summed * inverses[u]).astype(jnp.bfloat16)
            att_ref[here, cols] = attended
            product = g_ref[here, cols].astype(jnp.float32) * attended.astype(jnp.float32)
            drift = jnp.broadcast_to(jnp.sum(product, axis=1, keepdims=True), product.shape)
            drifts.append(drift)
            level_ref[here, cols] = peaks[u] + jnp.log2(totals[u])
            drift_ref[here, cols] = drift
        moved = [
            weight * (grad_prob - wide(drift, total_width))
            for weight, grad_prob, drift in zip(weights, grad_probs, drifts)
        ]
        factors = [inverse * score_scale for inverse in inverses]
        own_scores = [
            (part[:, :width] * wide(factor, width)).astype(jnp.bfloat16)
            for part, factor in zip(moved, factors)
        ]
        own_probs = [
            (weight[:, :width] * wide(inverse, width)).astype(jnp.bfloat16)
            for weight, inverse in zip(weights, inverses)
        ]
        for u, (i, cols, here) in enumerate(units):
            gq_ref[here, cols] = dot(moved[u].astype(jnp.bfloat16), keys[i], NN) * factors[u]
        for u, (i, cols, here) in enumerate(units):
            key_grads[i].append(dot(own_scores[u], q_ref[here, cols], TN))
            value_grads[i].append(dot(own_probs[u], g_ref[here, cols], TN))

    @pl.loop(0, half // (heads * head_dim))
    def _(group):
        columns = [head_columns(group * heads + i, head_dim) for i in range(heads)]
        units = [
            (i, cols, pl.ds(r, tile)) for i, cols in enumerate(columns) for r in range(0, rows, tile)
        ]
        keys = [far_rows(parts, 0, cols) for cols in columns]
        values = [far_rows(parts, 1, cols) for cols in columns]
        grads = [[[] for _ in columns] for _ in range(2)]
        for first in range(0, len(units), batch):
            work(units[first : first + batch], keys, values, *grads)
        for which, per_head in enumerate(grads):
            for cols, terms in zip(columns, per_head):
                total = functools.reduce(lambda a, b: a + b, terms).astype(jnp.bfloat16)
                start = 0
                for ref in grad_refs:
                    shape = ref.shape[:2] + (part_tok, head_dim)
                    count = math.prod(shape[:3])
                    ref[:, :, which, :, cols] = total[start : start + count].reshape(shape)
                    start += count


def near_backward_kernel(members, head_dim, blocks, block_ref, bias_ref, q_ref, g_ref, level_ref, drift_ref, far_gq_ref, *refs):
    parts, outs = refs[:members], refs[members:]
    chosen_ref, kept_ref, gq_ref, sent_ref, grad_ref = outs
    rows, half = q_ref.shape
    near = parts[0].shape[1]
    score_scale = 1.0 / math.sqrt(head_dim)

    @pl.loop(0, half // (GROUP * head_dim))
    def _(group):
        units = [
            (head_columns(group * GROUP + i, head_dim), pl.ds(start, count), used)
            for i in range(GROUP)
            for start, count, used in near_tiles(rows, near)
        ]
        keys = [near_rows(parts, 0, used, cols) for cols, here, used in units]
        values = [near_rows(parts, 1, used, cols) for cols, here, used in units]
        raws = [
            dot(q_ref[here, cols], key, NT) * base2_scale(head_dim)
            + bias_ref[here, : members * used]
            for (cols, here, used), key in zip(units, keys)
        ]
        grad_probs = [
            dot(g_ref[here, cols], value, NT) for (cols, here, used), value in zip(units, values)
        ]
        probs = [
            jnp.exp2(raw - wide(level_ref[here, cols], raw.shape[1]))
            for raw, (cols, here, used) in zip(raws, units)
        ]
        moved = [
            prob * (grad_prob - wide(drift_ref[here, cols], prob.shape[1]))
            for prob, grad_prob, (cols, here, used) in zip(probs, grad_probs, units)
        ]
        for (cols, here, used), part, key in zip(units, moved, keys):
            gq_ref[here, cols] = (
                dot(part.astype(jnp.bfloat16), key, NN) * score_scale + far_gq_ref[here, cols]
            ).astype(jnp.bfloat16)
        grads = []
        for (cols, here, used), part, prob in zip(units, moved, probs):
            own_score = (part[:, : CORES * used] * score_scale).astype(jnp.bfloat16)
            own_prob = prob[:, : CORES * used].astype(jnp.bfloat16)
            grads.append((dot(own_score, q_ref[here, cols], TN), dot(own_prob, g_ref[here, cols], TN)))
        low = near // 2
        for (cols, _, _), early, late in zip(units[0::2], grads[0::2], grads[1::2]):
            for which in range(2):
                for core in range(CORES):
                    top = late[which][core * near : core * near + low]
                    top += early[which][core * low : (core + 1) * low]
                    bottom = late[which][core * near + low : (core + 1) * near]
                    grad_ref[core, which, :low, cols] = top
                    grad_ref[core, which, low:, cols] = bottom
                    ref, first = (kept_ref, sent_ref)[core], which * near
                    ref[first : first + low, cols] = top.astype(ref.dtype)
                    ref[first + low : first + near, cols] = bottom.astype(ref.dtype)

    part_tok = near // blocks
    block = jnp.max(jnp.max(block_ref[...], axis=1, keepdims=True), axis=0, keepdims=True)
    for core in range(CORES):
        for which in range(2):
            chosen = grad_ref[core, which, :part_tok]
            for b in range(1, blocks):
                rows_b = grad_ref[core, which, b * part_tok : (b + 1) * part_tok]
                chosen = jnp.where(block == b, rows_b, chosen)
            chosen_ref[core, which] = chosen


def call(kernel, operands, outs, pairs, products, head_dim, in_specs=None, scratch=()):
    moved_bytes = sum(a.size * a.dtype.itemsize for a in operands)
    return pl.pallas_call(
        kernel,
        in_specs=in_specs or [WHOLE] * len(operands),
        out_specs=[WHOLE] * len(outs),
        out_shape=outs,
        scratch_shapes=scratch,
        compiler_params=LIMIT,
        cost_estimate=pl.CostEstimate(
            flops=4 * products * pairs * head_dim, bytes_accessed=moved_bytes, transcendentals=pairs
        ),
    )(*operands)


def shards(queries, keys, values, layout, grad_out):
    seq_count = lax.axis_size("seq")
    members = lax.axis_size("kv")
    tok_rows, feat_width = queries.shape
    blocks, part_tok = (keys.shape[0], keys.shape[1])
    blk_len = part_tok * members
    near = blocks * part_tok
    head_dim = feat_width // HEADS
    half = feat_width // CORES
    levels = seq_count // COLUMNS
    groups = members // CORES

    def hop(part, column_step, member_step):
        pairs = [
            (s * members + m, (s ^ column_step) * members + (m ^ member_step))
            for s in range(seq_count)
            for m in range(members)
        ]
        return lax.ppermute(part, ("seq", "kv"), pairs)

    def climb(part, d):
        return lax.ppermute(
            part, "seq", [(s, s + COLUMNS * d) for s in range(seq_count - COLUMNS * d)]
        )

    def sink(part, d):
        return lax.ppermute(
            part, "seq", [(s, s - COLUMNS * d) for s in range(COLUMNS * d, seq_count)]
        )

    mine, theirs, pair_mine, pair_theirs, block = pick_pair(layout.T, keys, values)
    own_pair = jnp.stack([pair_mine, hop(pair_theirs, 0, 1)])
    climbed = [climb(own_pair, d) for d in range(1, levels)]
    column = jnp.stack(climbed)
    chip_parts = [mine, hop(theirs, 0, 1)]
    near_parts = list(chip_parts)
    for group in range(1, groups):
        near_parts += [hop(part, 0, CORES * group) for part in chip_parts]
    sent_pair, _ = lax.optimization_barrier((own_pair, chip_parts[1]))
    cross_pairs = [hop(sent_pair, 1, CORES * group) for group in range(groups)]
    column, near_parts = lax.optimization_barrier((column, near_parts))
    near_parts = [part.reshape(2, near, half) for part in near_parts]
    crossing = [
        [column if (c, group) == (0, 0) else hop(column, c, CORES * group) for c in range(COLUMNS)]
        for group in range(groups)
    ]

    def rows_out(dtype):
        return pltpu.VMEM((tok_rows, half), dtype)

    def far_out(count):
        return pltpu.VMEM((count,) + own_pair.shape, jnp.bfloat16)

    low = 1
    near_pairs = HEADS // CORES * tok_rows * members * near
    far_width = members * seq_count * part_tok
    far_pairs = HEADS // CORES * tok_rows * far_width
    roomy = far_width <= 512
    far_plan = (tok_rows // 2, GROUP, 2 * GROUP) if roomy else (tok_rows // 8, 1, 1)

    near_sum, near_stat, bias, queries, grad_out = call(
        functools.partial(near_forward_kernel, members, blk_len, part_tok, head_dim),
        [pltpu.with_memory_space_constraint(a, pltpu.HBM) for a in (queries, grad_out)] + near_parts,
        [rows_out(jnp.float32)] * 2
        + [pltpu.VMEM((tok_rows, members * near), jnp.float32)]
        + [rows_out(jnp.bfloat16)] * 2,
        near_pairs,
        2,
        head_dim,
        [IN_HBM, IN_HBM] + [WHOLE] * members,
        [pltpu.SemaphoreType.DMA((half // (GROUP * head_dim) + 1,))],
    )
    far_parts = []
    for group, cross_pair in zip(crossing, cross_pairs):
        (same, other), _ = lax.optimization_barrier((group, near_stat))
        far_parts += [own_pair, same, cross_pair, other]
    attended, far_gq, level, drift, own_grad, cross_grad = call(
        functools.partial(far_kernel, groups, levels, head_dim, *far_plan),
        [queries, grad_out, near_sum, near_stat] + far_parts,
        [rows_out(jnp.bfloat16)]
        + [rows_out(jnp.float32)] * 3
        + [far_out(levels)] * COLUMNS,
        far_pairs,
        5,
        head_dim,
    )

    def add(own, cross):
        return (own.astype(jnp.float32) + cross.astype(jnp.float32)).astype(jnp.bfloat16)

    cross_low, cross_high = cross_grad[:low], cross_grad[low:]
    high = hop(cross_high, 1, 0)
    chosen, near_kept, grad_q, sent = call(
        functools.partial(near_backward_kernel, members, head_dim, blocks),
        [block, bias, queries, grad_out, level, drift, far_gq] + near_parts,
        [
            pltpu.VMEM((CORES, 2, part_tok, half), jnp.float32),
            pltpu.VMEM((2 * near, half), jnp.bfloat16),
            rows_out(jnp.bfloat16),
            pltpu.VMEM((2 * near, half), jnp.bfloat16),
        ],
        near_pairs,
        4,
        head_dim,
        scratch=[pltpu.VMEM((CORES, 2, near, half), jnp.float32)],
    )
    att_far = hop(attended, 0, 1)
    high, _, _ = lax.optimization_barrier((high, chosen, att_far))
    sums = [add(own_grad[d], high[d - low]) for d in range(low, levels)]
    cross_low, _ = lax.optimization_barrier((cross_low, sums))
    crossed = hop(cross_low, 1, 0)
    nothing = high[0, 0, 0, 0][None] * 0
    grad_q = grad_q + nothing
    gq_far = hop(grad_q, 0, 1)
    sent_far = hop(sent + nothing, 0, 1)
    sums = [add(own_grad[d], crossed[d]) for d in range(1, low)] + sums
    returned = [sink(part, d) for d, part in enumerate(sums, 1)] + [crossed[0]]
    attended, grad_q, grad_k, grad_v = join(
        [attended, att_far, grad_q, gq_far, near_kept, sent_far],
        [(tok_rows, feat_width)] * 2 + [(near, feat_width)] * 2,
    )
    returned, grad_k, grad_v = lax.optimization_barrier((returned, grad_k, grad_v))
    far_sent = chosen[1] + sum(part[1].astype(jnp.float32) for part in returned)
    far_sent = far_sent.astype(jnp.bfloat16)
    grad_k, grad_v = finish(
        [block, chosen, hop(far_sent, 0, 1)] + returned, [grad_k, grad_v]
    )
    return (attended, grad_q, grad_k.reshape(keys.shape), grad_v.reshape(values.shape))


def solution(mesh):
    return jax.shard_map(
        shards,
        mesh=mesh,
        in_specs=(P("seq", None), P("seq", "kv", None), P("seq", "kv", None), P(), P("seq", None)),
        out_specs=(P("seq", None), P("seq", None), P("seq", "kv", None), P("seq", "kv", None)),
        check_vma=False,
    )
```

```python
import functools
import math

import jax
import jax.numpy as jnp
from jax import lax
from jax.experimental import pallas as pl
from jax.experimental.pallas import tpu as pltpu
from jax.sharding import PartitionSpec as P

HEADS = 8
COLUMNS = 2
CORES = 2
GROUP = 2
SMALL = pl.CostEstimate(flops=0, bytes_accessed=0, transcendentals=0)
HIDDEN = -1e30
NT = (((1,), (1,)), ((), ()))
NN = (((1,), (0,)), ((), ()))
TN = (((0,), (0,)), ((), ()))
IN_HBM = pl.BlockSpec(memory_space=pltpu.HBM)
WHOLE = pl.BlockSpec(memory_space=pltpu.VMEM)
LIMIT = pltpu.CompilerParams(vmem_limit_bytes=12 * 1024 * 1024)


def dot(a, b, dims):
    return lax.dot_general(a, b, dims, preferred_element_type=jnp.float32)


def wide(rows, width):
    return jnp.concatenate([rows] * (width // rows.shape[1]), axis=1)


def base2_scale(head_dim):
    return math.log2(math.e) / math.sqrt(head_dim)


def pick_kernel(table_hbm, keys_hbm, values_hbm, mine_ref, theirs_ref, pair_ref, sent_ref, block_ref, table_ref, sems):
    window = lax.axis_index("seq")
    core = lax.axis_index("kv") % CORES
    _, blocks, part_tok, half = mine_ref.shape
    copies = [pltpu.make_async_copy(table_hbm, table_ref, sems.at[0])]
    for which, ref in enumerate((keys_hbm, values_hbm)):
        for side, out_ref in enumerate((mine_ref, theirs_ref)):
            cols = pl.ds(pl.multiple_of((core ^ side) * half, half), half)
            copies.append(
                pltpu.make_async_copy(ref.at[:, :, cols], out_ref.at[which], sems.at[len(copies)])
            )
    for copy in copies:
        copy.start()
    copies[0].wait()
    pick = jnp.minimum(window, lax.axis_size("seq") - 2)
    entry = lax.broadcasted_iota(jnp.int32, table_ref.shape, 0)
    row = lax.broadcasted_iota(jnp.int32, table_ref.shape, 1)
    here = (entry == pick) & (row == table_ref.shape[1] - 1)
    named = jnp.where(here, table_ref[...].astype(jnp.float32), -1.0)
    named = jnp.max(jnp.max(named, axis=1, keepdims=True), axis=0, keepdims=True)
    block = jnp.clip(named - (window * blocks).astype(jnp.float32), 0.0, blocks - 1.0)
    block_ref[...] = jnp.broadcast_to(block, block_ref.shape)
    block = jnp.broadcast_to(block, (part_tok, half))
    for copy in copies[1:]:
        copy.wait()
    for ref, out_ref in ((mine_ref, pair_ref), (theirs_ref, sent_ref)):
        for which in range(2):
            chosen = ref[which, 0].astype(jnp.float32)
            for b in range(1, blocks):
                chosen = jnp.where(block == b, ref[which, b].astype(jnp.float32), chosen)
            out_ref[which] = chosen.astype(out_ref.dtype)


def pick_pair(table, keys, values):
    blocks, part_tok, feat_width = keys.shape
    half = feat_width // CORES
    operands = [pltpu.with_memory_space_constraint(a, pltpu.HBM) for a in (table, keys, values)]
    return pl.pallas_call(
        pick_kernel,
        in_specs=[IN_HBM] * 3,
        out_specs=[WHOLE] * 5,
        out_shape=[pltpu.VMEM((2, blocks, part_tok, half), keys.dtype)] * 2
        + [pltpu.VMEM((2, part_tok, half), keys.dtype)] * 2
        + [pltpu.VMEM((8, 128), jnp.float32)],
        scratch_shapes=[pltpu.VMEM(table.shape, table.dtype), pltpu.SemaphoreType.DMA((5,))],
    )(*operands)


def join_kernel(att_ref, att_far, gq_ref, gq_far, kept_ref, near_far, att_out, gq_out, gk_out, gv_out, sems):
    core = lax.axis_index("kv") % CORES
    half, near = att_ref.shape[1], gk_out.shape[0]
    gk, gv = pl.ds(0, near), pl.ds(near, near)
    copies = []
    for out_ref, sides in (
        (att_out, (att_ref, att_far)),
        (gq_out, (gq_ref, gq_far)),
        (gk_out, (kept_ref.at[gk], near_far.at[gk])),
        (gv_out, (kept_ref.at[gv], near_far.at[gv])),
    ):
        for side, ref in enumerate(sides):
            cols = pl.ds(pl.multiple_of((core ^ side) * half, half), half)
            copies.append(pltpu.make_async_copy(ref, out_ref.at[:, cols], sems.at[len(copies)]))
    for copy in copies:
        copy.start()
    for copy in copies:
        copy.wait()


def join(operands, shapes):
    operands = [pltpu.with_memory_space_constraint(a, pltpu.VMEM) for a in operands]
    return pl.pallas_call(
        join_kernel,
        in_specs=[WHOLE] * len(operands),
        out_specs=[IN_HBM] * len(shapes),
        out_shape=[pltpu.HBM(shape, jnp.bfloat16) for shape in shapes],
        scratch_shapes=[pltpu.SemaphoreType.DMA((2 * len(shapes),))],
        cost_estimate=SMALL,
    )(*operands)


def finish_kernel(block_ref, chosen_ref, far_ref, *refs):
    arrived, outs, rows_ref, sems = refs[:-6], refs[-4:-2], refs[-2], refs[-1]
    core = lax.axis_index("kv") % CORES
    part_tok, half = far_ref.shape[1:]
    block = jnp.max(block_ref[...]).astype(jnp.int32)
    here = pl.ds(pl.multiple_of(block * part_tok, part_tok), part_tok)
    mine = pl.ds(pl.multiple_of(core * half, half), half)
    theirs = pl.ds(pl.multiple_of((core ^ 1) * half, half), half)
    copies = []
    for which, out_ref in enumerate(outs):
        total = chosen_ref[0, which]
        for ref in arrived:
            total += ref[0, which].astype(jnp.float32)
        rows_ref[which, :, mine] = total.astype(rows_ref.dtype)
        rows_ref[which, :, theirs] = far_ref[which]
        copies.append(pltpu.make_async_copy(rows_ref.at[which], out_ref.at[here], sems.at[which]))
        copies[-1].start()
    for copy in copies:
        copy.wait()


def finish(operands, outs):
    part_tok, half = operands[2].shape[1:]
    operands = [pltpu.with_memory_space_constraint(a, pltpu.VMEM) for a in operands]
    outs = [pltpu.with_memory_space_constraint(a, pltpu.HBM) for a in outs]
    return pl.pallas_call(
        finish_kernel,
        in_specs=[WHOLE] * len(operands) + [IN_HBM] * 2,
        out_specs=[IN_HBM] * 2,
        out_shape=[pltpu.HBM(a.shape, a.dtype) for a in outs],
        input_output_aliases={len(operands): 0, len(operands) + 1: 1},
        scratch_shapes=[
            pltpu.VMEM((2, part_tok, half * CORES), jnp.bfloat16),
            pltpu.SemaphoreType.DMA((2,)),
        ],
        cost_estimate=SMALL,
    )(*operands, *outs)


def near_tiles(rows, near):
    half = rows // 2
    return [(0, half, near // 2), (half, half, near)]


def fill_mask(members, near, blk_len, part_tok, bias_ref):
    member = lax.axis_index("kv")
    shift = part_tok.bit_length() - 1
    for start, count, used in near_tiles(bias_ref.shape[0], near):
        row = start + lax.broadcasted_iota(jnp.int32, (count, 1), 0)
        col = lax.broadcasted_iota(jnp.int32, (1, used), 1)
        key_tok = (col >> shift) * blk_len + (col & (part_tok - 1))
        for j in range(members):
            key_pos = key_tok + (member ^ j) * part_tok
            bias_ref[start : start + count, j * used : (j + 1) * used] = jnp.where(
                key_pos <= row, 0.0, HIDDEN
            )


def head_columns(head, head_dim):
    return pl.ds(pl.multiple_of(head * head_dim, head_dim), head_dim)


def near_rows(parts, which, used, cols):
    return jnp.concatenate([ref[which, :used, cols] for ref in parts], axis=0)


def near_forward_kernel(members, blk_len, part_tok, head_dim, q_hbm, g_hbm, *refs):
    parts, outs = refs[:members], refs[members:]
    out_ref, stat_ref, bias_ref, q_ref, g_ref, sems = outs
    rows, half = q_ref.shape
    near = parts[0].shape[1]
    slab = GROUP * head_dim
    core = lax.axis_index("kv") % CORES

    def fetch(group):
        there = pl.ds(pl.multiple_of(core * half + group * slab, slab), slab)
        here = pl.ds(pl.multiple_of(group * slab, slab), slab)
        return pltpu.make_async_copy(q_hbm.at[:, there], q_ref.at[:, here], sems.at[group])

    there = pl.ds(pl.multiple_of(core * half, half), half)
    last = pltpu.make_async_copy(g_hbm.at[:, there], g_ref, sems.at[half // slab])
    for group in range(half // slab):
        fetch(group).start()
    last.start()
    fill_mask(members, near, blk_len, part_tok, bias_ref)

    @pl.loop(0, half // slab)
    def _(group):
        fetch(group).wait()
        units = [
            (head_columns(group * GROUP + i, head_dim), pl.ds(start, count), used)
            for i in range(GROUP)
            for start, count, used in near_tiles(rows, near)
        ]
        raws = [
            dot(q_ref[here, cols], near_rows(parts, 0, used, cols), NT) * base2_scale(head_dim)
            + bias_ref[here, : members * used]
            for cols, here, used in units
        ]
        peaks = [jnp.max(raw, axis=1, keepdims=True) for raw in raws]
        weights = [jnp.exp2(raw - peak) for raw, peak in zip(raws, peaks)]
        totals = [jnp.sum(weight, axis=1, keepdims=True) for weight in weights]
        sums = [
            dot(weight.astype(jnp.bfloat16), near_rows(parts, 1, used, cols), NN)
            for weight, (cols, here, used) in zip(weights, units)
        ]
        for (cols, here, used), peak, total, summed in zip(units, peaks, totals, sums):
            level = peak + jnp.log2(total)
            stat_ref[here, cols] = jnp.broadcast_to(level, summed.shape)
            out_ref[here, cols] = summed * (1.0 / total)

    last.wait()


def far_rows(parts, which, cols):
    rows = []
    for pair_ref, column_ref in zip(parts[0::2], parts[1::2]):
        steps, cores, _, part_tok, _ = column_ref.shape
        rows.append(pair_ref[:, which, :, cols].reshape(cores * part_tok, cols.size))
        rows.append(column_ref[:, :, which, :, cols].reshape(steps * cores * part_tok, cols.size))
    return jnp.concatenate(rows, axis=0)


def far_kernel(groups, steps, head_dim, tile, heads, batch, q_ref, g_ref, sum_ref, stat_ref, *refs):
    parts = refs[: 2 * COLUMNS * groups]
    att_ref, gq_ref, level_ref, drift_ref, *grad_refs = refs[2 * COLUMNS * groups :]
    _, cores, _, part_tok, _ = grad_refs[0].shape
    rows, half = q_ref.shape
    span = steps * cores * part_tok
    width = COLUMNS * span
    score_scale = 1.0 / math.sqrt(head_dim)
    window = lax.axis_index("seq")
    level, side = window // COLUMNS, window % COLUMNS
    step = lax.broadcasted_iota(jnp.int32, (1, span), 1) >> ((cores * part_tok).bit_length() - 1)
    valid = [(step >= 1) & (step <= level), (step >= 1 - side) & (step <= level)]
    bias = jnp.concatenate([jnp.where(ok, 0.0, HIDDEN) for ok in valid] * groups, axis=1)
    total_width = groups * width

    def work(units, keys, values, key_grads, value_grads):
        raws = [
            dot(q_ref[here, cols], keys[i], NT) * base2_scale(head_dim) + bias
            for i, cols, here in units
        ]
        grad_probs = [dot(g_ref[here, cols], values[i], NT) for i, cols, here in units]
        near_levels = [stat_ref[here, cols] for i, cols, here in units]
        peaks = [
            jnp.maximum(near_level, jnp.max(raw, axis=1, keepdims=True))
            for near_level, raw in zip(near_levels, raws)
        ]
        near_weights = [jnp.exp2(near_level - peak) for near_level, peak in zip(near_levels, peaks)]
        weights = [jnp.exp2(raw - wide(peak, total_width)) for raw, peak in zip(raws, peaks)]
        totals = [
            near_weight + jnp.sum(weight, axis=1, keepdims=True)
            for near_weight, weight in zip(near_weights, weights)
        ]
        inverses = [1.0 / total for total in totals]
        sums = [
            dot(weight.astype(jnp.bfloat16), values[i], NN)
            for weight, (i, cols, here) in zip(weights, units)
        ]
        drifts = []
        for u, (i, cols, here) in enumerate(units):
            summed = sum_ref[here, cols] * near_weights[u] + sums[u]
            attended = (summed * inverses[u]).astype(jnp.bfloat16)
            att_ref[here, cols] = attended
            product = g_ref[here, cols].astype(jnp.float32) * attended.astype(jnp.float32)
            drift = jnp.broadcast_to(jnp.sum(product, axis=1, keepdims=True), product.shape)
            drifts.append(drift)
            level_ref[here, cols] = peaks[u] + jnp.log2(totals[u])
            drift_ref[here, cols] = drift
        moved = [
            weight * (grad_prob - wide(drift, total_width))
            for weight, grad_prob, drift in zip(weights, grad_probs, drifts)
        ]
        factors = [inverse * score_scale for inverse in inverses]
        own_scores = [
            (part[:, :width] * wide(factor, width)).astype(jnp.bfloat16)
            for part, factor in zip(moved, factors)
        ]
        own_probs = [
            (weight[:, :width] * wide(inverse, width)).astype(jnp.bfloat16)
            for weight, inverse in zip(weights, inverses)
        ]
        for u, (i, cols, here) in enumerate(units):
            gq_ref[here, cols] = dot(moved[u].astype(jnp.bfloat16), keys[i], NN) * factors[u]
        for u, (i, cols, here) in enumerate(units):
            key_grads[i].append(dot(own_scores[u], q_ref[here, cols], TN))
            value_grads[i].append(dot(own_probs[u], g_ref[here, cols], TN))

    @pl.loop(0, half // (heads * head_dim))
    def _(group):
        columns = [head_columns(group * heads + i, head_dim) for i in range(heads)]
        units = [
            (i, cols, pl.ds(r, tile)) for i, cols in enumerate(columns) for r in range(0, rows, tile)
        ]
        keys = [far_rows(parts, 0, cols) for cols in columns]
        values = [far_rows(parts, 1, cols) for cols in columns]
        grads = [[[] for _ in columns] for _ in range(2)]
        for first in range(0, len(units), batch):
            work(units[first : first + batch], keys, values, *grads)
        for which, per_head in enumerate(grads):
            for cols, terms in zip(columns, per_head):
                total = functools.reduce(lambda a, b: a + b, terms).astype(jnp.bfloat16)
                start = 0
                for ref in grad_refs:
                    shape = ref.shape[:2] + (part_tok, head_dim)
                    count = math.prod(shape[:3])
                    ref[:, :, which, :, cols] = total[start : start + count].reshape(shape)
                    start += count


def near_backward_kernel(members, head_dim, blocks, block_ref, bias_ref, q_ref, g_ref, level_ref, drift_ref, far_gq_ref, *refs):
    parts, outs = refs[:members], refs[members:]
    chosen_ref, kept_ref, gq_ref, sent_ref, grad_ref = outs
    rows, half = q_ref.shape
    near = parts[0].shape[1]
    score_scale = 1.0 / math.sqrt(head_dim)

    @pl.loop(0, half // (GROUP * head_dim))
    def _(group):
        units = [
            (head_columns(group * GROUP + i, head_dim), pl.ds(start, count), used)
            for i in range(GROUP)
            for start, count, used in near_tiles(rows, near)
        ]
        keys = [near_rows(parts, 0, used, cols) for cols, here, used in units]
        values = [near_rows(parts, 1, used, cols) for cols, here, used in units]
        raws = [
            dot(q_ref[here, cols], key, NT) * base2_scale(head_dim)
            + bias_ref[here, : members * used]
            for (cols, here, used), key in zip(units, keys)
        ]
        grad_probs = [
            dot(g_ref[here, cols], value, NT) for (cols, here, used), value in zip(units, values)
        ]
        probs = [
            jnp.exp2(raw - wide(level_ref[here, cols], raw.shape[1]))
            for raw, (cols, here, used) in zip(raws, units)
        ]
        moved = [
            prob * (grad_prob - wide(drift_ref[here, cols], prob.shape[1]))
            for prob, grad_prob, (cols, here, used) in zip(probs, grad_probs, units)
        ]
        for (cols, here, used), part, key in zip(units, moved, keys):
            gq_ref[here, cols] = (
                dot(part.astype(jnp.bfloat16), key, NN) * score_scale + far_gq_ref[here, cols]
            ).astype(jnp.bfloat16)
        grads = []
        for (cols, here, used), part, prob in zip(units, moved, probs):
            own_score = (part[:, : CORES * used] * score_scale).astype(jnp.bfloat16)
            own_prob = prob[:, : CORES * used].astype(jnp.bfloat16)
            grads.append((dot(own_score, q_ref[here, cols], TN), dot(own_prob, g_ref[here, cols], TN)))
        low = near // 2
        for (cols, _, _), early, late in zip(units[0::2], grads[0::2], grads[1::2]):
            for which in range(2):
                for core in range(CORES):
                    top = late[which][core * near : core * near + low]
                    top += early[which][core * low : (core + 1) * low]
                    bottom = late[which][core * near + low : (core + 1) * near]
                    grad_ref[core, which, :low, cols] = top
                    grad_ref[core, which, low:, cols] = bottom
                    ref, first = (kept_ref, sent_ref)[core], which * near
                    ref[first : first + low, cols] = top.astype(ref.dtype)
                    ref[first + low : first + near, cols] = bottom.astype(ref.dtype)

    part_tok = near // blocks
    block = jnp.max(jnp.max(block_ref[...], axis=1, keepdims=True), axis=0, keepdims=True)
    for core in range(CORES):
        for which in range(2):
            chosen = grad_ref[core, which, :part_tok]
            for b in range(1, blocks):
                rows_b = grad_ref[core, which, b * part_tok : (b + 1) * part_tok]
                chosen = jnp.where(block == b, rows_b, chosen)
            chosen_ref[core, which] = chosen


def call(kernel, operands, outs, pairs, products, head_dim, in_specs=None, scratch=()):
    moved_bytes = sum(a.size * a.dtype.itemsize for a in operands)
    return pl.pallas_call(
        kernel,
        in_specs=in_specs or [WHOLE] * len(operands),
        out_specs=[WHOLE] * len(outs),
        out_shape=outs,
        scratch_shapes=scratch,
        compiler_params=LIMIT,
        cost_estimate=pl.CostEstimate(
            flops=4 * products * pairs * head_dim, bytes_accessed=moved_bytes, transcendentals=pairs
        ),
    )(*operands)


def shards(queries, keys, values, layout, grad_out):
    seq_count = lax.axis_size("seq")
    members = lax.axis_size("kv")
    tok_rows, feat_width = queries.shape
    blocks, part_tok = (keys.shape[0], keys.shape[1])
    blk_len = part_tok * members
    near = blocks * part_tok
    head_dim = feat_width // HEADS
    half = feat_width // CORES
    levels = seq_count // COLUMNS
    groups = members // CORES

    def hop(part, column_step, member_step):
        pairs = [
            (s * members + m, (s ^ column_step) * members + (m ^ member_step))
            for s in range(seq_count)
            for m in range(members)
        ]
        return lax.ppermute(part, ("seq", "kv"), pairs)

    def climb(part, d):
        return lax.ppermute(
            part, "seq", [(s, s + COLUMNS * d) for s in range(seq_count - COLUMNS * d)]
        )

    def sink(part, d):
        return lax.ppermute(
            part, "seq", [(s, s - COLUMNS * d) for s in range(COLUMNS * d, seq_count)]
        )

    mine, theirs, pair_mine, pair_theirs, block = pick_pair(layout.T, keys, values)
    own_pair = jnp.stack([pair_mine, hop(pair_theirs, 0, 1)])
    climbed = [climb(own_pair, d) for d in range(1, levels)]
    column = jnp.stack(climbed)
    chip_parts = [mine, hop(theirs, 0, 1)]
    near_parts = list(chip_parts)
    for group in range(1, groups):
        near_parts += [hop(part, 0, CORES * group) for part in chip_parts]
    sent_pair, _ = lax.optimization_barrier((own_pair, chip_parts[1]))
    cross_pairs = [hop(sent_pair, 1, CORES * group) for group in range(groups)]
    column, near_parts = lax.optimization_barrier((column, near_parts))
    near_parts = [part.reshape(2, near, half) for part in near_parts]
    crossing = [
        [column if (c, group) == (0, 0) else hop(column, c, CORES * group) for c in range(COLUMNS)]
        for group in range(groups)
    ]

    def rows_out(dtype):
        return pltpu.VMEM((tok_rows, half), dtype)

    def far_out(count):
        return pltpu.VMEM((count,) + own_pair.shape, jnp.bfloat16)

    low = 1
    near_pairs = HEADS // CORES * tok_rows * members * near
    far_width = members * seq_count * part_tok
    far_pairs = HEADS // CORES * tok_rows * far_width
    roomy = far_width <= 512
    far_plan = (tok_rows // 2, GROUP, 2 * GROUP) if roomy else (tok_rows // 8, 1, 1)

    near_sum, near_stat, bias, queries, grad_out = call(
        functools.partial(near_forward_kernel, members, blk_len, part_tok, head_dim),
        [pltpu.with_memory_space_constraint(a, pltpu.HBM) for a in (queries, grad_out)] + near_parts,
        [rows_out(jnp.float32)] * 2
        + [pltpu.VMEM((tok_rows, members * near), jnp.float32)]
        + [rows_out(jnp.bfloat16)] * 2,
        near_pairs,
        2,
        head_dim,
        [IN_HBM, IN_HBM] + [WHOLE] * members,
        [pltpu.SemaphoreType.DMA((half // (GROUP * head_dim) + 1,))],
    )
    far_parts = []
    for group, cross_pair in zip(crossing, cross_pairs):
        (same, other), _ = lax.optimization_barrier((group, near_stat))
        far_parts += [own_pair, same, cross_pair, other]
    attended, far_gq, level, drift, own_grad, cross_grad = call(
        functools.partial(far_kernel, groups, levels, head_dim, *far_plan),
        [queries, grad_out, near_sum, near_stat] + far_parts,
        [rows_out(jnp.bfloat16)]
        + [rows_out(jnp.float32)] * 3
        + [far_out(levels)] * COLUMNS,
        far_pairs,
        5,
        head_dim,
    )

    def add(own, cross):
        return (own.astype(jnp.float32) + cross.astype(jnp.float32)).astype(jnp.bfloat16)

    cross_low, cross_high = cross_grad[:low], cross_grad[low:]
    high = hop(cross_high, 1, 0)
    chosen, near_kept, grad_q, sent = call(
        functools.partial(near_backward_kernel, members, head_dim, blocks),
        [block, bias, queries, grad_out, level, drift, far_gq] + near_parts,
        [
            pltpu.VMEM((CORES, 2, part_tok, half), jnp.float32),
            pltpu.VMEM((2 * near, half), jnp.bfloat16),
            rows_out(jnp.bfloat16),
            pltpu.VMEM((2 * near, half), jnp.bfloat16),
        ],
        near_pairs,
        4,
        head_dim,
        scratch=[pltpu.VMEM((CORES, 2, near, half), jnp.float32)],
    )
    att_far = hop(attended, 0, 1)
    high, _, _ = lax.optimization_barrier((high, chosen, att_far))
    sums = [add(own_grad[d], high[d - low]) for d in range(low, levels)]
    nothing = high[0, 0, 0, 0][None] * 0
    grad_q = grad_q + nothing
    gq_far = hop(grad_q, 0, 1)
    sent_far = hop(sent + nothing, 0, 1)
    cross_low, _ = lax.optimization_barrier((cross_low, sent_far))
    crossed = hop(cross_low, 1, 0)
    sums = [add(own_grad[d], crossed[d]) for d in range(1, low)] + sums
    returned = [sink(part, d) for d, part in enumerate(sums, 1)] + [crossed[0]]
    attended, grad_q, grad_k, grad_v = join(
        [attended, att_far, grad_q, gq_far, near_kept, sent_far],
        [(tok_rows, feat_width)] * 2 + [(near, feat_width)] * 2,
    )
    returned, grad_k, grad_v = lax.optimization_barrier((returned, grad_k, grad_v))
    far_sent = chosen[1] + sum(part[1].astype(jnp.float32) for part in returned)
    far_sent = far_sent.astype(jnp.bfloat16)
    grad_k, grad_v = finish(
        [block, chosen, hop(far_sent, 0, 1)] + returned, [grad_k, grad_v]
    )
    return (attended, grad_q, grad_k.reshape(keys.shape), grad_v.reshape(values.shape))


def solution(mesh):
    return jax.shard_map(
        shards,
        mesh=mesh,
        in_specs=(P("seq", None), P("seq", "kv", None), P("seq", "kv", None), P(), P("seq", None)),
        out_specs=(P("seq", None), P("seq", None), P("seq", "kv", None), P("seq", "kv", None)),
        check_vma=False,
    )
```

```python
import functools
import math

import jax
import jax.numpy as jnp
from jax import lax
from jax.experimental import pallas as pl
from jax.experimental.pallas import tpu as pltpu
from jax.sharding import PartitionSpec as P

HEADS = 8
COLUMNS = 2
CORES = 2
GROUP = 2
SMALL = pl.CostEstimate(flops=0, bytes_accessed=0, transcendentals=0)
HIDDEN = -1e30
NT = (((1,), (1,)), ((), ()))
NN = (((1,), (0,)), ((), ()))
TN = (((0,), (0,)), ((), ()))
IN_HBM = pl.BlockSpec(memory_space=pltpu.HBM)
WHOLE = pl.BlockSpec(memory_space=pltpu.VMEM)
LIMIT = pltpu.CompilerParams(vmem_limit_bytes=12 * 1024 * 1024)


def dot(a, b, dims):
    return lax.dot_general(a, b, dims, preferred_element_type=jnp.float32)


def wide(rows, width):
    return jnp.concatenate([rows] * (width // rows.shape[1]), axis=1)


def base2_scale(head_dim):
    return math.log2(math.e) / math.sqrt(head_dim)


def pick_kernel(table_hbm, keys_hbm, values_hbm, mine_ref, theirs_ref, pair_ref, sent_ref, block_ref, table_ref, sems):
    window = lax.axis_index("seq")
    core = lax.axis_index("kv") % CORES
    _, blocks, part_tok, half = mine_ref.shape
    copies = [pltpu.make_async_copy(table_hbm, table_ref, sems.at[0])]
    for which, ref in enumerate((keys_hbm, values_hbm)):
        for side, out_ref in enumerate((mine_ref, theirs_ref)):
            cols = pl.ds(pl.multiple_of((core ^ side) * half, half), half)
            copies.append(
                pltpu.make_async_copy(ref.at[:, :, cols], out_ref.at[which], sems.at[len(copies)])
            )
    for copy in copies:
        copy.start()
    copies[0].wait()
    pick = jnp.minimum(window, lax.axis_size("seq") - 2)
    entry = lax.broadcasted_iota(jnp.int32, table_ref.shape, 0)
    row = lax.broadcasted_iota(jnp.int32, table_ref.shape, 1)
    here = (entry == pick) & (row == table_ref.shape[1] - 1)
    named = jnp.where(here, table_ref[...].astype(jnp.float32), -1.0)
    named = jnp.max(jnp.max(named, axis=1, keepdims=True), axis=0, keepdims=True)
    block = jnp.clip(named - (window * blocks).astype(jnp.float32), 0.0, blocks - 1.0)
    block_ref[...] = jnp.broadcast_to(block, block_ref.shape)
    block = jnp.broadcast_to(block, (part_tok, half))
    for copy in copies[1:]:
        copy.wait()
    for ref, out_ref in ((mine_ref, pair_ref), (theirs_ref, sent_ref)):
        for which in range(2):
            chosen = ref[which, 0].astype(jnp.float32)
            for b in range(1, blocks):
                chosen = jnp.where(block == b, ref[which, b].astype(jnp.float32), chosen)
            out_ref[which] = chosen.astype(out_ref.dtype)


def pick_pair(table, keys, values):
    blocks, part_tok, feat_width = keys.shape
    half = feat_width // CORES
    operands = [pltpu.with_memory_space_constraint(a, pltpu.HBM) for a in (table, keys, values)]
    return pl.pallas_call(
        pick_kernel,
        in_specs=[IN_HBM] * 3,
        out_specs=[WHOLE] * 5,
        out_shape=[pltpu.VMEM((2, blocks, part_tok, half), keys.dtype)] * 2
        + [pltpu.VMEM((2, part_tok, half), keys.dtype)] * 2
        + [pltpu.VMEM((8, 128), jnp.float32)],
        scratch_shapes=[pltpu.VMEM(table.shape, table.dtype), pltpu.SemaphoreType.DMA((5,))],
    )(*operands)


def join_kernel(att_ref, att_far, gq_ref, gq_far, kept_ref, near_far, att_out, gq_out, gk_out, gv_out, sems):
    core = lax.axis_index("kv") % CORES
    half, near = att_ref.shape[1], gk_out.shape[0]
    gk, gv = pl.ds(0, near), pl.ds(near, near)
    copies = []
    for out_ref, sides in (
        (att_out, (att_ref, att_far)),
        (gq_out, (gq_ref, gq_far)),
        (gk_out, (kept_ref.at[gk], near_far.at[gk])),
        (gv_out, (kept_ref.at[gv], near_far.at[gv])),
    ):
        for side, ref in enumerate(sides):
            cols = pl.ds(pl.multiple_of((core ^ side) * half, half), half)
            copies.append(pltpu.make_async_copy(ref, out_ref.at[:, cols], sems.at[len(copies)]))
    for copy in copies:
        copy.start()
    for copy in copies:
        copy.wait()


def join(operands, shapes):
    operands = [pltpu.with_memory_space_constraint(a, pltpu.VMEM) for a in operands]
    return pl.pallas_call(
        join_kernel,
        in_specs=[WHOLE] * len(operands),
        out_specs=[IN_HBM] * len(shapes),
        out_shape=[pltpu.HBM(shape, jnp.bfloat16) for shape in shapes],
        scratch_shapes=[pltpu.SemaphoreType.DMA((2 * len(shapes),))],
        cost_estimate=SMALL,
    )(*operands)


def finish_kernel(block_ref, chosen_ref, far_ref, *refs):
    arrived, outs, rows_ref, sems = refs[:-6], refs[-4:-2], refs[-2], refs[-1]
    core = lax.axis_index("kv") % CORES
    part_tok, half = far_ref.shape[1:]
    block = jnp.max(block_ref[...]).astype(jnp.int32)
    here = pl.ds(pl.multiple_of(block * part_tok, part_tok), part_tok)
    mine = pl.ds(pl.multiple_of(core * half, half), half)
    theirs = pl.ds(pl.multiple_of((core ^ 1) * half, half), half)
    copies = []
    for which, out_ref in enumerate(outs):
        total = chosen_ref[0, which]
        for ref in arrived:
            total += ref[0, which].astype(jnp.float32)
        rows_ref[which, :, mine] = total.astype(rows_ref.dtype)
        rows_ref[which, :, theirs] = far_ref[which]
        copies.append(pltpu.make_async_copy(rows_ref.at[which], out_ref.at[here], sems.at[which]))
        copies[-1].start()
    for copy in copies:
        copy.wait()


def finish(operands, outs):
    part_tok, half = operands[2].shape[1:]
    operands = [pltpu.with_memory_space_constraint(a, pltpu.VMEM) for a in operands]
    outs = [pltpu.with_memory_space_constraint(a, pltpu.HBM) for a in outs]
    return pl.pallas_call(
        finish_kernel,
        in_specs=[WHOLE] * len(operands) + [IN_HBM] * 2,
        out_specs=[IN_HBM] * 2,
        out_shape=[pltpu.HBM(a.shape, a.dtype) for a in outs],
        input_output_aliases={len(operands): 0, len(operands) + 1: 1},
        scratch_shapes=[
            pltpu.VMEM((2, part_tok, half * CORES), jnp.bfloat16),
            pltpu.SemaphoreType.DMA((2,)),
        ],
        cost_estimate=SMALL,
    )(*operands, *outs)


def near_tiles(rows, near):
    half = rows // 2
    return [(0, half, near // 2), (half, half, near)]


def fill_mask(members, near, blk_len, part_tok, bias_ref):
    member = lax.axis_index("kv")
    shift = part_tok.bit_length() - 1
    for start, count, used in near_tiles(bias_ref.shape[0], near):
        row = start + lax.broadcasted_iota(jnp.int32, (count, 1), 0)
        col = lax.broadcasted_iota(jnp.int32, (1, used), 1)
        key_tok = (col >> shift) * blk_len + (col & (part_tok - 1))
        for j in range(members):
            key_pos = key_tok + (member ^ j) * part_tok
            bias_ref[start : start + count, j * used : (j + 1) * used] = jnp.where(
                key_pos <= row, 0.0, HIDDEN
            )


def head_columns(head, head_dim):
    return pl.ds(pl.multiple_of(head * head_dim, head_dim), head_dim)


def near_rows(parts, which, used, cols):
    return jnp.concatenate([ref[which, :used, cols] for ref in parts], axis=0)


def near_forward_kernel(members, blk_len, part_tok, head_dim, q_hbm, g_hbm, *refs):
    parts, outs = refs[:members], refs[members:]
    out_ref, stat_ref, bias_ref, q_ref, g_ref, sems = outs
    rows, half = q_ref.shape
    near = parts[0].shape[1]
    slab = GROUP * head_dim
    core = lax.axis_index("kv") % CORES

    def fetch(group):
        there = pl.ds(pl.multiple_of(core * half + group * slab, slab), slab)
        here = pl.ds(pl.multiple_of(group * slab, slab), slab)
        return pltpu.make_async_copy(q_hbm.at[:, there], q_ref.at[:, here], sems.at[group])

    there = pl.ds(pl.multiple_of(core * half, half), half)
    last = pltpu.make_async_copy(g_hbm.at[:, there], g_ref, sems.at[half // slab])
    for group in range(half // slab):
        fetch(group).start()
    last.start()
    fill_mask(members, near, blk_len, part_tok, bias_ref)

    @pl.loop(0, half // slab)
    def _(group):
        fetch(group).wait()
        units = [
            (head_columns(group * GROUP + i, head_dim), pl.ds(start, count), used)
            for i in range(GROUP)
            for start, count, used in near_tiles(rows, near)
        ]
        raws = [
            dot(q_ref[here, cols], near_rows(parts, 0, used, cols), NT) * base2_scale(head_dim)
            + bias_ref[here, : members * used]
            for cols, here, used in units
        ]
        peaks = [jnp.max(raw, axis=1, keepdims=True) for raw in raws]
        weights = [jnp.exp2(raw - peak) for raw, peak in zip(raws, peaks)]
        totals = [jnp.sum(weight, axis=1, keepdims=True) for weight in weights]
        sums = [
            dot(weight.astype(jnp.bfloat16), near_rows(parts, 1, used, cols), NN)
            for weight, (cols, here, used) in zip(weights, units)
        ]
        for (cols, here, used), peak, total, summed in zip(units, peaks, totals, sums):
            level = peak + jnp.log2(total)
            stat_ref[here, cols] = jnp.broadcast_to(level, summed.shape)
            out_ref[here, cols] = summed * (1.0 / total)

    last.wait()


def far_rows(parts, which, cols):
    rows = []
    for pair_ref, column_ref in zip(parts[0::2], parts[1::2]):
        steps, cores, _, part_tok, _ = column_ref.shape
        rows.append(pair_ref[:, which, :, cols].reshape(cores * part_tok, cols.size))
        rows.append(column_ref[:, :, which, :, cols].reshape(steps * cores * part_tok, cols.size))
    return jnp.concatenate(rows, axis=0)


def far_kernel(groups, steps, head_dim, tile, heads, batch, q_ref, g_ref, sum_ref, stat_ref, *refs):
    parts = refs[: 2 * COLUMNS * groups]
    att_ref, gq_ref, level_ref, drift_ref, *grad_refs = refs[2 * COLUMNS * groups :]
    _, cores, _, part_tok, _ = grad_refs[0].shape
    rows, half = q_ref.shape
    span = steps * cores * part_tok
    width = COLUMNS * span
    score_scale = 1.0 / math.sqrt(head_dim)
    window = lax.axis_index("seq")
    level, side = window // COLUMNS, window % COLUMNS
    step = lax.broadcasted_iota(jnp.int32, (1, span), 1) >> ((cores * part_tok).bit_length() - 1)
    valid = [(step >= 1) & (step <= level), (step >= 1 - side) & (step <= level)]
    bias = jnp.concatenate([jnp.where(ok, 0.0, HIDDEN) for ok in valid] * groups, axis=1)
    total_width = groups * width

    def work(units, keys, values, key_grads, value_grads):
        raws = [
            dot(q_ref[here, cols], keys[i], NT) * base2_scale(head_dim) + bias
            for i, cols, here in units
        ]
        grad_probs = [dot(g_ref[here, cols], values[i], NT) for i, cols, here in units]
        near_levels = [stat_ref[here, cols] for i, cols, here in units]
        peaks = [
            jnp.maximum(near_level, jnp.max(raw, axis=1, keepdims=True))
            for near_level, raw in zip(near_levels, raws)
        ]
        near_weights = [jnp.exp2(near_level - peak) for near_level, peak in zip(near_levels, peaks)]
        weights = [jnp.exp2(raw - wide(peak, total_width)) for raw, peak in zip(raws, peaks)]
        totals = [
            near_weight + jnp.sum(weight, axis=1, keepdims=True)
            for near_weight, weight in zip(near_weights, weights)
        ]
        inverses = [1.0 / total for total in totals]
        sums = [
            dot(weight.astype(jnp.bfloat16), values[i], NN)
            for weight, (i, cols, here) in zip(weights, units)
        ]
        drifts = []
        for u, (i, cols, here) in enumerate(units):
            summed = sum_ref[here, cols] * near_weights[u] + sums[u]
            attended = (summed * inverses[u]).astype(jnp.bfloat16)
            att_ref[here, cols] = attended
            product = g_ref[here, cols].astype(jnp.float32) * attended.astype(jnp.float32)
            drift = jnp.broadcast_to(jnp.sum(product, axis=1, keepdims=True), product.shape)
            drifts.append(drift)
            level_ref[here, cols] = peaks[u] + jnp.log2(totals[u])
            drift_ref[here, cols] = drift
        moved = [
            weight * (grad_prob - wide(drift, total_width))
            for weight, grad_prob, drift in zip(weights, grad_probs, drifts)
        ]
        factors = [inverse * score_scale for inverse in inverses]
        own_scores = [
            (part[:, :width] * wide(factor, width)).astype(jnp.bfloat16)
            for part, factor in zip(moved, factors)
        ]
        own_probs = [
            (weight[:, :width] * wide(inverse, width)).astype(jnp.bfloat16)
            for weight, inverse in zip(weights, inverses)
        ]
        for u, (i, cols, here) in enumerate(units):
            gq_ref[here, cols] = dot(moved[u].astype(jnp.bfloat16), keys[i], NN) * factors[u]
        for u, (i, cols, here) in enumerate(units):
            key_grads[i].append(dot(own_scores[u], q_ref[here, cols], TN))
            value_grads[i].append(dot(own_probs[u], g_ref[here, cols], TN))

    @pl.loop(0, half // (heads * head_dim))
    def _(group):
        columns = [head_columns(group * heads + i, head_dim) for i in range(heads)]
        units = [
            (i, cols, pl.ds(r, tile)) for i, cols in enumerate(columns) for r in range(0, rows, tile)
        ]
        keys = [far_rows(parts, 0, cols) for cols in columns]
        values = [far_rows(parts, 1, cols) for cols in columns]
        grads = [[[] for _ in columns] for _ in range(2)]
        for first in range(0, len(units), batch):
            work(units[first : first + batch], keys, values, *grads)
        for which, per_head in enumerate(grads):
            for cols, terms in zip(columns, per_head):
                total = functools.reduce(lambda a, b: a + b, terms).astype(jnp.bfloat16)
                start = 0
                for ref in grad_refs:
                    shape = ref.shape[:2] + (part_tok, head_dim)
                    count = math.prod(shape[:3])
                    ref[:, :, which, :, cols] = total[start : start + count].reshape(shape)
                    start += count


def near_backward_kernel(members, head_dim, blocks, block_ref, bias_ref, q_ref, g_ref, level_ref, drift_ref, far_gq_ref, *refs):
    parts, outs = refs[:members], refs[members:]
    chosen_ref, kept_ref, gq_ref, sent_ref, grad_ref = outs
    rows, half = q_ref.shape
    near = parts[0].shape[1]
    score_scale = 1.0 / math.sqrt(head_dim)

    @pl.loop(0, half // (GROUP * head_dim))
    def _(group):
        units = [
            (head_columns(group * GROUP + i, head_dim), pl.ds(start, count), used)
            for i in range(GROUP)
            for start, count, used in near_tiles(rows, near)
        ]
        keys = [near_rows(parts, 0, used, cols) for cols, here, used in units]
        values = [near_rows(parts, 1, used, cols) for cols, here, used in units]
        raws = [
            dot(q_ref[here, cols], key, NT) * base2_scale(head_dim)
            + bias_ref[here, : members * used]
            for (cols, here, used), key in zip(units, keys)
        ]
        grad_probs = [
            dot(g_ref[here, cols], value, NT) for (cols, here, used), value in zip(units, values)
        ]
        probs = [
            jnp.exp2(raw - wide(level_ref[here, cols], raw.shape[1]))
            for raw, (cols, here, used) in zip(raws, units)
        ]
        moved = [
            prob * (grad_prob - wide(drift_ref[here, cols], prob.shape[1]))
            for prob, grad_prob, (cols, here, used) in zip(probs, grad_probs, units)
        ]
        for (cols, here, used), part, key in zip(units, moved, keys):
            gq_ref[here, cols] = (
                dot(part.astype(jnp.bfloat16), key, NN) * score_scale + far_gq_ref[here, cols]
            ).astype(jnp.bfloat16)
        grads = []
        for (cols, here, used), part, prob in zip(units, moved, probs):
            own_score = (part[:, : CORES * used] * score_scale).astype(jnp.bfloat16)
            own_prob = prob[:, : CORES * used].astype(jnp.bfloat16)
            grads.append((dot(own_score, q_ref[here, cols], TN), dot(own_prob, g_ref[here, cols], TN)))
        low = near // 2
        for (cols, _, _), early, late in zip(units[0::2], grads[0::2], grads[1::2]):
            for which in range(2):
                for core in range(CORES):
                    top = late[which][core * near : core * near + low]
                    top += early[which][core * low : (core + 1) * low]
                    bottom = late[which][core * near + low : (core + 1) * near]
                    grad_ref[core, which, :low, cols] = top
                    grad_ref[core, which, low:, cols] = bottom
                    ref, first = (kept_ref, sent_ref)[core], which * near
                    ref[first : first + low, cols] = top.astype(ref.dtype)
                    ref[first + low : first + near, cols] = bottom.astype(ref.dtype)

    part_tok = near // blocks
    block = jnp.max(jnp.max(block_ref[...], axis=1, keepdims=True), axis=0, keepdims=True)
    for core in range(CORES):
        for which in range(2):
            chosen = grad_ref[core, which, :part_tok]
            for b in range(1, blocks):
                rows_b = grad_ref[core, which, b * part_tok : (b + 1) * part_tok]
                chosen = jnp.where(block == b, rows_b, chosen)
            chosen_ref[core, which] = chosen


def call(kernel, operands, outs, pairs, products, head_dim, in_specs=None, scratch=()):
    moved_bytes = sum(a.size * a.dtype.itemsize for a in operands)
    return pl.pallas_call(
        kernel,
        in_specs=in_specs or [WHOLE] * len(operands),
        out_specs=[WHOLE] * len(outs),
        out_shape=outs,
        scratch_shapes=scratch,
        compiler_params=LIMIT,
        cost_estimate=pl.CostEstimate(
            flops=4 * products * pairs * head_dim, bytes_accessed=moved_bytes, transcendentals=pairs
        ),
    )(*operands)


def shards(queries, keys, values, layout, grad_out):
    seq_count = lax.axis_size("seq")
    members = lax.axis_size("kv")
    tok_rows, feat_width = queries.shape
    blocks, part_tok = (keys.shape[0], keys.shape[1])
    blk_len = part_tok * members
    near = blocks * part_tok
    head_dim = feat_width // HEADS
    half = feat_width // CORES
    levels = seq_count // COLUMNS
    groups = members // CORES

    def hop(part, column_step, member_step):
        pairs = [
            (s * members + m, (s ^ column_step) * members + (m ^ member_step))
            for s in range(seq_count)
            for m in range(members)
        ]
        return lax.ppermute(part, ("seq", "kv"), pairs)

    def climb(part, d):
        return lax.ppermute(
            part, "seq", [(s, s + COLUMNS * d) for s in range(seq_count - COLUMNS * d)]
        )

    def sink(part, d):
        return lax.ppermute(
            part, "seq", [(s, s - COLUMNS * d) for s in range(COLUMNS * d, seq_count)]
        )

    mine, theirs, pair_mine, pair_theirs, block = pick_pair(layout.T, keys, values)
    own_pair = jnp.stack([pair_mine, hop(pair_theirs, 0, 1)])
    climbed = [climb(own_pair, d) for d in range(1, levels)]
    column = jnp.stack(climbed)
    chip_parts = [mine, hop(theirs, 0, 1)]
    near_parts = list(chip_parts)
    for group in range(1, groups):
        near_parts += [hop(part, 0, CORES * group) for part in chip_parts]
    sent_pair, _ = lax.optimization_barrier((own_pair, chip_parts[1]))
    cross_pairs = [hop(sent_pair, 1, CORES * group) for group in range(groups)]
    column, near_parts = lax.optimization_barrier((column, near_parts))
    near_parts = [part.reshape(2, near, half) for part in near_parts]
    crossing = [
        [column if (c, group) == (0, 0) else hop(column, c, CORES * group) for c in range(COLUMNS)]
        for group in range(groups)
    ]

    def rows_out(dtype):
        return pltpu.VMEM((tok_rows, half), dtype)

    def far_out(count):
        return pltpu.VMEM((count,) + own_pair.shape, jnp.bfloat16)

    low = 1
    near_pairs = HEADS // CORES * tok_rows * members * near
    far_width = members * seq_count * part_tok
    far_pairs = HEADS // CORES * tok_rows * far_width
    roomy = far_width <= 512
    far_plan = (tok_rows // 2, HEADS // CORES, 2 * GROUP) if roomy else (tok_rows // 8, 1, 1)

    near_sum, near_stat, bias, queries, grad_out = call(
        functools.partial(near_forward_kernel, members, blk_len, part_tok, head_dim),
        [pltpu.with_memory_space_constraint(a, pltpu.HBM) for a in (queries, grad_out)] + near_parts,
        [rows_out(jnp.float32)] * 2
        + [pltpu.VMEM((tok_rows, members * near), jnp.float32)]
        + [rows_out(jnp.bfloat16)] * 2,
        near_pairs,
        2,
        head_dim,
        [IN_HBM, IN_HBM] + [WHOLE] * members,
        [pltpu.SemaphoreType.DMA((half // (GROUP * head_dim) + 1,))],
    )
    far_parts = []
    for group, cross_pair in zip(crossing, cross_pairs):
        (same, other), _ = lax.optimization_barrier((group, near_stat))
        far_parts += [own_pair, same, cross_pair, other]
    attended, far_gq, level, drift, own_grad, cross_grad = call(
        functools.partial(far_kernel, groups, levels, head_dim, *far_plan),
        [queries, grad_out, near_sum, near_stat] + far_parts,
        [rows_out(jnp.bfloat16)]
        + [rows_out(jnp.float32)] * 3
        + [far_out(levels)] * COLUMNS,
        far_pairs,
        5,
        head_dim,
    )

    def add(own, cross):
        return (own.astype(jnp.float32) + cross.astype(jnp.float32)).astype(jnp.bfloat16)

    cross_low, cross_high = cross_grad[:low], cross_grad[low:]
    high = hop(cross_high, 1, 0)
    chosen, near_kept, grad_q, sent = call(
        functools.partial(near_backward_kernel, members, head_dim, blocks),
        [block, bias, queries, grad_out, level, drift, far_gq] + near_parts,
        [
            pltpu.VMEM((CORES, 2, part_tok, half), jnp.float32),
            pltpu.VMEM((2 * near, half), jnp.bfloat16),
            rows_out(jnp.bfloat16),
            pltpu.VMEM((2 * near, half), jnp.bfloat16),
        ],
        near_pairs,
        4,
        head_dim,
        scratch=[pltpu.VMEM((CORES, 2, near, half), jnp.float32)],
    )
    att_far = hop(attended, 0, 1)
    high, _, _ = lax.optimization_barrier((high, chosen, att_far))
    sums = [add(own_grad[d], high[d - low]) for d in range(low, levels)]
    nothing = high[0, 0, 0, 0][None] * 0
    grad_q = grad_q + nothing
    gq_far = hop(grad_q, 0, 1)
    sent_far = hop(sent + nothing, 0, 1)
    cross_low, _ = lax.optimization_barrier((cross_low, sent_far))
    crossed = hop(cross_low, 1, 0)
    sums = [add(own_grad[d], crossed[d]) for d in range(1, low)] + sums
    returned = [sink(part, d) for d, part in enumerate(sums, 1)] + [crossed[0]]
    attended, grad_q, grad_k, grad_v = join(
        [attended, att_far, grad_q, gq_far, near_kept, sent_far],
        [(tok_rows, feat_width)] * 2 + [(near, feat_width)] * 2,
    )
    returned, grad_k, grad_v = lax.optimization_barrier((returned, grad_k, grad_v))
    far_sent = chosen[1] + sum(part[1].astype(jnp.float32) for part in returned)
    far_sent = far_sent.astype(jnp.bfloat16)
    grad_k, grad_v = finish(
        [block, chosen, hop(far_sent, 0, 1)] + returned, [grad_k, grad_v]
    )
    return (attended, grad_q, grad_k.reshape(keys.shape), grad_v.reshape(values.shape))


def solution(mesh):
    return jax.shard_map(
        shards,
        mesh=mesh,
        in_specs=(P("seq", None), P("seq", "kv", None), P("seq", "kv", None), P(), P("seq", None)),
        out_specs=(P("seq", None), P("seq", None), P("seq", "kv", None), P("seq", "kv", None)),
        check_vma=False,
    )
```

```python
import functools
import math

import jax
import jax.numpy as jnp
from jax import lax
from jax.experimental import pallas as pl
from jax.experimental.pallas import tpu as pltpu
from jax.sharding import PartitionSpec as P

HEADS = 8
COLUMNS = 2
CORES = 2
GROUP = 2
SMALL = pl.CostEstimate(flops=0, bytes_accessed=0, transcendentals=0)
HIDDEN = -1e30
NT = (((1,), (1,)), ((), ()))
NN = (((1,), (0,)), ((), ()))
TN = (((0,), (0,)), ((), ()))
IN_HBM = pl.BlockSpec(memory_space=pltpu.HBM)
WHOLE = pl.BlockSpec(memory_space=pltpu.VMEM)
LIMIT = pltpu.CompilerParams(vmem_limit_bytes=12 * 1024 * 1024)


def dot(a, b, dims):
    return lax.dot_general(a, b, dims, preferred_element_type=jnp.float32)


def wide(rows, width):
    return jnp.concatenate([rows] * (width // rows.shape[1]), axis=1)


def base2_scale(head_dim):
    return math.log2(math.e) / math.sqrt(head_dim)


def pick_kernel(table_hbm, keys_hbm, values_hbm, mine_ref, theirs_ref, pair_ref, sent_ref, block_ref, table_ref, sems):
    window = lax.axis_index("seq")
    core = lax.axis_index("kv") % CORES
    _, blocks, part_tok, half = mine_ref.shape
    copies = [pltpu.make_async_copy(table_hbm, table_ref, sems.at[0])]
    for which, ref in enumerate((keys_hbm, values_hbm)):
        for side, out_ref in enumerate((mine_ref, theirs_ref)):
            cols = pl.ds(pl.multiple_of((core ^ side) * half, half), half)
            copies.append(
                pltpu.make_async_copy(ref.at[:, :, cols], out_ref.at[which], sems.at[len(copies)])
            )
    for copy in copies:
        copy.start()
    copies[0].wait()
    pick = jnp.minimum(window, lax.axis_size("seq") - 2)
    entry = lax.broadcasted_iota(jnp.int32, table_ref.shape, 0)
    row = lax.broadcasted_iota(jnp.int32, table_ref.shape, 1)
    here = (entry == pick) & (row == table_ref.shape[1] - 1)
    named = jnp.where(here, table_ref[...].astype(jnp.float32), -1.0)
    named = jnp.max(jnp.max(named, axis=1, keepdims=True), axis=0, keepdims=True)
    block = jnp.clip(named - (window * blocks).astype(jnp.float32), 0.0, blocks - 1.0)
    block_ref[...] = jnp.broadcast_to(block, block_ref.shape)
    block = jnp.broadcast_to(block, (part_tok, half))
    for copy in copies[1:]:
        copy.wait()
    for ref, out_ref in ((mine_ref, pair_ref), (theirs_ref, sent_ref)):
        for which in range(2):
            chosen = ref[which, 0].astype(jnp.float32)
            for b in range(1, blocks):
                chosen = jnp.where(block == b, ref[which, b].astype(jnp.float32), chosen)
            out_ref[which] = chosen.astype(out_ref.dtype)


def pick_pair(table, keys, values):
    blocks, part_tok, feat_width = keys.shape
    half = feat_width // CORES
    operands = [pltpu.with_memory_space_constraint(a, pltpu.HBM) for a in (table, keys, values)]
    return pl.pallas_call(
        pick_kernel,
        in_specs=[IN_HBM] * 3,
        out_specs=[WHOLE] * 5,
        out_shape=[pltpu.VMEM((2, blocks, part_tok, half), keys.dtype)] * 2
        + [pltpu.VMEM((2, part_tok, half), keys.dtype)] * 2
        + [pltpu.VMEM((8, 128), jnp.float32)],
        scratch_shapes=[pltpu.VMEM(table.shape, table.dtype), pltpu.SemaphoreType.DMA((5,))],
    )(*operands)


def join_kernel(att_ref, att_far, gq_ref, gq_far, kept_ref, near_far, att_out, gq_out, gk_out, gv_out, sems):
    core = lax.axis_index("kv") % CORES
    half, near = att_ref.shape[1], gk_out.shape[0]
    gk, gv = pl.ds(0, near), pl.ds(near, near)
    copies = []
    for out_ref, sides in (
        (att_out, (att_ref, att_far)),
        (gq_out, (gq_ref, gq_far)),
        (gk_out, (kept_ref.at[gk], near_far.at[gk])),
        (gv_out, (kept_ref.at[gv], near_far.at[gv])),
    ):
        for side, ref in enumerate(sides):
            cols = pl.ds(pl.multiple_of((core ^ side) * half, half), half)
            copies.append(pltpu.make_async_copy(ref, out_ref.at[:, cols], sems.at[len(copies)]))
    for copy in copies:
        copy.start()
    for copy in copies:
        copy.wait()


def join(operands, shapes):
    operands = [pltpu.with_memory_space_constraint(a, pltpu.VMEM) for a in operands]
    return pl.pallas_call(
        join_kernel,
        in_specs=[WHOLE] * len(operands),
        out_specs=[IN_HBM] * len(shapes),
        out_shape=[pltpu.HBM(shape, jnp.bfloat16) for shape in shapes],
        scratch_shapes=[pltpu.SemaphoreType.DMA((2 * len(shapes),))],
        cost_estimate=SMALL,
    )(*operands)


def finish_kernel(block_ref, chosen_ref, far_ref, *refs):
    arrived, outs, rows_ref, sems = refs[:-6], refs[-4:-2], refs[-2], refs[-1]
    core = lax.axis_index("kv") % CORES
    part_tok, half = far_ref.shape[1:]
    block = jnp.max(block_ref[...]).astype(jnp.int32)
    here = pl.ds(pl.multiple_of(block * part_tok, part_tok), part_tok)
    mine = pl.ds(pl.multiple_of(core * half, half), half)
    theirs = pl.ds(pl.multiple_of((core ^ 1) * half, half), half)
    copies = []
    for which, out_ref in enumerate(outs):
        total = chosen_ref[0, which]
        for ref in arrived:
            total += ref[0, which].astype(jnp.float32)
        rows_ref[which, :, mine] = total.astype(rows_ref.dtype)
        rows_ref[which, :, theirs] = far_ref[which]
        copies.append(pltpu.make_async_copy(rows_ref.at[which], out_ref.at[here], sems.at[which]))
        copies[-1].start()
    for copy in copies:
        copy.wait()


def finish(operands, outs):
    part_tok, half = operands[2].shape[1:]
    operands = [pltpu.with_memory_space_constraint(a, pltpu.VMEM) for a in operands]
    outs = [pltpu.with_memory_space_constraint(a, pltpu.HBM) for a in outs]
    return pl.pallas_call(
        finish_kernel,
        in_specs=[WHOLE] * len(operands) + [IN_HBM] * 2,
        out_specs=[IN_HBM] * 2,
        out_shape=[pltpu.HBM(a.shape, a.dtype) for a in outs],
        input_output_aliases={len(operands): 0, len(operands) + 1: 1},
        scratch_shapes=[
            pltpu.VMEM((2, part_tok, half * CORES), jnp.bfloat16),
            pltpu.SemaphoreType.DMA((2,)),
        ],
        cost_estimate=SMALL,
    )(*operands, *outs)


def near_tiles(rows, near):
    half = rows // 2
    return [(0, half, near // 2), (half, half, near)]


def fill_mask(members, near, blk_len, part_tok, bias_ref):
    member = lax.axis_index("kv")
    shift = part_tok.bit_length() - 1
    for start, count, used in near_tiles(bias_ref.shape[0], near):
        row = start + lax.broadcasted_iota(jnp.int32, (count, 1), 0)
        col = lax.broadcasted_iota(jnp.int32, (1, used), 1)
        key_tok = (col >> shift) * blk_len + (col & (part_tok - 1))
        for j in range(members):
            key_pos = key_tok + (member ^ j) * part_tok
            bias_ref[start : start + count, j * used : (j + 1) * used] = jnp.where(
                key_pos <= row, 0.0, HIDDEN
            )


def head_columns(head, head_dim):
    return pl.ds(pl.multiple_of(head * head_dim, head_dim), head_dim)


def near_rows(parts, which, used, cols):
    return jnp.concatenate([ref[which, :used, cols] for ref in parts], axis=0)


def near_forward_kernel(members, blk_len, part_tok, head_dim, q_hbm, g_hbm, *refs):
    parts, outs = refs[:members], refs[members:]
    out_ref, stat_ref, bias_ref, q_ref, g_ref, sems = outs
    rows, half = q_ref.shape
    near = parts[0].shape[1]
    slab = GROUP * head_dim
    core = lax.axis_index("kv") % CORES

    def fetch(group):
        there = pl.ds(pl.multiple_of(core * half + group * slab, slab), slab)
        here = pl.ds(pl.multiple_of(group * slab, slab), slab)
        return pltpu.make_async_copy(q_hbm.at[:, there], q_ref.at[:, here], sems.at[group])

    there = pl.ds(pl.multiple_of(core * half, half), half)
    last = pltpu.make_async_copy(g_hbm.at[:, there], g_ref, sems.at[half // slab])
    for group in range(half // slab):
        fetch(group).start()
    last.start()
    fill_mask(members, near, blk_len, part_tok, bias_ref)

    @pl.loop(0, half // slab)
    def _(group):
        fetch(group).wait()
        units = [
            (head_columns(group * GROUP + i, head_dim), pl.ds(start, count), used)
            for i in range(GROUP)
            for start, count, used in near_tiles(rows, near)
        ]
        raws = [
            dot(q_ref[here, cols], near_rows(parts, 0, used, cols), NT) * base2_scale(head_dim)
            + bias_ref[here, : members * used]
            for cols, here, used in units
        ]
        peaks = [jnp.max(raw, axis=1, keepdims=True) for raw in raws]
        weights = [jnp.exp2(raw - peak) for raw, peak in zip(raws, peaks)]
        totals = [jnp.sum(weight, axis=1, keepdims=True) for weight in weights]
        sums = [
            dot(weight.astype(jnp.bfloat16), near_rows(parts, 1, used, cols), NN)
            for weight, (cols, here, used) in zip(weights, units)
        ]
        for (cols, here, used), peak, total, summed in zip(units, peaks, totals, sums):
            level = peak + jnp.log2(total)
            stat_ref[here, cols] = jnp.broadcast_to(level, summed.shape)
            out_ref[here, cols] = summed * (1.0 / total)

    last.wait()


def far_rows(parts, which, cols):
    rows = []
    for pair_ref, column_ref in zip(parts[0::2], parts[1::2]):
        steps, cores, _, part_tok, _ = column_ref.shape
        rows.append(pair_ref[:, which, :, cols].reshape(cores * part_tok, cols.size))
        rows.append(column_ref[:, :, which, :, cols].reshape(steps * cores * part_tok, cols.size))
    return jnp.concatenate(rows, axis=0)


def far_kernel(groups, steps, head_dim, tile, heads, batch, q_ref, g_ref, sum_ref, stat_ref, *refs):
    parts = refs[: 2 * COLUMNS * groups]
    att_ref, gq_ref, level_ref, drift_ref, *grad_refs = refs[2 * COLUMNS * groups :]
    _, cores, _, part_tok, _ = grad_refs[0].shape
    rows, half = q_ref.shape
    span = steps * cores * part_tok
    width = COLUMNS * span
    score_scale = 1.0 / math.sqrt(head_dim)
    window = lax.axis_index("seq")
    level, side = window // COLUMNS, window % COLUMNS
    step = lax.broadcasted_iota(jnp.int32, (1, span), 1) >> ((cores * part_tok).bit_length() - 1)
    valid = [(step >= 1) & (step <= level), (step >= 1 - side) & (step <= level)]
    bias = jnp.concatenate([jnp.where(ok, 0.0, HIDDEN) for ok in valid] * groups, axis=1)
    total_width = groups * width

    def work(units, keys, values, key_grads, value_grads):
        raws = [
            dot(q_ref[here, cols], keys[i], NT) * base2_scale(head_dim) + bias
            for i, cols, here in units
        ]
        grad_probs = [dot(g_ref[here, cols], values[i], NT) for i, cols, here in units]
        near_levels = [stat_ref[here, cols] for i, cols, here in units]
        peaks = [
            jnp.maximum(near_level, jnp.max(raw, axis=1, keepdims=True))
            for near_level, raw in zip(near_levels, raws)
        ]
        near_weights = [jnp.exp2(near_level - peak) for near_level, peak in zip(near_levels, peaks)]
        weights = [jnp.exp2(raw - wide(peak, total_width)) for raw, peak in zip(raws, peaks)]
        totals = [
            near_weight + jnp.sum(weight, axis=1, keepdims=True)
            for near_weight, weight in zip(near_weights, weights)
        ]
        inverses = [1.0 / total for total in totals]
        sums = [
            dot(weight.astype(jnp.bfloat16), values[i], NN)
            for weight, (i, cols, here) in zip(weights, units)
        ]
        drifts = []
        for u, (i, cols, here) in enumerate(units):
            summed = sum_ref[here, cols] * near_weights[u] + sums[u]
            attended = (summed * inverses[u]).astype(jnp.bfloat16)
            att_ref[here, cols] = attended
            product = g_ref[here, cols].astype(jnp.float32) * attended.astype(jnp.float32)
            drift = jnp.broadcast_to(jnp.sum(product, axis=1, keepdims=True), product.shape)
            drifts.append(drift)
            level_ref[here, cols] = peaks[u] + jnp.log2(totals[u])
            drift_ref[here, cols] = drift
        moved = [
            weight * (grad_prob - wide(drift, total_width))
            for weight, grad_prob, drift in zip(weights, grad_probs, drifts)
        ]
        factors = [inverse * score_scale for inverse in inverses]
        own_scores = [
            (part[:, :width] * wide(factor, width)).astype(jnp.bfloat16)
            for part, factor in zip(moved, factors)
        ]
        own_probs = [
            (weight[:, :width] * wide(inverse, width)).astype(jnp.bfloat16)
            for weight, inverse in zip(weights, inverses)
        ]
        for u, (i, cols, here) in enumerate(units):
            gq_ref[here, cols] = dot(moved[u].astype(jnp.bfloat16), keys[i], NN) * factors[u]
        for u, (i, cols, here) in enumerate(units):
            key_grads[i].append(dot(own_scores[u], q_ref[here, cols], TN))
            value_grads[i].append(dot(own_probs[u], g_ref[here, cols], TN))

    @pl.loop(0, half // (heads * head_dim))
    def _(group):
        columns = [head_columns(group * heads + i, head_dim) for i in range(heads)]
        units = [
            (i, cols, pl.ds(r, tile)) for i, cols in enumerate(columns) for r in range(0, rows, tile)
        ]
        keys = [far_rows(parts, 0, cols) for cols in columns]
        values = [far_rows(parts, 1, cols) for cols in columns]
        grads = [[[] for _ in columns] for _ in range(2)]
        for first in range(0, len(units), batch):
            work(units[first : first + batch], keys, values, *grads)
        for which, per_head in enumerate(grads):
            for cols, terms in zip(columns, per_head):
                total = functools.reduce(lambda a, b: a + b, terms).astype(jnp.bfloat16)
                start = 0
                for ref in grad_refs:
                    shape = ref.shape[:2] + (part_tok, head_dim)
                    count = math.prod(shape[:3])
                    ref[:, :, which, :, cols] = total[start : start + count].reshape(shape)
                    start += count


def near_backward_kernel(members, head_dim, blocks, block_ref, bias_ref, q_ref, g_ref, level_ref, drift_ref, far_gq_ref, *refs):
    parts, outs = refs[:members], refs[members:]
    chosen_ref, kept_ref, gq_ref, sent_ref, grad_ref = outs
    rows, half = q_ref.shape
    near = parts[0].shape[1]
    score_scale = 1.0 / math.sqrt(head_dim)

    @pl.loop(0, half // (GROUP * head_dim))
    def _(group):
        units = [
            (head_columns(group * GROUP + i, head_dim), pl.ds(start, count), used)
            for i in range(GROUP)
            for start, count, used in near_tiles(rows, near)
        ]
        keys = [near_rows(parts, 0, used, cols) for cols, here, used in units]
        values = [near_rows(parts, 1, used, cols) for cols, here, used in units]
        raws = [
            dot(q_ref[here, cols], key, NT) * base2_scale(head_dim)
            + bias_ref[here, : members * used]
            for (cols, here, used), key in zip(units, keys)
        ]
        grad_probs = [
            dot(g_ref[here, cols], value, NT) for (cols, here, used), value in zip(units, values)
        ]
        probs = [
            jnp.exp2(raw - wide(level_ref[here, cols], raw.shape[1]))
            for raw, (cols, here, used) in zip(raws, units)
        ]
        moved = [
            prob * (grad_prob - wide(drift_ref[here, cols], prob.shape[1]))
            for prob, grad_prob, (cols, here, used) in zip(probs, grad_probs, units)
        ]
        for (cols, here, used), part, key in zip(units, moved, keys):
            gq_ref[here, cols] = (
                dot(part.astype(jnp.bfloat16), key, NN) * score_scale + far_gq_ref[here, cols]
            ).astype(jnp.bfloat16)
        grads = []
        for (cols, here, used), part, prob in zip(units, moved, probs):
            own_score = (part[:, : CORES * used] * score_scale).astype(jnp.bfloat16)
            own_prob = prob[:, : CORES * used].astype(jnp.bfloat16)
            grads.append((dot(own_score, q_ref[here, cols], TN), dot(own_prob, g_ref[here, cols], TN)))
        low = near // 2
        for (cols, _, _), early, late in zip(units[0::2], grads[0::2], grads[1::2]):
            for which in range(2):
                for core in range(CORES):
                    top = late[which][core * near : core * near + low]
                    top += early[which][core * low : (core + 1) * low]
                    bottom = late[which][core * near + low : (core + 1) * near]
                    grad_ref[core, which, :low, cols] = top
                    grad_ref[core, which, low:, cols] = bottom
                    ref, first = (kept_ref, sent_ref)[core], which * near
                    ref[first : first + low, cols] = top.astype(ref.dtype)
                    ref[first + low : first + near, cols] = bottom.astype(ref.dtype)

    part_tok = near // blocks
    block = jnp.max(jnp.max(block_ref[...], axis=1, keepdims=True), axis=0, keepdims=True)
    for core in range(CORES):
        for which in range(2):
            chosen = grad_ref[core, which, :part_tok]
            for b in range(1, blocks):
                rows_b = grad_ref[core, which, b * part_tok : (b + 1) * part_tok]
                chosen = jnp.where(block == b, rows_b, chosen)
            chosen_ref[core, which] = chosen


def call(kernel, operands, outs, pairs, products, head_dim, in_specs=None, scratch=()):
    moved_bytes = sum(a.size * a.dtype.itemsize for a in operands)
    return pl.pallas_call(
        kernel,
        in_specs=in_specs or [WHOLE] * len(operands),
        out_specs=[WHOLE] * len(outs),
        out_shape=outs,
        scratch_shapes=scratch,
        compiler_params=LIMIT,
        cost_estimate=pl.CostEstimate(
            flops=4 * products * pairs * head_dim, bytes_accessed=moved_bytes, transcendentals=pairs
        ),
    )(*operands)


def shards(queries, keys, values, layout, grad_out):
    seq_count = lax.axis_size("seq")
    members = lax.axis_size("kv")
    tok_rows, feat_width = queries.shape
    blocks, part_tok = (keys.shape[0], keys.shape[1])
    blk_len = part_tok * members
    near = blocks * part_tok
    head_dim = feat_width // HEADS
    half = feat_width // CORES
    levels = seq_count // COLUMNS
    groups = members // CORES

    def hop(part, column_step, member_step):
        pairs = [
            (s * members + m, (s ^ column_step) * members + (m ^ member_step))
            for s in range(seq_count)
            for m in range(members)
        ]
        return lax.ppermute(part, ("seq", "kv"), pairs)

    def climb(part, d):
        return lax.ppermute(
            part, "seq", [(s, s + COLUMNS * d) for s in range(seq_count - COLUMNS * d)]
        )

    def sink(part, d):
        return lax.ppermute(
            part, "seq", [(s, s - COLUMNS * d) for s in range(COLUMNS * d, seq_count)]
        )

    mine, theirs, pair_mine, pair_theirs, block = pick_pair(layout.T, keys, values)
    own_pair = jnp.stack([pair_mine, hop(pair_theirs, 0, 1)])
    climbed = [climb(own_pair, d) for d in range(1, levels)]
    column = jnp.stack(climbed)
    chip_parts = [mine, hop(theirs, 0, 1)]
    near_parts = list(chip_parts)
    for group in range(1, groups):
        near_parts += [hop(part, 0, CORES * group) for part in chip_parts]
    sent_pair, _ = lax.optimization_barrier((own_pair, chip_parts[1]))
    cross_pairs = [hop(sent_pair, 1, CORES * group) for group in range(groups)]
    column, near_parts = lax.optimization_barrier((column, near_parts))
    near_parts = [part.reshape(2, near, half) for part in near_parts]
    crossing = [
        [column if (c, group) == (0, 0) else hop(column, c, CORES * group) for c in range(COLUMNS)]
        for group in range(groups)
    ]

    def rows_out(dtype):
        return pltpu.VMEM((tok_rows, half), dtype)

    def far_out(count):
        return pltpu.VMEM((count,) + own_pair.shape, jnp.bfloat16)

    low = 1
    near_pairs = HEADS // CORES * tok_rows * members * near
    far_width = members * seq_count * part_tok
    far_pairs = HEADS // CORES * tok_rows * far_width
    roomy = far_width <= 512
    far_plan = (tok_rows // 2, HEADS // CORES, GROUP) if roomy else (tok_rows // 8, 1, 1)

    near_sum, near_stat, bias, queries, grad_out = call(
        functools.partial(near_forward_kernel, members, blk_len, part_tok, head_dim),
        [pltpu.with_memory_space_constraint(a, pltpu.HBM) for a in (queries, grad_out)] + near_parts,
        [rows_out(jnp.float32)] * 2
        + [pltpu.VMEM((tok_rows, members * near), jnp.float32)]
        + [rows_out(jnp.bfloat16)] * 2,
        near_pairs,
        2,
        head_dim,
        [IN_HBM, IN_HBM] + [WHOLE] * members,
        [pltpu.SemaphoreType.DMA((half // (GROUP * head_dim) + 1,))],
    )
    far_parts = []
    for group, cross_pair in zip(crossing, cross_pairs):
        (same, other), _ = lax.optimization_barrier((group, near_stat))
        far_parts += [own_pair, same, cross_pair, other]
    attended, far_gq, level, drift, own_grad, cross_grad = call(
        functools.partial(far_kernel, groups, levels, head_dim, *far_plan),
        [queries, grad_out, near_sum, near_stat] + far_parts,
        [rows_out(jnp.bfloat16)]
        + [rows_out(jnp.float32)] * 3
        + [far_out(levels)] * COLUMNS,
        far_pairs,
        5,
        head_dim,
    )

    def add(own, cross):
        return (own.astype(jnp.float32) + cross.astype(jnp.float32)).astype(jnp.bfloat16)

    cross_low, cross_high = cross_grad[:low], cross_grad[low:]
    high = hop(cross_high, 1, 0)
    chosen, near_kept, grad_q, sent = call(
        functools.partial(near_backward_kernel, members, head_dim, blocks),
        [block, bias, queries, grad_out, level, drift, far_gq] + near_parts,
        [
            pltpu.VMEM((CORES, 2, part_tok, half), jnp.float32),
            pltpu.VMEM((2 * near, half), jnp.bfloat16),
            rows_out(jnp.bfloat16),
            pltpu.VMEM((2 * near, half), jnp.bfloat16),
        ],
        near_pairs,
        4,
        head_dim,
        scratch=[pltpu.VMEM((CORES, 2, near, half), jnp.float32)],
    )
    att_far = hop(attended, 0, 1)
    high, _, _ = lax.optimization_barrier((high, chosen, att_far))
    sums = [add(own_grad[d], high[d - low]) for d in range(low, levels)]
    nothing = high[0, 0, 0, 0][None] * 0
    grad_q = grad_q + nothing
    gq_far = hop(grad_q, 0, 1)
    sent_far = hop(sent + nothing, 0, 1)
    cross_low, _ = lax.optimization_barrier((cross_low, sent_far))
    crossed = hop(cross_low, 1, 0)
    sums = [add(own_grad[d], crossed[d]) for d in range(1, low)] + sums
    returned = [sink(part, d) for d, part in enumerate(sums, 1)] + [crossed[0]]
    attended, grad_q, grad_k, grad_v = join(
        [attended, att_far, grad_q, gq_far, near_kept, sent_far],
        [(tok_rows, feat_width)] * 2 + [(near, feat_width)] * 2,
    )
    returned, grad_k, grad_v = lax.optimization_barrier((returned, grad_k, grad_v))
    far_sent = chosen[1] + sum(part[1].astype(jnp.float32) for part in returned)
    far_sent = far_sent.astype(jnp.bfloat16)
    grad_k, grad_v = finish(
        [block, chosen, hop(far_sent, 0, 1)] + returned, [grad_k, grad_v]
    )
    return (attended, grad_q, grad_k.reshape(keys.shape), grad_v.reshape(values.shape))


def solution(mesh):
    return jax.shard_map(
        shards,
        mesh=mesh,
        in_specs=(P("seq", None), P("seq", "kv", None), P("seq", "kv", None), P(), P("seq", None)),
        out_specs=(P("seq", None), P("seq", None), P("seq", "kv", None), P("seq", "kv", None)),
        check_vma=False,
    )
```
